32 devices in a mesh: grp: 4 (over x, core), seq: 8 (over z, y).
Axes of the slice: x: 2, y: 2, z: 4, core: 2. Of those that a mesh axis runs over, the one named last changes fastest.
Arguments:
- queries: bfloat16 [4096, 512], P(('grp', 'seq')), may hold values from -4.5 to 5.5
- key_vectors: bfloat16 [4096, 512], P(('grp', 'seq')), may hold values from -4.5 to 5.5
- value_vectors: bfloat16 [4096, 1024], P(('grp', 'seq')), may hold values from -6 to 6
- input_gate: float32 [4, 4096], P(None, ('grp', 'seq')), may hold values from -4 to 114
- forget_gate: float32 [4, 4096], P(None, ('grp', 'seq')), may hold values from -3 to 25
Outputs:
- hidden_states: bfloat16 [4096, 1024], P(('grp', 'seq'))
The draws below stay inside these ranges and needn't reach their ends.
All inputs are finite; a program needn't handle non-finite values.
Results may differ from the reference program's by a relative error of at most 0.028.
Values sent between devices are 32-bit elements; how exact they have to be, the bound alone decides.
No kernel may reach another device: no remote copies, remote signals or barrier semaphores. Data moves between devices by JAX's collectives and lax.ppermute only.
A program may use at most 64 MiB of HBM per device.

```python
import jax
import jax.numpy as jnp
from jax import lax

HEAD_GROUP = 4
KEY_DIM = 128
VAL_DIM = 256
TOK_DEV = 128
TOKEN_COUNT = 4096


def draw_queries(key, part):
    seed_one = jax.random.fold_in(key, 11)
    sample = jnp.clip(jax.random.normal(seed_one, (TOKEN_COUNT, HEAD_GROUP * KEY_DIM), jnp.float32), -5.0, 5.0)
    return (sample + 0.5).astype(jnp.bfloat16)


def draw_key_vectors(key, part):
    seed_one = jax.random.fold_in(key, 23)
    sample = jnp.clip(jax.random.normal(seed_one, (TOKEN_COUNT, HEAD_GROUP * KEY_DIM), jnp.float32), -5.0, 5.0)
    return (sample + 0.5).astype(jnp.bfloat16)


def draw_input_gate(key, part):
    gate_seeds = jax.random.split(jax.random.fold_in(key, 37), 2)
    token_part = jax.random.uniform(gate_seeds[0], (HEAD_GROUP, TOKEN_COUNT), jnp.float32, -4.0, 4.0)
    segment_length = max(TOK_DEV // 4, 1)
    level_offsets = jax.random.uniform(gate_seeds[1], (HEAD_GROUP, TOKEN_COUNT // segment_length), jnp.float32, 0.0, 100.0)
    sample = token_part + jnp.repeat(level_offsets, segment_length, axis=1)
    return sample


def draw_forget_gate(key, part):
    random_seeds = jax.random.split(jax.random.fold_in(key, 53), 6)
    slow_count = HEAD_GROUP // 2
    head_order = jax.random.permutation(random_seeds[0], HEAD_GROUP)
    lagging_variant = (head_order < slow_count)[:, None]
    blocks = TOKEN_COUNT // TOK_DEV
    block_factor = jnp.repeat(jnp.exp(jax.random.uniform(random_seeds[1], (HEAD_GROUP, blocks), jnp.float32, -0.7, 0.7)), TOK_DEV, axis=1)
    token_factor = jnp.exp(jax.random.uniform(random_seeds[2], (HEAD_GROUP, TOKEN_COUNT), jnp.float32, -0.7, 0.7))
    head_factor = jnp.exp(jax.random.uniform(random_seeds[3], (HEAD_GROUP, 1), jnp.float32, -0.5, 0.5))
    fast_rate = max(0.025, 3.0 / TOK_DEV)
    forget_factor = jnp.where(lagging_variant, 0.3 / TOKEN_COUNT, fast_rate) * head_factor * block_factor * token_factor
    spike_events = lagging_variant & (jax.random.uniform(random_seeds[4], (HEAD_GROUP, TOKEN_COUNT), jnp.float32) < 4.0 / TOKEN_COUNT)
    spike_factor = jax.random.uniform(random_seeds[5], (HEAD_GROUP, TOKEN_COUNT), jnp.float32, 0.22, 0.69)
    forget_factor = jnp.where(spike_events, spike_factor, forget_factor)
    return -forget_factor - jnp.log(-jnp.expm1(-forget_factor))


def block_levels(stream_key, shape, cuts, least, largest):
    def one(axis_at, blocks):
        steps = jax.random.uniform(jax.random.fold_in(jax.random.fold_in(stream_key, 6), axis_at), (blocks,), jnp.float32, least / len(cuts), largest / len(cuts))
        return jnp.repeat(jnp.exp(steps), shape[axis_at] // blocks).reshape((-1,) + (1,) * (len(shape) - axis_at - 1))

    loudness = one(*cuts[0])
    for cut in cuts[1:]:
        loudness = loudness * one(*cut)
    return loudness


def normal_values(key, shape, scale, bound, cuts=(), held_as=jnp.bfloat16):
    level = block_levels(key, shape, cuts, -0.22, 0.18) if cuts else 1.0
    array = jax.random.normal(key, shape, jnp.float32) * scale * level
    return jnp.minimum(jnp.maximum(array, -bound), bound).astype(held_as)


def setup_inputs(seed: int = 0) -> dict:
    key_of = jax.random.split(jax.random.key(seed), 6)
    queries = draw_queries(jax.random.fold_in(key_of[5], 71), 0)
    key_vectors = draw_key_vectors(jax.random.fold_in(key_of[5], 71), 0)
    value_vectors = normal_values(key_of[2], (TOKEN_COUNT, HEAD_GROUP * VAL_DIM), 1.0, 6.0, ((0, 32),))
    input_gate = draw_input_gate(jax.random.fold_in(key_of[5], 71), 0)
    forget_gate = draw_forget_gate(jax.random.fold_in(key_of[5], 71), 0)
    return dict(queries=queries, key_vectors=key_vectors, value_vectors=value_vectors, input_gate=input_gate, forget_gate=forget_gate)


exact_precision_mode = lax.Precision.HIGHEST
floor_value = -1.0e30


def combine_states(earlier, later):
    early_matrix, early_vector, early_top, early_decay = earlier
    late_matrix, late_vector, late_top, late_decay = later
    joined = jnp.maximum(early_top + late_decay, late_top)
    early_weight = jnp.exp(early_top + late_decay - joined)
    late_weight = jnp.exp(late_top - joined)
    new_matrix = early_weight[..., None, None] * early_matrix + late_weight[..., None, None] * late_matrix
    new_vector = early_weight[..., None] * early_vector + late_weight[..., None] * late_vector
    return (new_matrix, new_vector, joined, early_decay + late_decay)


def block_step(prefix, pieces):
    query_block, key_block, value_block, in_gate, fo_gate = pieces
    length = query_block.shape[0]
    query_scaling = KEY_DIM ** -0.5
    query_widened = query_block.astype(jnp.float32).reshape(length, HEAD_GROUP, KEY_DIM).transpose(1, 0, 2)
    key_widened = key_block.astype(jnp.float32).reshape(length, HEAD_GROUP, KEY_DIM).transpose(1, 0, 2)
    value_widened = value_block.astype(jnp.float32).reshape(length, HEAD_GROUP, VAL_DIM).transpose(1, 0, 2)
    cumulative = jnp.cumsum(jax.nn.log_sigmoid(fo_gate), axis=1)
    block_decay = cumulative[:, -1]
    weight_log = block_decay[:, None] - cumulative + in_gate
    block_top = jnp.max(weight_log, axis=1)
    weight_tensor = jnp.exp(weight_log - block_top[:, None])
    memory_matrix = jnp.einsum("cdx,cdn->cxn", key_widened, weight_tensor[:, :, None] * value_widened, precision=exact_precision_mode)
    vector = jnp.einsum("hsk,hs->hk", key_widened, weight_tensor, precision=exact_precision_mode)
    local_state = (memory_matrix, vector, block_top, block_decay)
    scores = jnp.einsum("htk,hsk->hts", query_widened, key_widened, precision=exact_precision_mode) * query_scaling
    log_decay = cumulative[:, :, None] - cumulative[:, None, :] + in_gate[:, None, :]
    rows = lax.broadcasted_iota(jnp.int32, (length, length), 0)
    cols = lax.broadcasted_iota(jnp.int32, (length, length), 1)
    log_decay = jnp.where((rows >= cols)[None], log_decay, -jnp.inf)
    row_top = jnp.max(log_decay, axis=2)
    weighted = jnp.exp(log_decay - row_top[:, :, None]) * scores
    inner_den = jnp.sum(weighted, axis=2)
    weighted_bf = lax.optimization_barrier(weighted.astype(jnp.bfloat16))
    inner_num = jnp.einsum("hts,hsv->htv", weighted_bf.astype(jnp.float32), value_widened, precision=exact_precision_mode)
    previous_memory_matrix, prev_vector, prev_top, prev_decay = prefix
    stab = jnp.maximum(cumulative + prev_top[:, None], row_top)
    inner_factor = jnp.exp(row_top - stab)
    outer_factor = jnp.exp(cumulative + prev_top[:, None] - stab)
    carried_numerator = jnp.einsum("cps,csz->cpz", query_widened, previous_memory_matrix, precision=exact_precision_mode) * query_scaling
    carried_den = jnp.einsum("htk,hk->ht", query_widened, prev_vector, precision=exact_precision_mode) * query_scaling
    numer = inner_factor[:, :, None] * inner_num + outer_factor[:, :, None] * carried_numerator
    denom = inner_factor * inner_den + outer_factor * carried_den
    output = numer / jnp.maximum(jnp.abs(denom), jnp.exp(-stab))[:, :, None]
    output = output.transpose(1, 0, 2).reshape(length, HEAD_GROUP * VAL_DIM).astype(jnp.bfloat16)
    return combine_states(prefix, local_state), output


def reference(queries, key_vectors, value_vectors, input_gate, forget_gate):
    blocks = TOKEN_COUNT // TOK_DEV
    query_blocks = queries.reshape(blocks, TOK_DEV, HEAD_GROUP * KEY_DIM)
    key_blocks = key_vectors.reshape(blocks, TOK_DEV, HEAD_GROUP * KEY_DIM)
    value_blocks = value_vectors.reshape(blocks, TOK_DEV, HEAD_GROUP * VAL_DIM)
    in_blocks = input_gate.reshape(HEAD_GROUP, blocks, TOK_DEV).transpose(1, 0, 2)
    fo_blocks = forget_gate.reshape(HEAD_GROUP, blocks, TOK_DEV).transpose(1, 0, 2)
    start = (jnp.zeros((HEAD_GROUP, KEY_DIM, VAL_DIM), jnp.float32), jnp.zeros((HEAD_GROUP, KEY_DIM), jnp.float32),
             jnp.full((HEAD_GROUP,), floor_value, jnp.float32), jnp.zeros((HEAD_GROUP,), jnp.float32))
    final_state, outputs = lax.scan(block_step, start, (query_blocks, key_blocks, value_blocks, in_blocks, fo_blocks))
    return outputs.reshape(TOKEN_COUNT, HEAD_GROUP * VAL_DIM)
```

```python
import functools

import jax
import jax.numpy as jnp
from jax import lax
from jax.experimental import pallas as pl
from jax.experimental.pallas import tpu as pltpu
from jax.sharding import PartitionSpec as P

floor_value = -1e30
LANES = 128
AXES = ("grp", "seq")


def split_two(x):
    high = x.astype(jnp.bfloat16)
    low = (x - high.astype(jnp.float32)).astype(jnp.bfloat16)
    return high, low


def split_three(x):
    high = x.astype(jnp.bfloat16)
    rest = x - high.astype(jnp.float32)
    mid = rest.astype(jnp.bfloat16)
    low = (rest - mid.astype(jnp.float32)).astype(jnp.bfloat16)
    return high, mid, low


def dot(a, b):
    return jnp.dot(a, b, preferred_element_type=jnp.float32)


def dot_last(a, b):
    return lax.dot_general(a, b, (((1,), (1,)), ((), ())), preferred_element_type=jnp.float32)


def log_forget(forget):
    return jnp.minimum(forget, 0.0) - jnp.log1p(jnp.exp(-jnp.abs(forget)))


def triangle(length, lower):
    rows = lax.broadcasted_iota(jnp.int32, (length, length), 0)
    cols = lax.broadcasted_iota(jnp.int32, (length, length), 1)
    return rows >= cols if lower else rows <= cols


def cumulative_rows(logf):
    ones = triangle(logf.shape[1], False).astype(jnp.bfloat16)
    high, mid, low = split_three(logf)
    return (dot(low, ones) + dot(mid, ones)) + dot(high, ones)


def cumulative_columns(logf):
    ones = triangle(logf.shape[1], True).astype(jnp.bfloat16)
    high, mid, low = split_three(logf)
    return (dot_last(ones, low) + dot_last(ones, mid)) + dot_last(ones, high)


def state_kernel(key_rows, k_ref, v_ref, in_ref, fo_ref, msg_ref):
    heads, length = in_ref.shape
    key_dim = k_ref.shape[1] // heads
    value_dim = v_ref.shape[1] // heads
    parts = value_dim // LANES
    per_head = key_dim // key_rows
    matrix_rows = parts * key_rows
    pad_rows = msg_ref.shape[1] - matrix_rows - 3
    cumul = cumulative_rows(log_forget(fo_ref[...]))
    level = in_ref[...] - cumul
    level_top = jnp.max(level, axis=1, keepdims=True)
    weight = jnp.exp(level - level_top)
    decay = cumul[:, length - 1 : length]
    top = decay + level_top
    for head in range(heads):
        keys = k_ref[:, head * key_dim : (head + 1) * key_dim]
        values = v_ref[:, head * value_dim : (head + 1) * value_dim]
        row = weight[head : head + 1, :]
        high, low = split_two(keys.astype(jnp.float32).T * row)
        matrix = dot(
            jnp.concatenate([high, low], axis=1), jnp.concatenate([values, values], axis=0)
        )
        high, mid, low = split_three(row)
        vector = (dot(low, keys) + dot(mid, keys)) + dot(high, keys)
        tail = [
            vector,
            jnp.broadcast_to(top[head : head + 1, :], (1, key_dim)),
            jnp.broadcast_to(decay[head : head + 1, :], (1, key_dim)),
        ]
        if pad_rows:
            tail.append(jnp.zeros((pad_rows, key_dim), jnp.float32))
        tail = jnp.concatenate(tail, axis=0)
        for piece in range(per_head):
            slot = head * per_head + piece
            for part in range(parts):
                msg_ref[slot, part * key_rows : (part + 1) * key_rows, :] = matrix[
                    piece * key_rows : (piece + 1) * key_rows, part * LANES : (part + 1) * LANES
                ]
            msg_ref[slot, matrix_rows:, :] = tail


def scan_kernel(matrix_rows, in_ref, out_ref):
    count, rows, lanes = in_ref.shape
    at_top = lax.broadcasted_iota(jnp.int32, (rows, lanes), 0) == matrix_rows + 1

    def step(block, carry):
        state, top = carry
        out_ref[block] = jnp.where(at_top, top, state)
        piece = in_ref[block]
        own_top = piece[matrix_rows + 1 : matrix_rows + 2, :]
        moved = top + piece[matrix_rows + 2 : matrix_rows + 3, :]
        joined = jnp.maximum(moved, own_top)
        state = jnp.exp(moved - joined) * state + jnp.exp(own_top - joined) * piece
        return state, joined

    carry = (
        jnp.zeros((rows, lanes), jnp.float32),
        jnp.full((1, lanes), floor_value, jnp.float32),
    )
    lax.fori_loop(0, count, step, carry, unroll=min(count, 32))


def inner_kernel(q_ref, k_ref, v_ref, in_ref, fo_ref, num_ref, stat_ref):
    heads, length = in_ref.shape
    key_dim = q_ref.shape[1] // heads
    value_dim = v_ref.shape[1] // heads
    logf = log_forget(fo_ref[...])
    level = in_ref[...] - cumulative_rows(logf)
    stat_ref[:, 0:heads] = cumulative_columns(logf)
    causal = triangle(length, True)
    for head in range(heads):
        queries = q_ref[:, head * key_dim : (head + 1) * key_dim]
        keys = k_ref[:, head * key_dim : (head + 1) * key_dim]
        values = v_ref[:, head * value_dim : (head + 1) * value_dim]
        scores = dot_last(queries, keys) * (key_dim**-0.5)
        masked = jnp.where(causal, level[head : head + 1, :], -jnp.inf)
        row_level = jnp.max(masked, axis=1, keepdims=True)
        weighted = jnp.exp(masked - row_level) * scores
        stat_ref[:, heads + head : heads + head + 1] = row_level
        stat_ref[:, 2 * heads + head : 2 * heads + head + 1] = jnp.sum(
            weighted, axis=1, keepdims=True
        )
        num_ref[:, head * value_dim : (head + 1) * value_dim] = dot(
            weighted.astype(jnp.bfloat16), values
        )


def outer_kernel(key_rows, q_ref, msg_ref, num_ref, stat_ref, out_ref, left_ref):
    count, rows, _ = msg_ref.shape
    heads = stat_ref.shape[1] // 3
    key_dim = q_ref.shape[1] // heads
    value_dim = num_ref.shape[1] // heads
    parts = value_dim // LANES
    per_head = key_dim // key_rows
    matrix_rows = parts * key_rows
    scaling = key_dim**-0.5
    for head in range(heads):
        first = head * per_head
        columns = []
        for part in range(parts):
            place = slice(part * key_rows, (part + 1) * key_rows)
            if key_rows % 8 == 0:
                columns.append(
                    msg_ref[first : first + per_head, place, :].reshape(key_dim, LANES)
                )
            else:
                for piece in range(per_head):
                    left_ref[piece * key_rows : (piece + 1) * key_rows, :] = msg_ref[
                        first + piece, place, :
                    ]
                columns.append(left_ref[...])
        high, low = split_two(jnp.concatenate(columns, axis=1))
        queries = q_ref[:, head * key_dim : (head + 1) * key_dim]
        carried = dot(
            jnp.concatenate([queries, queries], axis=1), jnp.concatenate([high, low], axis=0)
        )
        vector = msg_ref[first, matrix_rows : matrix_rows + 1, :]
        top = msg_ref[first, matrix_rows + 1 : matrix_rows + 2, 0:1]
        carried_den = jnp.sum(queries.astype(jnp.float32) * vector, axis=1, keepdims=True)
        cumul = stat_ref[:, head : head + 1]
        row_level = stat_ref[:, heads + head : heads + head + 1]
        inner_den = stat_ref[:, 2 * heads + head : 2 * heads + head + 1]
        joined = jnp.maximum(row_level, top)
        inner_factor = jnp.exp(row_level - joined)
        outer_factor = jnp.exp(top - joined) * scaling
        denom = inner_factor * inner_den + outer_factor * carried_den
        floor = jnp.exp(-(cumul + joined))
        inverse = 1.0 / jnp.maximum(jnp.abs(denom), floor)
        numer = (
            inner_factor * num_ref[:, head * value_dim : (head + 1) * value_dim]
            + outer_factor * carried
        )
        out_ref[:, head * value_dim : (head + 1) * value_dim] = (numer * inverse).astype(
            out_ref.dtype
        )


def on_device(device_count, queries, key_vectors, value_vectors, input_gate, forget_gate):
    heads, length = input_gate.shape
    key_dim = queries.shape[1] // heads
    value_dim = value_vectors.shape[1] // heads
    key_rows = heads * key_dim // device_count
    matrix_rows = (value_dim // LANES) * key_rows
    rows = -(-(matrix_rows + 3) // 8) * 8
    message = jax.ShapeDtypeStruct((device_count, rows, LANES), jnp.float32)
    params = pltpu.CompilerParams(vmem_limit_bytes=48 * 1024 * 1024)

    own = pl.pallas_call(
        functools.partial(state_kernel, key_rows), out_shape=message, compiler_params=params
    )(key_vectors, value_vectors, input_gate, forget_gate)
    gathered = lax.all_to_all(own, AXES, 0, 0)
    inner_num, stats = pl.pallas_call(
        inner_kernel,
        out_shape=(
            jax.ShapeDtypeStruct((length, heads * value_dim), jnp.float32),
            jax.ShapeDtypeStruct((length, 3 * heads), jnp.float32),
        ),
        compiler_params=params,
    )(queries, key_vectors, value_vectors, input_gate, forget_gate)
    before = pl.pallas_call(
        functools.partial(scan_kernel, matrix_rows), out_shape=message, compiler_params=params
    )(gathered)
    carried = lax.all_to_all(before, AXES, 0, 0)
    return pl.pallas_call(
        functools.partial(outer_kernel, key_rows),
        out_shape=jax.ShapeDtypeStruct((length, heads * value_dim), jnp.bfloat16),
        scratch_shapes=[pltpu.VMEM((key_dim, LANES), jnp.float32)],
        compiler_params=params,
    )(queries, carried, inner_num, stats)


def solution(mesh):
    device_count = mesh.shape["grp"] * mesh.shape["seq"]
    return jax.shard_map(
        functools.partial(on_device, device_count),
        mesh=mesh,
        in_specs=(
            P(AXES, None),
            P(AXES, None),
            P(AXES, None),
            P(None, AXES),
            P(None, AXES),
        ),
        out_specs=P(AXES, None),
        check_vma=False,
    )
```

```python
import functools

import jax
import jax.numpy as jnp
from jax import lax
from jax.experimental import pallas as pl
from jax.experimental.pallas import tpu as pltpu
from jax.sharding import PartitionSpec as P

floor_value = -1e30
LANES = 128
AXES = ("grp", "seq")


def split_two(x):
    high = x.astype(jnp.bfloat16)
    low = (x - high.astype(jnp.float32)).astype(jnp.bfloat16)
    return high, low


def split_three(x):
    high = x.astype(jnp.bfloat16)
    rest = x - high.astype(jnp.float32)
    mid = rest.astype(jnp.bfloat16)
    low = (rest - mid.astype(jnp.float32)).astype(jnp.bfloat16)
    return high, mid, low


def dot(a, b):
    return jnp.dot(a, b, preferred_element_type=jnp.float32)


def dot_last(a, b):
    return lax.dot_general(a, b, (((1,), (1,)), ((), ())), preferred_element_type=jnp.float32)


def log_forget(forget):
    return jnp.minimum(forget, 0.0) - jnp.log1p(jnp.exp(-jnp.abs(forget)))


def triangle(length, lower):
    rows = lax.broadcasted_iota(jnp.int32, (length, length), 0)
    cols = lax.broadcasted_iota(jnp.int32, (length, length), 1)
    return rows >= cols if lower else rows <= cols


def cumulative_rows(logf):
    ones = triangle(logf.shape[1], False).astype(jnp.bfloat16)
    high, mid, low = split_three(logf)
    return (dot(low, ones) + dot(mid, ones)) + dot(high, ones)


def cumulative_columns(logf):
    ones = triangle(logf.shape[1], True).astype(jnp.bfloat16)
    high, mid, low = split_three(logf)
    return (dot_last(ones, low) + dot_last(ones, mid)) + dot_last(ones, high)


def message_rows(matrix_rows):
    return matrix_rows + 2


def state_kernel(
    key_rows, k_hbm, v_hbm, in_hbm, fo_hbm, msg_ref, k_ref, v_ref, in_ref, fo_ref, arrived
):
    copies = [
        pltpu.make_async_copy(source, target, arrived.at[place])
        for place, (source, target) in enumerate(
            ((fo_hbm, fo_ref), (in_hbm, in_ref), (k_hbm, k_ref), (v_hbm, v_ref))
        )
    ]
    for copy in copies:
        copy.start()
    heads, length = in_ref.shape
    key_dim = k_ref.shape[1] // heads
    value_dim = v_ref.shape[1] // heads
    parts = value_dim // LANES
    per_head = key_dim // key_rows
    matrix_rows = parts * key_rows
    left = lax.broadcasted_iota(jnp.int32, (1, LANES), 1) < LANES // 2
    copies[0].wait()
    cumul = cumulative_rows(log_forget(fo_ref[...]))
    copies[1].wait()
    level = in_ref[...] - cumul
    level_top = jnp.max(level, axis=1, keepdims=True)
    weight = jnp.exp(level - level_top)
    decay = cumul[:, length - 1 : length]
    top = decay + level_top
    copies[2].wait()
    copies[3].wait()
    for head in range(heads):
        keys = k_ref[:, head * key_dim : (head + 1) * key_dim]
        values = v_ref[:, head * value_dim : (head + 1) * value_dim]
        row = weight[head : head + 1, :]
        high, low = split_two(keys.astype(jnp.float32).T * row)
        matrix = dot(
            jnp.concatenate([high, low], axis=1), jnp.concatenate([values, values], axis=0)
        )
        high, mid, low = split_three(row)
        vector = (dot(low, keys) + dot(mid, keys)) + dot(high, keys)
        scalars = jnp.where(left, top[head : head + 1, :], decay[head : head + 1, :])
        for piece in range(per_head):
            slot = head * per_head + piece
            for part in range(parts):
                msg_ref[slot, part * key_rows : (part + 1) * key_rows, 0, :] = matrix[
                    piece * key_rows : (piece + 1) * key_rows, part * LANES : (part + 1) * LANES
                ]
            msg_ref[slot, matrix_rows : matrix_rows + 1, 0, :] = vector
            msg_ref[slot, matrix_rows + 1 : matrix_rows + 2, 0, :] = scalars


def scan_kernel(in_ref, out_ref):
    count, rows, _, lanes = in_ref.shape
    left = lax.broadcasted_iota(jnp.int32, (1, lanes), 1) < lanes // 2

    def step(block, carry):
        state, top = carry
        out_ref[block, 0 : rows - 1, 0, :] = state
        out_ref[block, rows - 1 : rows, 0, :] = top
        piece = in_ref[block, 0 : rows - 1, 0, :]
        own = in_ref[block, rows - 1 : rows, 0, :]
        swapped = pltpu.roll(own, lanes // 2, 1)
        own_top = jnp.where(left, own, swapped)
        moved = top + jnp.where(left, swapped, own)
        joined = jnp.maximum(moved, own_top)
        state = jnp.exp(moved - joined) * state + jnp.exp(own_top - joined) * piece
        return state, joined

    carry = (
        jnp.zeros((rows - 1, lanes), jnp.float32),
        jnp.full((1, lanes), floor_value, jnp.float32),
    )
    lax.fori_loop(0, count, step, carry, unroll=min(count, 32))


def inner_kernel(q_ref, k_ref, v_ref, in_ref, fo_ref, num_ref, stat_ref):
    heads, length = in_ref.shape
    key_dim = q_ref.shape[1] // heads
    value_dim = v_ref.shape[1] // heads
    logf = log_forget(fo_ref[...])
    level = in_ref[...] - cumulative_rows(logf)
    stat_ref[:, 0:heads] = cumulative_columns(logf)
    causal = triangle(length, True)
    for head in range(heads):
        queries = q_ref[:, head * key_dim : (head + 1) * key_dim]
        keys = k_ref[:, head * key_dim : (head + 1) * key_dim]
        values = v_ref[:, head * value_dim : (head + 1) * value_dim]
        scores = dot_last(queries, keys) * (key_dim**-0.5)
        masked = jnp.where(causal, level[head : head + 1, :], -jnp.inf)
        row_level = jnp.max(masked, axis=1, keepdims=True)
        weighted = jnp.exp(masked - row_level) * scores
        stat_ref[:, heads + head : heads + head + 1] = row_level
        stat_ref[:, 2 * heads + head : 2 * heads + head + 1] = jnp.sum(
            weighted, axis=1, keepdims=True
        )
        num_ref[:, head * value_dim : (head + 1) * value_dim] = dot(
            weighted.astype(jnp.bfloat16), values
        )


def outer_kernel(
    key_rows, q_ref, msg_ref, num_ref, stat_ref, out_hbm, piece_ref, out_ref, done
):
    heads = stat_ref.shape[1] // 3
    key_dim = q_ref.shape[1] // heads
    value_dim = num_ref.shape[1] // heads
    parts = value_dim // LANES
    per_head = key_dim // key_rows
    matrix_rows = parts * key_rows
    scaling = key_dim**-0.5

    head_of = lax.broadcasted_iota(jnp.int32, (1, heads), 1)
    top = jnp.zeros((1, heads), jnp.float32)
    vectors = []
    for head in range(heads):
        first = head * per_head
        own_top = msg_ref[first, matrix_rows + 1 : matrix_rows + 2, 0, :]
        top = jnp.where(head_of == head, own_top[:, 0:1], top)
        vector = msg_ref[first, matrix_rows : matrix_rows + 1, 0, :]
        zero = jnp.zeros_like(vector)
        vectors.append(jnp.concatenate([zero] * head + [vector] + [zero] * (heads - 1 - head), 1))
    terms = split_three(jnp.concatenate(vectors, axis=0))
    queries = q_ref[...]
    carried_den = dot_last(queries, terms[2]) + dot_last(queries, terms[1])
    carried_den = (carried_den + dot_last(queries, terms[0])) * scaling
    cumul = stat_ref[:, 0:heads]
    row_level = stat_ref[:, heads : 2 * heads]
    inner_den = stat_ref[:, 2 * heads : 3 * heads]
    joined = jnp.maximum(row_level, top)
    inner_factor = jnp.exp(row_level - joined)
    outer_factor = jnp.exp(top - joined)
    denom = inner_factor * inner_den + outer_factor * carried_den
    inverse = 1.0 / jnp.maximum(jnp.abs(denom), jnp.exp(-(cumul + joined)))
    inner_factor = inner_factor * inverse
    outer_factor = outer_factor * (inverse * scaling)

    copies = []
    for head in range(heads):
        first = head * per_head
        columns = []
        for part in range(parts):
            place = slice(part * key_rows, (part + 1) * key_rows)
            if key_rows % 8 == 0:
                columns.append(
                    msg_ref[first : first + per_head, place, 0, :].reshape(key_dim, LANES)
                )
            else:
                for piece in range(per_head):
                    piece_ref[piece * key_rows : (piece + 1) * key_rows, :] = msg_ref[
                        first + piece, place, 0, :
                    ]
                columns.append(piece_ref[...])
        high, low = split_two(jnp.concatenate(columns, axis=1))
        query = queries[:, head * key_dim : (head + 1) * key_dim]
        carried = dot(
            jnp.concatenate([query, query], axis=1), jnp.concatenate([high, low], axis=0)
        )
        place = pl.ds(head * value_dim, value_dim)
        out_ref[:, place] = (
            inner_factor[:, head : head + 1] * num_ref[:, place]
            + outer_factor[:, head : head + 1] * carried
        ).astype(out_ref.dtype)
        copy = pltpu.make_async_copy(out_ref.at[:, place], out_hbm.at[:, place], done.at[head])
        copy.start()
        copies.append(copy)
    for copy in copies:
        copy.wait()


def on_device(device_count, queries, key_vectors, value_vectors, input_gate, forget_gate):
    heads, length = input_gate.shape
    key_dim = queries.shape[1] // heads
    value_dim = value_vectors.shape[1] // heads
    key_rows = heads * key_dim // device_count
    matrix_rows = (value_dim // LANES) * key_rows
    message = jax.ShapeDtypeStruct(
        (device_count, message_rows(matrix_rows), 1, LANES), jnp.float32
    )
    params = pltpu.CompilerParams(vmem_limit_bytes=48 * 1024 * 1024)
    hbm = pl.BlockSpec(memory_space=pltpu.HBM)
    output = jax.ShapeDtypeStruct((length, heads * value_dim), jnp.bfloat16)
    operands = (key_vectors, value_vectors, input_gate, forget_gate)

    own = pl.pallas_call(
        functools.partial(state_kernel, key_rows),
        out_shape=message,
        in_specs=[hbm] * len(operands),
        scratch_shapes=[pltpu.VMEM(array.shape, array.dtype) for array in operands]
        + [pltpu.SemaphoreType.DMA((len(operands),))],
        compiler_params=params,
    )(*(pltpu.with_memory_space_constraint(array, pltpu.HBM) for array in operands))
    gathered = lax.all_to_all(own, AXES, 0, 0)
    inner_num, stats = pl.pallas_call(
        inner_kernel,
        out_shape=(
            jax.ShapeDtypeStruct((length, heads * value_dim), jnp.float32),
            jax.ShapeDtypeStruct((length, 3 * heads), jnp.float32),
        ),
        compiler_params=params,
    )(queries, *operands)
    before = pl.pallas_call(scan_kernel, out_shape=message, compiler_params=params)(gathered)
    carried = lax.all_to_all(before, AXES, 0, 0)
    return pl.pallas_call(
        functools.partial(outer_kernel, key_rows),
        out_shape=output,
        out_specs=hbm,
        scratch_shapes=[
            pltpu.VMEM((key_dim, LANES), jnp.float32),
            pltpu.VMEM(output.shape, output.dtype),
            pltpu.SemaphoreType.DMA((heads,)),
        ],
        compiler_params=params,
    )(queries, carried, inner_num, stats)


def solution(mesh):
    device_count = mesh.shape["grp"] * mesh.shape["seq"]
    return jax.shard_map(
        functools.partial(on_device, device_count),
        mesh=mesh,
        in_specs=(
            P(AXES, None),
            P(AXES, None),
            P(AXES, None),
            P(None, AXES),
            P(None, AXES),
        ),
        out_specs=P(AXES, None),
        check_vma=False,
    )
```

```python
import functools

import jax
import jax.numpy as jnp
from jax import lax
from jax.experimental import pallas as pl
from jax.experimental.pallas import tpu as pltpu
from jax.sharding import PartitionSpec as P

floor_value = -1e30
LANES = 128
AXES = ("grp", "seq")


def split_two(x):
    high = x.astype(jnp.bfloat16)
    low = (x - high.astype(jnp.float32)).astype(jnp.bfloat16)
    return high, low


def split_three(x):
    high = x.astype(jnp.bfloat16)
    rest = x - high.astype(jnp.float32)
    mid = rest.astype(jnp.bfloat16)
    low = (rest - mid.astype(jnp.float32)).astype(jnp.bfloat16)
    return high, mid, low


def dot(a, b):
    return jnp.dot(a, b, preferred_element_type=jnp.float32)


def dot_last(a, b):
    return lax.dot_general(a, b, (((1,), (1,)), ((), ())), preferred_element_type=jnp.float32)


def log_forget(forget):
    return jnp.minimum(forget, 0.0) - jnp.log1p(jnp.exp(-jnp.abs(forget)))


def triangle(length, lower):
    rows = lax.broadcasted_iota(jnp.int32, (length, length), 0)
    cols = lax.broadcasted_iota(jnp.int32, (length, length), 1)
    return rows >= cols if lower else rows <= cols


def cumulative_rows(logf):
    ones = triangle(logf.shape[1], False).astype(jnp.bfloat16)
    high, mid, low = split_three(logf)
    return (dot(low, ones) + dot(mid, ones)) + dot(high, ones)


def cumulative_columns(logf):
    ones = triangle(logf.shape[1], True).astype(jnp.bfloat16)
    high, mid, low = split_three(logf)
    return (dot_last(ones, low) + dot_last(ones, mid)) + dot_last(ones, high)


def own_place():
    return lax.axis_index(AXES[0]) * lax.axis_size(AXES[1]) + lax.axis_index(AXES[1])


def exchange(pieces):
    count = len(pieces)
    return [pieces[0]] + [
        lax.ppermute(pieces[step], AXES, [(place, place ^ step) for place in range(count)])
        for step in range(1, count)
    ]


def message_rows(matrix_rows):
    return matrix_rows + 2


def state_kernel(
    key_rows, k_hbm, v_hbm, in_hbm, fo_hbm, *refs
):
    *out_refs, msg_ref, k_ref, v_ref, in_ref, fo_ref, arrived = refs
    copies = [
        pltpu.make_async_copy(source, target, arrived.at[place])
        for place, (source, target) in enumerate(
            ((fo_hbm, fo_ref), (in_hbm, in_ref), (k_hbm, k_ref), (v_hbm, v_ref))
        )
    ]
    for copy in copies:
        copy.start()
    heads, length = in_ref.shape
    key_dim = k_ref.shape[1] // heads
    value_dim = v_ref.shape[1] // heads
    parts = value_dim // LANES
    per_head = key_dim // key_rows
    matrix_rows = parts * key_rows
    left = lax.broadcasted_iota(jnp.int32, (1, LANES), 1) < LANES // 2
    copies[0].wait()
    cumul = cumulative_rows(log_forget(fo_ref[...]))
    copies[1].wait()
    level = in_ref[...] - cumul
    level_top = jnp.max(level, axis=1, keepdims=True)
    weight = jnp.exp(level - level_top)
    decay = cumul[:, length - 1 : length]
    top = decay + level_top
    copies[2].wait()
    copies[3].wait()
    for head in range(heads):
        keys = k_ref[:, head * key_dim : (head + 1) * key_dim]
        values = v_ref[:, head * value_dim : (head + 1) * value_dim]
        row = weight[head : head + 1, :]
        high, low = split_two(keys.astype(jnp.float32).T * row)
        matrix = dot(
            jnp.concatenate([high, low], axis=1), jnp.concatenate([values, values], axis=0)
        )
        high, mid, low = split_three(row)
        vector = (dot(low, keys) + dot(mid, keys)) + dot(high, keys)
        scalars = jnp.where(left, top[head : head + 1, :], decay[head : head + 1, :])
        for piece in range(per_head):
            slot = head * per_head + piece
            for part in range(parts):
                msg_ref[slot, part * key_rows : (part + 1) * key_rows, 0, :] = matrix[
                    piece * key_rows : (piece + 1) * key_rows, part * LANES : (part + 1) * LANES
                ]
            msg_ref[slot, matrix_rows : matrix_rows + 1, 0, :] = vector
            msg_ref[slot, matrix_rows + 1 : matrix_rows + 2, 0, :] = scalars
    me = own_place()
    for step, out_ref in enumerate(out_refs):
        out_ref[...] = msg_ref[me ^ step]


def scan_kernel(*refs):
    *refs, in_ref, out_ref = refs
    count, rows, _, lanes = in_ref.shape
    me = own_place()
    for step in range(count):
        in_ref[me ^ step] = refs[step][...]
    left = lax.broadcasted_iota(jnp.int32, (1, lanes), 1) < lanes // 2

    def step(block, carry):
        state, top = carry
        out_ref[block, 0 : rows - 1, 0, :] = state
        out_ref[block, rows - 1 : rows, 0, :] = top
        piece = in_ref[block, 0 : rows - 1, 0, :]
        own = in_ref[block, rows - 1 : rows, 0, :]
        swapped = pltpu.roll(own, lanes // 2, 1)
        own_top = jnp.where(left, own, swapped)
        moved = top + jnp.where(left, swapped, own)
        joined = jnp.maximum(moved, own_top)
        state = jnp.exp(moved - joined) * state + jnp.exp(own_top - joined) * piece
        return state, joined

    carry = (
        jnp.zeros((rows - 1, lanes), jnp.float32),
        jnp.full((1, lanes), floor_value, jnp.float32),
    )
    lax.fori_loop(0, count, step, carry, unroll=min(count, 32))
    for step in range(count):
        refs[count + step][...] = out_ref[me ^ step]


def inner_kernel(q_ref, k_ref, v_ref, in_ref, fo_ref, num_ref, stat_ref):
    heads, length = in_ref.shape
    key_dim = q_ref.shape[1] // heads
    value_dim = v_ref.shape[1] // heads
    logf = log_forget(fo_ref[...])
    level = in_ref[...] - cumulative_rows(logf)
    stat_ref[:, 0:heads] = cumulative_columns(logf)
    causal = triangle(length, True)
    for head in range(heads):
        queries = q_ref[:, head * key_dim : (head + 1) * key_dim]
        keys = k_ref[:, head * key_dim : (head + 1) * key_dim]
        values = v_ref[:, head * value_dim : (head + 1) * value_dim]
        scores = dot_last(queries, keys) * (key_dim**-0.5)
        masked = jnp.where(causal, level[head : head + 1, :], -jnp.inf)
        row_level = jnp.max(masked, axis=1, keepdims=True)
        weighted = jnp.exp(masked - row_level) * scores
        stat_ref[:, heads + head : heads + head + 1] = row_level
        stat_ref[:, 2 * heads + head : 2 * heads + head + 1] = jnp.sum(
            weighted, axis=1, keepdims=True
        )
        num_ref[:, head * value_dim : (head + 1) * value_dim] = dot(
            weighted.astype(jnp.bfloat16), values
        )


def outer_kernel(
    key_rows, q_ref, num_ref, stat_ref, *refs
):
    *refs, out_hbm, msg_ref, piece_ref, out_ref, done = refs
    me = own_place()
    for step, ref in enumerate(refs):
        msg_ref[me ^ step] = ref[...]
    heads = stat_ref.shape[1] // 3
    key_dim = q_ref.shape[1] // heads
    value_dim = num_ref.shape[1] // heads
    parts = value_dim // LANES
    per_head = key_dim // key_rows
    matrix_rows = parts * key_rows
    scaling = key_dim**-0.5

    head_of = lax.broadcasted_iota(jnp.int32, (1, heads), 1)
    top = jnp.zeros((1, heads), jnp.float32)
    vectors = []
    for head in range(heads):
        first = head * per_head
        own_top = msg_ref[first, matrix_rows + 1 : matrix_rows + 2, 0, :]
        top = jnp.where(head_of == head, own_top[:, 0:1], top)
        vector = msg_ref[first, matrix_rows : matrix_rows + 1, 0, :]
        zero = jnp.zeros_like(vector)
        vectors.append(jnp.concatenate([zero] * head + [vector] + [zero] * (heads - 1 - head), 1))
    terms = split_three(jnp.concatenate(vectors, axis=0))
    queries = q_ref[...]
    carried_den = dot_last(queries, terms[2]) + dot_last(queries, terms[1])
    carried_den = (carried_den + dot_last(queries, terms[0])) * scaling
    cumul = stat_ref[:, 0:heads]
    row_level = stat_ref[:, heads : 2 * heads]
    inner_den = stat_ref[:, 2 * heads : 3 * heads]
    joined = jnp.maximum(row_level, top)
    inner_factor = jnp.exp(row_level - joined)
    outer_factor = jnp.exp(top - joined)
    denom = inner_factor * inner_den + outer_factor * carried_den
    inverse = 1.0 / jnp.maximum(jnp.abs(denom), jnp.exp(-(cumul + joined)))
    inner_factor = inner_factor * inverse
    outer_factor = outer_factor * (inverse * scaling)

    copies = []
    for head in range(heads):
        first = head * per_head
        columns = []
        for part in range(parts):
            place = slice(part * key_rows, (part + 1) * key_rows)
            if key_rows % 8 == 0:
                columns.append(
                    msg_ref[first : first + per_head, place, 0, :].reshape(key_dim, LANES)
                )
            else:
                for piece in range(per_head):
                    piece_ref[piece * key_rows : (piece + 1) * key_rows, :] = msg_ref[
                        first + piece, place, 0, :
                    ]
                columns.append(piece_ref[...])
        high, low = split_two(jnp.concatenate(columns, axis=1))
        query = queries[:, head * key_dim : (head + 1) * key_dim]
        carried = dot(
            jnp.concatenate([query, query], axis=1), jnp.concatenate([high, low], axis=0)
        )
        place = pl.ds(head * value_dim, value_dim)
        out_ref[:, place] = (
            inner_factor[:, head : head + 1] * num_ref[:, place]
            + outer_factor[:, head : head + 1] * carried
        ).astype(out_ref.dtype)
        copy = pltpu.make_async_copy(out_ref.at[:, place], out_hbm.at[:, place], done.at[head])
        copy.start()
        copies.append(copy)
    for copy in copies:
        copy.wait()


def on_device(device_count, queries, key_vectors, value_vectors, input_gate, forget_gate):
    heads, length = input_gate.shape
    key_dim = queries.shape[1] // heads
    value_dim = value_vectors.shape[1] // heads
    key_rows = heads * key_dim // device_count
    matrix_rows = (value_dim // LANES) * key_rows
    message = jax.ShapeDtypeStruct((message_rows(matrix_rows), 1, LANES), jnp.float32)
    messages = (message,) * device_count
    stacked = pltpu.VMEM((device_count,) + message.shape, message.dtype)
    params = pltpu.CompilerParams(vmem_limit_bytes=48 * 1024 * 1024)
    hbm = pl.BlockSpec(memory_space=pltpu.HBM)
    output = jax.ShapeDtypeStruct((length, heads * value_dim), jnp.bfloat16)
    operands = (key_vectors, value_vectors, input_gate, forget_gate)

    own = pl.pallas_call(
        functools.partial(state_kernel, key_rows),
        out_shape=messages,
        in_specs=[hbm] * len(operands),
        scratch_shapes=[stacked]
        + [pltpu.VMEM(array.shape, array.dtype) for array in operands]
        + [pltpu.SemaphoreType.DMA((len(operands),))],
        compiler_params=params,
    )(*(pltpu.with_memory_space_constraint(array, pltpu.HBM) for array in operands))
    gathered = exchange(own)
    inner_num, stats = pl.pallas_call(
        inner_kernel,
        out_shape=(
            jax.ShapeDtypeStruct((length, heads * value_dim), jnp.float32),
            jax.ShapeDtypeStruct((length, 3 * heads), jnp.float32),
        ),
        compiler_params=params,
    )(queries, *operands)
    before = pl.pallas_call(
        scan_kernel,
        out_shape=messages,
        scratch_shapes=[stacked, stacked],
        compiler_params=params,
    )(*gathered)
    carried = exchange(before)
    return pl.pallas_call(
        functools.partial(outer_kernel, key_rows),
        out_shape=output,
        out_specs=hbm,
        scratch_shapes=[
            stacked,
            pltpu.VMEM((key_dim, LANES), jnp.float32),
            pltpu.VMEM(output.shape, output.dtype),
            pltpu.SemaphoreType.DMA((heads,)),
        ],
        compiler_params=params,
    )(queries, inner_num, stats, *carried)


def solution(mesh):
    device_count = mesh.shape["grp"] * mesh.shape["seq"]
    return jax.shard_map(
        functools.partial(on_device, device_count),
        mesh=mesh,
        in_specs=(
            P(AXES, None),
            P(AXES, None),
            P(AXES, None),
            P(None, AXES),
            P(None, AXES),
        ),
        out_specs=P(AXES, None),
        check_vma=False,
    )
```

```python
import functools

import jax
import jax.numpy as jnp
from jax import lax
from jax.experimental import pallas as pl
from jax.experimental.pallas import tpu as pltpu
from jax.sharding import PartitionSpec as P

floor_value = -1e30
LANES = 128
AXES = ("grp", "seq")
CHUNKS = 2


def split_two(x):
    high = x.astype(jnp.bfloat16)
    low = (x - high.astype(jnp.float32)).astype(jnp.bfloat16)
    return high, low


def split_three(x):
    high = x.astype(jnp.bfloat16)
    rest = x - high.astype(jnp.float32)
    mid = rest.astype(jnp.bfloat16)
    low = (rest - mid.astype(jnp.float32)).astype(jnp.bfloat16)
    return high, mid, low


def dot(a, b):
    return jnp.dot(a, b, preferred_element_type=jnp.float32)


def dot_last(a, b):
    return lax.dot_general(a, b, (((1,), (1,)), ((), ())), preferred_element_type=jnp.float32)


def log_forget(forget):
    return jnp.minimum(forget, 0.0) - jnp.log1p(jnp.exp(-jnp.abs(forget)))


def triangle(length, lower):
    rows = lax.broadcasted_iota(jnp.int32, (length, length), 0)
    cols = lax.broadcasted_iota(jnp.int32, (length, length), 1)
    return rows >= cols if lower else rows <= cols


def cumulative_rows(logf):
    ones = triangle(logf.shape[1], False).astype(jnp.bfloat16)
    high, mid, low = split_three(logf)
    return (dot(low, ones) + dot(mid, ones)) + dot(high, ones)


def cumulative_columns(logf):
    ones = triangle(logf.shape[1], True).astype(jnp.bfloat16)
    high, mid, low = split_three(logf)
    return (dot_last(ones, low) + dot_last(ones, mid)) + dot_last(ones, high)


def message_rows(matrix_rows):
    return matrix_rows + 2


def state_kernel(
    key_rows, k_hbm, v_hbm, in_hbm, fo_hbm, *refs
):
    *msg_refs, k_ref, v_ref, in_ref, fo_ref, arrived = refs
    copies = [
        pltpu.make_async_copy(source, target, arrived.at[place])
        for place, (source, target) in enumerate(
            ((fo_hbm, fo_ref), (in_hbm, in_ref), (k_hbm, k_ref), (v_hbm, v_ref))
        )
    ]
    for copy in copies:
        copy.start()
    heads, length = in_ref.shape
    key_dim = k_ref.shape[1] // heads
    value_dim = v_ref.shape[1] // heads
    parts = value_dim // LANES
    per_head = key_dim // key_rows
    matrix_rows = parts * key_rows
    chunk_heads = heads // len(msg_refs)
    left = lax.broadcasted_iota(jnp.int32, (1, LANES), 1) < LANES // 2
    copies[0].wait()
    cumul = cumulative_rows(log_forget(fo_ref[...]))
    copies[1].wait()
    level = in_ref[...] - cumul
    level_top = jnp.max(level, axis=1, keepdims=True)
    weight = jnp.exp(level - level_top)
    decay = cumul[:, length - 1 : length]
    top = decay + level_top
    copies[2].wait()
    copies[3].wait()
    for head in range(heads):
        keys = k_ref[:, head * key_dim : (head + 1) * key_dim]
        values = v_ref[:, head * value_dim : (head + 1) * value_dim]
        row = weight[head : head + 1, :]
        high, low = split_two(keys.astype(jnp.float32).T * row)
        matrix = dot(
            jnp.concatenate([high, low], axis=1), jnp.concatenate([values, values], axis=0)
        )
        high, mid, low = split_three(row)
        vector = (dot(low, keys) + dot(mid, keys)) + dot(high, keys)
        scalars = jnp.where(left, top[head : head + 1, :], decay[head : head + 1, :])
        msg_ref = msg_refs[head // chunk_heads]
        for piece in range(per_head):
            slot = head % chunk_heads * per_head + piece
            for part in range(parts):
                msg_ref[slot, part * key_rows : (part + 1) * key_rows, 0, :] = matrix[
                    piece * key_rows : (piece + 1) * key_rows, part * LANES : (part + 1) * LANES
                ]
            msg_ref[slot, matrix_rows : matrix_rows + 1, 0, :] = vector
            msg_ref[slot, matrix_rows + 1 : matrix_rows + 2, 0, :] = scalars


def scan_kernel(in_ref, out_ref):
    count, rows, _, lanes = in_ref.shape
    left = lax.broadcasted_iota(jnp.int32, (1, lanes), 1) < lanes // 2

    def step(block, carry):
        state, top = carry
        out_ref[block, 0 : rows - 1, 0, :] = state
        out_ref[block, rows - 1 : rows, 0, :] = top
        piece = in_ref[block, 0 : rows - 1, 0, :]
        own = in_ref[block, rows - 1 : rows, 0, :]
        swapped = pltpu.roll(own, lanes // 2, 1)
        own_top = jnp.where(left, own, swapped)
        moved = top + jnp.where(left, swapped, own)
        joined = jnp.maximum(moved, own_top)
        state = jnp.exp(moved - joined) * state + jnp.exp(own_top - joined) * piece
        return state, joined

    carry = (
        jnp.zeros((rows - 1, lanes), jnp.float32),
        jnp.full((1, lanes), floor_value, jnp.float32),
    )
    lax.fori_loop(0, count, step, carry, unroll=min(count, 32))


def inner_kernel(q_ref, k_ref, v_ref, in_ref, fo_ref, num_ref, stat_ref):
    heads, length = in_ref.shape
    key_dim = q_ref.shape[1] // heads
    value_dim = v_ref.shape[1] // heads
    logf = log_forget(fo_ref[...])
    level = in_ref[...] - cumulative_rows(logf)
    stat_ref[:, 0:heads] = cumulative_columns(logf)
    causal = triangle(length, True)
    for head in range(heads):
        queries = q_ref[:, head * key_dim : (head + 1) * key_dim]
        keys = k_ref[:, head * key_dim : (head + 1) * key_dim]
        values = v_ref[:, head * value_dim : (head + 1) * value_dim]
        scores = dot_last(queries, keys) * (key_dim**-0.5)
        masked = jnp.where(causal, level[head : head + 1, :], -jnp.inf)
        row_level = jnp.max(masked, axis=1, keepdims=True)
        weighted = jnp.exp(masked - row_level) * scores
        stat_ref[:, heads + head : heads + head + 1] = row_level
        stat_ref[:, 2 * heads + head : 2 * heads + head + 1] = jnp.sum(
            weighted, axis=1, keepdims=True
        )
        num_ref[:, head * value_dim : (head + 1) * value_dim] = dot(
            weighted.astype(jnp.bfloat16), values
        )


def outer_kernel(
    key_rows, q_ref, num_ref, stat_ref, *refs
):
    *msg_refs, out_hbm, piece_ref, out_ref, done = refs
    heads = stat_ref.shape[1] // 3
    chunk_heads = heads // len(msg_refs)
    key_dim = q_ref.shape[1] // heads
    value_dim = num_ref.shape[1] // heads
    parts = value_dim // LANES
    per_head = key_dim // key_rows
    matrix_rows = parts * key_rows
    scaling = key_dim**-0.5

    head_of = lax.broadcasted_iota(jnp.int32, (1, heads), 1)
    top = jnp.zeros((1, heads), jnp.float32)
    vectors = []
    for head in range(heads):
        msg_ref = msg_refs[head // chunk_heads]
        first = head % chunk_heads * per_head
        own_top = msg_ref[first, matrix_rows + 1 : matrix_rows + 2, 0, :]
        top = jnp.where(head_of == head, own_top[:, 0:1], top)
        vector = msg_ref[first, matrix_rows : matrix_rows + 1, 0, :]
        zero = jnp.zeros_like(vector)
        vectors.append(jnp.concatenate([zero] * head + [vector] + [zero] * (heads - 1 - head), 1))
    terms = split_three(jnp.concatenate(vectors, axis=0))
    queries = q_ref[...]
    carried_den = dot_last(queries, terms[2]) + dot_last(queries, terms[1])
    carried_den = (carried_den + dot_last(queries, terms[0])) * scaling
    cumul = stat_ref[:, 0:heads]
    row_level = stat_ref[:, heads : 2 * heads]
    inner_den = stat_ref[:, 2 * heads : 3 * heads]
    joined = jnp.maximum(row_level, top)
    inner_factor = jnp.exp(row_level - joined)
    outer_factor = jnp.exp(top - joined)
    denom = inner_factor * inner_den + outer_factor * carried_den
    inverse = 1.0 / jnp.maximum(jnp.abs(denom), jnp.exp(-(cumul + joined)))
    inner_factor = inner_factor * inverse
    outer_factor = outer_factor * (inverse * scaling)

    copies = []
    for head in range(heads):
        msg_ref = msg_refs[head // chunk_heads]
        first = head % chunk_heads * per_head
        columns = []
        for part in range(parts):
            place = slice(part * key_rows, (part + 1) * key_rows)
            if key_rows % 8 == 0:
                columns.append(
                    msg_ref[first : first + per_head, place, 0, :].reshape(key_dim, LANES)
                )
            else:
                for piece in range(per_head):
                    piece_ref[piece * key_rows : (piece + 1) * key_rows, :] = msg_ref[
                        first + piece, place, 0, :
                    ]
                columns.append(piece_ref[...])
        high, low = split_two(jnp.concatenate(columns, axis=1))
        query = queries[:, head * key_dim : (head + 1) * key_dim]
        carried = dot(
            jnp.concatenate([query, query], axis=1), jnp.concatenate([high, low], axis=0)
        )
        place = pl.ds(head * value_dim, value_dim)
        out_ref[:, place] = (
            inner_factor[:, head : head + 1] * num_ref[:, place]
            + outer_factor[:, head : head + 1] * carried
        ).astype(out_ref.dtype)
        copy = pltpu.make_async_copy(out_ref.at[:, place], out_hbm.at[:, place], done.at[head])
        copy.start()
        copies.append(copy)
    for copy in copies:
        copy.wait()


def on_device(device_count, queries, key_vectors, value_vectors, input_gate, forget_gate):
    heads, length = input_gate.shape
    key_dim = queries.shape[1] // heads
    value_dim = value_vectors.shape[1] // heads
    chunks = CHUNKS if heads % CHUNKS == 0 else 1
    key_rows = heads // chunks * key_dim // device_count
    matrix_rows = (value_dim // LANES) * key_rows
    message = jax.ShapeDtypeStruct(
        (device_count, message_rows(matrix_rows), 1, LANES), jnp.float32
    )
    params = pltpu.CompilerParams(vmem_limit_bytes=48 * 1024 * 1024)
    hbm = pl.BlockSpec(memory_space=pltpu.HBM)
    output = jax.ShapeDtypeStruct((length, heads * value_dim), jnp.bfloat16)
    operands = (key_vectors, value_vectors, input_gate, forget_gate)

    own = pl.pallas_call(
        functools.partial(state_kernel, key_rows),
        out_shape=(message,) * chunks,
        in_specs=[hbm] * len(operands),
        scratch_shapes=[pltpu.VMEM(array.shape, array.dtype) for array in operands]
        + [pltpu.SemaphoreType.DMA((len(operands),))],
        compiler_params=params,
    )(*(pltpu.with_memory_space_constraint(array, pltpu.HBM) for array in operands))
    gathered = [lax.all_to_all(array, AXES, 0, 0) for array in own]
    inner_num, stats = pl.pallas_call(
        inner_kernel,
        out_shape=(
            jax.ShapeDtypeStruct((length, heads * value_dim), jnp.float32),
            jax.ShapeDtypeStruct((length, 3 * heads), jnp.float32),
        ),
        compiler_params=params,
    )(queries, *operands)
    scan = pl.pallas_call(scan_kernel, out_shape=message, compiler_params=params)
    carried = [lax.all_to_all(scan(array), AXES, 0, 0) for array in gathered]
    return pl.pallas_call(
        functools.partial(outer_kernel, key_rows),
        out_shape=output,
        out_specs=hbm,
        scratch_shapes=[
            pltpu.VMEM((key_dim, LANES), jnp.float32),
            pltpu.VMEM(output.shape, output.dtype),
            pltpu.SemaphoreType.DMA((heads,)),
        ],
        compiler_params=params,
    )(queries, inner_num, stats, *carried)


def solution(mesh):
    device_count = mesh.shape["grp"] * mesh.shape["seq"]
    return jax.shard_map(
        functools.partial(on_device, device_count),
        mesh=mesh,
        in_specs=(
            P(AXES, None),
            P(AXES, None),
            P(AXES, None),
            P(None, AXES),
            P(None, AXES),
        ),
        out_specs=P(AXES, None),
        check_vma=False,
    )
```

```python
import functools

import jax
import jax.numpy as jnp
from jax import lax
from jax.experimental import pallas as pl
from jax.experimental.pallas import tpu as pltpu
from jax.sharding import PartitionSpec as P

floor_value = -1e30
LANES = 128
AXES = ("grp", "seq")


def split_two(x):
    high = x.astype(jnp.bfloat16)
    low = (x - high.astype(jnp.float32)).astype(jnp.bfloat16)
    return high, low


def split_three(x):
    high = x.astype(jnp.bfloat16)
    rest = x - high.astype(jnp.float32)
    mid = rest.astype(jnp.bfloat16)
    low = (rest - mid.astype(jnp.float32)).astype(jnp.bfloat16)
    return high, mid, low


def dot(a, b):
    return jnp.dot(a, b, preferred_element_type=jnp.float32)


def dot_last(a, b):
    return lax.dot_general(a, b, (((1,), (1,)), ((), ())), preferred_element_type=jnp.float32)


def log_forget(forget):
    return jnp.minimum(forget, 0.0) - jnp.log1p(jnp.exp(-jnp.abs(forget)))


def triangle(length, lower):
    rows = lax.broadcasted_iota(jnp.int32, (length, length), 0)
    cols = lax.broadcasted_iota(jnp.int32, (length, length), 1)
    return rows >= cols if lower else rows <= cols


def cumulative_rows(logf):
    ones = triangle(logf.shape[1], False).astype(jnp.bfloat16)
    high, mid, low = split_three(logf)
    return (dot(low, ones) + dot(mid, ones)) + dot(high, ones)


def cumulative_columns(logf):
    ones = triangle(logf.shape[1], True).astype(jnp.bfloat16)
    high, mid, low = split_three(logf)
    return (dot_last(ones, low) + dot_last(ones, mid)) + dot_last(ones, high)


def message_rows(matrix_rows):
    return matrix_rows + 2


def state_kernel(
    key_rows, k_hbm, v_hbm, in_hbm, fo_hbm, msg_ref, k_ref, v_ref, in_ref, fo_ref, arrived
):
    copies = [
        pltpu.make_async_copy(source, target, arrived.at[place])
        for place, (source, target) in enumerate(
            ((fo_hbm, fo_ref), (in_hbm, in_ref), (k_hbm, k_ref), (v_hbm, v_ref))
        )
    ]
    for copy in copies:
        copy.start()
    heads, length = in_ref.shape
    key_dim = k_ref.shape[1] // heads
    value_dim = v_ref.shape[1] // heads
    parts = value_dim // LANES
    per_head = key_dim // key_rows
    matrix_rows = parts * key_rows
    left = lax.broadcasted_iota(jnp.int32, (1, LANES), 1) < LANES // 2
    copies[0].wait()
    cumul = cumulative_rows(log_forget(fo_ref[...]))
    copies[1].wait()
    level = in_ref[...] - cumul
    level_top = jnp.max(level, axis=1, keepdims=True)
    weight = jnp.exp(level - level_top)
    decay = cumul[:, length - 1 : length]
    top = decay + level_top
    copies[2].wait()
    copies[3].wait()
    for head in range(heads):
        keys = k_ref[:, head * key_dim : (head + 1) * key_dim]
        values = v_ref[:, head * value_dim : (head + 1) * value_dim]
        row = weight[head : head + 1, :]
        high, low = split_two(keys.astype(jnp.float32).T * row)
        matrix = dot(
            jnp.concatenate([high, low], axis=1), jnp.concatenate([values, values], axis=0)
        )
        high, mid, low = split_three(row)
        vector = (dot(low, keys) + dot(mid, keys)) + dot(high, keys)
        scalars = jnp.where(left, top[head : head + 1, :], decay[head : head + 1, :])
        for piece in range(per_head):
            slot = head * per_head + piece
            for part in range(parts):
                msg_ref[slot, part * key_rows : (part + 1) * key_rows, 0, :] = matrix[
                    piece * key_rows : (piece + 1) * key_rows, part * LANES : (part + 1) * LANES
                ]
            msg_ref[slot, matrix_rows : matrix_rows + 1, 0, :] = vector
            msg_ref[slot, matrix_rows + 1 : matrix_rows + 2, 0, :] = scalars


def read_state(ref, place):
    rows, _, lanes = ref.shape[1:]
    left = lax.broadcasted_iota(jnp.int32, (1, lanes), 1) < lanes // 2
    own = ref[place, rows - 1 : rows, 0, :]
    swapped = pltpu.roll(own, lanes // 2, 1)
    return (
        ref[place, 0 : rows - 1, 0, :],
        jnp.where(left, own, swapped),
        jnp.where(left, swapped, own),
    )


def join(earlier, later):
    early_state, early_top, early_decay = earlier
    late_state, late_top, late_decay = later
    moved = early_top + late_decay
    joined = jnp.maximum(moved, late_top)
    state = jnp.exp(moved - joined) * early_state + jnp.exp(late_top - joined) * late_state
    return state, joined, early_decay + late_decay


def group_kernel(in_ref, out_ref):
    count, rows, _, lanes = in_ref.shape
    groups = out_ref.shape[0]
    length = count // groups
    left = lax.broadcasted_iota(jnp.int32, (1, lanes), 1) < lanes // 2

    def group_sum(group):
        total = read_state(in_ref, group * length)
        for block in range(1, length):
            total = join(total, read_state(in_ref, group * length + block))
        state, top, decay = total
        out_ref[group, 0 : rows - 1, 0, :] = state
        out_ref[group, rows - 1 : rows, 0, :] = jnp.where(left, top, decay)

    for group in range(groups):
        group_sum(group)


def scan_kernel(in_ref, own_ref, other_ref, out_ref):
    count, rows, _, lanes = in_ref.shape
    groups = own_ref.shape[0]
    length = count // groups
    upper = lax.axis_index(AXES[1]) >= length

    def pick(one, other):
        return jax.tree.map(lambda a, b: jnp.where(upper, a, b), one, other)

    before = (
        jnp.zeros((rows - 1, lanes), jnp.float32),
        jnp.full((1, lanes), floor_value, jnp.float32),
        jnp.zeros((1, lanes), jnp.float32),
    )
    for group in range(groups):
        own = read_state(own_ref, group)
        other = read_state(other_ref, group)
        middle = join(before, pick(other, own))
        running = pick(middle, before)
        for block in range(length):
            place = group * length + block
            out_ref[place, 0 : rows - 1, 0, :] = running[0]
            out_ref[place, rows - 1 : rows, 0, :] = running[1]
            if block < length - 1:
                running = join(running, read_state(in_ref, place))
        before = join(middle, pick(own, other))


def inner_kernel(q_ref, k_ref, v_ref, in_ref, fo_ref, num_ref, stat_ref):
    heads, length = in_ref.shape
    key_dim = q_ref.shape[1] // heads
    value_dim = v_ref.shape[1] // heads
    logf = log_forget(fo_ref[...])
    level = in_ref[...] - cumulative_rows(logf)
    stat_ref[:, 0:heads] = cumulative_columns(logf)
    causal = triangle(length, True)
    for head in range(heads):
        queries = q_ref[:, head * key_dim : (head + 1) * key_dim]
        keys = k_ref[:, head * key_dim : (head + 1) * key_dim]
        values = v_ref[:, head * value_dim : (head + 1) * value_dim]
        scores = dot_last(queries, keys) * (key_dim**-0.5)
        masked = jnp.where(causal, level[head : head + 1, :], -jnp.inf)
        row_level = jnp.max(masked, axis=1, keepdims=True)
        weighted = jnp.exp(masked - row_level) * scores
        stat_ref[:, heads + head : heads + head + 1] = row_level
        stat_ref[:, 2 * heads + head : 2 * heads + head + 1] = jnp.sum(
            weighted, axis=1, keepdims=True
        )
        num_ref[:, head * value_dim : (head + 1) * value_dim] = dot(
            weighted.astype(jnp.bfloat16), values
        )


def outer_kernel(
    key_rows, q_ref, msg_ref, num_ref, stat_ref, out_hbm, piece_ref, out_ref, done
):
    heads = stat_ref.shape[1] // 3
    key_dim = q_ref.shape[1] // heads
    value_dim = num_ref.shape[1] // heads
    parts = value_dim // LANES
    per_head = key_dim // key_rows
    matrix_rows = parts * key_rows
    scaling = key_dim**-0.5

    head_of = lax.broadcasted_iota(jnp.int32, (1, heads), 1)
    top = jnp.zeros((1, heads), jnp.float32)
    vectors = []
    for head in range(heads):
        first = head * per_head
        own_top = msg_ref[first, matrix_rows + 1 : matrix_rows + 2, 0, :]
        top = jnp.where(head_of == head, own_top[:, 0:1], top)
        vector = msg_ref[first, matrix_rows : matrix_rows + 1, 0, :]
        zero = jnp.zeros_like(vector)
        vectors.append(jnp.concatenate([zero] * head + [vector] + [zero] * (heads - 1 - head), 1))
    terms = split_three(jnp.concatenate(vectors, axis=0))
    queries = q_ref[...]
    carried_den = dot_last(queries, terms[2]) + dot_last(queries, terms[1])
    carried_den = (carried_den + dot_last(queries, terms[0])) * scaling
    cumul = stat_ref[:, 0:heads]
    row_level = stat_ref[:, heads : 2 * heads]
    inner_den = stat_ref[:, 2 * heads : 3 * heads]
    joined = jnp.maximum(row_level, top)
    inner_factor = jnp.exp(row_level - joined)
    outer_factor = jnp.exp(top - joined)
    denom = inner_factor * inner_den + outer_factor * carried_den
    inverse = 1.0 / jnp.maximum(jnp.abs(denom), jnp.exp(-(cumul + joined)))
    inner_factor = inner_factor * inverse
    outer_factor = outer_factor * (inverse * scaling)

    copies = []
    for head in range(heads):
        first = head * per_head
        columns = []
        for part in range(parts):
            place = slice(part * key_rows, (part + 1) * key_rows)
            if key_rows % 8 == 0:
                columns.append(
                    msg_ref[first : first + per_head, place, 0, :].reshape(key_dim, LANES)
                )
            else:
                for piece in range(per_head):
                    piece_ref[piece * key_rows : (piece + 1) * key_rows, :] = msg_ref[
                        first + piece, place, 0, :
                    ]
                columns.append(piece_ref[...])
        high, low = split_two(jnp.concatenate(columns, axis=1))
        query = queries[:, head * key_dim : (head + 1) * key_dim]
        carried = dot(
            jnp.concatenate([query, query], axis=1), jnp.concatenate([high, low], axis=0)
        )
        place = pl.ds(head * value_dim, value_dim)
        out_ref[:, place] = (
            inner_factor[:, head : head + 1] * num_ref[:, place]
            + outer_factor[:, head : head + 1] * carried
        ).astype(out_ref.dtype)
        copy = pltpu.make_async_copy(out_ref.at[:, place], out_hbm.at[:, place], done.at[head])
        copy.start()
        copies.append(copy)
    for copy in copies:
        copy.wait()


def on_device(groups, group_length, queries, key_vectors, value_vectors, input_gate, forget_gate):
    heads, length = input_gate.shape
    key_dim = queries.shape[1] // heads
    value_dim = value_vectors.shape[1] // heads
    half = group_length // 2
    members = groups * half
    halves = [
        [group * group_length + side * half + block for group in range(groups) for block in range(half)]
        for side in range(2)
    ]
    key_rows = heads * key_dim // members
    matrix_rows = (value_dim // LANES) * key_rows
    piece = (message_rows(matrix_rows), 1, LANES)
    message = jax.ShapeDtypeStruct((members,) + piece, jnp.float32)
    params = pltpu.CompilerParams(vmem_limit_bytes=48 * 1024 * 1024)
    hbm = pl.BlockSpec(memory_space=pltpu.HBM)
    output = jax.ShapeDtypeStruct((length, heads * value_dim), jnp.bfloat16)
    operands = (key_vectors, value_vectors, input_gate, forget_gate)

    own = pl.pallas_call(
        functools.partial(state_kernel, key_rows),
        out_shape=message,
        in_specs=[hbm] * len(operands),
        scratch_shapes=[pltpu.VMEM(array.shape, array.dtype) for array in operands]
        + [pltpu.SemaphoreType.DMA((len(operands),))],
        compiler_params=params,
    )(*(pltpu.with_memory_space_constraint(array, pltpu.HBM) for array in operands))
    gathered = lax.all_to_all(own, AXES, 0, 0, axis_index_groups=halves)
    own_sums = pl.pallas_call(
        group_kernel,
        out_shape=jax.ShapeDtypeStruct((groups,) + piece, jnp.float32),
        compiler_params=params,
    )(gathered)
    other_sums = lax.ppermute(
        own_sums, AXES[1], [(place, (place + half) % group_length) for place in range(group_length)]
    )
    inner_num, stats = pl.pallas_call(
        inner_kernel,
        out_shape=(
            jax.ShapeDtypeStruct((length, heads * value_dim), jnp.float32),
            jax.ShapeDtypeStruct((length, 3 * heads), jnp.float32),
        ),
        compiler_params=params,
    )(queries, *operands)
    before = pl.pallas_call(scan_kernel, out_shape=message, compiler_params=params)(
        gathered, own_sums, other_sums
    )
    carried = lax.all_to_all(before, AXES, 0, 0, axis_index_groups=halves)
    return pl.pallas_call(
        functools.partial(outer_kernel, key_rows),
        out_shape=output,
        out_specs=hbm,
        scratch_shapes=[
            pltpu.VMEM((key_dim, LANES), jnp.float32),
            pltpu.VMEM(output.shape, output.dtype),
            pltpu.SemaphoreType.DMA((heads,)),
        ],
        compiler_params=params,
    )(queries, carried, inner_num, stats)


def solution(mesh):
    return jax.shard_map(
        functools.partial(on_device, mesh.shape["grp"], mesh.shape["seq"]),
        mesh=mesh,
        in_specs=(
            P(AXES, None),
            P(AXES, None),
            P(AXES, None),
            P(None, AXES),
            P(None, AXES),
        ),
        out_specs=P(AXES, None),
        check_vma=False,
    )
```

```python
import functools

import jax
import jax.numpy as jnp
from jax import lax
from jax.experimental import pallas as pl
from jax.experimental.pallas import tpu as pltpu
from jax.sharding import PartitionSpec as P

floor_value = -1e30
LANES = 128
AXES = ("grp", "seq")


def split_two(x):
    high = x.astype(jnp.bfloat16)
    low = (x - high.astype(jnp.float32)).astype(jnp.bfloat16)
    return high, low


def split_three(x):
    high = x.astype(jnp.bfloat16)
    rest = x - high.astype(jnp.float32)
    mid = rest.astype(jnp.bfloat16)
    low = (rest - mid.astype(jnp.float32)).astype(jnp.bfloat16)
    return high, mid, low


def dot(a, b):
    return jnp.dot(a, b, preferred_element_type=jnp.float32)


def dot_last(a, b):
    return lax.dot_general(a, b, (((1,), (1,)), ((), ())), preferred_element_type=jnp.float32)


def log_forget(forget):
    return jnp.minimum(forget, 0.0) - jnp.log1p(jnp.exp(-jnp.abs(forget)))


def triangle(length, lower):
    rows = lax.broadcasted_iota(jnp.int32, (length, length), 0)
    cols = lax.broadcasted_iota(jnp.int32, (length, length), 1)
    return rows >= cols if lower else rows <= cols


def cumulative_rows(logf):
    ones = triangle(logf.shape[1], False).astype(jnp.bfloat16)
    high, mid, low = split_three(logf)
    return (dot(low, ones) + dot(mid, ones)) + dot(high, ones)


def cumulative_columns(logf):
    ones = triangle(logf.shape[1], True).astype(jnp.bfloat16)
    high, mid, low = split_three(logf)
    return (dot_last(ones, low) + dot_last(ones, mid)) + dot_last(ones, high)


TAIL = 8
VECTOR, TOP, DECAY = range(3)


def member(quad):
    return lax.rem(lax.axis_index(AXES[1]), quad)


def tail_rows(vector, top, decay):
    rest = jnp.zeros((TAIL - 3, vector.shape[1]), jnp.float32)
    return jnp.concatenate([vector, top, decay, rest], axis=0)


def put_state(ref, state, top, decay):
    matrix_rows = ref.shape[0] - TAIL
    ref[0:matrix_rows, :] = state[0:matrix_rows, :]
    place = lax.broadcasted_iota(jnp.int32, (TAIL, ref.shape[1]), 0)
    tail = jnp.where(place == TOP, top, state[matrix_rows:, :])
    ref[matrix_rows:, :] = jnp.where(place == DECAY, decay, tail)


def tail_row(ref, row):
    first = ref.shape[0] - TAIL + row
    return ref[first : first + 1, :]


def state_kernel(k_hbm, v_hbm, in_hbm, fo_hbm, *refs):
    *out_refs, k_ref, v_ref, in_ref, fo_ref, scalar_ref, arrived = refs
    copies = [
        pltpu.make_async_copy(source, target, arrived.at[place])
        for place, (source, target) in enumerate(
            ((fo_hbm, fo_ref), (in_hbm, in_ref), (k_hbm, k_ref), (v_hbm, v_ref))
        )
    ]
    for copy in copies:
        copy.start()
    heads, length = in_ref.shape
    key_dim = k_ref.shape[1] // heads
    value_dim = v_ref.shape[1] // heads
    parts = value_dim // LANES
    copies[0].wait()
    cumul = cumulative_rows(log_forget(fo_ref[...]))
    copies[1].wait()
    level = in_ref[...] - cumul
    level_top = jnp.max(level, axis=1, keepdims=True)
    decay = cumul[:, length - 1 : length]
    scalar_ref[0] = jnp.exp(level - level_top)
    scalar_ref[1] = jnp.broadcast_to(decay + level_top, (heads, length))
    scalar_ref[2] = jnp.broadcast_to(decay, (heads, length))
    copies[2].wait()
    copies[3].wait()
    me = member(heads)
    for step, out_ref in enumerate(out_refs):
        head = me ^ step
        keys = k_ref[:, pl.ds(pl.multiple_of(head * key_dim, LANES), key_dim)]
        values = v_ref[:, pl.ds(pl.multiple_of(head * value_dim, LANES), value_dim)]
        row, top, decay = (scalar_ref[place, pl.ds(head, 1), :] for place in range(3))
        high, low = split_two(keys.astype(jnp.float32).T * row)
        matrix = dot(
            jnp.concatenate([high, low], axis=1), jnp.concatenate([values, values], axis=0)
        )
        for part in range(parts):
            out_ref[part * key_dim : (part + 1) * key_dim, :] = matrix[
                :, part * LANES : (part + 1) * LANES
            ]
        high, mid, low = split_three(row)
        vector = (dot(low, keys) + dot(mid, keys)) + dot(high, keys)
        out_ref[parts * key_dim :, :] = tail_rows(vector, top, decay)


def read_scalars(refs, scalar_ref, me):
    for step, ref in enumerate(refs):
        scalar_ref[0, pl.ds(me ^ step, 1), :] = tail_row(ref, TOP)
        scalar_ref[1, pl.ds(me ^ step, 1), :] = tail_row(ref, DECAY)
    count = len(refs)
    tops = [scalar_ref[0, place : place + 1, :] for place in range(count)]
    decays = [scalar_ref[1, place : place + 1, :] for place in range(count)]
    return tops, decays


def weights_of(tops, decays):
    moved, total = [], jnp.zeros_like(decays[0])
    for top, decay in zip(reversed(tops), reversed(decays)):
        moved.append(top + total)
        total = total + decay
    moved.reverse()
    joined = functools.reduce(jnp.maximum, moved)
    return [jnp.exp(top - joined) for top in moved], joined, total


def quad_kernel(*refs):
    *refs, out_ref, scalar_ref = refs
    me = member(len(refs))
    weights, top, decay = weights_of(*read_scalars(refs, scalar_ref, me))
    for place, weight in enumerate(weights):
        scalar_ref[0, place : place + 1, :] = weight
    total = 0.0
    for step, ref in enumerate(refs):
        total = total + scalar_ref[0, pl.ds(me ^ step, 1), :] * ref[...]
    put_state(out_ref, total, top, decay)


def later_side(axis, bit):
    return (lax.axis_index(axis) & bit) != 0


def extend(is_later, other_ref, before_ref):
    other_top = tail_row(other_ref, TOP)
    if before_ref is None:
        decay = jnp.where(is_later, tail_row(other_ref, DECAY), 0.0)
        return (
            jnp.where(is_later, other_ref[...], 0.0),
            jnp.where(is_later, other_top, floor_value),
            decay,
        )
    before_top = tail_row(before_ref, TOP)
    before_decay = tail_row(before_ref, DECAY)
    moved = other_top + before_decay
    top = jnp.where(is_later, jnp.maximum(moved, before_top), before_top)
    other_weight = jnp.where(is_later, jnp.exp(moved - top), 0.0)
    state = other_weight * other_ref[...] + jnp.exp(before_top - top) * before_ref[...]
    decay = jnp.where(is_later, tail_row(other_ref, DECAY), 0.0) + before_decay
    return state, top, decay


def butterfly_kernel(axis, bit, *refs):
    total_ref, other_ref, *before, out_total, out_before = refs
    is_later = later_side(axis, bit)
    own_top, own_decay = tail_row(total_ref, TOP), tail_row(total_ref, DECAY)
    other_top, other_decay = tail_row(other_ref, TOP), tail_row(other_ref, DECAY)
    own_moved = own_top + jnp.where(is_later, 0.0, other_decay)
    other_moved = other_top + jnp.where(is_later, own_decay, 0.0)
    top = jnp.maximum(own_moved, other_moved)
    total = (
        jnp.exp(own_moved - top) * total_ref[...] + jnp.exp(other_moved - top) * other_ref[...]
    )
    put_state(out_total, total, top, own_decay + other_decay)
    put_state(out_before, *extend(is_later, other_ref, before[0] if before else None))


def prefix_kernel(axis, bit, quad, *refs):
    other_ref, before_ref, *refs = refs
    pieces, out_refs, (scalar_ref, weight_ref) = refs[:quad], refs[quad : 2 * quad], refs[2 * quad :]
    me = member(quad)
    start, top, _ = extend(later_side(axis, bit), other_ref, before_ref)
    tops, decays = read_scalars(pieces, scalar_ref, me)
    zero = jnp.zeros_like(top)
    for place in range(quad):
        weights, joined, _ = weights_of([top] + tops[:place], [zero] + decays[:place])
        weights += [zero] * (quad - place)
        for index, weight in enumerate(weights):
            weight_ref[place, index : index + 1, :] = weight
        scalar_ref[0, place : place + 1, :] = joined
    for step, out_ref in enumerate(out_refs):
        place = me ^ step
        state = weight_ref[place, 0:1, :] * start
        for index, piece in enumerate(pieces):
            state = state + weight_ref[place, pl.ds(1 + (me ^ index), 1), :] * piece[...]
        put_state(out_ref, state, scalar_ref[0, pl.ds(place, 1), :], zero)


def inner_kernel(q_ref, k_ref, v_ref, in_ref, fo_ref, num_ref, stat_ref):
    heads, length = in_ref.shape
    key_dim = q_ref.shape[1] // heads
    value_dim = v_ref.shape[1] // heads
    logf = log_forget(fo_ref[...])
    level = in_ref[...] - cumulative_rows(logf)
    stat_ref[:, 0:heads] = cumulative_columns(logf)
    causal = triangle(length, True)
    for head in range(heads):
        queries = q_ref[:, head * key_dim : (head + 1) * key_dim]
        keys = k_ref[:, head * key_dim : (head + 1) * key_dim]
        values = v_ref[:, head * value_dim : (head + 1) * value_dim]
        scores = dot_last(queries, keys) * (key_dim**-0.5)
        masked = jnp.where(causal, level[head : head + 1, :], -jnp.inf)
        row_level = jnp.max(masked, axis=1, keepdims=True)
        weighted = jnp.exp(masked - row_level) * scores
        stat_ref[:, heads + head : heads + head + 1] = row_level
        stat_ref[:, 2 * heads + head : 2 * heads + head + 1] = jnp.sum(
            weighted, axis=1, keepdims=True
        )
        num_ref[:, head * value_dim : (head + 1) * value_dim] = dot(
            weighted.astype(jnp.bfloat16), values
        )


def outer_kernel(q_ref, num_ref, stat_ref, *refs):
    *message_refs, out_hbm, state_ref, out_ref, done = refs
    heads = stat_ref.shape[1] // 3
    key_dim = q_ref.shape[1] // heads
    value_dim = num_ref.shape[1] // heads
    parts = value_dim // LANES
    scaling = key_dim**-0.5
    me = member(heads)
    for step, ref in enumerate(message_refs):
        state_ref[me ^ step] = ref[...]

    head_of = lax.broadcasted_iota(jnp.int32, (1, heads), 1)
    top = jnp.zeros((1, heads), jnp.float32)
    vectors = []
    for head in range(heads):
        tail = state_ref[head, parts * key_dim :, :]
        top = jnp.where(head_of == head, tail[TOP : TOP + 1, 0:1], top)
        vector = tail[VECTOR : VECTOR + 1, :]
        zero = jnp.zeros_like(vector)
        vectors.append(jnp.concatenate([zero] * head + [vector] + [zero] * (heads - 1 - head), 1))
    terms = split_three(jnp.concatenate(vectors, axis=0))
    queries = q_ref[...]
    carried_den = dot_last(queries, terms[2]) + dot_last(queries, terms[1])
    carried_den = (carried_den + dot_last(queries, terms[0])) * scaling
    cumul = stat_ref[:, 0:heads]
    row_level = stat_ref[:, heads : 2 * heads]
    inner_den = stat_ref[:, 2 * heads : 3 * heads]
    joined = jnp.maximum(row_level, top)
    inner_factor = jnp.exp(row_level - joined)
    outer_factor = jnp.exp(top - joined)
    denom = inner_factor * inner_den + outer_factor * carried_den
    inverse = 1.0 / jnp.maximum(jnp.abs(denom), jnp.exp(-(cumul + joined)))
    inner_factor = inner_factor * inverse
    outer_factor = outer_factor * (inverse * scaling)

    copies = []
    for head in range(heads):
        matrix = jnp.concatenate(
            [state_ref[head, part * key_dim : (part + 1) * key_dim, :] for part in range(parts)], 1
        )
        high, low = split_two(matrix)
        query = queries[:, head * key_dim : (head + 1) * key_dim]
        carried = dot(
            jnp.concatenate([query, query], axis=1), jnp.concatenate([high, low], axis=0)
        )
        place = pl.ds(head * value_dim, value_dim)
        out_ref[:, place] = (
            inner_factor[:, head : head + 1] * num_ref[:, place]
            + outer_factor[:, head : head + 1] * carried
        ).astype(out_ref.dtype)
        copy = pltpu.make_async_copy(out_ref.at[:, place], out_hbm.at[:, place], done.at[head])
        copy.start()
        copies.append(copy)
    for copy in copies:
        copy.wait()


def swap(array, axis, step):
    count = lax.axis_size(axis)
    return lax.ppermute(array, axis, [(place, place ^ step) for place in range(count)])


def exchange(pieces):
    return [pieces[0]] + [
        swap(pieces[step], AXES[1], step) for step in range(1, len(pieces))
    ]


def on_device(groups, group_length, queries, key_vectors, value_vectors, input_gate, forget_gate):
    heads, length = input_gate.shape
    key_dim = queries.shape[1] // heads
    value_dim = value_vectors.shape[1] // heads
    message = jax.ShapeDtypeStruct(
        (value_dim // LANES * key_dim + TAIL, LANES), jnp.float32
    )
    messages = (message,) * heads
    params = pltpu.CompilerParams(vmem_limit_bytes=48 * 1024 * 1024)
    hbm = pl.BlockSpec(memory_space=pltpu.HBM)
    scalars = pltpu.VMEM((3, heads, LANES), jnp.float32)
    output = jax.ShapeDtypeStruct((length, heads * value_dim), jnp.bfloat16)
    operands = (key_vectors, value_vectors, input_gate, forget_gate)
    levels = []
    for axis, bit, size in ((AXES[1], heads, group_length), (AXES[0], 1, groups)):
        while bit < size:
            levels.append((axis, bit))
            bit *= 2

    own = pl.pallas_call(
        state_kernel,
        out_shape=messages,
        in_specs=[hbm] * len(operands),
        scratch_shapes=[pltpu.VMEM(array.shape, array.dtype) for array in operands]
        + [scalars, pltpu.SemaphoreType.DMA((len(operands),))],
        compiler_params=params,
    )(*(pltpu.with_memory_space_constraint(array, pltpu.HBM) for array in operands))
    pieces = exchange(own)
    inner_num, stats = pl.pallas_call(
        inner_kernel,
        out_shape=(
            jax.ShapeDtypeStruct((length, heads * value_dim), jnp.float32),
            jax.ShapeDtypeStruct((length, 3 * heads), jnp.float32),
        ),
        compiler_params=params,
    )(queries, *operands)
    total = pl.pallas_call(
        quad_kernel, out_shape=message, scratch_shapes=[scalars], compiler_params=params
    )(*pieces)
    before = []
    for axis, bit in levels[:-1]:
        other = swap(total, axis, bit)
        total, *before = pl.pallas_call(
            functools.partial(butterfly_kernel, axis, bit),
            out_shape=(message, message),
            compiler_params=params,
        )(total, other, *before)
    axis, bit = levels[-1]
    other = swap(total, axis, bit)
    states = pl.pallas_call(
        functools.partial(prefix_kernel, axis, bit, heads),
        out_shape=messages,
        scratch_shapes=[scalars, pltpu.VMEM((heads, 1 + heads, LANES), jnp.float32)],
        compiler_params=params,
    )(other, *before, *pieces)
    carried = exchange(states)
    return pl.pallas_call(
        outer_kernel,
        out_shape=output,
        out_specs=hbm,
        scratch_shapes=[
            pltpu.VMEM((heads,) + message.shape, message.dtype),
            pltpu.VMEM(output.shape, output.dtype),
            pltpu.SemaphoreType.DMA((heads,)),
        ],
        compiler_params=params,
    )(queries, inner_num, stats, *carried)


def solution(mesh):
    return jax.shard_map(
        functools.partial(on_device, mesh.shape["grp"], mesh.shape["seq"]),
        mesh=mesh,
        in_specs=(
            P(AXES, None),
            P(AXES, None),
            P(AXES, None),
            P(None, AXES),
            P(None, AXES),
        ),
        out_specs=P(AXES, None),
        check_vma=False,
    )
```

```python
import functools

import jax
import jax.numpy as jnp
from jax import lax
from jax.experimental import pallas as pl
from jax.experimental.pallas import tpu as pltpu
from jax.sharding import PartitionSpec as P

floor_value = -1e30
LANES = 128
AXES = ("grp", "seq")


def split_two(x):
    high = x.astype(jnp.bfloat16)
    low = (x - high.astype(jnp.float32)).astype(jnp.bfloat16)
    return high, low


def split_three(x):
    high = x.astype(jnp.bfloat16)
    rest = x - high.astype(jnp.float32)
    mid = rest.astype(jnp.bfloat16)
    low = (rest - mid.astype(jnp.float32)).astype(jnp.bfloat16)
    return high, mid, low


def dot(a, b):
    return jnp.dot(a, b, preferred_element_type=jnp.float32)


def dot_last(a, b):
    return lax.dot_general(a, b, (((1,), (1,)), ((), ())), preferred_element_type=jnp.float32)


def log_forget(forget):
    return jnp.minimum(forget, 0.0) - jnp.log1p(jnp.exp(-jnp.abs(forget)))


def triangle(length, lower):
    rows = lax.broadcasted_iota(jnp.int32, (length, length), 0)
    cols = lax.broadcasted_iota(jnp.int32, (length, length), 1)
    return rows >= cols if lower else rows <= cols


def cumulative_rows(logf):
    ones = triangle(logf.shape[1], False).astype(jnp.bfloat16)
    high, mid, low = split_three(logf)
    return (dot(low, ones) + dot(mid, ones)) + dot(high, ones)


def cumulative_columns(logf):
    ones = triangle(logf.shape[1], True).astype(jnp.bfloat16)
    high, mid, low = split_three(logf)
    return (dot_last(ones, low) + dot_last(ones, mid)) + dot_last(ones, high)


TAIL = 8
VECTOR, TOP, DECAY = range(3)


def member(quad):
    return lax.rem(lax.axis_index(AXES[1]), quad)


def tail_rows(vector, top, decay):
    rest = jnp.zeros((TAIL - 3, vector.shape[1]), jnp.float32)
    return jnp.concatenate([vector, top, decay, rest], axis=0)


def put_state(ref, state, top, decay):
    matrix_rows = ref.shape[0] - TAIL
    ref[0:matrix_rows, :] = state[0:matrix_rows, :]
    place = lax.broadcasted_iota(jnp.int32, (TAIL, ref.shape[1]), 0)
    tail = jnp.where(place == TOP, top, state[matrix_rows:, :])
    ref[matrix_rows:, :] = jnp.where(place == DECAY, decay, tail)


def tail_row(ref, row):
    first = ref.shape[0] - TAIL + row
    return ref[first : first + 1, :]


def state_kernel(k_hbm, v_hbm, in_hbm, fo_hbm, *refs):
    *out_refs, k_ref, v_ref, in_ref, fo_ref, scalar_ref, arrived = refs
    copies = [
        pltpu.make_async_copy(source, target, arrived.at[place])
        for place, (source, target) in enumerate(
            ((fo_hbm, fo_ref), (in_hbm, in_ref), (k_hbm, k_ref), (v_hbm, v_ref))
        )
    ]
    for copy in copies:
        copy.start()
    heads, length = in_ref.shape
    key_dim = k_ref.shape[1] // heads
    value_dim = v_ref.shape[1] // heads
    parts = value_dim // LANES
    copies[0].wait()
    cumul = cumulative_rows(log_forget(fo_ref[...]))
    copies[1].wait()
    level = in_ref[...] - cumul
    level_top = jnp.max(level, axis=1, keepdims=True)
    decay = cumul[:, length - 1 : length]
    scalar_ref[0] = jnp.exp(level - level_top)
    scalar_ref[1] = jnp.broadcast_to(decay + level_top, (heads, length))
    scalar_ref[2] = jnp.broadcast_to(decay, (heads, length))
    copies[2].wait()
    copies[3].wait()
    me = member(heads)
    for step in range(heads):
        head = me ^ step
        keys = k_ref[:, pl.ds(pl.multiple_of(head * key_dim, LANES), key_dim)]
        values = v_ref[:, pl.ds(pl.multiple_of(head * value_dim, LANES), value_dim)]
        row, top, decay = (scalar_ref[place, pl.ds(head, 1), :] for place in range(3))
        high, low = split_two(keys.astype(jnp.float32).T * row)
        matrix = dot(
            jnp.concatenate([high, low], axis=1), jnp.concatenate([values, values], axis=0)
        )
        high, mid, low = split_three(row)
        vector = (dot(low, keys) + dot(mid, keys)) + dot(high, keys)
        for part in range(parts):
            out_ref = out_refs[part * heads + step]
            out_ref[0:key_dim, :] = matrix[:, part * LANES : (part + 1) * LANES]
            out_ref[key_dim:, :] = tail_rows(vector, top, decay)


def read_scalars(refs, scalar_ref, me):
    for step, ref in enumerate(refs):
        scalar_ref[0, pl.ds(me ^ step, 1), :] = tail_row(ref, TOP)
        scalar_ref[1, pl.ds(me ^ step, 1), :] = tail_row(ref, DECAY)
    count = len(refs)
    tops = [scalar_ref[0, place : place + 1, :] for place in range(count)]
    decays = [scalar_ref[1, place : place + 1, :] for place in range(count)]
    return tops, decays


def weights_of(tops, decays):
    moved, total = [], jnp.zeros_like(decays[0])
    for top, decay in zip(reversed(tops), reversed(decays)):
        moved.append(top + total)
        total = total + decay
    moved.reverse()
    joined = functools.reduce(jnp.maximum, moved)
    return [jnp.exp(top - joined) for top in moved], joined, total


def quad_kernel(*refs):
    *refs, out_ref, scalar_ref = refs
    me = member(len(refs))
    weights, top, decay = weights_of(*read_scalars(refs, scalar_ref, me))
    for place, weight in enumerate(weights):
        scalar_ref[0, place : place + 1, :] = weight
    total = 0.0
    for step, ref in enumerate(refs):
        total = total + scalar_ref[0, pl.ds(me ^ step, 1), :] * ref[...]
    put_state(out_ref, total, top, decay)


def later_side(axis, bit):
    return (lax.axis_index(axis) & bit) != 0


def extend(is_later, other_ref, before_ref):
    other_top = tail_row(other_ref, TOP)
    if before_ref is None:
        decay = jnp.where(is_later, tail_row(other_ref, DECAY), 0.0)
        return (
            jnp.where(is_later, other_ref[...], 0.0),
            jnp.where(is_later, other_top, floor_value),
            decay,
        )
    before_top = tail_row(before_ref, TOP)
    before_decay = tail_row(before_ref, DECAY)
    moved = other_top + before_decay
    top = jnp.where(is_later, jnp.maximum(moved, before_top), before_top)
    other_weight = jnp.where(is_later, jnp.exp(moved - top), 0.0)
    state = other_weight * other_ref[...] + jnp.exp(before_top - top) * before_ref[...]
    decay = jnp.where(is_later, tail_row(other_ref, DECAY), 0.0) + before_decay
    return state, top, decay


def butterfly_kernel(axis, bit, *refs):
    total_ref, other_ref, *before, out_total, out_before = refs
    is_later = later_side(axis, bit)
    own_top, own_decay = tail_row(total_ref, TOP), tail_row(total_ref, DECAY)
    other_top, other_decay = tail_row(other_ref, TOP), tail_row(other_ref, DECAY)
    own_moved = own_top + jnp.where(is_later, 0.0, other_decay)
    other_moved = other_top + jnp.where(is_later, own_decay, 0.0)
    top = jnp.maximum(own_moved, other_moved)
    total = (
        jnp.exp(own_moved - top) * total_ref[...] + jnp.exp(other_moved - top) * other_ref[...]
    )
    put_state(out_total, total, top, own_decay + other_decay)
    put_state(out_before, *extend(is_later, other_ref, before[0] if before else None))


def prefix_kernel(axis, bit, quad, *refs):
    other_ref, before_ref, *refs = refs
    pieces, out_refs, (scalar_ref, weight_ref) = refs[:quad], refs[quad : 2 * quad], refs[2 * quad :]
    me = member(quad)
    start, top, _ = extend(later_side(axis, bit), other_ref, before_ref)
    tops, decays = read_scalars(pieces, scalar_ref, me)
    zero = jnp.zeros_like(top)
    for place in range(quad):
        weights, joined, _ = weights_of([top] + tops[:place], [zero] + decays[:place])
        weights += [zero] * (quad - place)
        for index, weight in enumerate(weights):
            weight_ref[place, index : index + 1, :] = weight
        scalar_ref[0, place : place + 1, :] = joined
    for step, out_ref in enumerate(out_refs):
        place = me ^ step
        state = weight_ref[place, 0:1, :] * start
        for index, piece in enumerate(pieces):
            state = state + weight_ref[place, pl.ds(1 + (me ^ index), 1), :] * piece[...]
        put_state(out_ref, state, scalar_ref[0, pl.ds(place, 1), :], zero)


def inner_kernel(q_ref, k_ref, v_ref, in_ref, fo_ref, num_ref, stat_ref):
    heads, length = in_ref.shape
    key_dim = q_ref.shape[1] // heads
    value_dim = v_ref.shape[1] // heads
    logf = log_forget(fo_ref[...])
    level = in_ref[...] - cumulative_rows(logf)
    stat_ref[:, 0:heads] = cumulative_columns(logf)
    causal = triangle(length, True)
    for head in range(heads):
        queries = q_ref[:, head * key_dim : (head + 1) * key_dim]
        keys = k_ref[:, head * key_dim : (head + 1) * key_dim]
        values = v_ref[:, head * value_dim : (head + 1) * value_dim]
        scores = dot_last(queries, keys) * (key_dim**-0.5)
        masked = jnp.where(causal, level[head : head + 1, :], -jnp.inf)
        row_level = jnp.max(masked, axis=1, keepdims=True)
        weighted = jnp.exp(masked - row_level) * scores
        stat_ref[:, heads + head : heads + head + 1] = row_level
        stat_ref[:, 2 * heads + head : 2 * heads + head + 1] = jnp.sum(
            weighted, axis=1, keepdims=True
        )
        num_ref[:, head * value_dim : (head + 1) * value_dim] = dot(
            weighted.astype(jnp.bfloat16), values
        )


def outer_kernel(q_ref, num_ref, stat_ref, *refs):
    *message_refs, out_hbm, state_ref, out_ref, done = refs
    heads = stat_ref.shape[1] // 3
    key_dim = q_ref.shape[1] // heads
    value_dim = num_ref.shape[1] // heads
    parts = value_dim // LANES
    scaling = key_dim**-0.5
    me = member(heads)
    for part in range(parts):
        for step in range(heads):
            state_ref[part, me ^ step] = message_refs[part * heads + step][...]

    head_of = lax.broadcasted_iota(jnp.int32, (1, heads), 1)
    top = jnp.zeros((1, heads), jnp.float32)
    vectors = []
    for head in range(heads):
        tail = state_ref[0, head, key_dim:, :]
        top = jnp.where(head_of == head, tail[TOP : TOP + 1, 0:1], top)
        vector = tail[VECTOR : VECTOR + 1, :]
        zero = jnp.zeros_like(vector)
        vectors.append(jnp.concatenate([zero] * head + [vector] + [zero] * (heads - 1 - head), 1))
    terms = split_three(jnp.concatenate(vectors, axis=0))
    queries = q_ref[...]
    carried_den = dot_last(queries, terms[2]) + dot_last(queries, terms[1])
    carried_den = (carried_den + dot_last(queries, terms[0])) * scaling
    cumul = stat_ref[:, 0:heads]
    row_level = stat_ref[:, heads : 2 * heads]
    inner_den = stat_ref[:, 2 * heads : 3 * heads]
    joined = jnp.maximum(row_level, top)
    inner_factor = jnp.exp(row_level - joined)
    outer_factor = jnp.exp(top - joined)
    denom = inner_factor * inner_den + outer_factor * carried_den
    inverse = 1.0 / jnp.maximum(jnp.abs(denom), jnp.exp(-(cumul + joined)))
    inner_factor = inner_factor * inverse
    outer_factor = outer_factor * (inverse * scaling)

    copies = []
    for head in range(heads):
        matrix = jnp.concatenate(
            [state_ref[part, head, 0:key_dim, :] for part in range(parts)], 1
        )
        high, low = split_two(matrix)
        query = queries[:, head * key_dim : (head + 1) * key_dim]
        carried = dot(
            jnp.concatenate([query, query], axis=1), jnp.concatenate([high, low], axis=0)
        )
        place = pl.ds(head * value_dim, value_dim)
        out_ref[:, place] = (
            inner_factor[:, head : head + 1] * num_ref[:, place]
            + outer_factor[:, head : head + 1] * carried
        ).astype(out_ref.dtype)
        copy = pltpu.make_async_copy(out_ref.at[:, place], out_hbm.at[:, place], done.at[head])
        copy.start()
        copies.append(copy)
    for copy in copies:
        copy.wait()


def swap(array, axis, step):
    count = lax.axis_size(axis)
    return lax.ppermute(array, axis, [(place, place ^ step) for place in range(count)])


def exchange(pieces):
    return [pieces[0]] + [
        swap(pieces[step], AXES[1], step) for step in range(1, len(pieces))
    ]


def on_device(groups, group_length, queries, key_vectors, value_vectors, input_gate, forget_gate):
    heads, length = input_gate.shape
    key_dim = queries.shape[1] // heads
    value_dim = value_vectors.shape[1] // heads
    parts = value_dim // LANES
    message = jax.ShapeDtypeStruct((key_dim + TAIL, LANES), jnp.float32)
    messages = (message,) * heads
    params = pltpu.CompilerParams(vmem_limit_bytes=48 * 1024 * 1024)
    hbm = pl.BlockSpec(memory_space=pltpu.HBM)
    scalars = pltpu.VMEM((3, heads, LANES), jnp.float32)
    output = jax.ShapeDtypeStruct((length, heads * value_dim), jnp.bfloat16)
    operands = (key_vectors, value_vectors, input_gate, forget_gate)
    levels = []
    for axis, bit, size in ((AXES[1], heads, group_length), (AXES[0], 1, groups)):
        while bit < size:
            levels.append((axis, bit))
            bit *= 2

    own = pl.pallas_call(
        state_kernel,
        out_shape=messages * parts,
        in_specs=[hbm] * len(operands),
        scratch_shapes=[pltpu.VMEM(array.shape, array.dtype) for array in operands]
        + [scalars, pltpu.SemaphoreType.DMA((len(operands),))],
        compiler_params=params,
    )(*(pltpu.with_memory_space_constraint(array, pltpu.HBM) for array in operands))
    inner_num, stats = pl.pallas_call(
        inner_kernel,
        out_shape=(
            jax.ShapeDtypeStruct((length, heads * value_dim), jnp.float32),
            jax.ShapeDtypeStruct((length, 3 * heads), jnp.float32),
        ),
        compiler_params=params,
    )(queries, *operands)
    join_quad = pl.pallas_call(
        quad_kernel, out_shape=message, scratch_shapes=[scalars], compiler_params=params
    )
    prefixes = pl.pallas_call(
        functools.partial(prefix_kernel, *levels[-1], heads),
        out_shape=messages,
        scratch_shapes=[scalars, pltpu.VMEM((heads, 1 + heads, LANES), jnp.float32)],
        compiler_params=params,
    )
    pieces = [exchange(own[part * heads : (part + 1) * heads]) for part in range(parts)]
    totals = [join_quad(*array) for array in pieces]
    before = [[] for _ in range(parts)]
    for axis, bit in levels[:-1]:
        join_level = pl.pallas_call(
            functools.partial(butterfly_kernel, axis, bit),
            out_shape=(message, message),
            compiler_params=params,
        )
        others = [swap(array, axis, bit) for array in totals]
        for part in range(parts):
            totals[part], *before[part] = join_level(totals[part], others[part], *before[part])
    others = [swap(array, *levels[-1]) for array in totals]
    carried = []
    for part in range(parts):
        carried += exchange(prefixes(others[part], *before[part], *pieces[part]))
    return pl.pallas_call(
        outer_kernel,
        out_shape=output,
        out_specs=hbm,
        scratch_shapes=[
            pltpu.VMEM((parts, heads) + message.shape, message.dtype),
            pltpu.VMEM(output.shape, output.dtype),
            pltpu.SemaphoreType.DMA((heads,)),
        ],
        compiler_params=params,
    )(queries, inner_num, stats, *carried)


def solution(mesh):
    return jax.shard_map(
        functools.partial(on_device, mesh.shape["grp"], mesh.shape["seq"]),
        mesh=mesh,
        in_specs=(
            P(AXES, None),
            P(AXES, None),
            P(AXES, None),
            P(None, AXES),
            P(None, AXES),
        ),
        out_specs=P(AXES, None),
        check_vma=False,
    )
```

```python
import functools

import jax
import jax.numpy as jnp
from jax import lax
from jax.experimental import pallas as pl
from jax.experimental.pallas import tpu as pltpu
from jax.sharding import PartitionSpec as P

floor_value = -1e30
LANES = 128
AXES = ("grp", "seq")


def split_two(x):
    high = x.astype(jnp.bfloat16)
    low = (x - high.astype(jnp.float32)).astype(jnp.bfloat16)
    return high, low


def split_three(x):
    high = x.astype(jnp.bfloat16)
    rest = x - high.astype(jnp.float32)
    mid = rest.astype(jnp.bfloat16)
    low = (rest - mid.astype(jnp.float32)).astype(jnp.bfloat16)
    return high, mid, low


def dot(a, b):
    return jnp.dot(a, b, preferred_element_type=jnp.float32)


def dot_last(a, b):
    return lax.dot_general(a, b, (((1,), (1,)), ((), ())), preferred_element_type=jnp.float32)


def log_forget(forget):
    return jnp.minimum(forget, 0.0) - jnp.log1p(jnp.exp(-jnp.abs(forget)))


def triangle(length, lower):
    rows = lax.broadcasted_iota(jnp.int32, (length, length), 0)
    cols = lax.broadcasted_iota(jnp.int32, (length, length), 1)
    return rows >= cols if lower else rows <= cols


def cumulative_rows(logf):
    ones = triangle(logf.shape[1], False).astype(jnp.bfloat16)
    high, mid, low = split_three(logf)
    return (dot(low, ones) + dot(mid, ones)) + dot(high, ones)


def cumulative_columns(logf):
    ones = triangle(logf.shape[1], True).astype(jnp.bfloat16)
    high, mid, low = split_three(logf)
    return (dot_last(ones, low) + dot_last(ones, mid)) + dot_last(ones, high)


TAIL = 8
VECTOR, TOP, DECAY = range(3)


def tail_rows(vector, top, decay):
    rest = jnp.zeros((TAIL - 3, vector.shape[1]), jnp.float32)
    return jnp.concatenate([vector, top, decay, rest], axis=0)


def put_state(ref, state, top, decay):
    matrix_rows = ref.shape[0] - TAIL
    ref[0:matrix_rows, :] = state[0:matrix_rows, :]
    place = lax.broadcasted_iota(jnp.int32, (TAIL, ref.shape[1]), 0)
    tail = jnp.where(place == TOP, top, state[matrix_rows:, :])
    ref[matrix_rows:, :] = jnp.where(place == DECAY, decay, tail)


def tail_row(ref, row):
    first = ref.shape[0] - TAIL + row
    return ref[first : first + 1, :]


def state_kernel(k_hbm, v_hbm, in_hbm, fo_hbm, *refs):
    out_ref, k_ref, v_ref, in_ref, fo_ref, arrived = refs
    copies = [
        pltpu.make_async_copy(source, target, arrived.at[place])
        for place, (source, target) in enumerate(
            ((fo_hbm, fo_ref), (in_hbm, in_ref), (k_hbm, k_ref), (v_hbm, v_ref))
        )
    ]
    for copy in copies:
        copy.start()
    heads, length = in_ref.shape
    key_dim = k_ref.shape[1] // heads
    value_dim = v_ref.shape[1] // heads
    parts = value_dim // LANES
    copies[0].wait()
    cumul = cumulative_rows(log_forget(fo_ref[...]))
    copies[1].wait()
    level = in_ref[...] - cumul
    level_top = jnp.max(level, axis=1, keepdims=True)
    decay = cumul[:, length - 1 : length]
    weight = jnp.exp(level - level_top)
    top = decay + level_top
    copies[2].wait()
    copies[3].wait()
    for head in range(heads):
        keys = k_ref[:, head * key_dim : (head + 1) * key_dim]
        values = v_ref[:, head * value_dim : (head + 1) * value_dim]
        row = weight[head : head + 1, :]
        high, low = split_two(keys.astype(jnp.float32).T * row)
        matrix = dot(
            jnp.concatenate([high, low], axis=1), jnp.concatenate([values, values], axis=0)
        )
        for part in range(parts):
            out_ref[head, part * key_dim : (part + 1) * key_dim, :] = matrix[
                :, part * LANES : (part + 1) * LANES
            ]
        high, mid, low = split_three(row)
        vector = (dot(low, keys) + dot(mid, keys)) + dot(high, keys)
        out_ref[head, parts * key_dim :, :] = tail_rows(
            vector,
            jnp.broadcast_to(top[head : head + 1, :], vector.shape),
            jnp.broadcast_to(decay[head : head + 1, :], vector.shape),
        )


def weights_of(tops, decays):
    moved, total = [], jnp.zeros_like(decays[0])
    for top, decay in zip(reversed(tops), reversed(decays)):
        moved.append(top + total)
        total = total + decay
    moved.reverse()
    joined = functools.reduce(jnp.maximum, moved)
    return [jnp.exp(top - joined) for top in moved], joined, total


def tops_and_decays(pieces):
    return [tail_row(piece, TOP) for piece in pieces], [tail_row(piece, DECAY) for piece in pieces]


def quad_kernel(in_ref, out_ref):
    pieces = [in_ref.at[place] for place in range(in_ref.shape[0])]
    weights, top, decay = weights_of(*tops_and_decays(pieces))
    total = 0.0
    for weight, piece in zip(weights, pieces):
        total = total + weight * piece[...]
    put_state(out_ref, total, top, decay)


def later_side(axis, bit):
    return (lax.axis_index(axis) & bit) != 0


def extend(is_later, other_ref, before_ref):
    other_top = tail_row(other_ref, TOP)
    if before_ref is None:
        decay = jnp.where(is_later, tail_row(other_ref, DECAY), 0.0)
        return (
            jnp.where(is_later, other_ref[...], 0.0),
            jnp.where(is_later, other_top, floor_value),
            decay,
        )
    before_top = tail_row(before_ref, TOP)
    before_decay = tail_row(before_ref, DECAY)
    moved = other_top + before_decay
    top = jnp.where(is_later, jnp.maximum(moved, before_top), before_top)
    other_weight = jnp.where(is_later, jnp.exp(moved - top), 0.0)
    state = other_weight * other_ref[...] + jnp.exp(before_top - top) * before_ref[...]
    decay = jnp.where(is_later, tail_row(other_ref, DECAY), 0.0) + before_decay
    return state, top, decay


def butterfly_kernel(axis, bit, *refs):
    total_ref, other_ref, *before, out_total, out_before = refs
    is_later = later_side(axis, bit)
    own_top, own_decay = tail_row(total_ref, TOP), tail_row(total_ref, DECAY)
    other_top, other_decay = tail_row(other_ref, TOP), tail_row(other_ref, DECAY)
    own_moved = own_top + jnp.where(is_later, 0.0, other_decay)
    other_moved = other_top + jnp.where(is_later, own_decay, 0.0)
    top = jnp.maximum(own_moved, other_moved)
    total = (
        jnp.exp(own_moved - top) * total_ref[...] + jnp.exp(other_moved - top) * other_ref[...]
    )
    put_state(out_total, total, top, own_decay + other_decay)
    put_state(out_before, *extend(is_later, other_ref, before[0] if before else None))


def prefix_kernel(axis, bit, other_ref, before_ref, in_ref, out_ref):
    pieces = [in_ref.at[place] for place in range(in_ref.shape[0])]
    start, top, _ = extend(later_side(axis, bit), other_ref, before_ref)
    tops, decays = tops_and_decays(pieces)
    zero = jnp.zeros_like(top)
    for place in range(len(pieces)):
        weights, joined, _ = weights_of([top] + tops[:place], [zero] + decays[:place])
        state = weights[0] * start
        for weight, piece in zip(weights[1:], pieces):
            state = state + weight * piece[...]
        put_state(out_ref.at[place], state, joined, zero)


def inner_kernel(q_ref, k_ref, v_ref, in_ref, fo_ref, num_ref, stat_ref):
    heads, length = in_ref.shape
    key_dim = q_ref.shape[1] // heads
    value_dim = v_ref.shape[1] // heads
    logf = log_forget(fo_ref[...])
    level = in_ref[...] - cumulative_rows(logf)
    stat_ref[:, 0:heads] = cumulative_columns(logf)
    causal = triangle(length, True)
    for head in range(heads):
        queries = q_ref[:, head * key_dim : (head + 1) * key_dim]
        keys = k_ref[:, head * key_dim : (head + 1) * key_dim]
        values = v_ref[:, head * value_dim : (head + 1) * value_dim]
        scores = dot_last(queries, keys) * (key_dim**-0.5)
        masked = jnp.where(causal, level[head : head + 1, :], -jnp.inf)
        row_level = jnp.max(masked, axis=1, keepdims=True)
        weighted = jnp.exp(masked - row_level) * scores
        stat_ref[:, heads + head : heads + head + 1] = row_level
        stat_ref[:, 2 * heads + head : 2 * heads + head + 1] = jnp.sum(
            weighted, axis=1, keepdims=True
        )
        num_ref[:, head * value_dim : (head + 1) * value_dim] = dot(
            weighted.astype(jnp.bfloat16), values
        )


def outer_kernel(q_ref, num_ref, stat_ref, *refs):
    state_ref, out_hbm, out_ref, done = refs
    heads = stat_ref.shape[1] // 3
    key_dim = q_ref.shape[1] // heads
    value_dim = num_ref.shape[1] // heads
    parts = value_dim // LANES
    scaling = key_dim**-0.5

    head_of = lax.broadcasted_iota(jnp.int32, (1, heads), 1)
    top = jnp.zeros((1, heads), jnp.float32)
    vectors = []
    for head in range(heads):
        tail = state_ref[head, parts * key_dim :, :]
        top = jnp.where(head_of == head, tail[TOP : TOP + 1, 0:1], top)
        vector = tail[VECTOR : VECTOR + 1, :]
        zero = jnp.zeros_like(vector)
        vectors.append(jnp.concatenate([zero] * head + [vector] + [zero] * (heads - 1 - head), 1))
    terms = split_three(jnp.concatenate(vectors, axis=0))
    queries = q_ref[...]
    carried_den = dot_last(queries, terms[2]) + dot_last(queries, terms[1])
    carried_den = (carried_den + dot_last(queries, terms[0])) * scaling
    cumul = stat_ref[:, 0:heads]
    row_level = stat_ref[:, heads : 2 * heads]
    inner_den = stat_ref[:, 2 * heads : 3 * heads]
    joined = jnp.maximum(row_level, top)
    inner_factor = jnp.exp(row_level - joined)
    outer_factor = jnp.exp(top - joined)
    denom = inner_factor * inner_den + outer_factor * carried_den
    inverse = 1.0 / jnp.maximum(jnp.abs(denom), jnp.exp(-(cumul + joined)))
    inner_factor = inner_factor * inverse
    outer_factor = outer_factor * (inverse * scaling)

    copies = []
    for head in range(heads):
        matrix = jnp.concatenate(
            [state_ref[head, part * key_dim : (part + 1) * key_dim, :] for part in range(parts)], 1
        )
        high, low = split_two(matrix)
        query = queries[:, head * key_dim : (head + 1) * key_dim]
        carried = dot(
            jnp.concatenate([query, query], axis=1), jnp.concatenate([high, low], axis=0)
        )
        place = pl.ds(head * value_dim, value_dim)
        out_ref[:, place] = (
            inner_factor[:, head : head + 1] * num_ref[:, place]
            + outer_factor[:, head : head + 1] * carried
        ).astype(out_ref.dtype)
        copy = pltpu.make_async_copy(out_ref.at[:, place], out_hbm.at[:, place], done.at[head])
        copy.start()
        copies.append(copy)
    for copy in copies:
        copy.wait()


def swap(array, axis, bit, one_way=False):
    pairs = [
        (place, place ^ bit)
        for place in range(lax.axis_size(axis))
        if not (one_way and place & bit)
    ]
    return lax.ppermute(array, axis, pairs)


def exchange(array):
    quad = array.shape[0]
    groups = [
        list(range(first, first + quad)) for first in range(0, lax.axis_size(AXES[1]), quad)
    ]
    return lax.all_to_all(array, AXES[1], 0, 0, axis_index_groups=groups)


def on_device(groups, group_length, queries, key_vectors, value_vectors, input_gate, forget_gate):
    heads, length = input_gate.shape
    key_dim = queries.shape[1] // heads
    value_dim = value_vectors.shape[1] // heads
    message = jax.ShapeDtypeStruct(
        (value_dim // LANES * key_dim + TAIL, LANES), jnp.float32
    )
    messages = jax.ShapeDtypeStruct((heads,) + message.shape, message.dtype)
    params = pltpu.CompilerParams(vmem_limit_bytes=48 * 1024 * 1024)
    hbm = pl.BlockSpec(memory_space=pltpu.HBM)
    output = jax.ShapeDtypeStruct((length, heads * value_dim), jnp.bfloat16)
    operands = (key_vectors, value_vectors, input_gate, forget_gate)
    levels = []
    for axis, bit, size in ((AXES[1], heads, group_length), (AXES[0], 1, groups)):
        while bit < size:
            levels.append((axis, bit))
            bit *= 2

    own = pl.pallas_call(
        state_kernel,
        out_shape=messages,
        in_specs=[hbm] * len(operands),
        scratch_shapes=[pltpu.VMEM(array.shape, array.dtype) for array in operands]
        + [pltpu.SemaphoreType.DMA((len(operands),))],
        compiler_params=params,
    )(*(pltpu.with_memory_space_constraint(array, pltpu.HBM) for array in operands))
    pieces = exchange(own)
    inner_num, stats = pl.pallas_call(
        inner_kernel,
        out_shape=(
            jax.ShapeDtypeStruct((length, heads * value_dim), jnp.float32),
            jax.ShapeDtypeStruct((length, 3 * heads), jnp.float32),
        ),
        compiler_params=params,
    )(queries, *operands)
    total = pl.pallas_call(quad_kernel, out_shape=message, compiler_params=params)(pieces)
    before = []
    for axis, bit in levels[:-1]:
        other = swap(total, axis, bit)
        total, *before = pl.pallas_call(
            functools.partial(butterfly_kernel, axis, bit),
            out_shape=(message, message),
            compiler_params=params,
        )(total, other, *before)
    axis, bit = levels[-1]
    other = swap(total, axis, bit, one_way=True)
    states = pl.pallas_call(
        functools.partial(prefix_kernel, axis, bit), out_shape=messages, compiler_params=params
    )(other, *before, pieces)
    carried = exchange(states)
    return pl.pallas_call(
        outer_kernel,
        out_shape=output,
        out_specs=hbm,
        scratch_shapes=[
            pltpu.VMEM(output.shape, output.dtype),
            pltpu.SemaphoreType.DMA((heads,)),
        ],
        compiler_params=params,
    )(queries, inner_num, stats, carried)


def solution(mesh):
    return jax.shard_map(
        functools.partial(on_device, mesh.shape["grp"], mesh.shape["seq"]),
        mesh=mesh,
        in_specs=(
            P(AXES, None),
            P(AXES, None),
            P(AXES, None),
            P(None, AXES),
            P(None, AXES),
        ),
        out_specs=P(AXES, None),
        check_vma=False,
    )
```

```python
import functools

import jax
import jax.numpy as jnp
from jax import lax
from jax.experimental import pallas as pl
from jax.experimental.pallas import tpu as pltpu
from jax.sharding import PartitionSpec as P

floor_value = -1e30
LANES = 128
AXES = ("grp", "seq")


def split_two(x):
    high = x.astype(jnp.bfloat16)
    low = (x - high.astype(jnp.float32)).astype(jnp.bfloat16)
    return high, low


def split_three(x):
    high = x.astype(jnp.bfloat16)
    rest = x - high.astype(jnp.float32)
    mid = rest.astype(jnp.bfloat16)
    low = (rest - mid.astype(jnp.float32)).astype(jnp.bfloat16)
    return high, mid, low


def dot(a, b):
    return jnp.dot(a, b, preferred_element_type=jnp.float32)


def dot_last(a, b):
    return lax.dot_general(a, b, (((1,), (1,)), ((), ())), preferred_element_type=jnp.float32)


def log_forget(forget):
    return jnp.minimum(forget, 0.0) - jnp.log1p(jnp.exp(-jnp.abs(forget)))


def triangle(length, lower):
    rows = lax.broadcasted_iota(jnp.int32, (length, length), 0)
    cols = lax.broadcasted_iota(jnp.int32, (length, length), 1)
    return rows >= cols if lower else rows <= cols


def cumulative_rows(logf):
    ones = triangle(logf.shape[1], False).astype(jnp.bfloat16)
    high, mid, low = split_three(logf)
    return (dot(low, ones) + dot(mid, ones)) + dot(high, ones)


def cumulative_columns(logf):
    ones = triangle(logf.shape[1], True).astype(jnp.bfloat16)
    high, mid, low = split_three(logf)
    return (dot_last(ones, low) + dot_last(ones, mid)) + dot_last(ones, high)


TAIL = 8
VECTOR, TOP, DECAY = range(3)


def member(quad):
    return lax.rem(lax.axis_index(AXES[1]), quad)


def tail_rows(vector, top, decay):
    rest = jnp.zeros((TAIL - 3, vector.shape[1]), jnp.float32)
    return jnp.concatenate([vector, top, decay, rest], axis=0)


def put_state(ref, state, top, decay):
    matrix_rows = ref.shape[0] - TAIL
    ref[0:matrix_rows, :] = state[0:matrix_rows, :]
    place = lax.broadcasted_iota(jnp.int32, (TAIL, ref.shape[1]), 0)
    tail = jnp.where(place == TOP, top, state[matrix_rows:, :])
    ref[matrix_rows:, :] = jnp.where(place == DECAY, decay, tail)


def tail_row(ref, row):
    first = ref.shape[0] - TAIL + row
    return ref[first : first + 1, :]


def state_kernel(k_hbm, v_hbm, in_hbm, fo_hbm, *refs):
    *out_refs, k_ref, v_ref, in_ref, fo_ref, scalar_ref, arrived = refs
    copies = [
        pltpu.make_async_copy(source, target, arrived.at[place])
        for place, (source, target) in enumerate(
            ((fo_hbm, fo_ref), (in_hbm, in_ref), (k_hbm, k_ref), (v_hbm, v_ref))
        )
    ]
    for copy in copies:
        copy.start()
    heads, length = in_ref.shape
    key_dim = k_ref.shape[1] // heads
    value_dim = v_ref.shape[1] // heads
    parts = value_dim // LANES
    copies[0].wait()
    cumul = cumulative_rows(log_forget(fo_ref[...]))
    copies[1].wait()
    level = in_ref[...] - cumul
    level_top = jnp.max(level, axis=1, keepdims=True)
    decay = cumul[:, length - 1 : length]
    scalar_ref[0] = jnp.exp(level - level_top)
    scalar_ref[1] = jnp.broadcast_to(decay + level_top, (heads, length))
    scalar_ref[2] = jnp.broadcast_to(decay, (heads, length))
    copies[2].wait()
    copies[3].wait()
    me = member(heads)
    for step in range(heads):
        head = me ^ step
        keys = k_ref[:, pl.ds(pl.multiple_of(head * key_dim, LANES), key_dim)]
        values = v_ref[:, pl.ds(pl.multiple_of(head * value_dim, LANES), value_dim)]
        row, top, decay = (scalar_ref[place, pl.ds(head, 1), :] for place in range(3))
        high, low = split_two(keys.astype(jnp.float32).T * row)
        matrix = dot(
            jnp.concatenate([high, low], axis=1), jnp.concatenate([values, values], axis=0)
        )
        out_ref = out_refs[step]
        for part in range(parts):
            out_ref[part * key_dim : (part + 1) * key_dim, :] = matrix[
                :, part * LANES : (part + 1) * LANES
            ]
        high, mid, low = split_three(row)
        vector = (dot(low, keys) + dot(mid, keys)) + dot(high, keys)
        out_ref[parts * key_dim :, :] = tail_rows(vector, top, decay)


def read_scalars(refs, scalar_ref, me):
    for step, ref in enumerate(refs):
        scalar_ref[0, pl.ds(me ^ step, 1), :] = tail_row(ref, TOP)
        scalar_ref[1, pl.ds(me ^ step, 1), :] = tail_row(ref, DECAY)
    count = len(refs)
    tops = [scalar_ref[0, place : place + 1, :] for place in range(count)]
    decays = [scalar_ref[1, place : place + 1, :] for place in range(count)]
    return tops, decays


def weights_of(tops, decays):
    moved, total = [], jnp.zeros_like(decays[0])
    for top, decay in zip(reversed(tops), reversed(decays)):
        moved.append(top + total)
        total = total + decay
    moved.reverse()
    joined = functools.reduce(jnp.maximum, moved)
    return [jnp.exp(top - joined) for top in moved], joined, total


def chunk_of(ref, part, rows):
    matrix_rows = rows - TAIL
    first = part * matrix_rows
    return jnp.concatenate([ref[first : first + matrix_rows, :], ref[ref.shape[0] - TAIL :, :]], 0)


def quad_kernel(quad, *refs):
    refs, out_refs, scalar_ref = refs[:quad], refs[quad:-1], refs[-1]
    me = member(quad)
    weights, top, decay = weights_of(*read_scalars(refs, scalar_ref, me))
    for place, weight in enumerate(weights):
        scalar_ref[0, place : place + 1, :] = weight
    weights = [scalar_ref[0, pl.ds(me ^ step, 1), :] for step in range(quad)]
    for part, out_ref in enumerate(out_refs):
        total = 0.0
        for weight, ref in zip(weights, refs):
            total = total + weight * chunk_of(ref, part, out_ref.shape[0])
        put_state(out_ref, total, top, decay)


def later_side(axis, bit):
    return (lax.axis_index(axis) & bit) != 0


def extend(is_later, other_ref, before_ref):
    other_top = tail_row(other_ref, TOP)
    if before_ref is None:
        decay = jnp.where(is_later, tail_row(other_ref, DECAY), 0.0)
        return (
            jnp.where(is_later, other_ref[...], 0.0),
            jnp.where(is_later, other_top, floor_value),
            decay,
        )
    before_top = tail_row(before_ref, TOP)
    before_decay = tail_row(before_ref, DECAY)
    moved = other_top + before_decay
    top = jnp.where(is_later, jnp.maximum(moved, before_top), before_top)
    other_weight = jnp.where(is_later, jnp.exp(moved - top), 0.0)
    state = other_weight * other_ref[...] + jnp.exp(before_top - top) * before_ref[...]
    decay = jnp.where(is_later, tail_row(other_ref, DECAY), 0.0) + before_decay
    return state, top, decay


def butterfly_kernel(axis, bit, *refs):
    total_ref, other_ref, *before, out_total, out_before = refs
    is_later = later_side(axis, bit)
    own_top, own_decay = tail_row(total_ref, TOP), tail_row(total_ref, DECAY)
    other_top, other_decay = tail_row(other_ref, TOP), tail_row(other_ref, DECAY)
    own_moved = own_top + jnp.where(is_later, 0.0, other_decay)
    other_moved = other_top + jnp.where(is_later, own_decay, 0.0)
    top = jnp.maximum(own_moved, other_moved)
    total = (
        jnp.exp(own_moved - top) * total_ref[...] + jnp.exp(other_moved - top) * other_ref[...]
    )
    put_state(out_total, total, top, own_decay + other_decay)
    put_state(out_before, *extend(is_later, other_ref, before[0] if before else None))


def prefix_kernel(axis, bit, quad, part, *refs):
    other_ref, before_ref, *refs = refs
    pieces, out_refs, (scalar_ref, weight_ref) = refs[:quad], refs[quad : 2 * quad], refs[2 * quad :]
    me = member(quad)
    start, top, _ = extend(later_side(axis, bit), other_ref, before_ref)
    tops, decays = read_scalars(pieces, scalar_ref, me)
    zero = jnp.zeros_like(top)
    rows = other_ref.shape[0]
    for place in range(quad):
        weights, joined, _ = weights_of([top] + tops[:place], [zero] + decays[:place])
        weights += [zero] * (quad - place)
        for index, weight in enumerate(weights):
            weight_ref[place, index : index + 1, :] = weight
        scalar_ref[0, place : place + 1, :] = joined
    for step, out_ref in enumerate(out_refs):
        place = me ^ step
        state = weight_ref[place, 0:1, :] * start
        for index, piece in enumerate(pieces):
            weight = weight_ref[place, pl.ds(1 + (me ^ index), 1), :]
            state = state + weight * chunk_of(piece, part, rows)
        put_state(out_ref, state, scalar_ref[0, pl.ds(place, 1), :], zero)


def inner_kernel(q_ref, k_ref, v_ref, in_ref, fo_ref, num_ref, stat_ref):
    heads, length = in_ref.shape
    key_dim = q_ref.shape[1] // heads
    value_dim = v_ref.shape[1] // heads
    logf = log_forget(fo_ref[...])
    level = in_ref[...] - cumulative_rows(logf)
    stat_ref[:, 0:heads] = cumulative_columns(logf)
    causal = triangle(length, True)
    for head in range(heads):
        queries = q_ref[:, head * key_dim : (head + 1) * key_dim]
        keys = k_ref[:, head * key_dim : (head + 1) * key_dim]
        values = v_ref[:, head * value_dim : (head + 1) * value_dim]
        scores = dot_last(queries, keys) * (key_dim**-0.5)
        masked = jnp.where(causal, level[head : head + 1, :], -jnp.inf)
        row_level = jnp.max(masked, axis=1, keepdims=True)
        weighted = jnp.exp(masked - row_level) * scores
        stat_ref[:, heads + head : heads + head + 1] = row_level
        stat_ref[:, 2 * heads + head : 2 * heads + head + 1] = jnp.sum(
            weighted, axis=1, keepdims=True
        )
        num_ref[:, head * value_dim : (head + 1) * value_dim] = dot(
            weighted.astype(jnp.bfloat16), values
        )


def outer_kernel(q_ref, num_ref, stat_ref, *refs):
    *message_refs, out_hbm, state_ref, out_ref, done = refs
    heads = stat_ref.shape[1] // 3
    key_dim = q_ref.shape[1] // heads
    value_dim = num_ref.shape[1] // heads
    parts = value_dim // LANES
    scaling = key_dim**-0.5
    me = member(heads)
    for part in range(parts):
        for step in range(heads):
            state_ref[part, me ^ step] = message_refs[part * heads + step][...]

    head_of = lax.broadcasted_iota(jnp.int32, (1, heads), 1)
    top = jnp.zeros((1, heads), jnp.float32)
    vectors = []
    for head in range(heads):
        tail = state_ref[0, head, key_dim:, :]
        top = jnp.where(head_of == head, tail[TOP : TOP + 1, 0:1], top)
        vector = tail[VECTOR : VECTOR + 1, :]
        zero = jnp.zeros_like(vector)
        vectors.append(jnp.concatenate([zero] * head + [vector] + [zero] * (heads - 1 - head), 1))
    terms = split_three(jnp.concatenate(vectors, axis=0))
    queries = q_ref[...]
    carried_den = dot_last(queries, terms[2]) + dot_last(queries, terms[1])
    carried_den = (carried_den + dot_last(queries, terms[0])) * scaling
    cumul = stat_ref[:, 0:heads]
    row_level = stat_ref[:, heads : 2 * heads]
    inner_den = stat_ref[:, 2 * heads : 3 * heads]
    joined = jnp.maximum(row_level, top)
    inner_factor = jnp.exp(row_level - joined)
    outer_factor = jnp.exp(top - joined)
    denom = inner_factor * inner_den + outer_factor * carried_den
    inverse = 1.0 / jnp.maximum(jnp.abs(denom), jnp.exp(-(cumul + joined)))
    inner_factor = inner_factor * inverse
    outer_factor = outer_factor * (inverse * scaling)

    copies = []
    for head in range(heads):
        matrix = jnp.concatenate(
            [state_ref[part, head, 0:key_dim, :] for part in range(parts)], 1
        )
        high, low = split_two(matrix)
        query = queries[:, head * key_dim : (head + 1) * key_dim]
        carried = dot(
            jnp.concatenate([query, query], axis=1), jnp.concatenate([high, low], axis=0)
        )
        place = pl.ds(head * value_dim, value_dim)
        out_ref[:, place] = (
            inner_factor[:, head : head + 1] * num_ref[:, place]
            + outer_factor[:, head : head + 1] * carried
        ).astype(out_ref.dtype)
        copy = pltpu.make_async_copy(out_ref.at[:, place], out_hbm.at[:, place], done.at[head])
        copy.start()
        copies.append(copy)
    for copy in copies:
        copy.wait()


def swap(array, axis, step):
    count = lax.axis_size(axis)
    return lax.ppermute(array, axis, [(place, place ^ step) for place in range(count)])


def exchange(pieces):
    return [pieces[0]] + [
        swap(pieces[step], AXES[1], step) for step in range(1, len(pieces))
    ]


def on_device(groups, group_length, queries, key_vectors, value_vectors, input_gate, forget_gate):
    heads, length = input_gate.shape
    key_dim = queries.shape[1] // heads
    value_dim = value_vectors.shape[1] // heads
    parts = value_dim // LANES
    whole = jax.ShapeDtypeStruct((parts * key_dim + TAIL, LANES), jnp.float32)
    message = jax.ShapeDtypeStruct((key_dim + TAIL, LANES), jnp.float32)
    params = pltpu.CompilerParams(vmem_limit_bytes=48 * 1024 * 1024)
    hbm = pl.BlockSpec(memory_space=pltpu.HBM)
    scalars = pltpu.VMEM((3, heads, LANES), jnp.float32)
    output = jax.ShapeDtypeStruct((length, heads * value_dim), jnp.bfloat16)
    operands = (key_vectors, value_vectors, input_gate, forget_gate)
    levels = []
    for axis, bit, size in ((AXES[1], heads, group_length), (AXES[0], 1, groups)):
        while bit < size:
            levels.append((axis, bit))
            bit *= 2

    own = pl.pallas_call(
        state_kernel,
        out_shape=(whole,) * heads,
        in_specs=[hbm] * len(operands),
        scratch_shapes=[pltpu.VMEM(array.shape, array.dtype) for array in operands]
        + [scalars, pltpu.SemaphoreType.DMA((len(operands),))],
        compiler_params=params,
    )(*(pltpu.with_memory_space_constraint(array, pltpu.HBM) for array in operands))
    inner_num, stats = pl.pallas_call(
        inner_kernel,
        out_shape=(
            jax.ShapeDtypeStruct((length, heads * value_dim), jnp.float32),
            jax.ShapeDtypeStruct((length, 3 * heads), jnp.float32),
        ),
        compiler_params=params,
    )(queries, *operands)
    pieces = exchange(own)
    totals = pl.pallas_call(
        functools.partial(quad_kernel, heads),
        out_shape=(message,) * parts,
        scratch_shapes=[scalars],
        compiler_params=params,
    )(*pieces)
    totals = list(totals)
    before = [[] for _ in range(parts)]
    for axis, bit in levels[:-1]:
        join_level = pl.pallas_call(
            functools.partial(butterfly_kernel, axis, bit),
            out_shape=(message, message),
            compiler_params=params,
        )
        others = [swap(array, axis, bit) for array in totals]
        for part in range(parts):
            totals[part], *before[part] = join_level(totals[part], others[part], *before[part])
    others = [swap(array, *levels[-1]) for array in totals]
    carried = []
    for part in range(parts):
        states = pl.pallas_call(
            functools.partial(prefix_kernel, *levels[-1], heads, part),
            out_shape=(message,) * heads,
            scratch_shapes=[scalars, pltpu.VMEM((heads, 1 + heads, LANES), jnp.float32)],
            compiler_params=params,
        )(others[part], *before[part], *pieces)
        carried += exchange(states)
    return pl.pallas_call(
        outer_kernel,
        out_shape=output,
        out_specs=hbm,
        scratch_shapes=[
            pltpu.VMEM((parts, heads) + message.shape, message.dtype),
            pltpu.VMEM(output.shape, output.dtype),
            pltpu.SemaphoreType.DMA((heads,)),
        ],
        compiler_params=params,
    )(queries, inner_num, stats, *carried)


def solution(mesh):
    return jax.shard_map(
        functools.partial(on_device, mesh.shape["grp"], mesh.shape["seq"]),
        mesh=mesh,
        in_specs=(
            P(AXES, None),
            P(AXES, None),
            P(AXES, None),
            P(None, AXES),
            P(None, AXES),
        ),
        out_specs=P(AXES, None),
        check_vma=False,
    )
```

```python
import functools

import jax
import jax.numpy as jnp
from jax import lax
from jax.experimental import pallas as pl
from jax.experimental.pallas import tpu as pltpu
from jax.sharding import PartitionSpec as P

floor_value = -1e30
LANES = 128
AXES = ("grp", "seq")


def split_two(x):
    high = x.astype(jnp.bfloat16)
    low = (x - high.astype(jnp.float32)).astype(jnp.bfloat16)
    return high, low


def split_three(x):
    high = x.astype(jnp.bfloat16)
    rest = x - high.astype(jnp.float32)
    mid = rest.astype(jnp.bfloat16)
    low = (rest - mid.astype(jnp.float32)).astype(jnp.bfloat16)
    return high, mid, low


def dot(a, b):
    return jnp.dot(a, b, preferred_element_type=jnp.float32)


def dot_last(a, b):
    return lax.dot_general(a, b, (((1,), (1,)), ((), ())), preferred_element_type=jnp.float32)


def log_forget(forget):
    return jnp.minimum(forget, 0.0) - jnp.log1p(jnp.exp(-jnp.abs(forget)))


def triangle(length, lower):
    rows = lax.broadcasted_iota(jnp.int32, (length, length), 0)
    cols = lax.broadcasted_iota(jnp.int32, (length, length), 1)
    return rows >= cols if lower else rows <= cols


def cumulative_rows(logf):
    ones = triangle(logf.shape[1], False).astype(jnp.bfloat16)
    high, mid, low = split_three(logf)
    return (dot(low, ones) + dot(mid, ones)) + dot(high, ones)


def cumulative_columns(logf):
    ones = triangle(logf.shape[1], True).astype(jnp.bfloat16)
    high, mid, low = split_three(logf)
    return (dot_last(ones, low) + dot_last(ones, mid)) + dot_last(ones, high)


TAIL = 8
VECTOR, TOP, DECAY = range(3)


def member(quad):
    return lax.rem(lax.axis_index(AXES[1]), quad)


def tail_rows(vector, top, decay):
    rest = jnp.zeros((TAIL - 3, vector.shape[1]), jnp.float32)
    return jnp.concatenate([vector, top, decay, rest], axis=0)


def put_state(ref, state, top, decay):
    matrix_rows = ref.shape[0] - TAIL
    ref[0:matrix_rows, :] = state[0:matrix_rows, :]
    place = lax.broadcasted_iota(jnp.int32, (TAIL, ref.shape[1]), 0)
    tail = jnp.where(place == TOP, top, state[matrix_rows:, :])
    ref[matrix_rows:, :] = jnp.where(place == DECAY, decay, tail)


def tail_row(ref, row):
    first = ref.shape[0] - TAIL + row
    return ref[first : first + 1, :]


def state_kernel(k_hbm, v_hbm, in_hbm, fo_hbm, *refs):
    *out_refs, k_ref, v_ref, in_ref, fo_ref, scalar_ref, arrived = refs
    copies = [
        pltpu.make_async_copy(source, target, arrived.at[place])
        for place, (source, target) in enumerate(
            ((fo_hbm, fo_ref), (in_hbm, in_ref), (k_hbm, k_ref), (v_hbm, v_ref))
        )
    ]
    for copy in copies:
        copy.start()
    heads, length = in_ref.shape
    key_dim = k_ref.shape[1] // heads
    value_dim = v_ref.shape[1] // heads
    parts = value_dim // LANES
    copies[0].wait()
    cumul = cumulative_rows(log_forget(fo_ref[...]))
    copies[1].wait()
    level = in_ref[...] - cumul
    level_top = jnp.max(level, axis=1, keepdims=True)
    decay = cumul[:, length - 1 : length]
    scalar_ref[0] = jnp.exp(level - level_top)
    scalar_ref[1] = jnp.broadcast_to(decay + level_top, (heads, length))
    scalar_ref[2] = jnp.broadcast_to(decay, (heads, length))
    copies[2].wait()
    copies[3].wait()
    me = member(heads)
    for step in range(heads):
        head = me ^ step
        keys = k_ref[:, pl.ds(pl.multiple_of(head * key_dim, LANES), key_dim)]
        values = v_ref[:, pl.ds(pl.multiple_of(head * value_dim, LANES), value_dim)]
        row, top, decay = (scalar_ref[place, pl.ds(head, 1), :] for place in range(3))
        high, low = split_two(keys.astype(jnp.float32).T * row)
        matrix = dot(
            jnp.concatenate([high, low], axis=1), jnp.concatenate([values, values], axis=0)
        )
        out_ref = out_refs[step]
        for part in range(parts):
            out_ref[part * key_dim : (part + 1) * key_dim, :] = matrix[
                :, part * LANES : (part + 1) * LANES
            ]
        high, mid, low = split_three(row)
        vector = (dot(low, keys) + dot(mid, keys)) + dot(high, keys)
        out_ref[parts * key_dim :, :] = tail_rows(vector, top, decay)


def read_scalars(refs, scalar_ref, me):
    for step, ref in enumerate(refs):
        scalar_ref[0, pl.ds(me ^ step, 1), :] = tail_row(ref, TOP)
        scalar_ref[1, pl.ds(me ^ step, 1), :] = tail_row(ref, DECAY)
    count = len(refs)
    tops = [scalar_ref[0, place : place + 1, :] for place in range(count)]
    decays = [scalar_ref[1, place : place + 1, :] for place in range(count)]
    return tops, decays


def weights_of(tops, decays):
    moved, total = [], jnp.zeros_like(decays[0])
    for top, decay in zip(reversed(tops), reversed(decays)):
        moved.append(top + total)
        total = total + decay
    moved.reverse()
    joined = functools.reduce(jnp.maximum, moved)
    return [jnp.exp(top - joined) for top in moved], joined, total


def chunk_of(ref, part, rows):
    matrix_rows = rows - TAIL
    first = part * matrix_rows
    return jnp.concatenate([ref[first : first + matrix_rows, :], ref[ref.shape[0] - TAIL :, :]], 0)


def quad_kernel(quad, *refs):
    refs, out_refs, scalar_ref = refs[:quad], refs[quad:-1], refs[-1]
    me = member(quad)
    weights, top, decay = weights_of(*read_scalars(refs, scalar_ref, me))
    for place, weight in enumerate(weights):
        scalar_ref[0, place : place + 1, :] = weight
    weights = [scalar_ref[0, pl.ds(me ^ step, 1), :] for step in range(quad)]
    for part, out_ref in enumerate(out_refs):
        total = 0.0
        for weight, ref in zip(weights, refs):
            total = total + weight * chunk_of(ref, part, out_ref.shape[0])
        put_state(out_ref, total, top, decay)


def later_side(axis, bit):
    return (lax.axis_index(axis) & bit) != 0


def extend(is_later, other_ref, before_ref):
    other_top = tail_row(other_ref, TOP)
    if before_ref is None:
        decay = jnp.where(is_later, tail_row(other_ref, DECAY), 0.0)
        return (
            jnp.where(is_later, other_ref[...], 0.0),
            jnp.where(is_later, other_top, floor_value),
            decay,
        )
    before_top = tail_row(before_ref, TOP)
    before_decay = tail_row(before_ref, DECAY)
    moved = other_top + before_decay
    top = jnp.where(is_later, jnp.maximum(moved, before_top), before_top)
    other_weight = jnp.where(is_later, jnp.exp(moved - top), 0.0)
    state = other_weight * other_ref[...] + jnp.exp(before_top - top) * before_ref[...]
    decay = jnp.where(is_later, tail_row(other_ref, DECAY), 0.0) + before_decay
    return state, top, decay


def butterfly_kernel(axis, bit, *refs):
    total_ref, other_ref, *before, out_total, out_before = refs
    is_later = later_side(axis, bit)
    own_top, own_decay = tail_row(total_ref, TOP), tail_row(total_ref, DECAY)
    other_top, other_decay = tail_row(other_ref, TOP), tail_row(other_ref, DECAY)
    own_moved = own_top + jnp.where(is_later, 0.0, other_decay)
    other_moved = other_top + jnp.where(is_later, own_decay, 0.0)
    top = jnp.maximum(own_moved, other_moved)
    total = (
        jnp.exp(own_moved - top) * total_ref[...] + jnp.exp(other_moved - top) * other_ref[...]
    )
    put_state(out_total, total, top, own_decay + other_decay)
    put_state(out_before, *extend(is_later, other_ref, before[0] if before else None))


def prefix_kernel(axis, bit, quad, parts, *refs):
    others, befores, refs = refs[:parts], refs[parts : 2 * parts], refs[2 * parts :]
    pieces, out_refs, (scalar_ref, weight_ref) = refs[:quad], refs[quad : 2 * quad], refs[2 * quad :]
    me = member(quad)
    is_later = later_side(axis, bit)
    starts = [extend(is_later, other, before) for other, before in zip(others, befores)]
    top = starts[0][1]
    tops, decays = read_scalars(pieces, scalar_ref, me)
    zero = jnp.zeros_like(top)
    rows = others[0].shape[0]
    for place in range(quad):
        weights, joined, _ = weights_of([top] + tops[:place], [zero] + decays[:place])
        weights += [zero] * (quad - place)
        for index, weight in enumerate(weights):
            weight_ref[place, index : index + 1, :] = weight
        scalar_ref[0, place : place + 1, :] = joined
    for step, out_ref in enumerate(out_refs):
        place = me ^ step
        weights = [weight_ref[place, pl.ds(1 + (me ^ index), 1), :] for index in range(quad)]
        for part, (start, _, _) in enumerate(starts):
            state = weight_ref[place, 0:1, :] * start
            for weight, piece in zip(weights, pieces):
                state = state + weight * chunk_of(piece, part, rows)
            first = part * (rows - TAIL)
            out_ref[first : first + rows - TAIL, :] = state[0 : rows - TAIL, :]
        vector = state[rows - TAIL : rows - TAIL + 1, :]
        tail = tail_rows(vector, scalar_ref[0, pl.ds(place, 1), :], zero)
        out_ref[out_ref.shape[0] - TAIL :, :] = tail


CUMUL, ROW_LEVEL, INNER_DEN = range(3)


def inner_kernel(q_ref, k_ref, v_ref, in_ref, fo_ref, num_ref, stat_ref):
    heads, length = in_ref.shape
    key_dim = q_ref.shape[1] // heads
    value_dim = v_ref.shape[1] // heads
    logf = log_forget(fo_ref[...])
    level = in_ref[...] - cumulative_rows(logf)
    cumul = cumulative_columns(logf)
    causal = triangle(length, True)
    for head in range(heads):
        queries = q_ref[:, head * key_dim : (head + 1) * key_dim]
        keys = k_ref[:, head * key_dim : (head + 1) * key_dim]
        values = v_ref[:, head * value_dim : (head + 1) * value_dim]
        scores = dot_last(queries, keys) * (key_dim**-0.5)
        masked = jnp.where(causal, level[head : head + 1, :], -jnp.inf)
        row_level = jnp.max(masked, axis=1, keepdims=True)
        weighted = jnp.exp(masked - row_level) * scores
        stat_ref[head, :, CUMUL : CUMUL + 1] = cumul[:, head : head + 1]
        stat_ref[head, :, ROW_LEVEL : ROW_LEVEL + 1] = row_level
        stat_ref[head, :, INNER_DEN : INNER_DEN + 1] = jnp.sum(weighted, axis=1, keepdims=True)
        num_ref[head] = dot(weighted.astype(jnp.bfloat16), values)


def add_carried(head, q_ref, num_ref, stat_ref, message_ref):
    length, value_dim = num_ref.shape[1:]
    key_dim = q_ref.shape[1] // num_ref.shape[0]
    parts = value_dim // LANES
    scaling = key_dim**-0.5
    query = q_ref[:, pl.ds(pl.multiple_of(head * key_dim, LANES), key_dim)]
    matrix = jnp.concatenate(
        [message_ref[part * key_dim : (part + 1) * key_dim, :] for part in range(parts)], 1
    )
    high, low = split_two(matrix)
    carried = dot(jnp.concatenate([query, query], axis=1), jnp.concatenate([high, low], axis=0))
    stats = stat_ref[head]
    cumul, row_level, inner_den = (stats[:, place : place + 1] for place in range(3))
    top = tail_row(message_ref, TOP)[:, 0:1]
    carried_den = jnp.sum(
        query.astype(jnp.float32) * tail_row(message_ref, VECTOR), axis=1, keepdims=True
    )
    joined = jnp.maximum(row_level, top)
    inner_factor = jnp.exp(row_level - joined)
    outer_factor = jnp.exp(top - joined) * scaling
    denom = inner_factor * inner_den + outer_factor * carried_den
    inverse = 1.0 / jnp.maximum(jnp.abs(denom), jnp.exp(-(cumul + joined)))
    return (inner_factor * inverse) * num_ref[head] + (outer_factor * inverse) * carried


def part_kernel(steps, q_ref, num_ref, stat_ref, *refs):
    me = member(num_ref.shape[0])
    count = len(steps)
    for step, message_ref, out_ref in zip(steps, refs[:count], refs[count:]):
        head = me ^ step
        out_ref[...] = add_carried(head, q_ref, num_ref, stat_ref, message_ref).astype(
            out_ref.dtype
        )


def last_kernel(q_ref, num_ref, stat_ref, message_ref, *refs):
    *done_refs, out_hbm, own_ref, done = refs
    heads, _, value_dim = num_ref.shape
    me = member(heads)

    def place(step, source):
        columns = pl.ds(pl.multiple_of((me ^ step) * value_dim, LANES), value_dim)
        copy = pltpu.make_async_copy(source, out_hbm.at[:, columns], done.at[step])
        copy.start()
        return copy

    copies = [place(step, ref) for step, ref in enumerate(done_refs)]
    own_ref[...] = add_carried(me ^ (heads - 1), q_ref, num_ref, stat_ref, message_ref).astype(
        own_ref.dtype
    )
    copies.append(place(heads - 1, own_ref))
    for copy in copies:
        copy.wait()


def swap(array, axis, step):
    count = lax.axis_size(axis)
    return lax.ppermute(array, axis, [(place, place ^ step) for place in range(count)])


def exchange(pieces):
    return [pieces[0]] + [
        swap(pieces[step], AXES[1], step) for step in range(1, len(pieces))
    ]


def on_device(groups, group_length, queries, key_vectors, value_vectors, input_gate, forget_gate):
    heads, length = input_gate.shape
    key_dim = queries.shape[1] // heads
    value_dim = value_vectors.shape[1] // heads
    parts = value_dim // LANES
    whole = jax.ShapeDtypeStruct((parts * key_dim + TAIL, LANES), jnp.float32)
    message = jax.ShapeDtypeStruct((key_dim + TAIL, LANES), jnp.float32)
    params = pltpu.CompilerParams(vmem_limit_bytes=48 * 1024 * 1024)
    hbm = pl.BlockSpec(memory_space=pltpu.HBM)
    scalars = pltpu.VMEM((3, heads, LANES), jnp.float32)
    output = jax.ShapeDtypeStruct((length, heads * value_dim), jnp.bfloat16)
    operands = (key_vectors, value_vectors, input_gate, forget_gate)
    levels = []
    for axis, bit, size in ((AXES[1], heads, group_length), (AXES[0], 1, groups)):
        while bit < size:
            levels.append((axis, bit))
            bit *= 2

    own = pl.pallas_call(
        state_kernel,
        out_shape=(whole,) * heads,
        in_specs=[hbm] * len(operands),
        scratch_shapes=[pltpu.VMEM(array.shape, array.dtype) for array in operands]
        + [scalars, pltpu.SemaphoreType.DMA((len(operands),))],
        compiler_params=params,
    )(*(pltpu.with_memory_space_constraint(array, pltpu.HBM) for array in operands))
    inner_num, stats = pl.pallas_call(
        inner_kernel,
        out_shape=(
            jax.ShapeDtypeStruct((heads, length, value_dim), jnp.float32),
            jax.ShapeDtypeStruct((heads, length, 3), jnp.float32),
        ),
        compiler_params=params,
    )(queries, *operands)
    pieces = exchange(own)
    totals = pl.pallas_call(
        functools.partial(quad_kernel, heads),
        out_shape=(message,) * parts,
        scratch_shapes=[scalars],
        compiler_params=params,
    )(*pieces)
    totals = list(totals)
    before = [[] for _ in range(parts)]
    for axis, bit in levels[:-1]:
        join_level = pl.pallas_call(
            functools.partial(butterfly_kernel, axis, bit),
            out_shape=(message, message),
            compiler_params=params,
        )
        others = [swap(array, axis, bit) for array in totals]
        for part in range(parts):
            totals[part], *before[part] = join_level(totals[part], others[part], *before[part])
    others = [swap(array, *levels[-1]) for array in totals]
    starts = []
    for part in range(parts):
        starts += before[part]
    states = pl.pallas_call(
        functools.partial(prefix_kernel, *levels[-1], heads, parts),
        out_shape=(whole,) * heads,
        scratch_shapes=[scalars, pltpu.VMEM((heads, 1 + heads, LANES), jnp.float32)],
        compiler_params=params,
    )(*others, *starts, *pieces)
    carried = exchange(states)
    column = jax.ShapeDtypeStruct((length, value_dim), output.dtype)
    columns = []
    for steps in [(0, 1)] + [(step,) for step in range(2, heads - 1)]:
        columns += pl.pallas_call(
            functools.partial(part_kernel, steps),
            out_shape=(column,) * len(steps),
            compiler_params=params,
        )(queries, inner_num, stats, *(carried[step] for step in steps))
    return pl.pallas_call(
        last_kernel,
        out_shape=output,
        out_specs=hbm,
        scratch_shapes=[
            pltpu.VMEM(column.shape, column.dtype),
            pltpu.SemaphoreType.DMA((heads,)),
        ],
        compiler_params=params,
    )(queries, inner_num, stats, carried[-1], *columns)


def solution(mesh):
    return jax.shard_map(
        functools.partial(on_device, mesh.shape["grp"], mesh.shape["seq"]),
        mesh=mesh,
        in_specs=(
            P(AXES, None),
            P(AXES, None),
            P(AXES, None),
            P(None, AXES),
            P(None, AXES),
        ),
        out_specs=P(AXES, None),
        check_vma=False,
    )
```

```python
import functools

import jax
import jax.numpy as jnp
from jax import lax
from jax.experimental import pallas as pl
from jax.experimental.pallas import tpu as pltpu
from jax.sharding import PartitionSpec as P

floor_value = -1e30
LANES = 128
AXES = ("grp", "seq")


def split_two(x):
    high = x.astype(jnp.bfloat16)
    low = (x - high.astype(jnp.float32)).astype(jnp.bfloat16)
    return high, low


def split_three(x):
    high = x.astype(jnp.bfloat16)
    rest = x - high.astype(jnp.float32)
    mid = rest.astype(jnp.bfloat16)
    low = (rest - mid.astype(jnp.float32)).astype(jnp.bfloat16)
    return high, mid, low


def dot(a, b):
    return jnp.dot(a, b, preferred_element_type=jnp.float32)


def dot_last(a, b):
    return lax.dot_general(a, b, (((1,), (1,)), ((), ())), preferred_element_type=jnp.float32)


def log_forget(forget):
    return jnp.minimum(forget, 0.0) - jnp.log1p(jnp.exp(-jnp.abs(forget)))


def triangle(length, lower):
    rows = lax.broadcasted_iota(jnp.int32, (length, length), 0)
    cols = lax.broadcasted_iota(jnp.int32, (length, length), 1)
    return rows >= cols if lower else rows <= cols


def cumulative_rows(logf):
    ones = triangle(logf.shape[1], False).astype(jnp.bfloat16)
    high, mid, low = split_three(logf)
    return (dot(low, ones) + dot(mid, ones)) + dot(high, ones)


def cumulative_columns(logf):
    ones = triangle(logf.shape[1], True).astype(jnp.bfloat16)
    high, mid, low = split_three(logf)
    return (dot_last(ones, low) + dot_last(ones, mid)) + dot_last(ones, high)


SIDES = 2
TAIL = 8
VECTOR, TOP, DECAY = range(3)


def member(quad):
    return lax.rem(lax.axis_index(AXES[1]), quad)


def own_side():
    return lax.rem(lax.axis_index(AXES[0]), SIDES)


def tail_row(ref, row, slot=0):
    return ref[pl.ds(ref.shape[0] - TAIL + 3 * slot + row, 1), :]


def load(ref, slot=0, slots=1):
    key_dim = (ref.shape[0] - TAIL) // slots
    rows = [tail_row(ref, row, slot) for row in range(3)]
    return (ref[slot * key_dim : (slot + 1) * key_dim, :], *rows)


def store(ref, *states):
    key_dim = states[0][0].shape[0]
    rows = []
    for slot, (matrix, *tail) in enumerate(states):
        ref[slot * key_dim : (slot + 1) * key_dim, :] = matrix
        rows += tail
    rows.append(jnp.zeros((TAIL - len(rows), ref.shape[1]), jnp.float32))
    ref[len(states) * key_dim :, :] = jnp.concatenate(rows, axis=0)


def join(earlier, later):
    early_matrix, early_vector, early_top, early_decay = earlier
    late_matrix, late_vector, late_top, late_decay = later
    moved = early_top + late_decay
    joined = jnp.maximum(moved, late_top)
    early_weight, late_weight = jnp.exp(moved - joined), jnp.exp(late_top - joined)
    return (
        early_weight * early_matrix + late_weight * late_matrix,
        early_weight * early_vector + late_weight * late_vector,
        joined,
        early_decay + late_decay,
    )


def choose(condition, one, other):
    return jax.tree.map(lambda a, b: jnp.where(condition, a, b), one, other)


def nothing(like):
    matrix, vector, top, decay = like
    zero = jnp.zeros_like(decay)
    return jnp.zeros_like(matrix), jnp.zeros_like(vector), zero + floor_value, zero


def state_kernel(k_hbm, v_hbm, in_hbm, fo_hbm, *refs):
    own_ref, send_ref, k_ref, v_ref, in_ref, fo_ref, arrived = refs
    copies = [
        pltpu.make_async_copy(source, target, arrived.at[place])
        for place, (source, target) in enumerate(
            ((fo_hbm, fo_ref), (in_hbm, in_ref), (k_hbm, k_ref), (v_hbm, v_ref))
        )
    ]
    for copy in copies:
        copy.start()
    heads, length = in_ref.shape
    key_dim = k_ref.shape[1] // heads
    value_dim = v_ref.shape[1] // heads
    copies[0].wait()
    cumul = cumulative_rows(log_forget(fo_ref[...]))
    copies[1].wait()
    level = in_ref[...] - cumul
    level_top = jnp.max(level, axis=1, keepdims=True)
    decay = cumul[:, length - 1 : length]
    weight = jnp.exp(level - level_top)
    top = decay + level_top
    first = own_side() == 0
    copies[2].wait()
    copies[3].wait()
    for head in range(heads):
        keys = k_ref[:, head * key_dim : (head + 1) * key_dim]
        values = v_ref[:, head * value_dim : (head + 1) * value_dim]
        row = weight[head : head + 1, :]
        high, low = split_two(keys.astype(jnp.float32).T * row)
        matrix = dot(
            jnp.concatenate([high, low], axis=1), jnp.concatenate([values, values], axis=0)
        )
        high, mid, low = split_three(row)
        vector = (dot(low, keys) + dot(mid, keys)) + dot(high, keys)
        tail = (
            vector,
            jnp.broadcast_to(top[head : head + 1, :], vector.shape),
            jnp.broadcast_to(decay[head : head + 1, :], vector.shape),
        )
        left, right = matrix[:, :LANES], matrix[:, LANES:]
        store(own_ref.at[head], (jnp.where(first, left, right), *tail))
        store(send_ref.at[head], (jnp.where(first, right, left), *tail))


def pack_kernel(own_ref, other_ref, *out_refs):
    me, first = member(len(out_refs)), own_side() == 0
    for step, out_ref in enumerate(out_refs):
        own, other = load(own_ref.at[me ^ step]), load(other_ref.at[me ^ step])
        store(out_ref, choose(first, own, other), choose(first, other, own))


def read_scalars(refs, scalar_ref, me, slot):
    for step, ref in enumerate(refs):
        scalar_ref[0, pl.ds(me ^ step, 1), :] = tail_row(ref, TOP, slot)
        scalar_ref[1, pl.ds(me ^ step, 1), :] = tail_row(ref, DECAY, slot)
    count = len(refs)
    tops = [scalar_ref[0, place : place + 1, :] for place in range(count)]
    decays = [scalar_ref[1, place : place + 1, :] for place in range(count)]
    return tops, decays


def weights_of(tops, decays):
    moved, total = [], jnp.zeros_like(decays[0])
    for top, decay in zip(reversed(tops), reversed(decays)):
        moved.append(top + total)
        total = total + decay
    moved.reverse()
    joined = functools.reduce(jnp.maximum, moved)
    return [jnp.exp(top - joined) for top in moved], joined, total


def weighted_sum(weights, states):
    matrix, vector = 0.0, 0.0
    for weight, state in zip(weights, states):
        matrix = matrix + weight * state[0]
        vector = vector + weight * state[1]
    return matrix, vector


def quad_kernel(*refs):
    *refs, out_ref, scalar_ref = refs
    me = member(len(refs))
    totals = []
    for slot in range(SIDES):
        scalars = scalar_ref.at[slot]
        weights, top, decay = weights_of(*read_scalars(refs, scalars, me, slot))
        for place, weight in enumerate(weights):
            scalars[2, place : place + 1, :] = weight
        weights = [scalars[2, pl.ds(me ^ step, 1), :] for step in range(len(refs))]
        totals.append((*weighted_sum(weights, [load(ref, slot, SIDES) for ref in refs]), top, decay))
    store(out_ref, *totals)


def later_side(axis, bit):
    return (lax.axis_index(axis) & bit) != 0


def extend(is_later, other, before):
    return choose(is_later, join(other, before), before)


def butterfly_kernel(axis, bit, slots, *refs):
    total_ref, other_ref, *before_refs, out_total, out_before = refs
    is_later = later_side(axis, bit)
    totals, befores = [], []
    for slot in range(slots):
        total, other = load(total_ref, slot, slots), load(other_ref, slot, slots)
        before = load(before_refs[0], slot, slots) if before_refs else nothing(total)
        totals.append(join(choose(is_later, other, total), choose(is_later, total, other)))
        befores.append(extend(is_later, other, before))
    store(out_total, *totals)
    store(out_before, *befores)


def pair_kernel(in_ref, out_ref):
    store(out_ref, join(*(load(in_ref, slot, SIDES) for slot in range(SIDES))))


def prefix_kernel(axis, bit, quad, other_ref, group_ref, within_ref, *refs):
    *refs, scalar_ref, weight_ref = refs
    first = len(refs) - 2 * quad
    before_refs, pieces, out_refs = refs[:first], refs[first : first + quad], refs[first + quad :]
    me = member(quad)
    other = load(other_ref)
    before = load(before_refs[0]) if before_refs else nothing(other)
    start = extend(later_side(axis, bit), other, before)
    results = [[] for _ in range(quad)]
    for slot in range(SIDES):
        at_quad = join(start, load(within_ref, slot, SIDES))
        scalars, kept = scalar_ref.at[slot], weight_ref.at[slot]
        tops, decays = read_scalars(pieces, scalars, me, slot)
        zero = jnp.zeros_like(tops[0])
        for place in range(quad):
            weights, joined, _ = weights_of([at_quad[2]] + tops[:place], [zero] + decays[:place])
            weights += [zero] * (quad - place)
            for index, weight in enumerate(weights):
                kept[place, index : index + 1, :] = weight
            scalars[2, place : place + 1, :] = joined
        states = [at_quad] + [load(piece, slot, SIDES) for piece in pieces]
        for step in range(quad):
            place = me ^ step
            weights = [kept[place, 0:1, :]]
            weights += [kept[place, pl.ds(1 + (me ^ index), 1), :] for index in range(quad)]
            top = scalars[2, pl.ds(place, 1), :]
            results[step].append((*weighted_sum(weights, states), top, zero))
        start = join(start, load(group_ref, slot, SIDES))
    for out_ref, states in zip(out_refs, results):
        store(out_ref, *states)


def part_kernel(*refs):
    _, *refs, out_ref = refs
    key_dim = (refs[0].shape[0] - TAIL) // SIDES
    me, other = member(len(refs)), SIDES - 1 - own_side()
    for step, ref in enumerate(refs):
        out_ref[me ^ step] = ref[pl.ds(pl.multiple_of(other * key_dim, 8), key_dim), :]


def carry(query, matrix):
    high, low = split_two(matrix)
    return dot(jnp.concatenate([query, query], axis=1), jnp.concatenate([high, low], axis=0))


CUMUL, ROW_LEVEL, INNER_DEN = range(3)


def inner_kernel(q_ref, k_ref, v_ref, in_ref, fo_ref, num_ref, stat_ref):
    heads, length = in_ref.shape
    key_dim = q_ref.shape[1] // heads
    value_dim = v_ref.shape[1] // heads
    parts = value_dim // LANES
    logf = log_forget(fo_ref[...])
    level = in_ref[...] - cumulative_rows(logf)
    cumul = cumulative_columns(logf)
    causal = triangle(length, True)
    for head in range(heads):
        queries = q_ref[:, head * key_dim : (head + 1) * key_dim]
        keys = k_ref[:, head * key_dim : (head + 1) * key_dim]
        values = v_ref[:, head * value_dim : (head + 1) * value_dim]
        scores = dot_last(queries, keys) * (key_dim**-0.5)
        masked = jnp.where(causal, level[head : head + 1, :], -jnp.inf)
        row_level = jnp.max(masked, axis=1, keepdims=True)
        weighted = jnp.exp(masked - row_level) * scores
        stat_ref[head, :, CUMUL : CUMUL + 1] = cumul[:, head : head + 1]
        stat_ref[head, :, ROW_LEVEL : ROW_LEVEL + 1] = row_level
        stat_ref[head, :, INNER_DEN : INNER_DEN + 1] = jnp.sum(weighted, axis=1, keepdims=True)
        inner_num = dot(weighted.astype(jnp.bfloat16), values)
        for part in range(parts):
            num_ref[part, head] = inner_num[:, part * LANES : (part + 1) * LANES]


def outer_kernel(q_ref, num_ref, stat_ref, *refs):
    *refs, out_ref, factor_ref = refs
    heads = len(refs)
    key_dim = q_ref.shape[1] // heads
    scaling = key_dim**-0.5
    me, side = member(heads), own_side()
    for step, ref in enumerate(refs):
        head = me ^ step
        query = q_ref[:, pl.ds(pl.multiple_of(head * key_dim, LANES), key_dim)]
        carried = carry(query, ref[pl.ds(pl.multiple_of(side * key_dim, 8), key_dim), :])
        stats = stat_ref[head]
        cumul, row_level, inner_den = (stats[:, place : place + 1] for place in range(3))
        top = tail_row(ref, TOP, side)[:, 0:1]
        carried_den = jnp.sum(
            query.astype(jnp.float32) * tail_row(ref, VECTOR, side), axis=1, keepdims=True
        )
        joined = jnp.maximum(row_level, top)
        inner_factor = jnp.exp(row_level - joined)
        outer_factor = jnp.exp(top - joined) * scaling
        denom = inner_factor * inner_den + outer_factor * carried_den
        inverse = 1.0 / jnp.maximum(jnp.abs(denom), jnp.exp(-(cumul + joined)))
        inner_factor, outer_factor = inner_factor * inverse, outer_factor * inverse
        out_ref[head] = inner_factor * num_ref[side, head] + outer_factor * carried
        factor_ref[head, :, 0:1] = inner_factor
        factor_ref[head, :, 1:2] = outer_factor


def last_kernel(q_ref, num_ref, factor_ref, own_ref, state_ref, out_hbm, out_ref, done):
    heads, key_dim = state_ref.shape[:2]
    value_dim = out_ref.shape[1] // heads
    other = SIDES - 1 - own_side()
    copies = []
    for head in range(heads):
        carried = carry(q_ref[:, head * key_dim : (head + 1) * key_dim], state_ref[head])
        factors = factor_ref[head]
        late = factors[:, 0:1] * num_ref[other, head] + factors[:, 1:2] * carried
        early = own_ref[head]
        place = pl.ds(head * value_dim, value_dim)
        out_ref[:, place] = jnp.concatenate(
            [jnp.where(other == 0, late, early), jnp.where(other == 0, early, late)], axis=1
        ).astype(out_ref.dtype)
        copy = pltpu.make_async_copy(out_ref.at[:, place], out_hbm.at[:, place], done.at[head])
        copy.start()
        copies.append(copy)
    for copy in copies:
        copy.wait()


def swap(array, axis, step):
    count = lax.axis_size(axis)
    return lax.ppermute(array, axis, [(place, place ^ step) for place in range(count)])


def exchange(pieces):
    return [pieces[0]] + [swap(pieces[step], AXES[1], step) for step in range(1, len(pieces))]


def on_device(groups, group_length, queries, key_vectors, value_vectors, input_gate, forget_gate):
    heads, length = input_gate.shape
    key_dim = queries.shape[1] // heads
    value_dim = value_vectors.shape[1] // heads
    params = pltpu.CompilerParams(vmem_limit_bytes=48 * 1024 * 1024)
    hbm = pl.BlockSpec(memory_space=pltpu.HBM)

    def shape(*dims):
        return jax.ShapeDtypeStruct(dims, jnp.float32)

    def call(kernel, out_shape, *arrays, scratch=()):
        return pl.pallas_call(
            kernel, out_shape=out_shape, scratch_shapes=scratch, compiler_params=params
        )(*arrays)

    single = shape(key_dim + TAIL, LANES)
    double = shape(SIDES * key_dim + TAIL, LANES)
    halves = shape(heads, key_dim + TAIL, LANES)
    scalars = pltpu.VMEM((SIDES, 3, heads, LANES), jnp.float32)
    output = jax.ShapeDtypeStruct((length, heads * value_dim), jnp.bfloat16)
    operands = (key_vectors, value_vectors, input_gate, forget_gate)

    def levels(axis, bit, size):
        while bit < size:
            yield axis, bit
            bit *= 2

    own, send = pl.pallas_call(
        state_kernel,
        out_shape=(halves, halves),
        in_specs=[hbm] * len(operands),
        scratch_shapes=[pltpu.VMEM(array.shape, array.dtype) for array in operands]
        + [pltpu.SemaphoreType.DMA((len(operands),))],
        compiler_params=params,
    )(*(pltpu.with_memory_space_constraint(array, pltpu.HBM) for array in operands))
    packed = call(pack_kernel, (double,) * heads, own, swap(send, AXES[0], 1))
    pieces = exchange(packed)
    inner_num, stats = call(
        inner_kernel,
        (shape(value_dim // LANES, heads, length, LANES), shape(heads, length, 3)),
        queries,
        *operands,
    )
    group = call(quad_kernel, double, *pieces, scratch=[scalars])
    within = []
    for axis, bit in levels(AXES[1], heads, group_length):
        kernel = functools.partial(butterfly_kernel, axis, bit, SIDES)
        group, *within = call(kernel, (double, double), group, swap(group, axis, bit), *within)
    total = call(pair_kernel, single, group)
    before = []
    *steps, last = levels(AXES[0], SIDES, groups)
    for axis, bit in steps:
        kernel = functools.partial(butterfly_kernel, axis, bit, 1)
        total, *before = call(kernel, (single, single), total, swap(total, axis, bit), *before)
    states = call(
        functools.partial(prefix_kernel, *last, heads),
        (double,) * heads,
        swap(total, *last),
        group,
        *within,
        *before,
        *pieces,
        scratch=[scalars, pltpu.VMEM((SIDES, heads, 1 + heads, LANES), jnp.float32)],
    )
    carried = exchange(states)
    half = call(part_kernel, shape(heads, key_dim, LANES), stats, *carried)
    other_half = swap(half, AXES[0], 1)
    columns, factors = call(
        outer_kernel,
        (shape(heads, length, LANES), shape(heads, length, 2)),
        queries,
        inner_num,
        stats,
        *carried,
    )
    return pl.pallas_call(
        last_kernel,
        out_shape=output,
        out_specs=hbm,
        scratch_shapes=[
            pltpu.VMEM(output.shape, output.dtype),
            pltpu.SemaphoreType.DMA((heads,)),
        ],
        compiler_params=params,
    )(queries, inner_num, factors, columns, other_half)


def solution(mesh):
    return jax.shard_map(
        functools.partial(on_device, mesh.shape["grp"], mesh.shape["seq"]),
        mesh=mesh,
        in_specs=(
            P(AXES, None),
            P(AXES, None),
            P(AXES, None),
            P(None, AXES),
            P(None, AXES),
        ),
        out_specs=P(AXES, None),
        check_vma=False,
    )
```

```python
import functools

import jax
import jax.numpy as jnp
from jax import lax
from jax.experimental import pallas as pl
from jax.experimental.pallas import tpu as pltpu
from jax.sharding import PartitionSpec as P

floor_value = -1e30
LANES = 128
AXES = ("grp", "seq")


def split_two(x):
    high = x.astype(jnp.bfloat16)
    low = (x - high.astype(jnp.float32)).astype(jnp.bfloat16)
    return high, low


def split_three(x):
    high = x.astype(jnp.bfloat16)
    rest = x - high.astype(jnp.float32)
    mid = rest.astype(jnp.bfloat16)
    low = (rest - mid.astype(jnp.float32)).astype(jnp.bfloat16)
    return high, mid, low


def dot(a, b):
    return jnp.dot(a, b, preferred_element_type=jnp.float32)


def dot_last(a, b):
    return lax.dot_general(a, b, (((1,), (1,)), ((), ())), preferred_element_type=jnp.float32)


def log_forget(forget):
    return jnp.minimum(forget, 0.0) - jnp.log1p(jnp.exp(-jnp.abs(forget)))


def triangle(length, lower):
    rows = lax.broadcasted_iota(jnp.int32, (length, length), 0)
    cols = lax.broadcasted_iota(jnp.int32, (length, length), 1)
    return rows >= cols if lower else rows <= cols


def cumulative_rows(logf):
    ones = triangle(logf.shape[1], False).astype(jnp.bfloat16)
    high, mid, low = split_three(logf)
    return (dot(low, ones) + dot(mid, ones)) + dot(high, ones)


def cumulative_columns(logf):
    ones = triangle(logf.shape[1], True).astype(jnp.bfloat16)
    high, mid, low = split_three(logf)
    return (dot_last(ones, low) + dot_last(ones, mid)) + dot_last(ones, high)


SIDES = 2
TAIL = 8
VECTOR, TOP, DECAY = range(3)


def member(quad):
    return lax.rem(lax.axis_index(AXES[1]), quad)


def own_side():
    return lax.rem(lax.axis_index(AXES[0]), SIDES)


def reversed_bits(step, quad):
    bits = quad.bit_length() - 1
    return sum(((step >> bit) & 1) << (bits - 1 - bit) for bit in range(bits))


def partner(step, quad):
    distance = jnp.where(own_side() == 0, reversed_bits(step, quad), step)
    return member(quad) ^ distance


def tail_row(ref, row, slot=0):
    return ref[pl.ds(ref.shape[0] - TAIL + 3 * slot + row, 1), :]


def load(ref, slot=0, slots=1):
    key_dim = (ref.shape[0] - TAIL) // slots
    rows = [tail_row(ref, row, slot) for row in range(3)]
    return (ref[slot * key_dim : (slot + 1) * key_dim, :], *rows)


def store(ref, *states):
    key_dim = states[0][0].shape[0]
    rows = []
    for slot, (matrix, *tail) in enumerate(states):
        ref[slot * key_dim : (slot + 1) * key_dim, :] = matrix
        rows += tail
    rows.append(jnp.zeros((TAIL - len(rows), ref.shape[1]), jnp.float32))
    ref[len(states) * key_dim :, :] = jnp.concatenate(rows, axis=0)


def join(earlier, later):
    early_matrix, early_vector, early_top, early_decay = earlier
    late_matrix, late_vector, late_top, late_decay = later
    moved = early_top + late_decay
    joined = jnp.maximum(moved, late_top)
    early_weight, late_weight = jnp.exp(moved - joined), jnp.exp(late_top - joined)
    return (
        early_weight * early_matrix + late_weight * late_matrix,
        early_weight * early_vector + late_weight * late_vector,
        joined,
        early_decay + late_decay,
    )


def choose(condition, one, other):
    return jax.tree.map(lambda a, b: jnp.where(condition, a, b), one, other)


def nothing(like):
    matrix, vector, top, decay = like
    zero = jnp.zeros_like(decay)
    return jnp.zeros_like(matrix), jnp.zeros_like(vector), zero + floor_value, zero


def state_kernel(k_hbm, v_hbm, in_hbm, fo_hbm, *refs):
    own_ref, send_ref, k_ref, v_ref, in_ref, fo_ref, arrived = refs
    copies = [
        pltpu.make_async_copy(source, target, arrived.at[place])
        for place, (source, target) in enumerate(
            ((fo_hbm, fo_ref), (in_hbm, in_ref), (k_hbm, k_ref), (v_hbm, v_ref))
        )
    ]
    for copy in copies:
        copy.start()
    heads, length = in_ref.shape
    key_dim = k_ref.shape[1] // heads
    value_dim = v_ref.shape[1] // heads
    copies[0].wait()
    cumul = cumulative_rows(log_forget(fo_ref[...]))
    copies[1].wait()
    level = in_ref[...] - cumul
    level_top = jnp.max(level, axis=1, keepdims=True)
    decay = cumul[:, length - 1 : length]
    weight = jnp.exp(level - level_top)
    top = decay + level_top
    first = own_side() == 0
    copies[2].wait()
    copies[3].wait()
    for head in range(heads):
        keys = k_ref[:, head * key_dim : (head + 1) * key_dim]
        values = v_ref[:, head * value_dim : (head + 1) * value_dim]
        row = weight[head : head + 1, :]
        high, low = split_two(keys.astype(jnp.float32).T * row)
        matrix = dot(
            jnp.concatenate([high, low], axis=1), jnp.concatenate([values, values], axis=0)
        )
        high, mid, low = split_three(row)
        vector = (dot(low, keys) + dot(mid, keys)) + dot(high, keys)
        tail = (
            vector,
            jnp.broadcast_to(top[head : head + 1, :], vector.shape),
            jnp.broadcast_to(decay[head : head + 1, :], vector.shape),
        )
        left, right = matrix[:, :LANES], matrix[:, LANES:]
        store(own_ref.at[head], (jnp.where(first, left, right), *tail))
        store(send_ref.at[head], (jnp.where(first, right, left), *tail))


def pack_kernel(own_ref, other_ref, *refs):
    *refs, num_ref, stat_ref = refs
    inner_refs, out_refs = refs[:5], refs[5:]

    @pl.when(own_side() == 0)
    def _():
        inner_sums(*inner_refs, num_ref, stat_ref)

    first = own_side() == 0
    for step, out_ref in enumerate(out_refs):
        place = partner(step, len(out_refs))
        own, other = load(own_ref.at[place]), load(other_ref.at[place])
        store(out_ref, choose(first, own, other), choose(first, other, own))


def read_scalars(refs, scalar_ref, slot):
    count = len(refs)
    for step, ref in enumerate(refs):
        place = partner(step, count)
        scalar_ref[0, pl.ds(place, 1), :] = tail_row(ref, TOP, slot)
        scalar_ref[1, pl.ds(place, 1), :] = tail_row(ref, DECAY, slot)
    tops = [scalar_ref[0, place : place + 1, :] for place in range(count)]
    decays = [scalar_ref[1, place : place + 1, :] for place in range(count)]
    return tops, decays


def weights_of(tops, decays):
    moved, total = [], jnp.zeros_like(decays[0])
    for top, decay in zip(reversed(tops), reversed(decays)):
        moved.append(top + total)
        total = total + decay
    moved.reverse()
    joined = functools.reduce(jnp.maximum, moved)
    return [jnp.exp(top - joined) for top in moved], joined, total


def weighted_sum(weights, states):
    matrix, vector = 0.0, 0.0
    for weight, state in zip(weights, states):
        matrix = matrix + weight * state[0]
        vector = vector + weight * state[1]
    return matrix, vector


def quad_kernel(*refs):
    *refs, out_ref, scalar_ref = refs
    places = [partner(step, len(refs)) for step in range(len(refs))]
    totals = []
    for slot in range(SIDES):
        scalars = scalar_ref.at[slot]
        weights, top, decay = weights_of(*read_scalars(refs, scalars, slot))
        for place, weight in enumerate(weights):
            scalars[2, place : place + 1, :] = weight
        weights = [scalars[2, pl.ds(place, 1), :] for place in places]
        totals.append((*weighted_sum(weights, [load(ref, slot, SIDES) for ref in refs]), top, decay))
    store(out_ref, *totals)


def later_side(axis, bit):
    return (lax.axis_index(axis) & bit) != 0


def extend(is_later, other, before):
    return choose(is_later, join(other, before), before)


def butterfly_kernel(axis, bit, slots, *refs):
    total_ref, other_ref, *before_refs, out_total, out_before = refs
    is_later = later_side(axis, bit)
    totals, befores = [], []
    for slot in range(slots):
        total, other = load(total_ref, slot, slots), load(other_ref, slot, slots)
        before = load(before_refs[0], slot, slots) if before_refs else nothing(total)
        totals.append(join(choose(is_later, other, total), choose(is_later, total, other)))
        befores.append(extend(is_later, other, before))
    store(out_total, *totals)
    store(out_before, *befores)


def pair_kernel(in_ref, out_ref):
    store(out_ref, join(*(load(in_ref, slot, SIDES) for slot in range(SIDES))))


def prefix_kernel(axis, bit, quad, other_ref, group_ref, within_ref, *refs):
    *refs, scalar_ref, weight_ref = refs
    first = len(refs) - 2 * quad
    before_refs, pieces, out_refs = refs[:first], refs[first : first + quad], refs[first + quad :]
    places = [partner(step, quad) for step in range(quad)]
    other = load(other_ref)
    before = load(before_refs[0]) if before_refs else nothing(other)
    start = extend(later_side(axis, bit), other, before)
    results = [[] for _ in range(quad)]
    for slot in range(SIDES):
        at_quad = join(start, load(within_ref, slot, SIDES))
        scalars, kept = scalar_ref.at[slot], weight_ref.at[slot]
        tops, decays = read_scalars(pieces, scalars, slot)
        zero = jnp.zeros_like(tops[0])
        for place in range(quad):
            weights, joined, _ = weights_of([at_quad[2]] + tops[:place], [zero] + decays[:place])
            weights += [zero] * (quad - place)
            for index, weight in enumerate(weights):
                kept[place, index : index + 1, :] = weight
            scalars[2, place : place + 1, :] = joined
        states = [at_quad] + [load(piece, slot, SIDES) for piece in pieces]
        for step, place in enumerate(places):
            weights = [kept[place, 0:1, :]]
            weights += [kept[place, pl.ds(1 + index, 1), :] for index in places]
            top = scalars[2, pl.ds(place, 1), :]
            results[step].append((*weighted_sum(weights, states), top, zero))
        start = join(start, load(group_ref, slot, SIDES))
    for out_ref, states in zip(out_refs, results):
        store(out_ref, *states)


def part_kernel(*refs):
    _, *refs, out_ref = refs
    key_dim = (refs[0].shape[0] - TAIL) // SIDES
    other = SIDES - 1 - own_side()
    for step, ref in enumerate(refs):
        out_ref[partner(step, len(refs))] = ref[pl.ds(pl.multiple_of(other * key_dim, 8), key_dim), :]


def carry(query, matrix):
    high, low = split_two(matrix)
    return dot(jnp.concatenate([query, query], axis=1), jnp.concatenate([high, low], axis=0))


CUMUL, ROW_LEVEL, INNER_DEN = range(3)


def inner_kernel(q_ref, k_ref, v_ref, in_ref, fo_ref, early_num, early_stat, num_ref, stat_ref):
    @pl.when(own_side() != 0)
    def _():
        inner_sums(q_ref, k_ref, v_ref, in_ref, fo_ref, num_ref, stat_ref)

    @pl.when(own_side() == 0)
    def _():
        num_ref[...] = early_num[...]
        stat_ref[...] = early_stat[...]


def inner_sums(q_ref, k_ref, v_ref, in_ref, fo_ref, num_ref, stat_ref):
    heads, length = in_ref.shape
    key_dim = q_ref.shape[1] // heads
    value_dim = v_ref.shape[1] // heads
    parts = value_dim // LANES
    logf = log_forget(fo_ref[...])
    level = in_ref[...] - cumulative_rows(logf)
    cumul = cumulative_columns(logf)
    causal = triangle(length, True)
    for head in range(heads):
        queries = q_ref[:, head * key_dim : (head + 1) * key_dim]
        keys = k_ref[:, head * key_dim : (head + 1) * key_dim]
        values = v_ref[:, head * value_dim : (head + 1) * value_dim]
        scores = dot_last(queries, keys) * (key_dim**-0.5)
        masked = jnp.where(causal, level[head : head + 1, :], -jnp.inf)
        row_level = jnp.max(masked, axis=1, keepdims=True)
        weighted = jnp.exp(masked - row_level) * scores
        stat_ref[head, :, CUMUL : CUMUL + 1] = cumul[:, head : head + 1]
        stat_ref[head, :, ROW_LEVEL : ROW_LEVEL + 1] = row_level
        stat_ref[head, :, INNER_DEN : INNER_DEN + 1] = jnp.sum(weighted, axis=1, keepdims=True)
        inner_num = dot(weighted.astype(jnp.bfloat16), values)
        for part in range(parts):
            num_ref[part, head] = inner_num[:, part * LANES : (part + 1) * LANES]


def outer_kernel(q_ref, num_ref, stat_ref, *refs):
    *refs, out_ref, factor_ref = refs
    heads = len(refs)
    key_dim = q_ref.shape[1] // heads
    scaling = key_dim**-0.5
    side = own_side()
    for step, ref in enumerate(refs):
        head = partner(step, heads)
        query = q_ref[:, pl.ds(pl.multiple_of(head * key_dim, LANES), key_dim)]
        carried = carry(query, ref[pl.ds(pl.multiple_of(side * key_dim, 8), key_dim), :])
        stats = stat_ref[head]
        cumul, row_level, inner_den = (stats[:, place : place + 1] for place in range(3))
        top = tail_row(ref, TOP, side)[:, 0:1]
        carried_den = jnp.sum(
            query.astype(jnp.float32) * tail_row(ref, VECTOR, side), axis=1, keepdims=True
        )
        joined = jnp.maximum(row_level, top)
        inner_factor = jnp.exp(row_level - joined)
        outer_factor = jnp.exp(top - joined) * scaling
        denom = inner_factor * inner_den + outer_factor * carried_den
        inverse = 1.0 / jnp.maximum(jnp.abs(denom), jnp.exp(-(cumul + joined)))
        inner_factor, outer_factor = inner_factor * inverse, outer_factor * inverse
        out_ref[head] = inner_factor * num_ref[side, head] + outer_factor * carried
        factor_ref[head, :, 0:1] = inner_factor
        factor_ref[head, :, 1:2] = outer_factor


def last_kernel(q_ref, num_ref, factor_ref, own_ref, state_ref, out_hbm, out_ref, done):
    heads, key_dim = state_ref.shape[:2]
    value_dim = out_ref.shape[1] // heads
    other = SIDES - 1 - own_side()
    copies = []
    for head in range(heads):
        carried = carry(q_ref[:, head * key_dim : (head + 1) * key_dim], state_ref[head])
        factors = factor_ref[head]
        late = factors[:, 0:1] * num_ref[other, head] + factors[:, 1:2] * carried
        early = own_ref[head]
        place = pl.ds(head * value_dim, value_dim)
        out_ref[:, place] = jnp.concatenate(
            [jnp.where(other == 0, late, early), jnp.where(other == 0, early, late)], axis=1
        ).astype(out_ref.dtype)
        copy = pltpu.make_async_copy(out_ref.at[:, place], out_hbm.at[:, place], done.at[head])
        copy.start()
        copies.append(copy)
    for copy in copies:
        copy.wait()


def swap(array, axis, step):
    count = lax.axis_size(axis)
    return lax.ppermute(array, axis, [(place, place ^ step) for place in range(count)])


def exchange(pieces):
    quad = len(pieces)
    groups, length = (lax.axis_size(axis) for axis in AXES)

    def pairs(step):
        for group in range(groups):
            distance = step if group % SIDES else reversed_bits(step, quad)
            for place in range(length):
                yield group * length + place, group * length + (place ^ distance)

    return [pieces[0]] + [
        lax.ppermute(pieces[step], AXES, list(pairs(step))) for step in range(1, quad)
    ]


def on_device(groups, group_length, queries, key_vectors, value_vectors, input_gate, forget_gate):
    heads, length = input_gate.shape
    key_dim = queries.shape[1] // heads
    value_dim = value_vectors.shape[1] // heads
    params = pltpu.CompilerParams(vmem_limit_bytes=48 * 1024 * 1024)
    hbm = pl.BlockSpec(memory_space=pltpu.HBM)

    def shape(*dims):
        return jax.ShapeDtypeStruct(dims, jnp.float32)

    def call(kernel, out_shape, *arrays, scratch=()):
        return pl.pallas_call(
            kernel, out_shape=out_shape, scratch_shapes=scratch, compiler_params=params
        )(*arrays)

    single = shape(key_dim + TAIL, LANES)
    double = shape(SIDES * key_dim + TAIL, LANES)
    halves = shape(heads, key_dim + TAIL, LANES)
    scalars = pltpu.VMEM((SIDES, 3, heads, LANES), jnp.float32)
    output = jax.ShapeDtypeStruct((length, heads * value_dim), jnp.bfloat16)
    operands = (key_vectors, value_vectors, input_gate, forget_gate)

    def levels(axis, bit, size):
        while bit < size:
            yield axis, bit
            bit *= 2

    own, send = pl.pallas_call(
        state_kernel,
        out_shape=(halves, halves),
        in_specs=[hbm] * len(operands),
        scratch_shapes=[pltpu.VMEM(array.shape, array.dtype) for array in operands]
        + [pltpu.SemaphoreType.DMA((len(operands),))],
        compiler_params=params,
    )(*(pltpu.with_memory_space_constraint(array, pltpu.HBM) for array in operands))
    inner_shapes = (shape(value_dim // LANES, heads, length, LANES), shape(heads, length, 3))
    *packed, early_num, early_stats = call(
        pack_kernel,
        (double,) * heads + inner_shapes,
        own,
        swap(send, AXES[0], 1),
        queries,
        *operands,
    )
    pieces = exchange(packed)
    inner_num, stats = call(
        inner_kernel, inner_shapes, queries, *operands, early_num, early_stats
    )
    group = call(quad_kernel, double, *pieces, scratch=[scalars])
    within = []
    for axis, bit in levels(AXES[1], heads, group_length):
        kernel = functools.partial(butterfly_kernel, axis, bit, SIDES)
        group, *within = call(kernel, (double, double), group, swap(group, axis, bit), *within)
    total = call(pair_kernel, single, group)
    before = []
    *steps, last = levels(AXES[0], SIDES, groups)
    for axis, bit in steps:
        kernel = functools.partial(butterfly_kernel, axis, bit, 1)
        total, *before = call(kernel, (single, single), total, swap(total, axis, bit), *before)
    states = call(
        functools.partial(prefix_kernel, *last, heads),
        (double,) * heads,
        swap(total, *last),
        group,
        *within,
        *before,
        *pieces,
        scratch=[scalars, pltpu.VMEM((SIDES, heads, 1 + heads, LANES), jnp.float32)],
    )
    carried = exchange(states)
    half = call(part_kernel, shape(heads, key_dim, LANES), stats, *carried)
    other_half = swap(half, AXES[0], 1)
    columns, factors = call(
        outer_kernel,
        (shape(heads, length, LANES), shape(heads, length, 2)),
        queries,
        inner_num,
        stats,
        *carried,
    )
    return pl.pallas_call(
        last_kernel,
        out_shape=output,
        out_specs=hbm,
        scratch_shapes=[
            pltpu.VMEM(output.shape, output.dtype),
            pltpu.SemaphoreType.DMA((heads,)),
        ],
        compiler_params=params,
    )(queries, inner_num, factors, columns, other_half)


def solution(mesh):
    return jax.shard_map(
        functools.partial(on_device, mesh.shape["grp"], mesh.shape["seq"]),
        mesh=mesh,
        in_specs=(
            P(AXES, None),
            P(AXES, None),
            P(AXES, None),
            P(None, AXES),
            P(None, AXES),
        ),
        out_specs=P(AXES, None),
        check_vma=False,
    )
```

```python
import functools

import jax
import jax.numpy as jnp
from jax import lax
from jax.experimental import pallas as pl
from jax.experimental.pallas import tpu as pltpu
from jax.sharding import PartitionSpec as P

floor_value = -1e30
LANES = 128
AXES = ("grp", "seq")


def split_two(x):
    high = x.astype(jnp.bfloat16)
    low = (x - high.astype(jnp.float32)).astype(jnp.bfloat16)
    return high, low


def split_three(x):
    high = x.astype(jnp.bfloat16)
    rest = x - high.astype(jnp.float32)
    mid = rest.astype(jnp.bfloat16)
    low = (rest - mid.astype(jnp.float32)).astype(jnp.bfloat16)
    return high, mid, low


def dot(a, b):
    return jnp.dot(a, b, preferred_element_type=jnp.float32)


def dot_last(a, b):
    return lax.dot_general(a, b, (((1,), (1,)), ((), ())), preferred_element_type=jnp.float32)


def log_forget(forget):
    return jnp.minimum(forget, 0.0) - jnp.log1p(jnp.exp(-jnp.abs(forget)))


def triangle(length, lower):
    rows = lax.broadcasted_iota(jnp.int32, (length, length), 0)
    cols = lax.broadcasted_iota(jnp.int32, (length, length), 1)
    return rows >= cols if lower else rows <= cols


def cumulative_rows(logf):
    ones = triangle(logf.shape[1], False).astype(jnp.bfloat16)
    high, mid, low = split_three(logf)
    return (dot(low, ones) + dot(mid, ones)) + dot(high, ones)


def cumulative_columns(logf):
    ones = triangle(logf.shape[1], True).astype(jnp.bfloat16)
    high, mid, low = split_three(logf)
    return (dot_last(ones, low) + dot_last(ones, mid)) + dot_last(ones, high)


TAIL = 8
VECTOR, TOP, DECAY = range(3)


def member(quad):
    return lax.rem(lax.axis_index(AXES[1]), quad)


def distances(quad, side):
    order = [0, quad - 1, *range(1, quad - 1)]
    bits = quad.bit_length() - 1
    if side:
        return order
    return [sum(((step >> bit) & 1) << (bits - 1 - bit) for bit in range(bits)) for step in order]


def partners(quad):
    even = (lax.axis_index(AXES[0]) & 1) == 0
    return [
        member(quad) ^ jnp.where(even, one, other)
        for one, other in zip(distances(quad, 0), distances(quad, 1))
    ]


def tail_rows(vector, top, decay):
    rest = jnp.zeros((TAIL - 3, vector.shape[1]), jnp.float32)
    return jnp.concatenate([vector, top, decay, rest], axis=0)


def put_state(ref, state, top, decay):
    matrix_rows = ref.shape[0] - TAIL
    ref[0:matrix_rows, :] = state[0:matrix_rows, :]
    place = lax.broadcasted_iota(jnp.int32, (TAIL, ref.shape[1]), 0)
    tail = jnp.where(place == TOP, top, state[matrix_rows:, :])
    ref[matrix_rows:, :] = jnp.where(place == DECAY, decay, tail)


def tail_row(ref, row):
    first = ref.shape[0] - TAIL + row
    return ref[first : first + 1, :]


def state_kernel(k_hbm, v_hbm, in_hbm, fo_hbm, *refs):
    *out_refs, k_ref, v_ref, in_ref, fo_ref, scalar_ref, arrived = refs
    copies = [
        pltpu.make_async_copy(source, target, arrived.at[place])
        for place, (source, target) in enumerate(
            ((fo_hbm, fo_ref), (in_hbm, in_ref), (k_hbm, k_ref), (v_hbm, v_ref))
        )
    ]
    for copy in copies:
        copy.start()
    heads, length = in_ref.shape
    key_dim = k_ref.shape[1] // heads
    value_dim = v_ref.shape[1] // heads
    parts = value_dim // LANES
    copies[0].wait()
    cumul = cumulative_rows(log_forget(fo_ref[...]))
    copies[1].wait()
    level = in_ref[...] - cumul
    level_top = jnp.max(level, axis=1, keepdims=True)
    decay = cumul[:, length - 1 : length]
    scalar_ref[0] = jnp.exp(level - level_top)
    scalar_ref[1] = jnp.broadcast_to(decay + level_top, (heads, length))
    scalar_ref[2] = jnp.broadcast_to(decay, (heads, length))
    copies[2].wait()
    copies[3].wait()
    for head, out_ref in zip(partners(heads), out_refs):
        keys = k_ref[:, pl.ds(pl.multiple_of(head * key_dim, LANES), key_dim)]
        values = v_ref[:, pl.ds(pl.multiple_of(head * value_dim, LANES), value_dim)]
        row, top, decay = (scalar_ref[place, pl.ds(head, 1), :] for place in range(3))
        high, low = split_two(keys.astype(jnp.float32).T * row)
        matrix = dot(
            jnp.concatenate([high, low], axis=1), jnp.concatenate([values, values], axis=0)
        )
        for part in range(parts):
            out_ref[part * key_dim : (part + 1) * key_dim, :] = matrix[
                :, part * LANES : (part + 1) * LANES
            ]
        high, mid, low = split_three(row)
        vector = (dot(low, keys) + dot(mid, keys)) + dot(high, keys)
        out_ref[parts * key_dim :, :] = tail_rows(vector, top, decay)


def read_scalars(refs, scalar_ref, places):
    for place, ref in zip(places, refs):
        scalar_ref[0, pl.ds(place, 1), :] = tail_row(ref, TOP)
        scalar_ref[1, pl.ds(place, 1), :] = tail_row(ref, DECAY)
    count = len(refs)
    tops = [scalar_ref[0, place : place + 1, :] for place in range(count)]
    decays = [scalar_ref[1, place : place + 1, :] for place in range(count)]
    return tops, decays


def weights_of(tops, decays):
    moved, total = [], jnp.zeros_like(decays[0])
    for top, decay in zip(reversed(tops), reversed(decays)):
        moved.append(top + total)
        total = total + decay
    moved.reverse()
    joined = functools.reduce(jnp.maximum, moved)
    return [jnp.exp(top - joined) for top in moved], joined, total


def quad_kernel(*refs):
    *refs, out_ref, scalar_ref = refs
    places = partners(len(refs))
    weights, top, decay = weights_of(*read_scalars(refs, scalar_ref, places))
    for place, weight in enumerate(weights):
        scalar_ref[0, place : place + 1, :] = weight
    total = 0.0
    for place, ref in zip(places, refs):
        total = total + scalar_ref[0, pl.ds(place, 1), :] * ref[...]
    put_state(out_ref, total, top, decay)


def later_side(axis, bit):
    return (lax.axis_index(axis) & bit) != 0


def extend(is_later, other_ref, before_ref):
    other_top = tail_row(other_ref, TOP)
    if before_ref is None:
        decay = jnp.where(is_later, tail_row(other_ref, DECAY), 0.0)
        return (
            jnp.where(is_later, other_ref[...], 0.0),
            jnp.where(is_later, other_top, floor_value),
            decay,
        )
    before_top = tail_row(before_ref, TOP)
    before_decay = tail_row(before_ref, DECAY)
    moved = other_top + before_decay
    top = jnp.where(is_later, jnp.maximum(moved, before_top), before_top)
    other_weight = jnp.where(is_later, jnp.exp(moved - top), 0.0)
    state = other_weight * other_ref[...] + jnp.exp(before_top - top) * before_ref[...]
    decay = jnp.where(is_later, tail_row(other_ref, DECAY), 0.0) + before_decay
    return state, top, decay


def butterfly_kernel(axis, bit, *refs):
    total_ref, other_ref, *before, out_total, out_before = refs
    is_later = later_side(axis, bit)
    own_top, own_decay = tail_row(total_ref, TOP), tail_row(total_ref, DECAY)
    other_top, other_decay = tail_row(other_ref, TOP), tail_row(other_ref, DECAY)
    own_moved = own_top + jnp.where(is_later, 0.0, other_decay)
    other_moved = other_top + jnp.where(is_later, own_decay, 0.0)
    top = jnp.maximum(own_moved, other_moved)
    total = (
        jnp.exp(own_moved - top) * total_ref[...] + jnp.exp(other_moved - top) * other_ref[...]
    )
    put_state(out_total, total, top, own_decay + other_decay)
    put_state(out_before, *extend(is_later, other_ref, before[0] if before else None))


def prefix_kernel(axis, bit, quad, *refs):
    other_ref, before_ref, *refs = refs
    pieces, out_refs, (scalar_ref, weight_ref) = refs[:quad], refs[quad : 2 * quad], refs[2 * quad :]
    places = partners(quad)
    start, top, _ = extend(later_side(axis, bit), other_ref, before_ref)
    tops, decays = read_scalars(pieces, scalar_ref, places)
    zero = jnp.zeros_like(top)
    for place in range(quad):
        weights, joined, _ = weights_of([top] + tops[:place], [zero] + decays[:place])
        weights += [zero] * (quad - place)
        for index, weight in enumerate(weights):
            weight_ref[place, index : index + 1, :] = weight
        scalar_ref[0, place : place + 1, :] = joined
    for place, out_ref in zip(places, out_refs):
        state = weight_ref[place, 0:1, :] * start
        for index, piece in zip(places, pieces):
            state = state + weight_ref[place, pl.ds(1 + index, 1), :] * piece[...]
        put_state(out_ref, state, scalar_ref[0, pl.ds(place, 1), :], zero)


CUMUL, ROW_LEVEL, INNER_DEN = range(3)


def inner_kernel(q_ref, k_ref, v_ref, in_ref, fo_ref, num_ref, stat_ref):
    heads, length = in_ref.shape
    key_dim = q_ref.shape[1] // heads
    value_dim = v_ref.shape[1] // heads
    logf = log_forget(fo_ref[...])
    level = in_ref[...] - cumulative_rows(logf)
    cumul = cumulative_columns(logf)
    causal = triangle(length, True)
    for head in range(heads):
        queries = q_ref[:, head * key_dim : (head + 1) * key_dim]
        keys = k_ref[:, head * key_dim : (head + 1) * key_dim]
        values = v_ref[:, head * value_dim : (head + 1) * value_dim]
        scores = dot_last(queries, keys) * (key_dim**-0.5)
        masked = jnp.where(causal, level[head : head + 1, :], -jnp.inf)
        row_level = jnp.max(masked, axis=1, keepdims=True)
        weighted = jnp.exp(masked - row_level) * scores
        stat_ref[head, :, CUMUL : CUMUL + 1] = cumul[:, head : head + 1]
        stat_ref[head, :, ROW_LEVEL : ROW_LEVEL + 1] = row_level
        stat_ref[head, :, INNER_DEN : INNER_DEN + 1] = jnp.sum(weighted, axis=1, keepdims=True)
        num_ref[head] = dot(weighted.astype(jnp.bfloat16), values)


def add_carried(head, q_ref, num_ref, stat_ref, message_ref):
    length, value_dim = num_ref.shape[1:]
    key_dim = q_ref.shape[1] // num_ref.shape[0]
    parts = value_dim // LANES
    scaling = key_dim**-0.5
    query = q_ref[:, pl.ds(pl.multiple_of(head * key_dim, LANES), key_dim)]
    matrix = jnp.concatenate(
        [message_ref[part * key_dim : (part + 1) * key_dim, :] for part in range(parts)], 1
    )
    high, low = split_two(matrix)
    carried = dot(jnp.concatenate([query, query], axis=1), jnp.concatenate([high, low], axis=0))
    stats = stat_ref[head]
    cumul, row_level, inner_den = (stats[:, place : place + 1] for place in range(3))
    top = tail_row(message_ref, TOP)[:, 0:1]
    carried_den = jnp.sum(
        query.astype(jnp.float32) * tail_row(message_ref, VECTOR), axis=1, keepdims=True
    )
    joined = jnp.maximum(row_level, top)
    inner_factor = jnp.exp(row_level - joined)
    outer_factor = jnp.exp(top - joined) * scaling
    denom = inner_factor * inner_den + outer_factor * carried_den
    inverse = 1.0 / jnp.maximum(jnp.abs(denom), jnp.exp(-(cumul + joined)))
    return (inner_factor * inverse) * num_ref[head] + (outer_factor * inverse) * carried


def part_kernel(steps, q_ref, num_ref, stat_ref, *refs):
    places = partners(num_ref.shape[0])
    count = len(steps)
    for step, message_ref, out_ref in zip(steps, refs[:count], refs[count:]):
        head = places[step]
        out_ref[...] = add_carried(head, q_ref, num_ref, stat_ref, message_ref).astype(
            out_ref.dtype
        )


def last_kernel(q_ref, num_ref, stat_ref, message_ref, *refs):
    *done_refs, out_hbm, own_ref, done = refs
    heads, _, value_dim = num_ref.shape
    places = partners(heads)

    def place(step, source):
        columns = pl.ds(pl.multiple_of(places[step] * value_dim, LANES), value_dim)
        copy = pltpu.make_async_copy(source, out_hbm.at[:, columns], done.at[step])
        copy.start()
        return copy

    copies = [place(step, ref) for step, ref in enumerate(done_refs)]
    own_ref[...] = add_carried(places[-1], q_ref, num_ref, stat_ref, message_ref).astype(
        own_ref.dtype
    )
    copies.append(place(heads - 1, own_ref))
    for copy in copies:
        copy.wait()


def swap(array, axis, step):
    count = lax.axis_size(axis)
    return lax.ppermute(array, axis, [(place, place ^ step) for place in range(count)])


def exchange(pieces):
    quad = len(pieces)
    groups, length = (lax.axis_size(axis) for axis in AXES)
    results = [pieces[0]]
    for step in range(1, quad):
        pairs = [
            (group * length + place, group * length + (place ^ distances(quad, group & 1)[step]))
            for group in range(groups)
            for place in range(length)
        ]
        results.append(lax.ppermute(pieces[step], AXES, pairs))
    return results


def on_device(groups, group_length, queries, key_vectors, value_vectors, input_gate, forget_gate):
    heads, length = input_gate.shape
    key_dim = queries.shape[1] // heads
    value_dim = value_vectors.shape[1] // heads
    message = jax.ShapeDtypeStruct(
        (value_dim // LANES * key_dim + TAIL, LANES), jnp.float32
    )
    messages = (message,) * heads
    params = pltpu.CompilerParams(vmem_limit_bytes=48 * 1024 * 1024)
    hbm = pl.BlockSpec(memory_space=pltpu.HBM)
    scalars = pltpu.VMEM((3, heads, LANES), jnp.float32)
    output = jax.ShapeDtypeStruct((length, heads * value_dim), jnp.bfloat16)
    operands = (key_vectors, value_vectors, input_gate, forget_gate)
    levels = []
    for axis, bit, size in ((AXES[1], heads, group_length), (AXES[0], 1, groups)):
        while bit < size:
            levels.append((axis, bit))
            bit *= 2

    own = pl.pallas_call(
        state_kernel,
        out_shape=messages,
        in_specs=[hbm] * len(operands),
        scratch_shapes=[pltpu.VMEM(array.shape, array.dtype) for array in operands]
        + [scalars, pltpu.SemaphoreType.DMA((len(operands),))],
        compiler_params=params,
    )(*(pltpu.with_memory_space_constraint(array, pltpu.HBM) for array in operands))
    pieces = exchange(own)
    inner_num, stats = pl.pallas_call(
        inner_kernel,
        out_shape=(
            jax.ShapeDtypeStruct((heads, length, value_dim), jnp.float32),
            jax.ShapeDtypeStruct((heads, length, 3), jnp.float32),
        ),
        compiler_params=params,
    )(queries, *operands)
    total = pl.pallas_call(
        quad_kernel, out_shape=message, scratch_shapes=[scalars], compiler_params=params
    )(*pieces)
    before = []
    for axis, bit in levels[:-1]:
        other = swap(total, axis, bit)
        total, *before = pl.pallas_call(
            functools.partial(butterfly_kernel, axis, bit),
            out_shape=(message, message),
            compiler_params=params,
        )(total, other, *before)
    axis, bit = levels[-1]
    other = swap(total, axis, bit)
    states = pl.pallas_call(
        functools.partial(prefix_kernel, axis, bit, heads),
        out_shape=messages,
        scratch_shapes=[scalars, pltpu.VMEM((heads, 1 + heads, LANES), jnp.float32)],
        compiler_params=params,
    )(other, *before, *pieces)
    carried = exchange(states)
    column = jax.ShapeDtypeStruct((length, value_dim), output.dtype)
    columns = []
    for steps in [(0, 1)] + [(step,) for step in range(2, heads - 1)]:
        columns += pl.pallas_call(
            functools.partial(part_kernel, steps),
            out_shape=(column,) * len(steps),
            compiler_params=params,
        )(queries, inner_num, stats, *(carried[step] for step in steps))
    return pl.pallas_call(
        last_kernel,
        out_shape=output,
        out_specs=hbm,
        scratch_shapes=[
            pltpu.VMEM(column.shape, column.dtype),
            pltpu.SemaphoreType.DMA((heads,)),
        ],
        compiler_params=params,
    )(queries, inner_num, stats, carried[-1], *columns)


def solution(mesh):
    return jax.shard_map(
        functools.partial(on_device, mesh.shape["grp"], mesh.shape["seq"]),
        mesh=mesh,
        in_specs=(
            P(AXES, None),
            P(AXES, None),
            P(AXES, None),
            P(None, AXES),
            P(None, AXES),
        ),
        out_specs=P(AXES, None),
        check_vma=False,
    )
```

```python
import functools

import jax
import jax.numpy as jnp
from jax import lax
from jax.experimental import pallas as pl
from jax.experimental.pallas import tpu as pltpu
from jax.sharding import PartitionSpec as P

floor_value = -1e30
LANES = 128
AXES = ("grp", "seq")


def split_two(x):
    high = x.astype(jnp.bfloat16)
    low = (x - high.astype(jnp.float32)).astype(jnp.bfloat16)
    return high, low


def split_three(x):
    high = x.astype(jnp.bfloat16)
    rest = x - high.astype(jnp.float32)
    mid = rest.astype(jnp.bfloat16)
    low = (rest - mid.astype(jnp.float32)).astype(jnp.bfloat16)
    return high, mid, low


def dot(a, b):
    return jnp.dot(a, b, preferred_element_type=jnp.float32)


def dot_last(a, b):
    return lax.dot_general(a, b, (((1,), (1,)), ((), ())), preferred_element_type=jnp.float32)


def log_forget(forget):
    return jnp.minimum(forget, 0.0) - jnp.log1p(jnp.exp(-jnp.abs(forget)))


def triangle(length, lower):
    rows = lax.broadcasted_iota(jnp.int32, (length, length), 0)
    cols = lax.broadcasted_iota(jnp.int32, (length, length), 1)
    return rows >= cols if lower else rows <= cols


def cumulative_rows(logf):
    ones = triangle(logf.shape[1], False).astype(jnp.bfloat16)
    high, mid, low = split_three(logf)
    return (dot(low, ones) + dot(mid, ones)) + dot(high, ones)


def cumulative_columns(logf):
    ones = triangle(logf.shape[1], True).astype(jnp.bfloat16)
    high, mid, low = split_three(logf)
    return (dot_last(ones, low) + dot_last(ones, mid)) + dot_last(ones, high)


TAIL = 8
VECTOR, TOP, DECAY = range(3)


def member(quad):
    return lax.rem(lax.axis_index(AXES[1]), quad)


def distances(quad, side):
    order = [0, 1, quad - 1, *range(2, quad - 1)]
    bits = quad.bit_length() - 1
    if side:
        return order
    return [sum(((step >> bit) & 1) << (bits - 1 - bit) for bit in range(bits)) for step in order]


def partners(quad):
    even = (lax.axis_index(AXES[0]) & 1) == 0
    return [
        member(quad) ^ jnp.where(even, one, other)
        for one, other in zip(distances(quad, 0), distances(quad, 1))
    ]


def tail_rows(vector, top, decay):
    rest = jnp.zeros((TAIL - 3, vector.shape[1]), jnp.float32)
    return jnp.concatenate([vector, top, decay, rest], axis=0)


def tail_row(ref, row):
    first = ref.shape[0] - TAIL + row
    return ref[first : first + 1, :]


def load(ref):
    return (ref[0 : ref.shape[0] - TAIL, :], *(tail_row(ref, row) for row in range(3)))


def store(ref, state):
    matrix, *tail = state
    ref[0 : matrix.shape[0], :] = matrix
    ref[matrix.shape[0] :, :] = tail_rows(*tail)


def join(earlier, later):
    early_matrix, early_vector, early_top, early_decay = earlier
    late_matrix, late_vector, late_top, late_decay = later
    moved = early_top + late_decay
    joined = jnp.maximum(moved, late_top)
    early_weight, late_weight = jnp.exp(moved - joined), jnp.exp(late_top - joined)
    return (
        early_weight * early_matrix + late_weight * late_matrix,
        early_weight * early_vector + late_weight * late_vector,
        joined,
        early_decay + late_decay,
    )


def choose(condition, one, other):
    return jax.tree.map(lambda a, b: jnp.where(condition, a, b), one, other)


def nothing(like):
    matrix, vector, top, decay = like
    zero = jnp.zeros_like(decay)
    return jnp.zeros_like(matrix), jnp.zeros_like(vector), zero + floor_value, zero


def state_kernel(k_hbm, v_hbm, in_hbm, fo_hbm, *refs):
    *out_refs, k_ref, v_ref, in_ref, fo_ref, scalar_ref, arrived = refs
    copies = [
        pltpu.make_async_copy(source, target, arrived.at[place])
        for place, (source, target) in enumerate(
            ((fo_hbm, fo_ref), (in_hbm, in_ref), (k_hbm, k_ref), (v_hbm, v_ref))
        )
    ]
    for copy in copies:
        copy.start()
    heads, length = in_ref.shape
    key_dim = k_ref.shape[1] // heads
    value_dim = v_ref.shape[1] // heads
    parts = value_dim // LANES
    copies[0].wait()
    cumul = cumulative_rows(log_forget(fo_ref[...]))
    copies[1].wait()
    level = in_ref[...] - cumul
    level_top = jnp.max(level, axis=1, keepdims=True)
    decay = cumul[:, length - 1 : length]
    scalar_ref[0] = jnp.exp(level - level_top)
    scalar_ref[1] = jnp.broadcast_to(decay + level_top, (heads, length))
    scalar_ref[2] = jnp.broadcast_to(decay, (heads, length))
    copies[2].wait()
    copies[3].wait()
    for head, out_ref in zip(partners(heads), out_refs):
        keys = k_ref[:, pl.ds(pl.multiple_of(head * key_dim, LANES), key_dim)]
        values = v_ref[:, pl.ds(pl.multiple_of(head * value_dim, LANES), value_dim)]
        row, top, decay = (scalar_ref[place, pl.ds(head, 1), :] for place in range(3))
        high, low = split_two(keys.astype(jnp.float32).T * row)
        matrix = dot(
            jnp.concatenate([high, low], axis=1), jnp.concatenate([values, values], axis=0)
        )
        for part in range(parts):
            out_ref[part * key_dim : (part + 1) * key_dim, :] = matrix[
                :, part * LANES : (part + 1) * LANES
            ]
        high, mid, low = split_three(row)
        vector = (dot(low, keys) + dot(mid, keys)) + dot(high, keys)
        out_ref[parts * key_dim :, :] = tail_rows(vector, top, decay)


def read_scalars(refs, scalar_ref, places):
    for place, ref in zip(places, refs):
        scalar_ref[0, pl.ds(place, 1), :] = tail_row(ref, TOP)
        scalar_ref[1, pl.ds(place, 1), :] = tail_row(ref, DECAY)
    count = len(refs)
    tops = [scalar_ref[0, place : place + 1, :] for place in range(count)]
    decays = [scalar_ref[1, place : place + 1, :] for place in range(count)]
    return tops, decays


def weights_of(tops, decays):
    moved, total = [], jnp.zeros_like(decays[0])
    for top, decay in zip(reversed(tops), reversed(decays)):
        moved.append(top + total)
        total = total + decay
    moved.reverse()
    joined = functools.reduce(jnp.maximum, moved)
    return [jnp.exp(top - joined) for top in moved], joined, total


def weighted_sum(weights, states):
    matrix, vector = 0.0, 0.0
    for weight, state in zip(weights, states):
        matrix = matrix + weight * state[0]
        vector = vector + weight * state[1]
    return matrix, vector


def quad_kernel(*refs):
    *refs, out_ref, scalar_ref = refs
    places = partners(len(refs))
    weights, top, decay = weights_of(*read_scalars(refs, scalar_ref, places))
    for place, weight in enumerate(weights):
        scalar_ref[0, place : place + 1, :] = weight
    weights = [scalar_ref[0, pl.ds(place, 1), :] for place in places]
    store(out_ref, (*weighted_sum(weights, [load(ref) for ref in refs]), top, decay))


def later_side(axis, bit):
    return (lax.axis_index(axis) & bit) != 0


def butterfly_kernel(axis, bit, *refs):
    total_ref, other_ref, *before_refs, out_total, out_before = refs
    is_later = later_side(axis, bit)
    total, other = load(total_ref), load(other_ref)
    before = load(before_refs[0]) if before_refs else nothing(total)
    store(out_total, join(choose(is_later, other, total), choose(is_later, total, other)))
    store(out_before, choose(is_later, join(other, before), before))


def gather_kernel(axis, bit, own_ref, other_ref, out_ref):
    is_later = later_side(axis, bit)
    count = out_ref.shape[0] // 2
    for place in range(count):
        own = own_ref[place] if own_ref.ndim == 3 else own_ref[...]
        other = other_ref[place] if other_ref.ndim == 3 else other_ref[...]
        out_ref[place] = jnp.where(is_later, other, own)
        out_ref[count + place] = jnp.where(is_later, own, other)


def prefix_kernel(quad, own_ref, other_ref, within_ref, *refs):
    *refs, scalar_ref, weight_ref = refs
    pieces, out_refs = refs[:quad], refs[quad:]
    places = partners(quad)
    me = lax.axis_index(AXES[0])
    even = (me & 1) == 0
    start = nothing(load(within_ref))
    for group in range(2 * own_ref.shape[0] - 1):
        same = even if group % 2 == 0 else jnp.logical_not(even)
        own, other = load(own_ref.at[group // 2]), load(other_ref.at[group // 2])
        start = choose(group < me, join(start, choose(same, own, other)), start)
    start = join(start, load(within_ref))
    tops, decays = read_scalars(pieces, scalar_ref, places)
    zero = jnp.zeros_like(tops[0])
    for place in range(quad):
        weights, joined, _ = weights_of([start[2]] + tops[:place], [zero] + decays[:place])
        weights += [zero] * (quad - place)
        for index, weight in enumerate(weights):
            weight_ref[place, index : index + 1, :] = weight
        scalar_ref[0, place : place + 1, :] = joined
    states = [start] + [load(piece) for piece in pieces]
    for place, out_ref in zip(places, out_refs):
        weights = [weight_ref[place, 0:1, :]]
        weights += [weight_ref[place, pl.ds(1 + index, 1), :] for index in places]
        top = scalar_ref[0, pl.ds(place, 1), :]
        store(out_ref, (*weighted_sum(weights, states), top, zero))


CUMUL, ROW_LEVEL, INNER_DEN = range(3)


def inner_kernel(q_ref, k_ref, v_ref, in_ref, fo_ref, num_ref, stat_ref):
    heads, length = in_ref.shape
    key_dim = q_ref.shape[1] // heads
    value_dim = v_ref.shape[1] // heads
    logf = log_forget(fo_ref[...])
    level = in_ref[...] - cumulative_rows(logf)
    cumul = cumulative_columns(logf)
    causal = triangle(length, True)
    for head in range(heads):
        queries = q_ref[:, head * key_dim : (head + 1) * key_dim]
        keys = k_ref[:, head * key_dim : (head + 1) * key_dim]
        values = v_ref[:, head * value_dim : (head + 1) * value_dim]
        scores = dot_last(queries, keys) * (key_dim**-0.5)
        masked = jnp.where(causal, level[head : head + 1, :], -jnp.inf)
        row_level = jnp.max(masked, axis=1, keepdims=True)
        weighted = jnp.exp(masked - row_level) * scores
        stat_ref[head, :, CUMUL : CUMUL + 1] = cumul[:, head : head + 1]
        stat_ref[head, :, ROW_LEVEL : ROW_LEVEL + 1] = row_level
        stat_ref[head, :, INNER_DEN : INNER_DEN + 1] = jnp.sum(weighted, axis=1, keepdims=True)
        num_ref[head] = dot(weighted.astype(jnp.bfloat16), values)


def add_carried(head, q_ref, num_ref, stat_ref, message_ref):
    length, value_dim = num_ref.shape[1:]
    key_dim = q_ref.shape[1] // num_ref.shape[0]
    parts = value_dim // LANES
    scaling = key_dim**-0.5
    query = q_ref[:, pl.ds(pl.multiple_of(head * key_dim, LANES), key_dim)]
    matrix = jnp.concatenate(
        [message_ref[part * key_dim : (part + 1) * key_dim, :] for part in range(parts)], 1
    )
    high, low = split_two(matrix)
    carried = dot(jnp.concatenate([query, query], axis=1), jnp.concatenate([high, low], axis=0))
    stats = stat_ref[head]
    cumul, row_level, inner_den = (stats[:, place : place + 1] for place in range(3))
    top = tail_row(message_ref, TOP)[:, 0:1]
    carried_den = jnp.sum(
        query.astype(jnp.float32) * tail_row(message_ref, VECTOR), axis=1, keepdims=True
    )
    joined = jnp.maximum(row_level, top)
    inner_factor = jnp.exp(row_level - joined)
    outer_factor = jnp.exp(top - joined) * scaling
    denom = inner_factor * inner_den + outer_factor * carried_den
    inverse = 1.0 / jnp.maximum(jnp.abs(denom), jnp.exp(-(cumul + joined)))
    return (inner_factor * inverse) * num_ref[head] + (outer_factor * inverse) * carried


def part_kernel(steps, q_ref, num_ref, stat_ref, *refs):
    places = partners(num_ref.shape[0])
    count = len(steps)
    for step, message_ref, out_ref in zip(steps, refs[:count], refs[count:]):
        head = places[step]
        out_ref[...] = add_carried(head, q_ref, num_ref, stat_ref, message_ref).astype(
            out_ref.dtype
        )


def last_kernel(q_ref, num_ref, stat_ref, message_ref, *refs):
    *done_refs, out_hbm, own_ref, done = refs
    heads, _, value_dim = num_ref.shape
    places = partners(heads)

    def place(step, source):
        columns = pl.ds(pl.multiple_of(places[step] * value_dim, LANES), value_dim)
        copy = pltpu.make_async_copy(source, out_hbm.at[:, columns], done.at[step])
        copy.start()
        return copy

    copies = [place(step, ref) for step, ref in enumerate(done_refs)]
    own_ref[...] = add_carried(places[-1], q_ref, num_ref, stat_ref, message_ref).astype(
        own_ref.dtype
    )
    copies.append(place(heads - 1, own_ref))
    for copy in copies:
        copy.wait()


def swap(array, axis, step):
    count = lax.axis_size(axis)
    return lax.ppermute(array, axis, [(place, place ^ step) for place in range(count)])


def exchange(pieces):
    quad = len(pieces)
    groups, length = (lax.axis_size(axis) for axis in AXES)
    results = [pieces[0]]
    for step in range(1, quad):
        pairs = [
            (group * length + place, group * length + (place ^ distances(quad, group & 1)[step]))
            for group in range(groups)
            for place in range(length)
        ]
        results.append(lax.ppermute(pieces[step], AXES, pairs))
    return results


def on_device(groups, group_length, queries, key_vectors, value_vectors, input_gate, forget_gate):
    heads, length = input_gate.shape
    key_dim = queries.shape[1] // heads
    value_dim = value_vectors.shape[1] // heads
    message = jax.ShapeDtypeStruct(
        (value_dim // LANES * key_dim + TAIL, LANES), jnp.float32
    )
    messages = (message,) * heads
    params = pltpu.CompilerParams(vmem_limit_bytes=48 * 1024 * 1024)
    hbm = pl.BlockSpec(memory_space=pltpu.HBM)
    scalars = pltpu.VMEM((3, heads, LANES), jnp.float32)
    output = jax.ShapeDtypeStruct((length, heads * value_dim), jnp.bfloat16)
    operands = (key_vectors, value_vectors, input_gate, forget_gate)
    own = pl.pallas_call(
        state_kernel,
        out_shape=messages,
        in_specs=[hbm] * len(operands),
        scratch_shapes=[pltpu.VMEM(array.shape, array.dtype) for array in operands]
        + [scalars, pltpu.SemaphoreType.DMA((len(operands),))],
        compiler_params=params,
    )(*(pltpu.with_memory_space_constraint(array, pltpu.HBM) for array in operands))
    pieces = exchange(own)
    inner_num, stats = pl.pallas_call(
        inner_kernel,
        out_shape=(
            jax.ShapeDtypeStruct((heads, length, value_dim), jnp.float32),
            jax.ShapeDtypeStruct((heads, length, 3), jnp.float32),
        ),
        compiler_params=params,
    )(queries, *operands)
    total = pl.pallas_call(
        quad_kernel, out_shape=message, scratch_shapes=[scalars], compiler_params=params
    )(*pieces)
    within = []
    bit = heads
    while bit < group_length:
        total, *within = pl.pallas_call(
            functools.partial(butterfly_kernel, AXES[1], bit),
            out_shape=(message, message),
            compiler_params=params,
        )(total, swap(total, AXES[1], bit), *within)
        bit *= 2
    sums = total
    bit, count = 2, 1
    while bit < groups:
        count *= 2
        sums = pl.pallas_call(
            functools.partial(gather_kernel, AXES[0], bit),
            out_shape=jax.ShapeDtypeStruct((count,) + message.shape, message.dtype),
            compiler_params=params,
        )(sums, swap(sums, AXES[0], bit))
        bit *= 2
    states = pl.pallas_call(
        functools.partial(prefix_kernel, heads),
        out_shape=messages,
        scratch_shapes=[scalars, pltpu.VMEM((heads, 1 + heads, LANES), jnp.float32)],
        compiler_params=params,
    )(sums, swap(sums, AXES[0], 1), *within, *pieces)
    carried = exchange(states)
    column = jax.ShapeDtypeStruct((length, value_dim), output.dtype)
    columns = []
    for steps in [(0, 1)] + [(step,) for step in range(2, heads - 1)]:
        columns += pl.pallas_call(
            functools.partial(part_kernel, steps),
            out_shape=(column,) * len(steps),
            compiler_params=params,
        )(queries, inner_num, stats, *(carried[step] for step in steps))
    return pl.pallas_call(
        last_kernel,
        out_shape=output,
        out_specs=hbm,
        scratch_shapes=[
            pltpu.VMEM(column.shape, column.dtype),
            pltpu.SemaphoreType.DMA((heads,)),
        ],
        compiler_params=params,
    )(queries, inner_num, stats, carried[-1], *columns)


def solution(mesh):
    return jax.shard_map(
        functools.partial(on_device, mesh.shape["grp"], mesh.shape["seq"]),
        mesh=mesh,
        in_specs=(
            P(AXES, None),
            P(AXES, None),
            P(AXES, None),
            P(None, AXES),
            P(None, AXES),
        ),
        out_specs=P(AXES, None),
        check_vma=False,
    )
```

```python
import functools

import jax
import jax.numpy as jnp
from jax import lax
from jax.experimental import pallas as pl
from jax.experimental.pallas import tpu as pltpu
from jax.sharding import PartitionSpec as P

floor_value = -1e30
LANES = 128
AXES = ("grp", "seq")


def split_two(x):
    high = x.astype(jnp.bfloat16)
    low = (x - high.astype(jnp.float32)).astype(jnp.bfloat16)
    return high, low


def split_three(x):
    high = x.astype(jnp.bfloat16)
    rest = x - high.astype(jnp.float32)
    mid = rest.astype(jnp.bfloat16)
    low = (rest - mid.astype(jnp.float32)).astype(jnp.bfloat16)
    return high, mid, low


def dot(a, b):
    return jnp.dot(a, b, preferred_element_type=jnp.float32)


def dot_last(a, b):
    return lax.dot_general(a, b, (((1,), (1,)), ((), ())), preferred_element_type=jnp.float32)


def log_forget(forget):
    return jnp.minimum(forget, 0.0) - jnp.log1p(jnp.exp(-jnp.abs(forget)))


def triangle(length, lower):
    rows = lax.broadcasted_iota(jnp.int32, (length, length), 0)
    cols = lax.broadcasted_iota(jnp.int32, (length, length), 1)
    return rows >= cols if lower else rows <= cols


def cumulative_rows(logf):
    ones = triangle(logf.shape[1], False).astype(jnp.bfloat16)
    high, mid, low = split_three(logf)
    return (dot(low, ones) + dot(mid, ones)) + dot(high, ones)


def cumulative_columns(logf):
    ones = triangle(logf.shape[1], True).astype(jnp.bfloat16)
    high, mid, low = split_three(logf)
    return (dot_last(ones, low) + dot_last(ones, mid)) + dot_last(ones, high)


TAIL = 8
VECTOR, TOP, DECAY = range(3)


def member(quad):
    return lax.rem(lax.axis_index(AXES[1]), quad)


def tail_rows(vector, top, decay):
    rest = jnp.zeros((TAIL - 3, vector.shape[1]), jnp.float32)
    return jnp.concatenate([vector, top, decay, rest], axis=0)


def put_state(ref, state, top, decay):
    matrix_rows = ref.shape[0] - TAIL
    ref[0:matrix_rows, :] = state[0:matrix_rows, :]
    place = lax.broadcasted_iota(jnp.int32, (TAIL, ref.shape[1]), 0)
    tail = jnp.where(place == TOP, top, state[matrix_rows:, :])
    ref[matrix_rows:, :] = jnp.where(place == DECAY, decay, tail)


def tail_row(ref, row):
    first = ref.shape[0] - TAIL + row
    return ref[first : first + 1, :]


def state_kernel(k_hbm, v_hbm, in_hbm, fo_hbm, *refs):
    *out_refs, k_ref, v_ref, in_ref, fo_ref, scalar_ref, arrived = refs
    copies = [
        pltpu.make_async_copy(source, target, arrived.at[place])
        for place, (source, target) in enumerate(
            ((fo_hbm, fo_ref), (in_hbm, in_ref), (k_hbm, k_ref), (v_hbm, v_ref))
        )
    ]
    for copy in copies:
        copy.start()
    heads, length = in_ref.shape
    key_dim = k_ref.shape[1] // heads
    value_dim = v_ref.shape[1] // heads
    parts = value_dim // LANES
    copies[0].wait()
    cumul = cumulative_rows(log_forget(fo_ref[...]))
    copies[1].wait()
    level = in_ref[...] - cumul
    level_top = jnp.max(level, axis=1, keepdims=True)
    decay = cumul[:, length - 1 : length]
    scalar_ref[0] = jnp.exp(level - level_top)
    scalar_ref[1] = jnp.broadcast_to(decay + level_top, (heads, length))
    scalar_ref[2] = jnp.broadcast_to(decay, (heads, length))
    copies[2].wait()
    copies[3].wait()
    me = member(heads)
    for step in range(heads):
        head = me ^ step
        keys = k_ref[:, pl.ds(pl.multiple_of(head * key_dim, LANES), key_dim)]
        values = v_ref[:, pl.ds(pl.multiple_of(head * value_dim, LANES), value_dim)]
        row, top, decay = (scalar_ref[place, pl.ds(head, 1), :] for place in range(3))
        high, low = split_two(keys.astype(jnp.float32).T * row)
        matrix = dot(
            jnp.concatenate([high, low], axis=1), jnp.concatenate([values, values], axis=0)
        )
        high, mid, low = split_three(row)
        vector = (dot(low, keys) + dot(mid, keys)) + dot(high, keys)
        for part in range(parts):
            out_ref = out_refs[part * heads + step]
            out_ref[0:key_dim, :] = matrix[:, part * LANES : (part + 1) * LANES]
            out_ref[key_dim:, :] = tail_rows(vector, top, decay)


def read_scalars(refs, scalar_ref, me):
    for step, ref in enumerate(refs):
        scalar_ref[0, pl.ds(me ^ step, 1), :] = tail_row(ref, TOP)
        scalar_ref[1, pl.ds(me ^ step, 1), :] = tail_row(ref, DECAY)
    count = len(refs)
    tops = [scalar_ref[0, place : place + 1, :] for place in range(count)]
    decays = [scalar_ref[1, place : place + 1, :] for place in range(count)]
    return tops, decays


def weights_of(tops, decays):
    moved, total = [], jnp.zeros_like(decays[0])
    for top, decay in zip(reversed(tops), reversed(decays)):
        moved.append(top + total)
        total = total + decay
    moved.reverse()
    joined = functools.reduce(jnp.maximum, moved)
    return [jnp.exp(top - joined) for top in moved], joined, total


def quad_kernel(*refs):
    *refs, out_ref, scalar_ref = refs
    me = member(len(refs))
    weights, top, decay = weights_of(*read_scalars(refs, scalar_ref, me))
    for place, weight in enumerate(weights):
        scalar_ref[0, place : place + 1, :] = weight
    total = 0.0
    for step, ref in enumerate(refs):
        total = total + scalar_ref[0, pl.ds(me ^ step, 1), :] * ref[...]
    put_state(out_ref, total, top, decay)


def later_side(axis, bit):
    return (lax.axis_index(axis) & bit) != 0


def extend(is_later, other_ref, before_ref):
    other_top = tail_row(other_ref, TOP)
    if before_ref is None:
        decay = jnp.where(is_later, tail_row(other_ref, DECAY), 0.0)
        return (
            jnp.where(is_later, other_ref[...], 0.0),
            jnp.where(is_later, other_top, floor_value),
            decay,
        )
    before_top = tail_row(before_ref, TOP)
    before_decay = tail_row(before_ref, DECAY)
    moved = other_top + before_decay
    top = jnp.where(is_later, jnp.maximum(moved, before_top), before_top)
    other_weight = jnp.where(is_later, jnp.exp(moved - top), 0.0)
    state = other_weight * other_ref[...] + jnp.exp(before_top - top) * before_ref[...]
    decay = jnp.where(is_later, tail_row(other_ref, DECAY), 0.0) + before_decay
    return state, top, decay


def butterfly_kernel(axis, bit, *refs):
    total_ref, other_ref, *before, out_total, out_before = refs
    is_later = later_side(axis, bit)
    own_top, own_decay = tail_row(total_ref, TOP), tail_row(total_ref, DECAY)
    other_top, other_decay = tail_row(other_ref, TOP), tail_row(other_ref, DECAY)
    own_moved = own_top + jnp.where(is_later, 0.0, other_decay)
    other_moved = other_top + jnp.where(is_later, own_decay, 0.0)
    top = jnp.maximum(own_moved, other_moved)
    total = (
        jnp.exp(own_moved - top) * total_ref[...] + jnp.exp(other_moved - top) * other_ref[...]
    )
    put_state(out_total, total, top, own_decay + other_decay)
    put_state(out_before, *extend(is_later, other_ref, before[0] if before else None))


def prefix_kernel(axis, bit, quad, *refs):
    other_ref, before_ref, *refs = refs
    pieces, out_refs, (scalar_ref, weight_ref) = refs[:quad], refs[quad : 2 * quad], refs[2 * quad :]
    me = member(quad)
    start, top, _ = extend(later_side(axis, bit), other_ref, before_ref)
    tops, decays = read_scalars(pieces, scalar_ref, me)
    zero = jnp.zeros_like(top)
    for place in range(quad):
        weights, joined, _ = weights_of([top] + tops[:place], [zero] + decays[:place])
        weights += [zero] * (quad - place)
        for index, weight in enumerate(weights):
            weight_ref[place, index : index + 1, :] = weight
        scalar_ref[0, place : place + 1, :] = joined
    for step, out_ref in enumerate(out_refs):
        place = me ^ step
        state = weight_ref[place, 0:1, :] * start
        for index, piece in enumerate(pieces):
            state = state + weight_ref[place, pl.ds(1 + (me ^ index), 1), :] * piece[...]
        put_state(out_ref, state, scalar_ref[0, pl.ds(place, 1), :], zero)


CUMUL, ROW_LEVEL, INNER_DEN = range(3)


def inner_kernel(q_ref, k_ref, v_ref, in_ref, fo_ref, num_ref, stat_ref):
    heads, length = in_ref.shape
    key_dim = q_ref.shape[1] // heads
    value_dim = v_ref.shape[1] // heads
    logf = log_forget(fo_ref[...])
    level = in_ref[...] - cumulative_rows(logf)
    cumul = cumulative_columns(logf)
    causal = triangle(length, True)
    for head in range(heads):
        queries = q_ref[:, head * key_dim : (head + 1) * key_dim]
        keys = k_ref[:, head * key_dim : (head + 1) * key_dim]
        values = v_ref[:, head * value_dim : (head + 1) * value_dim]
        scores = dot_last(queries, keys) * (key_dim**-0.5)
        masked = jnp.where(causal, level[head : head + 1, :], -jnp.inf)
        row_level = jnp.max(masked, axis=1, keepdims=True)
        weighted = jnp.exp(masked - row_level) * scores
        stat_ref[head, :, CUMUL : CUMUL + 1] = cumul[:, head : head + 1]
        stat_ref[head, :, ROW_LEVEL : ROW_LEVEL + 1] = row_level
        stat_ref[head, :, INNER_DEN : INNER_DEN + 1] = jnp.sum(weighted, axis=1, keepdims=True)
        num_ref[head] = dot(weighted.astype(jnp.bfloat16), values)


def add_carried(head, q_ref, num_ref, stat_ref, chunk_refs):
    length, value_dim = num_ref.shape[1:]
    key_dim = q_ref.shape[1] // num_ref.shape[0]
    scaling = key_dim**-0.5
    query = q_ref[:, pl.ds(pl.multiple_of(head * key_dim, LANES), key_dim)]
    matrix = jnp.concatenate([ref[0:key_dim, :] for ref in chunk_refs], axis=1)
    high, low = split_two(matrix)
    carried = dot(jnp.concatenate([query, query], axis=1), jnp.concatenate([high, low], axis=0))
    stats = stat_ref[head]
    cumul, row_level, inner_den = (stats[:, place : place + 1] for place in range(3))
    top = tail_row(chunk_refs[0], TOP)[:, 0:1]
    carried_den = jnp.sum(
        query.astype(jnp.float32) * tail_row(chunk_refs[0], VECTOR), axis=1, keepdims=True
    )
    joined = jnp.maximum(row_level, top)
    inner_factor = jnp.exp(row_level - joined)
    outer_factor = jnp.exp(top - joined) * scaling
    denom = inner_factor * inner_den + outer_factor * carried_den
    inverse = 1.0 / jnp.maximum(jnp.abs(denom), jnp.exp(-(cumul + joined)))
    return (inner_factor * inverse) * num_ref[head] + (outer_factor * inverse) * carried


def part_kernel(steps, q_ref, num_ref, stat_ref, *refs):
    me = member(num_ref.shape[0])
    parts = len(refs) // len(steps) - 1
    chunk_refs, out_refs = refs[: -len(steps)], refs[-len(steps) :]
    for place, (step, out_ref) in enumerate(zip(steps, out_refs)):
        own = chunk_refs[place * parts : (place + 1) * parts]
        out_ref[...] = add_carried(me ^ step, q_ref, num_ref, stat_ref, own).astype(out_ref.dtype)


def last_kernel(q_ref, num_ref, stat_ref, *refs):
    *refs, out_hbm, own_ref, done = refs
    heads, _, value_dim = num_ref.shape
    chunk_refs, done_refs = refs[: 1 - heads], refs[1 - heads :]
    me = member(heads)

    def place(step, source):
        columns = pl.ds(pl.multiple_of((me ^ step) * value_dim, LANES), value_dim)
        copy = pltpu.make_async_copy(source, out_hbm.at[:, columns], done.at[step])
        copy.start()
        return copy

    copies = [place(step, ref) for step, ref in enumerate(done_refs)]
    own = add_carried(me ^ (heads - 1), q_ref, num_ref, stat_ref, chunk_refs)
    own_ref[...] = own.astype(own_ref.dtype)
    copies.append(place(heads - 1, own_ref))
    for copy in copies:
        copy.wait()


def swap(array, axis, step):
    count = lax.axis_size(axis)
    return lax.ppermute(array, axis, [(place, place ^ step) for place in range(count)])


def exchange(pieces):
    return [pieces[0]] + [
        swap(pieces[step], AXES[1], step) for step in range(1, len(pieces))
    ]


def on_device(groups, group_length, queries, key_vectors, value_vectors, input_gate, forget_gate):
    heads, length = input_gate.shape
    key_dim = queries.shape[1] // heads
    value_dim = value_vectors.shape[1] // heads
    parts = value_dim // LANES
    message = jax.ShapeDtypeStruct((key_dim + TAIL, LANES), jnp.float32)
    messages = (message,) * heads
    params = pltpu.CompilerParams(vmem_limit_bytes=48 * 1024 * 1024)
    hbm = pl.BlockSpec(memory_space=pltpu.HBM)
    scalars = pltpu.VMEM((3, heads, LANES), jnp.float32)
    output = jax.ShapeDtypeStruct((length, heads * value_dim), jnp.bfloat16)
    operands = (key_vectors, value_vectors, input_gate, forget_gate)
    levels = []
    for axis, bit, size in ((AXES[1], heads, group_length), (AXES[0], 1, groups)):
        while bit < size:
            levels.append((axis, bit))
            bit *= 2

    own = pl.pallas_call(
        state_kernel,
        out_shape=messages * parts,
        in_specs=[hbm] * len(operands),
        scratch_shapes=[pltpu.VMEM(array.shape, array.dtype) for array in operands]
        + [scalars, pltpu.SemaphoreType.DMA((len(operands),))],
        compiler_params=params,
    )(*(pltpu.with_memory_space_constraint(array, pltpu.HBM) for array in operands))
    inner_num, stats = pl.pallas_call(
        inner_kernel,
        out_shape=(
            jax.ShapeDtypeStruct((heads, length, value_dim), jnp.float32),
            jax.ShapeDtypeStruct((heads, length, 3), jnp.float32),
        ),
        compiler_params=params,
    )(queries, *operands)
    join_quad = pl.pallas_call(
        quad_kernel, out_shape=message, scratch_shapes=[scalars], compiler_params=params
    )
    prefixes = pl.pallas_call(
        functools.partial(prefix_kernel, *levels[-1], heads),
        out_shape=messages,
        scratch_shapes=[scalars, pltpu.VMEM((heads, 1 + heads, LANES), jnp.float32)],
        compiler_params=params,
    )
    pieces = [exchange(own[part * heads : (part + 1) * heads]) for part in range(parts)]
    totals = [join_quad(*array) for array in pieces]
    before = [[] for _ in range(parts)]
    for axis, bit in levels[:-1]:
        join_level = pl.pallas_call(
            functools.partial(butterfly_kernel, axis, bit),
            out_shape=(message, message),
            compiler_params=params,
        )
        others = [swap(array, axis, bit) for array in totals]
        for part in range(parts):
            totals[part], *before[part] = join_level(totals[part], others[part], *before[part])
    others = [swap(array, *levels[-1]) for array in totals]
    carried = [exchange(prefixes(others[part], *before[part], *pieces[part])) for part in range(parts)]
    arrived = [[chunk[step] for chunk in carried] for step in range(heads)]
    column = jax.ShapeDtypeStruct((length, value_dim), output.dtype)
    columns = []
    for steps in [(0, 1)] + [(step,) for step in range(2, heads - 1)]:
        chunks = [chunk for step in steps for chunk in arrived[step]]
        columns += pl.pallas_call(
            functools.partial(part_kernel, steps),
            out_shape=(column,) * len(steps),
            compiler_params=params,
        )(queries, inner_num, stats, *chunks)
    return pl.pallas_call(
        last_kernel,
        out_shape=output,
        out_specs=hbm,
        scratch_shapes=[
            pltpu.VMEM(column.shape, column.dtype),
            pltpu.SemaphoreType.DMA((heads,)),
        ],
        compiler_params=params,
    )(queries, inner_num, stats, *arrived[-1], *columns)


def solution(mesh):
    return jax.shard_map(
        functools.partial(on_device, mesh.shape["grp"], mesh.shape["seq"]),
        mesh=mesh,
        in_specs=(
            P(AXES, None),
            P(AXES, None),
            P(AXES, None),
            P(None, AXES),
            P(None, AXES),
        ),
        out_specs=P(AXES, None),
        check_vma=False,
    )
```

```python
import functools

import jax
import jax.numpy as jnp
from jax import lax
from jax.experimental import pallas as pl
from jax.experimental.pallas import tpu as pltpu
from jax.sharding import PartitionSpec as P

floor_value = -1e30
LANES = 128
AXES = ("grp", "seq")


def split_two(x):
    high = x.astype(jnp.bfloat16)
    low = (x - high.astype(jnp.float32)).astype(jnp.bfloat16)
    return high, low


def split_three(x):
    high = x.astype(jnp.bfloat16)
    rest = x - high.astype(jnp.float32)
    mid = rest.astype(jnp.bfloat16)
    low = (rest - mid.astype(jnp.float32)).astype(jnp.bfloat16)
    return high, mid, low


def dot(a, b):
    return jnp.dot(a, b, preferred_element_type=jnp.float32)


def dot_last(a, b):
    return lax.dot_general(a, b, (((1,), (1,)), ((), ())), preferred_element_type=jnp.float32)


def log_forget(forget):
    return jnp.minimum(forget, 0.0) - jnp.log1p(jnp.exp(-jnp.abs(forget)))


def triangle(length, lower):
    rows = lax.broadcasted_iota(jnp.int32, (length, length), 0)
    cols = lax.broadcasted_iota(jnp.int32, (length, length), 1)
    return rows >= cols if lower else rows <= cols


def cumulative_rows(logf):
    ones = triangle(logf.shape[1], False).astype(jnp.bfloat16)
    high, mid, low = split_three(logf)
    return (dot(low, ones) + dot(mid, ones)) + dot(high, ones)


def cumulative_columns(logf):
    ones = triangle(logf.shape[1], True).astype(jnp.bfloat16)
    high, mid, low = split_three(logf)
    return (dot_last(ones, low) + dot_last(ones, mid)) + dot_last(ones, high)


TAIL = 8
VECTOR, TOP, DECAY = range(3)


def member(quad):
    return lax.rem(lax.axis_index(AXES[1]), quad)


def partners(quad):
    return [member(quad) ^ step for step in range(quad)]


def tail_rows(vector, top, decay):
    rest = jnp.zeros((TAIL - 3, vector.shape[1]), jnp.float32)
    return jnp.concatenate([vector, top, decay, rest], axis=0)


def tail_row(ref, row):
    first = ref.shape[0] - TAIL + row
    return ref[first : first + 1, :]


def load(ref):
    return (ref[0 : ref.shape[0] - TAIL, :], *(tail_row(ref, row) for row in range(3)))


def store(ref, state):
    matrix, *tail = state
    ref[0 : matrix.shape[0], :] = matrix
    ref[matrix.shape[0] :, :] = tail_rows(*tail)


def join(earlier, later):
    early_matrix, early_vector, early_top, early_decay = earlier
    late_matrix, late_vector, late_top, late_decay = later
    moved = early_top + late_decay
    joined = jnp.maximum(moved, late_top)
    early_weight, late_weight = jnp.exp(moved - joined), jnp.exp(late_top - joined)
    return (
        early_weight * early_matrix + late_weight * late_matrix,
        early_weight * early_vector + late_weight * late_vector,
        joined,
        early_decay + late_decay,
    )


def choose(condition, one, other):
    return jax.tree.map(lambda a, b: jnp.where(condition, a, b), one, other)


def nothing(like):
    matrix, vector, top, decay = like
    zero = jnp.zeros_like(decay)
    return jnp.zeros_like(matrix), jnp.zeros_like(vector), zero + floor_value, zero


def state_kernel(k_hbm, v_hbm, in_hbm, fo_hbm, *refs):
    *out_refs, k_ref, v_ref, in_ref, fo_ref, scalar_ref, arrived = refs
    copies = [
        pltpu.make_async_copy(source, target, arrived.at[place])
        for place, (source, target) in enumerate(
            ((fo_hbm, fo_ref), (in_hbm, in_ref), (k_hbm, k_ref), (v_hbm, v_ref))
        )
    ]
    for copy in copies:
        copy.start()
    heads, length = in_ref.shape
    key_dim = k_ref.shape[1] // heads
    value_dim = v_ref.shape[1] // heads
    parts = value_dim // LANES
    copies[0].wait()
    cumul = cumulative_rows(log_forget(fo_ref[...]))
    copies[1].wait()
    level = in_ref[...] - cumul
    level_top = jnp.max(level, axis=1, keepdims=True)
    decay = cumul[:, length - 1 : length]
    scalar_ref[0] = jnp.exp(level - level_top)
    scalar_ref[1] = jnp.broadcast_to(decay + level_top, (heads, length))
    scalar_ref[2] = jnp.broadcast_to(decay, (heads, length))
    copies[2].wait()
    copies[3].wait()
    for head, out_ref in zip(partners(heads), out_refs):
        keys = k_ref[:, pl.ds(pl.multiple_of(head * key_dim, LANES), key_dim)]
        values = v_ref[:, pl.ds(pl.multiple_of(head * value_dim, LANES), value_dim)]
        row, top, decay = (scalar_ref[place, pl.ds(head, 1), :] for place in range(3))
        high, low = split_two(keys.astype(jnp.float32).T * row)
        matrix = dot(
            jnp.concatenate([high, low], axis=1), jnp.concatenate([values, values], axis=0)
        )
        for part in range(parts):
            out_ref[part * key_dim : (part + 1) * key_dim, :] = matrix[
                :, part * LANES : (part + 1) * LANES
            ]
        high, mid, low = split_three(row)
        vector = (dot(low, keys) + dot(mid, keys)) + dot(high, keys)
        out_ref[parts * key_dim :, :] = tail_rows(vector, top, decay)


def read_scalars(refs, scalar_ref, places):
    for place, ref in zip(places, refs):
        scalar_ref[0, pl.ds(place, 1), :] = tail_row(ref, TOP)
        scalar_ref[1, pl.ds(place, 1), :] = tail_row(ref, DECAY)
    count = len(refs)
    tops = [scalar_ref[0, place : place + 1, :] for place in range(count)]
    decays = [scalar_ref[1, place : place + 1, :] for place in range(count)]
    return tops, decays


def weights_of(tops, decays):
    moved, total = [], jnp.zeros_like(decays[0])
    for top, decay in zip(reversed(tops), reversed(decays)):
        moved.append(top + total)
        total = total + decay
    moved.reverse()
    joined = functools.reduce(jnp.maximum, moved)
    return [jnp.exp(top - joined) for top in moved], joined, total


def weighted_sum(weights, states):
    matrix, vector = 0.0, 0.0
    for weight, state in zip(weights, states):
        matrix = matrix + weight * state[0]
        vector = vector + weight * state[1]
    return matrix, vector


def quad_kernel(*refs):
    *refs, out_ref, scalar_ref = refs
    places = partners(len(refs))
    weights, top, decay = weights_of(*read_scalars(refs, scalar_ref, places))
    for place, weight in enumerate(weights):
        scalar_ref[0, place : place + 1, :] = weight
    weights = [scalar_ref[0, pl.ds(place, 1), :] for place in places]
    store(out_ref, (*weighted_sum(weights, [load(ref) for ref in refs]), top, decay))


def later_side(axis, bit):
    return (lax.axis_index(axis) & bit) != 0


def butterfly_kernel(axis, bit, *refs):
    total_ref, other_ref, *before_refs, out_total, out_before = refs
    is_later = later_side(axis, bit)
    total, other = load(total_ref), load(other_ref)
    before = load(before_refs[0]) if before_refs else nothing(total)
    store(out_total, join(choose(is_later, other, total), choose(is_later, total, other)))
    store(out_before, choose(is_later, join(other, before), before))


def gather_kernel(axis, bit, own_ref, other_ref, out_ref):
    is_later = later_side(axis, bit)
    count = out_ref.shape[0] // 2
    for place in range(count):
        own = own_ref[place] if own_ref.ndim == 3 else own_ref[...]
        other = other_ref[place] if other_ref.ndim == 3 else other_ref[...]
        out_ref[place] = jnp.where(is_later, other, own)
        out_ref[count + place] = jnp.where(is_later, own, other)


def prefix_kernel(quad, own_ref, other_ref, within_ref, *refs):
    *refs, scalar_ref, weight_ref = refs
    pieces, out_refs = refs[:quad], refs[quad:]
    places = partners(quad)
    me = lax.axis_index(AXES[0])
    even = (me & 1) == 0
    start = nothing(load(within_ref))
    for group in range(2 * own_ref.shape[0] - 1):
        same = even if group % 2 == 0 else jnp.logical_not(even)
        own, other = load(own_ref.at[group // 2]), load(other_ref.at[group // 2])
        start = choose(group < me, join(start, choose(same, own, other)), start)
    start = join(start, load(within_ref))
    tops, decays = read_scalars(pieces, scalar_ref, places)
    zero = jnp.zeros_like(tops[0])
    for place in range(quad):
        weights, joined, _ = weights_of([start[2]] + tops[:place], [zero] + decays[:place])
        weights += [zero] * (quad - place)
        for index, weight in enumerate(weights):
            weight_ref[place, index : index + 1, :] = weight
        scalar_ref[0, place : place + 1, :] = joined
    states = [start] + [load(piece) for piece in pieces]
    for place, out_ref in zip(places, out_refs):
        weights = [weight_ref[place, 0:1, :]]
        weights += [weight_ref[place, pl.ds(1 + index, 1), :] for index in places]
        top = scalar_ref[0, pl.ds(place, 1), :]
        store(out_ref, (*weighted_sum(weights, states), top, zero))


CUMUL, ROW_LEVEL, INNER_DEN = range(3)


def inner_kernel(q_ref, k_ref, v_ref, in_ref, fo_ref, num_ref, stat_ref):
    heads, length = in_ref.shape
    key_dim = q_ref.shape[1] // heads
    value_dim = v_ref.shape[1] // heads
    logf = log_forget(fo_ref[...])
    level = in_ref[...] - cumulative_rows(logf)
    cumul = cumulative_columns(logf)
    causal = triangle(length, True)
    for head in range(heads):
        queries = q_ref[:, head * key_dim : (head + 1) * key_dim]
        keys = k_ref[:, head * key_dim : (head + 1) * key_dim]
        values = v_ref[:, head * value_dim : (head + 1) * value_dim]
        scores = dot_last(queries, keys) * (key_dim**-0.5)
        masked = jnp.where(causal, level[head : head + 1, :], -jnp.inf)
        row_level = jnp.max(masked, axis=1, keepdims=True)
        weighted = jnp.exp(masked - row_level) * scores
        stat_ref[head, :, CUMUL : CUMUL + 1] = cumul[:, head : head + 1]
        stat_ref[head, :, ROW_LEVEL : ROW_LEVEL + 1] = row_level
        stat_ref[head, :, INNER_DEN : INNER_DEN + 1] = jnp.sum(weighted, axis=1, keepdims=True)
        num_ref[head] = dot(weighted.astype(jnp.bfloat16), values)


def add_carried(head, q_ref, num_ref, stat_ref, message_ref):
    length, value_dim = num_ref.shape[1:]
    key_dim = q_ref.shape[1] // num_ref.shape[0]
    parts = value_dim // LANES
    scaling = key_dim**-0.5
    query = q_ref[:, pl.ds(pl.multiple_of(head * key_dim, LANES), key_dim)]
    matrix = jnp.concatenate(
        [message_ref[part * key_dim : (part + 1) * key_dim, :] for part in range(parts)], 1
    )
    high, low = split_two(matrix)
    carried = dot(jnp.concatenate([query, query], axis=1), jnp.concatenate([high, low], axis=0))
    stats = stat_ref[head]
    cumul, row_level, inner_den = (stats[:, place : place + 1] for place in range(3))
    top = tail_row(message_ref, TOP)[:, 0:1]
    carried_den = jnp.sum(
        query.astype(jnp.float32) * tail_row(message_ref, VECTOR), axis=1, keepdims=True
    )
    joined = jnp.maximum(row_level, top)
    inner_factor = jnp.exp(row_level - joined)
    outer_factor = jnp.exp(top - joined) * scaling
    denom = inner_factor * inner_den + outer_factor * carried_den
    inverse = 1.0 / jnp.maximum(jnp.abs(denom), jnp.exp(-(cumul + joined)))
    return (inner_factor * inverse) * num_ref[head] + (outer_factor * inverse) * carried


def part_kernel(steps, q_ref, num_ref, stat_ref, *refs):
    places = partners(num_ref.shape[0])
    count = len(steps)
    for step, message_ref, out_ref in zip(steps, refs[:count], refs[count:]):
        head = places[step]
        out_ref[...] = add_carried(head, q_ref, num_ref, stat_ref, message_ref).astype(
            out_ref.dtype
        )


def last_kernel(q_ref, num_ref, stat_ref, message_ref, *refs):
    *done_refs, out_hbm, own_ref, done = refs
    heads, _, value_dim = num_ref.shape
    places = partners(heads)

    def place(step, source):
        columns = pl.ds(pl.multiple_of(places[step] * value_dim, LANES), value_dim)
        copy = pltpu.make_async_copy(source, out_hbm.at[:, columns], done.at[step])
        copy.start()
        return copy

    copies = [place(step, ref) for step, ref in enumerate(done_refs)]
    own_ref[...] = add_carried(places[-1], q_ref, num_ref, stat_ref, message_ref).astype(
        own_ref.dtype
    )
    copies.append(place(heads - 1, own_ref))
    for copy in copies:
        copy.wait()


def swap(array, axis, step):
    count = lax.axis_size(axis)
    return lax.ppermute(array, axis, [(place, place ^ step) for place in range(count)])


def exchange(pieces):
    return [pieces[0]] + [swap(pieces[step], AXES[1], step) for step in range(1, len(pieces))]


def on_device(groups, group_length, queries, key_vectors, value_vectors, input_gate, forget_gate):
    heads, length = input_gate.shape
    key_dim = queries.shape[1] // heads
    value_dim = value_vectors.shape[1] // heads
    message = jax.ShapeDtypeStruct(
        (value_dim // LANES * key_dim + TAIL, LANES), jnp.float32
    )
    messages = (message,) * heads
    params = pltpu.CompilerParams(vmem_limit_bytes=48 * 1024 * 1024)
    hbm = pl.BlockSpec(memory_space=pltpu.HBM)
    scalars = pltpu.VMEM((3, heads, LANES), jnp.float32)
    output = jax.ShapeDtypeStruct((length, heads * value_dim), jnp.bfloat16)
    operands = (key_vectors, value_vectors, input_gate, forget_gate)
    own = pl.pallas_call(
        state_kernel,
        out_shape=messages,
        in_specs=[hbm] * len(operands),
        scratch_shapes=[pltpu.VMEM(array.shape, array.dtype) for array in operands]
        + [scalars, pltpu.SemaphoreType.DMA((len(operands),))],
        compiler_params=params,
    )(*(pltpu.with_memory_space_constraint(array, pltpu.HBM) for array in operands))
    pieces = exchange(own)
    inner_num, stats = pl.pallas_call(
        inner_kernel,
        out_shape=(
            jax.ShapeDtypeStruct((heads, length, value_dim), jnp.float32),
            jax.ShapeDtypeStruct((heads, length, 3), jnp.float32),
        ),
        compiler_params=params,
    )(queries, *operands)
    total = pl.pallas_call(
        quad_kernel, out_shape=message, scratch_shapes=[scalars], compiler_params=params
    )(*pieces)
    within = []
    bit = heads
    while bit < group_length:
        total, *within = pl.pallas_call(
            functools.partial(butterfly_kernel, AXES[1], bit),
            out_shape=(message, message),
            compiler_params=params,
        )(total, swap(total, AXES[1], bit), *within)
        bit *= 2
    sums = total
    bit, count = 2, 1
    while bit < groups:
        count *= 2
        sums = pl.pallas_call(
            functools.partial(gather_kernel, AXES[0], bit),
            out_shape=jax.ShapeDtypeStruct((count,) + message.shape, message.dtype),
            compiler_params=params,
        )(sums, swap(sums, AXES[0], bit))
        bit *= 2
    states = pl.pallas_call(
        functools.partial(prefix_kernel, heads),
        out_shape=messages,
        scratch_shapes=[scalars, pltpu.VMEM((heads, 1 + heads, LANES), jnp.float32)],
        compiler_params=params,
    )(sums, swap(sums, AXES[0], 1), *within, *pieces)
    carried = exchange(states)
    column = jax.ShapeDtypeStruct((length, value_dim), output.dtype)
    columns = []
    for steps in [(0, 1)] + [(step,) for step in range(2, heads - 1)]:
        columns += pl.pallas_call(
            functools.partial(part_kernel, steps),
            out_shape=(column,) * len(steps),
            compiler_params=params,
        )(queries, inner_num, stats, *(carried[step] for step in steps))
    return pl.pallas_call(
        last_kernel,
        out_shape=output,
        out_specs=hbm,
        scratch_shapes=[
            pltpu.VMEM(column.shape, column.dtype),
            pltpu.SemaphoreType.DMA((heads,)),
        ],
        compiler_params=params,
    )(queries, inner_num, stats, carried[-1], *columns)


def solution(mesh):
    return jax.shard_map(
        functools.partial(on_device, mesh.shape["grp"], mesh.shape["seq"]),
        mesh=mesh,
        in_specs=(
            P(AXES, None),
            P(AXES, None),
            P(AXES, None),
            P(None, AXES),
            P(None, AXES),
        ),
        out_specs=P(AXES, None),
        check_vma=False,
    )
```

```python
import functools

import jax
import jax.numpy as jnp
from jax import lax
from jax.experimental import pallas as pl
from jax.experimental.pallas import tpu as pltpu
from jax.sharding import PartitionSpec as P

floor_value = -1e30
LANES = 128
AXES = ("grp", "seq")


def split_two(x):
    high = x.astype(jnp.bfloat16)
    low = (x - high.astype(jnp.float32)).astype(jnp.bfloat16)
    return high, low


def split_three(x):
    high = x.astype(jnp.bfloat16)
    rest = x - high.astype(jnp.float32)
    mid = rest.astype(jnp.bfloat16)
    low = (rest - mid.astype(jnp.float32)).astype(jnp.bfloat16)
    return high, mid, low


def dot(a, b):
    return jnp.dot(a, b, preferred_element_type=jnp.float32)


def dot_last(a, b):
    return lax.dot_general(a, b, (((1,), (1,)), ((), ())), preferred_element_type=jnp.float32)


def log_forget(forget):
    return jnp.minimum(forget, 0.0) - jnp.log1p(jnp.exp(-jnp.abs(forget)))


def triangle(length, lower):
    rows = lax.broadcasted_iota(jnp.int32, (length, length), 0)
    cols = lax.broadcasted_iota(jnp.int32, (length, length), 1)
    return rows >= cols if lower else rows <= cols


def cumulative_rows(logf):
    ones = triangle(logf.shape[1], False).astype(jnp.bfloat16)
    high, mid, low = split_three(logf)
    return (dot(low, ones) + dot(mid, ones)) + dot(high, ones)


def cumulative_columns(logf):
    ones = triangle(logf.shape[1], True).astype(jnp.bfloat16)
    high, mid, low = split_three(logf)
    return (dot_last(ones, low) + dot_last(ones, mid)) + dot_last(ones, high)


SIDES = 2
TAIL = 8
VECTOR, TOP, DECAY = range(3)


def member(quad):
    return lax.rem(lax.axis_index(AXES[1]), quad)


def own_side():
    return lax.rem(lax.axis_index(AXES[0]), SIDES)


def tail_row(ref, row, slot=0):
    return ref[pl.ds(ref.shape[0] - TAIL + 3 * slot + row, 1), :]


def load(ref, slot=0, slots=1):
    key_dim = (ref.shape[0] - TAIL) // slots
    rows = [tail_row(ref, row, slot) for row in range(3)]
    return (ref[slot * key_dim : (slot + 1) * key_dim, :], *rows)


def store(ref, *states):
    key_dim = states[0][0].shape[0]
    rows = []
    for slot, (matrix, *tail) in enumerate(states):
        ref[slot * key_dim : (slot + 1) * key_dim, :] = matrix
        rows += tail
    rows.append(jnp.zeros((TAIL - len(rows), ref.shape[1]), jnp.float32))
    ref[len(states) * key_dim :, :] = jnp.concatenate(rows, axis=0)


def join(earlier, later):
    early_matrix, early_vector, early_top, early_decay = earlier
    late_matrix, late_vector, late_top, late_decay = later
    moved = early_top + late_decay
    joined = jnp.maximum(moved, late_top)
    early_weight, late_weight = jnp.exp(moved - joined), jnp.exp(late_top - joined)
    return (
        early_weight * early_matrix + late_weight * late_matrix,
        early_weight * early_vector + late_weight * late_vector,
        joined,
        early_decay + late_decay,
    )


def choose(condition, one, other):
    return jax.tree.map(lambda a, b: jnp.where(condition, a, b), one, other)


def nothing(like):
    matrix, vector, top, decay = like
    zero = jnp.zeros_like(decay)
    return jnp.zeros_like(matrix), jnp.zeros_like(vector), zero + floor_value, zero


def state_kernel(k_hbm, v_hbm, in_hbm, fo_hbm, *refs):
    own_ref, send_ref, k_ref, v_ref, in_ref, fo_ref, arrived = refs
    copies = [
        pltpu.make_async_copy(source, target, arrived.at[place])
        for place, (source, target) in enumerate(
            ((fo_hbm, fo_ref), (in_hbm, in_ref), (k_hbm, k_ref), (v_hbm, v_ref))
        )
    ]
    for copy in copies:
        copy.start()
    heads, length = in_ref.shape
    key_dim = k_ref.shape[1] // heads
    value_dim = v_ref.shape[1] // heads
    copies[0].wait()
    cumul = cumulative_rows(log_forget(fo_ref[...]))
    copies[1].wait()
    level = in_ref[...] - cumul
    level_top = jnp.max(level, axis=1, keepdims=True)
    decay = cumul[:, length - 1 : length]
    weight = jnp.exp(level - level_top)
    top = decay + level_top
    first = own_side() == 0
    copies[2].wait()
    copies[3].wait()
    for head in range(heads):
        keys = k_ref[:, head * key_dim : (head + 1) * key_dim]
        values = v_ref[:, head * value_dim : (head + 1) * value_dim]
        row = weight[head : head + 1, :]
        high, low = split_two(keys.astype(jnp.float32).T * row)
        matrix = dot(
            jnp.concatenate([high, low], axis=1), jnp.concatenate([values, values], axis=0)
        )
        high, mid, low = split_three(row)
        vector = (dot(low, keys) + dot(mid, keys)) + dot(high, keys)
        tail = (
            vector,
            jnp.broadcast_to(top[head : head + 1, :], vector.shape),
            jnp.broadcast_to(decay[head : head + 1, :], vector.shape),
        )
        left, right = matrix[:, :LANES], matrix[:, LANES:]
        store(own_ref.at[head], (jnp.where(first, left, right), *tail))
        store(send_ref.at[head], (jnp.where(first, right, left), *tail))


def pack_kernel(own_ref, other_ref, *refs):
    hbm_refs, refs = refs[:5], refs[5:]
    *out_refs, num_ref, stat_ref = refs[:-6]
    copied, arrived = refs[-6:-1], refs[-1]
    me, first = member(len(out_refs)), own_side() == 0
    copies = [
        pltpu.make_async_copy(source, target, arrived.at[place])
        for place, (source, target) in enumerate(zip(hbm_refs, copied))
    ]

    @pl.when(first)
    def _():
        for copy in copies:
            copy.start()
        for copy in copies:
            copy.wait()
        inner_sums(*copied, num_ref, stat_ref)

    for step, out_ref in enumerate(out_refs):
        own, other = load(own_ref.at[me ^ step]), load(other_ref.at[me ^ step])
        store(out_ref, choose(first, own, other), choose(first, other, own))


def read_scalars(refs, scalar_ref, me, slot):
    for step, ref in enumerate(refs):
        scalar_ref[0, pl.ds(me ^ step, 1), :] = tail_row(ref, TOP, slot)
        scalar_ref[1, pl.ds(me ^ step, 1), :] = tail_row(ref, DECAY, slot)
    count = len(refs)
    tops = [scalar_ref[0, place : place + 1, :] for place in range(count)]
    decays = [scalar_ref[1, place : place + 1, :] for place in range(count)]
    return tops, decays


def weights_of(tops, decays):
    moved, total = [], jnp.zeros_like(decays[0])
    for top, decay in zip(reversed(tops), reversed(decays)):
        moved.append(top + total)
        total = total + decay
    moved.reverse()
    joined = functools.reduce(jnp.maximum, moved)
    return [jnp.exp(top - joined) for top in moved], joined, total


def weighted_sum(weights, states):
    matrix, vector = 0.0, 0.0
    for weight, state in zip(weights, states):
        matrix = matrix + weight * state[0]
        vector = vector + weight * state[1]
    return matrix, vector


def quad_kernel(*refs):
    *refs, out_ref, scalar_ref = refs
    me = member(len(refs))
    totals = []
    for slot in range(SIDES):
        scalars = scalar_ref.at[slot]
        weights, top, decay = weights_of(*read_scalars(refs, scalars, me, slot))
        for place, weight in enumerate(weights):
            scalars[2, place : place + 1, :] = weight
        weights = [scalars[2, pl.ds(me ^ step, 1), :] for step in range(len(refs))]
        totals.append((*weighted_sum(weights, [load(ref, slot, SIDES) for ref in refs]), top, decay))
    store(out_ref, *totals)


def later_side(axis, bit):
    return (lax.axis_index(axis) & bit) != 0


def extend(is_later, other, before):
    return choose(is_later, join(other, before), before)


def butterfly_kernel(axis, bit, slots, *refs):
    total_ref, other_ref, *before_refs, out_total, out_before = refs
    is_later = later_side(axis, bit)
    totals, befores = [], []
    for slot in range(slots):
        total, other = load(total_ref, slot, slots), load(other_ref, slot, slots)
        before = load(before_refs[0], slot, slots) if before_refs else nothing(total)
        totals.append(join(choose(is_later, other, total), choose(is_later, total, other)))
        befores.append(extend(is_later, other, before))
    store(out_total, *totals)
    store(out_before, *befores)


def pair_kernel(in_ref, out_ref):
    store(out_ref, join(*(load(in_ref, slot, SIDES) for slot in range(SIDES))))


def prefix_kernel(axis, bit, quad, other_ref, group_ref, within_ref, *refs):
    *refs, scalar_ref, weight_ref = refs
    first = len(refs) - 2 * quad
    before_refs, pieces, out_refs = refs[:first], refs[first : first + quad], refs[first + quad :]
    me = member(quad)
    other = load(other_ref)
    before = load(before_refs[0]) if before_refs else nothing(other)
    start = extend(later_side(axis, bit), other, before)
    results = [[] for _ in range(quad)]
    for slot in range(SIDES):
        at_quad = join(start, load(within_ref, slot, SIDES))
        scalars, kept = scalar_ref.at[slot], weight_ref.at[slot]
        tops, decays = read_scalars(pieces, scalars, me, slot)
        zero = jnp.zeros_like(tops[0])
        for place in range(quad):
            weights, joined, _ = weights_of([at_quad[2]] + tops[:place], [zero] + decays[:place])
            weights += [zero] * (quad - place)
            for index, weight in enumerate(weights):
                kept[place, index : index + 1, :] = weight
            scalars[2, place : place + 1, :] = joined
        states = [at_quad] + [load(piece, slot, SIDES) for piece in pieces]
        for step in range(quad):
            place = me ^ step
            weights = [kept[place, 0:1, :]]
            weights += [kept[place, pl.ds(1 + (me ^ index), 1), :] for index in range(quad)]
            top = scalars[2, pl.ds(place, 1), :]
            results[step].append((*weighted_sum(weights, states), top, zero))
        start = join(start, load(group_ref, slot, SIDES))
    for out_ref, states in zip(out_refs, results):
        store(out_ref, *states)


def part_kernel(*refs):
    _, *refs, out_ref = refs
    key_dim = (refs[0].shape[0] - TAIL) // SIDES
    me, other = member(len(refs)), SIDES - 1 - own_side()
    for step, ref in enumerate(refs):
        out_ref[me ^ step] = ref[pl.ds(pl.multiple_of(other * key_dim, 8), key_dim), :]


def carry(query, matrix):
    high, low = split_two(matrix)
    return dot(jnp.concatenate([query, query], axis=1), jnp.concatenate([high, low], axis=0))


CUMUL, ROW_LEVEL, INNER_DEN = range(3)


def inner_kernel(q_ref, k_ref, v_ref, in_ref, fo_ref, early_num, early_stat, num_ref, stat_ref):
    @pl.when(own_side() != 0)
    def _():
        inner_sums(q_ref, k_ref, v_ref, in_ref, fo_ref, num_ref, stat_ref)

    @pl.when(own_side() == 0)
    def _():
        num_ref[...] = early_num[...]
        stat_ref[...] = early_stat[...]


def inner_sums(q_ref, k_ref, v_ref, in_ref, fo_ref, num_ref, stat_ref):
    heads, length = in_ref.shape
    key_dim = q_ref.shape[1] // heads
    value_dim = v_ref.shape[1] // heads
    parts = value_dim // LANES
    logf = log_forget(fo_ref[...])
    level = in_ref[...] - cumulative_rows(logf)
    cumul = cumulative_columns(logf)
    causal = triangle(length, True)
    for head in range(heads):
        queries = q_ref[:, head * key_dim : (head + 1) * key_dim]
        keys = k_ref[:, head * key_dim : (head + 1) * key_dim]
        values = v_ref[:, head * value_dim : (head + 1) * value_dim]
        scores = dot_last(queries, keys) * (key_dim**-0.5)
        masked = jnp.where(causal, level[head : head + 1, :], -jnp.inf)
        row_level = jnp.max(masked, axis=1, keepdims=True)
        weighted = jnp.exp(masked - row_level) * scores
        stat_ref[head, :, CUMUL : CUMUL + 1] = cumul[:, head : head + 1]
        stat_ref[head, :, ROW_LEVEL : ROW_LEVEL + 1] = row_level
        stat_ref[head, :, INNER_DEN : INNER_DEN + 1] = jnp.sum(weighted, axis=1, keepdims=True)
        inner_num = dot(weighted.astype(jnp.bfloat16), values)
        for part in range(parts):
            num_ref[part, head] = inner_num[:, part * LANES : (part + 1) * LANES]


def outer_kernel(q_ref, num_ref, stat_ref, *refs):
    *refs, out_ref, factor_ref = refs
    heads = len(refs)
    key_dim = q_ref.shape[1] // heads
    scaling = key_dim**-0.5
    me, side = member(heads), own_side()
    for step, ref in enumerate(refs):
        head = me ^ step
        query = q_ref[:, pl.ds(pl.multiple_of(head * key_dim, LANES), key_dim)]
        carried = carry(query, ref[pl.ds(pl.multiple_of(side * key_dim, 8), key_dim), :])
        stats = stat_ref[head]
        cumul, row_level, inner_den = (stats[:, place : place + 1] for place in range(3))
        top = tail_row(ref, TOP, side)[:, 0:1]
        carried_den = jnp.sum(
            query.astype(jnp.float32) * tail_row(ref, VECTOR, side), axis=1, keepdims=True
        )
        joined = jnp.maximum(row_level, top)
        inner_factor = jnp.exp(row_level - joined)
        outer_factor = jnp.exp(top - joined) * scaling
        denom = inner_factor * inner_den + outer_factor * carried_den
        inverse = 1.0 / jnp.maximum(jnp.abs(denom), jnp.exp(-(cumul + joined)))
        inner_factor, outer_factor = inner_factor * inverse, outer_factor * inverse
        out_ref[head] = inner_factor * num_ref[side, head] + outer_factor * carried
        factor_ref[head, :, 0:1] = inner_factor
        factor_ref[head, :, 1:2] = outer_factor


def last_kernel(q_ref, num_ref, factor_ref, own_ref, state_ref, out_hbm, out_ref, done):
    heads, key_dim = state_ref.shape[:2]
    value_dim = out_ref.shape[1] // heads
    other = SIDES - 1 - own_side()
    copies = []
    for head in range(heads):
        carried = carry(q_ref[:, head * key_dim : (head + 1) * key_dim], state_ref[head])
        factors = factor_ref[head]
        late = factors[:, 0:1] * num_ref[other, head] + factors[:, 1:2] * carried
        early = own_ref[head]
        place = pl.ds(head * value_dim, value_dim)
        out_ref[:, place] = jnp.concatenate(
            [jnp.where(other == 0, late, early), jnp.where(other == 0, early, late)], axis=1
        ).astype(out_ref.dtype)
        copy = pltpu.make_async_copy(out_ref.at[:, place], out_hbm.at[:, place], done.at[head])
        copy.start()
        copies.append(copy)
    for copy in copies:
        copy.wait()


def swap(array, axis, step):
    count = lax.axis_size(axis)
    return lax.ppermute(array, axis, [(place, place ^ step) for place in range(count)])


def exchange(pieces):
    return [pieces[0]] + [swap(pieces[step], AXES[1], step) for step in range(1, len(pieces))]


def on_device(groups, group_length, queries, key_vectors, value_vectors, input_gate, forget_gate):
    heads, length = input_gate.shape
    key_dim = queries.shape[1] // heads
    value_dim = value_vectors.shape[1] // heads
    params = pltpu.CompilerParams(vmem_limit_bytes=48 * 1024 * 1024)
    hbm = pl.BlockSpec(memory_space=pltpu.HBM)

    def shape(*dims):
        return jax.ShapeDtypeStruct(dims, jnp.float32)

    def call(kernel, out_shape, *arrays, scratch=()):
        return pl.pallas_call(
            kernel, out_shape=out_shape, scratch_shapes=scratch, compiler_params=params
        )(*arrays)

    single = shape(key_dim + TAIL, LANES)
    double = shape(SIDES * key_dim + TAIL, LANES)
    halves = shape(heads, key_dim + TAIL, LANES)
    scalars = pltpu.VMEM((SIDES, 3, heads, LANES), jnp.float32)
    output = jax.ShapeDtypeStruct((length, heads * value_dim), jnp.bfloat16)
    operands = (key_vectors, value_vectors, input_gate, forget_gate)

    def levels(axis, bit, size):
        while bit < size:
            yield axis, bit
            bit *= 2

    own, send = pl.pallas_call(
        state_kernel,
        out_shape=(halves, halves),
        in_specs=[hbm] * len(operands),
        scratch_shapes=[pltpu.VMEM(array.shape, array.dtype) for array in operands]
        + [pltpu.SemaphoreType.DMA((len(operands),))],
        compiler_params=params,
    )(*(pltpu.with_memory_space_constraint(array, pltpu.HBM) for array in operands))
    inner_shapes = (shape(value_dim // LANES, heads, length, LANES), shape(heads, length, 3))
    inputs = (queries, *operands)
    vmem = pl.BlockSpec(memory_space=pltpu.VMEM)
    *packed, early_num, early_stats = pl.pallas_call(
        pack_kernel,
        out_shape=(double,) * heads + inner_shapes,
        in_specs=[vmem] * 2 + [hbm] * len(inputs),
        scratch_shapes=[pltpu.VMEM(array.shape, array.dtype) for array in inputs]
        + [pltpu.SemaphoreType.DMA((len(inputs),))],
        compiler_params=params,
    )(
        own,
        swap(send, AXES[0], 1),
        *(pltpu.with_memory_space_constraint(array, pltpu.HBM) for array in inputs),
    )
    pieces = exchange(packed)
    inner_num, stats = call(inner_kernel, inner_shapes, *inputs, early_num, early_stats)
    group = call(quad_kernel, double, *pieces, scratch=[scalars])
    within = []
    for axis, bit in levels(AXES[1], heads, group_length):
        kernel = functools.partial(butterfly_kernel, axis, bit, SIDES)
        group, *within = call(kernel, (double, double), group, swap(group, axis, bit), *within)
    total = call(pair_kernel, single, group)
    before = []
    *steps, last = levels(AXES[0], SIDES, groups)
    for axis, bit in steps:
        kernel = functools.partial(butterfly_kernel, axis, bit, 1)
        total, *before = call(kernel, (single, single), total, swap(total, axis, bit), *before)
    states = call(
        functools.partial(prefix_kernel, *last, heads),
        (double,) * heads,
        swap(total, *last),
        group,
        *within,
        *before,
        *pieces,
        scratch=[scalars, pltpu.VMEM((SIDES, heads, 1 + heads, LANES), jnp.float32)],
    )
    carried = exchange(states)
    half = call(part_kernel, shape(heads, key_dim, LANES), stats, *carried)
    other_half = swap(half, AXES[0], 1)
    columns, factors = call(
        outer_kernel,
        (shape(heads, length, LANES), shape(heads, length, 2)),
        queries,
        inner_num,
        stats,
        *carried,
    )
    return pl.pallas_call(
        last_kernel,
        out_shape=output,
        out_specs=hbm,
        scratch_shapes=[
            pltpu.VMEM(output.shape, output.dtype),
            pltpu.SemaphoreType.DMA((heads,)),
        ],
        compiler_params=params,
    )(queries, inner_num, factors, columns, other_half)


def solution(mesh):
    return jax.shard_map(
        functools.partial(on_device, mesh.shape["grp"], mesh.shape["seq"]),
        mesh=mesh,
        in_specs=(
            P(AXES, None),
            P(AXES, None),
            P(AXES, None),
            P(None, AXES),
            P(None, AXES),
        ),
        out_specs=P(AXES, None),
        check_vma=False,
    )
```

```python
import functools

import jax
import jax.numpy as jnp
from jax import lax
from jax.experimental import pallas as pl
from jax.experimental.pallas import tpu as pltpu
from jax.sharding import PartitionSpec as P

floor_value = -1e30
LANES = 128
AXES = ("grp", "seq")


def split_two(x):
    high = x.astype(jnp.bfloat16)
    low = (x - high.astype(jnp.float32)).astype(jnp.bfloat16)
    return high, low


def split_three(x):
    high = x.astype(jnp.bfloat16)
    rest = x - high.astype(jnp.float32)
    mid = rest.astype(jnp.bfloat16)
    low = (rest - mid.astype(jnp.float32)).astype(jnp.bfloat16)
    return high, mid, low


def dot(a, b):
    return jnp.dot(a, b, preferred_element_type=jnp.float32)


def dot_last(a, b):
    return lax.dot_general(a, b, (((1,), (1,)), ((), ())), preferred_element_type=jnp.float32)


def log_forget(forget):
    return jnp.minimum(forget, 0.0) - jnp.log1p(jnp.exp(-jnp.abs(forget)))


def triangle(length, lower):
    rows = lax.broadcasted_iota(jnp.int32, (length, length), 0)
    cols = lax.broadcasted_iota(jnp.int32, (length, length), 1)
    return rows >= cols if lower else rows <= cols


def cumulative_rows(logf):
    ones = triangle(logf.shape[1], False).astype(jnp.bfloat16)
    high, mid, low = split_three(logf)
    return (dot(low, ones) + dot(mid, ones)) + dot(high, ones)


def cumulative_columns(logf):
    ones = triangle(logf.shape[1], True).astype(jnp.bfloat16)
    high, mid, low = split_three(logf)
    return (dot_last(ones, low) + dot_last(ones, mid)) + dot_last(ones, high)


TAIL = 8
VECTOR, TOP, DECAY = range(3)


def member(quad):
    return lax.rem(lax.axis_index(AXES[1]), quad)


def partners(quad):
    return [member(quad) ^ step for step in range(quad)]


def tail_rows(vector, top, decay):
    rest = jnp.zeros((TAIL - 3, vector.shape[1]), jnp.float32)
    return jnp.concatenate([vector, top, decay, rest], axis=0)


def tail_row(ref, row):
    first = ref.shape[0] - TAIL + row
    return ref[first : first + 1, :]


def load(ref):
    return (ref[0 : ref.shape[0] - TAIL, :], *(tail_row(ref, row) for row in range(3)))


def store(ref, state):
    matrix, *tail = state
    ref[0 : matrix.shape[0], :] = matrix
    ref[matrix.shape[0] :, :] = tail_rows(*tail)


def join(earlier, later):
    early_matrix, early_vector, early_top, early_decay = earlier
    late_matrix, late_vector, late_top, late_decay = later
    moved = early_top + late_decay
    joined = jnp.maximum(moved, late_top)
    early_weight, late_weight = jnp.exp(moved - joined), jnp.exp(late_top - joined)
    return (
        early_weight * early_matrix + late_weight * late_matrix,
        early_weight * early_vector + late_weight * late_vector,
        joined,
        early_decay + late_decay,
    )


def choose(condition, one, other):
    return jax.tree.map(lambda a, b: jnp.where(condition, a, b), one, other)


def nothing(like):
    matrix, vector, top, decay = like
    zero = jnp.zeros_like(decay)
    return jnp.zeros_like(matrix), jnp.zeros_like(vector), zero + floor_value, zero


def state_kernel(k_hbm, v_hbm, in_hbm, fo_hbm, *refs):
    *out_refs, k_ref, v_ref, in_ref, fo_ref, scalar_ref, arrived = refs
    copies = [
        pltpu.make_async_copy(source, target, arrived.at[place])
        for place, (source, target) in enumerate(
            ((fo_hbm, fo_ref), (in_hbm, in_ref), (k_hbm, k_ref), (v_hbm, v_ref))
        )
    ]
    for copy in copies:
        copy.start()
    heads, length = in_ref.shape
    key_dim = k_ref.shape[1] // heads
    value_dim = v_ref.shape[1] // heads
    parts = value_dim // LANES
    for copy in copies:
        copy.wait()
    cumul = cumulative_rows(log_forget(fo_ref[...]))
    level = in_ref[...] - cumul
    level_top = jnp.max(level, axis=1, keepdims=True)
    decay = cumul[:, length - 1 : length]
    scalar_ref[0] = jnp.exp(level - level_top)
    scalar_ref[1] = jnp.broadcast_to(decay + level_top, (heads, length))
    scalar_ref[2] = jnp.broadcast_to(decay, (heads, length))
    for head, out_ref in zip(partners(heads), out_refs):
        keys = k_ref[:, pl.ds(pl.multiple_of(head * key_dim, LANES), key_dim)]
        values = v_ref[:, pl.ds(pl.multiple_of(head * value_dim, LANES), value_dim)]
        row, top, decay = (scalar_ref[place, pl.ds(head, 1), :] for place in range(3))
        high, low = split_two(keys.astype(jnp.float32).T * row)
        matrix = dot(
            jnp.concatenate([high, low], axis=1), jnp.concatenate([values, values], axis=0)
        )
        for part in range(parts):
            out_ref[part * key_dim : (part + 1) * key_dim, :] = matrix[
                :, part * LANES : (part + 1) * LANES
            ]
        high, mid, low = split_three(row)
        vector = (dot(low, keys) + dot(mid, keys)) + dot(high, keys)
        out_ref[parts * key_dim :, :] = tail_rows(vector, top, decay)


def read_scalars(refs, scalar_ref, places):
    for place, ref in zip(places, refs):
        scalar_ref[0, pl.ds(place, 1), :] = tail_row(ref, TOP)
        scalar_ref[1, pl.ds(place, 1), :] = tail_row(ref, DECAY)
    count = len(refs)
    tops = [scalar_ref[0, place : place + 1, :] for place in range(count)]
    decays = [scalar_ref[1, place : place + 1, :] for place in range(count)]
    return tops, decays


def weights_of(tops, decays):
    moved, total = [], jnp.zeros_like(decays[0])
    for top, decay in zip(reversed(tops), reversed(decays)):
        moved.append(top + total)
        total = total + decay
    moved.reverse()
    joined = functools.reduce(jnp.maximum, moved)
    return [jnp.exp(top - joined) for top in moved], joined, total


def weighted_sum(weights, states):
    matrix, vector = 0.0, 0.0
    for weight, state in zip(weights, states):
        matrix = matrix + weight * state[0]
        vector = vector + weight * state[1]
    return matrix, vector


def quad_kernel(*refs):
    *refs, out_ref, scalar_ref = refs
    places = partners(len(refs))
    weights, top, decay = weights_of(*read_scalars(refs, scalar_ref, places))
    for place, weight in enumerate(weights):
        scalar_ref[0, place : place + 1, :] = weight
    weights = [scalar_ref[0, pl.ds(place, 1), :] for place in places]
    store(out_ref, (*weighted_sum(weights, [load(ref) for ref in refs]), top, decay))


def later_side(axis, bit):
    return (lax.axis_index(axis) & bit) != 0


def butterfly_kernel(axis, bit, *refs):
    total_ref, other_ref, *before_refs, out_total, out_before = refs
    is_later = later_side(axis, bit)
    total, other = load(total_ref), load(other_ref)
    before = load(before_refs[0]) if before_refs else nothing(total)
    store(out_total, join(choose(is_later, other, total), choose(is_later, total, other)))
    store(out_before, choose(is_later, join(other, before), before))


def gather_kernel(axis, bit, own_ref, other_ref, out_ref):
    is_later = later_side(axis, bit)
    count = out_ref.shape[0] // 2
    for place in range(count):
        own = own_ref[place] if own_ref.ndim == 3 else own_ref[...]
        other = other_ref[place] if other_ref.ndim == 3 else other_ref[...]
        out_ref[place] = jnp.where(is_later, other, own)
        out_ref[count + place] = jnp.where(is_later, own, other)


def prefix_kernel(quad, own_ref, other_ref, within_ref, *refs):
    *refs, scalar_ref, weight_ref = refs
    pieces, out_refs = refs[:quad], refs[quad:]
    places = partners(quad)
    me = lax.axis_index(AXES[0])
    even = (me & 1) == 0
    within = load(within_ref)
    sums = [(load(own_ref.at[pair]), load(other_ref.at[pair])) for pair in range(own_ref.shape[0])]
    tops, decays, earlier = [], [], []
    for own, other in sums:
        for one, two in ((own, other), (other, own)):
            before = len(tops) < me
            tops.append(jnp.where(before, jnp.where(even, one[2], two[2]), floor_value))
            decays.append(jnp.where(before, jnp.where(even, one[3], two[3]), 0.0))
            earlier.append(before)
    weights, top, _ = weights_of(tops + [within[2]], decays + [within[3]])
    weights[:-1] = [jnp.where(before, w, 0.0) for before, w in zip(earlier, weights)]
    terms = [(weights[-1], within)]
    for pair, (own, other) in enumerate(sums):
        one, two = weights[2 * pair], weights[2 * pair + 1]
        terms.append((jnp.where(even, one, two), own))
        terms.append((jnp.where(even, two, one), other))
    start = (*weighted_sum(*zip(*terms)), top)
    tops, decays = read_scalars(pieces, scalar_ref, places)
    zero = jnp.zeros_like(tops[0])
    for place in range(quad):
        weights, joined, _ = weights_of([start[2]] + tops[:place], [zero] + decays[:place])
        weights += [zero] * (quad - place)
        for index, weight in enumerate(weights):
            weight_ref[place, index : index + 1, :] = weight
        scalar_ref[0, place : place + 1, :] = joined
    states = [start] + [load(piece) for piece in pieces]
    for place, out_ref in zip(places, out_refs):
        weights = [weight_ref[place, 0:1, :]]
        weights += [weight_ref[place, pl.ds(1 + index, 1), :] for index in places]
        top = scalar_ref[0, pl.ds(place, 1), :]
        store(out_ref, (*weighted_sum(weights, states), top, zero))


CUMUL, ROW_LEVEL, INNER_DEN = range(3)


def inner_kernel(q_ref, k_ref, v_ref, in_ref, fo_ref, num_ref, stat_ref):
    heads, length = in_ref.shape
    key_dim = q_ref.shape[1] // heads
    value_dim = v_ref.shape[1] // heads
    logf = log_forget(fo_ref[...])
    level = in_ref[...] - cumulative_rows(logf)
    cumul = cumulative_columns(logf)
    causal = triangle(length, True)
    for head in range(heads):
        queries = q_ref[:, head * key_dim : (head + 1) * key_dim]
        keys = k_ref[:, head * key_dim : (head + 1) * key_dim]
        values = v_ref[:, head * value_dim : (head + 1) * value_dim]
        scores = dot_last(queries, keys) * (key_dim**-0.5)
        masked = jnp.where(causal, level[head : head + 1, :], -jnp.inf)
        row_level = jnp.max(masked, axis=1, keepdims=True)
        weighted = jnp.exp(masked - row_level) * scores
        stat_ref[head, :, CUMUL : CUMUL + 1] = cumul[:, head : head + 1]
        stat_ref[head, :, ROW_LEVEL : ROW_LEVEL + 1] = row_level
        stat_ref[head, :, INNER_DEN : INNER_DEN + 1] = jnp.sum(weighted, axis=1, keepdims=True)
        num_ref[head] = dot(weighted.astype(jnp.bfloat16), values)


def add_carried(head, q_ref, num_ref, stat_ref, message_ref):
    length, value_dim = num_ref.shape[1:]
    key_dim = q_ref.shape[1] // num_ref.shape[0]
    parts = value_dim // LANES
    scaling = key_dim**-0.5
    query = q_ref[:, pl.ds(pl.multiple_of(head * key_dim, LANES), key_dim)]
    matrix = jnp.concatenate(
        [message_ref[part * key_dim : (part + 1) * key_dim, :] for part in range(parts)], 1
    )
    high, low = split_two(matrix)
    carried = dot(jnp.concatenate([query, query], axis=1), jnp.concatenate([high, low], axis=0))
    stats = stat_ref[head]
    cumul, row_level, inner_den = (stats[:, place : place + 1] for place in range(3))
    top = tail_row(message_ref, TOP)[:, 0:1]
    carried_den = jnp.sum(
        query.astype(jnp.float32) * tail_row(message_ref, VECTOR), axis=1, keepdims=True
    )
    joined = jnp.maximum(row_level, top)
    inner_factor = jnp.exp(row_level - joined)
    outer_factor = jnp.exp(top - joined) * scaling
    denom = inner_factor * inner_den + outer_factor * carried_den
    inverse = 1.0 / jnp.maximum(jnp.abs(denom), jnp.exp(-(cumul + joined)))
    return (inner_factor * inverse) * num_ref[head] + (outer_factor * inverse) * carried


def part_kernel(steps, q_ref, num_ref, stat_ref, *refs):
    places = partners(num_ref.shape[0])
    count = len(steps)
    for step, message_ref, out_ref in zip(steps, refs[:count], refs[count:]):
        head = places[step]
        out_ref[...] = add_carried(head, q_ref, num_ref, stat_ref, message_ref).astype(
            out_ref.dtype
        )


def last_kernel(q_ref, num_ref, stat_ref, message_ref, *refs):
    *done_refs, out_hbm, own_ref, done = refs
    heads, _, value_dim = num_ref.shape
    places = partners(heads)

    def place(step, source):
        columns = pl.ds(pl.multiple_of(places[step] * value_dim, LANES), value_dim)
        copy = pltpu.make_async_copy(source, out_hbm.at[:, columns], done.at[step])
        copy.start()
        return copy

    copies = [place(step, ref) for step, ref in enumerate(done_refs)]
    own_ref[...] = add_carried(places[-1], q_ref, num_ref, stat_ref, message_ref).astype(
        own_ref.dtype
    )
    copies.append(place(heads - 1, own_ref))
    for copy in copies:
        copy.wait()


def swap(array, axis, step):
    count = lax.axis_size(axis)
    return lax.ppermute(array, axis, [(place, place ^ step) for place in range(count)])


def exchange(pieces):
    return [pieces[0]] + [swap(pieces[step], AXES[1], step) for step in range(1, len(pieces))]


def on_device(groups, group_length, queries, key_vectors, value_vectors, input_gate, forget_gate):
    heads, length = input_gate.shape
    key_dim = queries.shape[1] // heads
    value_dim = value_vectors.shape[1] // heads
    message = jax.ShapeDtypeStruct(
        (value_dim // LANES * key_dim + TAIL, LANES), jnp.float32
    )
    messages = (message,) * heads
    params = pltpu.CompilerParams(vmem_limit_bytes=48 * 1024 * 1024)
    hbm = pl.BlockSpec(memory_space=pltpu.HBM)
    scalars = pltpu.VMEM((3, heads, LANES), jnp.float32)
    output = jax.ShapeDtypeStruct((length, heads * value_dim), jnp.bfloat16)
    operands = (key_vectors, value_vectors, input_gate, forget_gate)
    own = pl.pallas_call(
        state_kernel,
        out_shape=messages,
        in_specs=[hbm] * len(operands),
        scratch_shapes=[pltpu.VMEM(array.shape, array.dtype) for array in operands]
        + [scalars, pltpu.SemaphoreType.DMA((len(operands),))],
        compiler_params=params,
    )(*(pltpu.with_memory_space_constraint(array, pltpu.HBM) for array in operands))
    pieces = exchange(own)
    inner_num, stats = pl.pallas_call(
        inner_kernel,
        out_shape=(
            jax.ShapeDtypeStruct((heads, length, value_dim), jnp.float32),
            jax.ShapeDtypeStruct((heads, length, 3), jnp.float32),
        ),
        compiler_params=params,
    )(queries, *operands)
    total = pl.pallas_call(
        quad_kernel, out_shape=message, scratch_shapes=[scalars], compiler_params=params
    )(*pieces)
    within = []
    bit = heads
    while bit < group_length:
        total, *within = pl.pallas_call(
            functools.partial(butterfly_kernel, AXES[1], bit),
            out_shape=(message, message),
            compiler_params=params,
        )(total, swap(total, AXES[1], bit), *within)
        bit *= 2
    sums = total
    bit, count = 2, 1
    while bit < groups:
        count *= 2
        sums = pl.pallas_call(
            functools.partial(gather_kernel, AXES[0], bit),
            out_shape=jax.ShapeDtypeStruct((count,) + message.shape, message.dtype),
            compiler_params=params,
        )(sums, swap(sums, AXES[0], bit))
        bit *= 2
    states = pl.pallas_call(
        functools.partial(prefix_kernel, heads),
        out_shape=messages,
        scratch_shapes=[scalars, pltpu.VMEM((heads, 1 + heads, LANES), jnp.float32)],
        compiler_params=params,
    )(sums, swap(sums, AXES[0], 1), *within, *pieces)
    carried = exchange(states)
    column = jax.ShapeDtypeStruct((length, value_dim), output.dtype)
    columns = {}
    for steps in [(0, *range(2, heads - 1)), (1,)]:
        outs = pl.pallas_call(
            functools.partial(part_kernel, steps),
            out_shape=(column,) * len(steps),
            compiler_params=params,
        )(queries, inner_num, stats, *(carried[step] for step in steps))
        columns.update(zip(steps, outs))
    return pl.pallas_call(
        last_kernel,
        out_shape=output,
        out_specs=hbm,
        scratch_shapes=[
            pltpu.VMEM(column.shape, column.dtype),
            pltpu.SemaphoreType.DMA((heads,)),
        ],
        compiler_params=params,
    )(queries, inner_num, stats, carried[-1], *(columns[step] for step in range(heads - 1)))


def solution(mesh):
    return jax.shard_map(
        functools.partial(on_device, mesh.shape["grp"], mesh.shape["seq"]),
        mesh=mesh,
        in_specs=(
            P(AXES, None),
            P(AXES, None),
            P(AXES, None),
            P(None, AXES),
            P(None, AXES),
        ),
        out_specs=P(AXES, None),
        check_vma=False,
    )
```

```python
import functools

import jax
import jax.numpy as jnp
from jax import lax
from jax.experimental import pallas as pl
from jax.experimental.pallas import tpu as pltpu
from jax.sharding import PartitionSpec as P

floor_value = -1e30
LANES = 128
AXES = ("grp", "seq")


def split_two(x):
    high = x.astype(jnp.bfloat16)
    low = (x - high.astype(jnp.float32)).astype(jnp.bfloat16)
    return high, low


def split_three(x):
    high = x.astype(jnp.bfloat16)
    rest = x - high.astype(jnp.float32)
    mid = rest.astype(jnp.bfloat16)
    low = (rest - mid.astype(jnp.float32)).astype(jnp.bfloat16)
    return high, mid, low


def dot(a, b):
    return jnp.dot(a, b, preferred_element_type=jnp.float32)


def dot_last(a, b):
    return lax.dot_general(a, b, (((1,), (1,)), ((), ())), preferred_element_type=jnp.float32)


def log_forget(forget):
    return jnp.minimum(forget, 0.0) - jnp.log1p(jnp.exp(-jnp.abs(forget)))


def triangle(length, lower):
    rows = lax.broadcasted_iota(jnp.int32, (length, length), 0)
    cols = lax.broadcasted_iota(jnp.int32, (length, length), 1)
    return rows >= cols if lower else rows <= cols


def cumulative_rows(logf):
    ones = triangle(logf.shape[1], False).astype(jnp.bfloat16)
    high, mid, low = split_three(logf)
    return (dot(low, ones) + dot(mid, ones)) + dot(high, ones)


def cumulative_columns(logf):
    ones = triangle(logf.shape[1], True).astype(jnp.bfloat16)
    high, mid, low = split_three(logf)
    return (dot_last(ones, low) + dot_last(ones, mid)) + dot_last(ones, high)


TAIL = 8
VECTOR, TOP, DECAY = range(3)


def member(quad):
    return lax.rem(lax.axis_index(AXES[1]), quad)


def distances(quad):
    return [0, *range(quad - 2, 0, -1), quad - 1]


def partners(quad):
    return [member(quad) ^ distance for distance in distances(quad)]


def tail_rows(vector, top, decay):
    rest = jnp.zeros((TAIL - 3, vector.shape[1]), jnp.float32)
    return jnp.concatenate([vector, top, decay, rest], axis=0)


def tail_row(ref, row):
    first = ref.shape[0] - TAIL + row
    return ref[first : first + 1, :]


def load(ref):
    return (ref[0 : ref.shape[0] - TAIL, :], *(tail_row(ref, row) for row in range(3)))


def store(ref, state):
    matrix, *tail = state
    ref[0 : matrix.shape[0], :] = matrix
    ref[matrix.shape[0] :, :] = tail_rows(*tail)


def join(earlier, later):
    early_matrix, early_vector, early_top, early_decay = earlier
    late_matrix, late_vector, late_top, late_decay = later
    moved = early_top + late_decay
    joined = jnp.maximum(moved, late_top)
    early_weight, late_weight = jnp.exp(moved - joined), jnp.exp(late_top - joined)
    return (
        early_weight * early_matrix + late_weight * late_matrix,
        early_weight * early_vector + late_weight * late_vector,
        joined,
        early_decay + late_decay,
    )


def choose(condition, one, other):
    return jax.tree.map(lambda a, b: jnp.where(condition, a, b), one, other)


def nothing(like):
    matrix, vector, top, decay = like
    zero = jnp.zeros_like(decay)
    return jnp.zeros_like(matrix), jnp.zeros_like(vector), zero + floor_value, zero


def state_kernel(k_hbm, v_hbm, in_hbm, fo_hbm, *refs):
    *out_refs, k_ref, v_ref, in_ref, fo_ref, scalar_ref, arrived = refs
    copies = [
        pltpu.make_async_copy(source, target, arrived.at[place])
        for place, (source, target) in enumerate(
            ((fo_hbm, fo_ref), (in_hbm, in_ref), (k_hbm, k_ref), (v_hbm, v_ref))
        )
    ]
    for copy in copies:
        copy.start()
    heads, length = in_ref.shape
    key_dim = k_ref.shape[1] // heads
    value_dim = v_ref.shape[1] // heads
    parts = value_dim // LANES
    copies[0].wait()
    cumul = cumulative_rows(log_forget(fo_ref[...]))
    copies[1].wait()
    level = in_ref[...] - cumul
    level_top = jnp.max(level, axis=1, keepdims=True)
    decay = cumul[:, length - 1 : length]
    scalar_ref[0] = jnp.exp(level - level_top)
    scalar_ref[1] = jnp.broadcast_to(decay + level_top, (heads, length))
    scalar_ref[2] = jnp.broadcast_to(decay, (heads, length))
    copies[2].wait()
    copies[3].wait()
    for head, out_ref in zip(partners(heads), out_refs):
        keys = k_ref[:, pl.ds(pl.multiple_of(head * key_dim, LANES), key_dim)]
        values = v_ref[:, pl.ds(pl.multiple_of(head * value_dim, LANES), value_dim)]
        row, top, decay = (scalar_ref[place, pl.ds(head, 1), :] for place in range(3))
        high, low = split_two(keys.astype(jnp.float32).T * row)
        matrix = dot(
            jnp.concatenate([high, low], axis=1), jnp.concatenate([values, values], axis=0)
        )
        for part in range(parts):
            out_ref[part * key_dim : (part + 1) * key_dim, :] = matrix[
                :, part * LANES : (part + 1) * LANES
            ]
        high, mid, low = split_three(row)
        vector = (dot(low, keys) + dot(mid, keys)) + dot(high, keys)
        out_ref[parts * key_dim :, :] = tail_rows(vector, top, decay)


def read_scalars(refs, scalar_ref, places):
    for place, ref in zip(places, refs):
        scalar_ref[0, pl.ds(place, 1), :] = tail_row(ref, TOP)
        scalar_ref[1, pl.ds(place, 1), :] = tail_row(ref, DECAY)
    count = len(refs)
    tops = [scalar_ref[0, place : place + 1, :] for place in range(count)]
    decays = [scalar_ref[1, place : place + 1, :] for place in range(count)]
    return tops, decays


def weights_of(tops, decays):
    moved, total = [], jnp.zeros_like(decays[0])
    for top, decay in zip(reversed(tops), reversed(decays)):
        moved.append(top + total)
        total = total + decay
    moved.reverse()
    joined = functools.reduce(jnp.maximum, moved)
    return [jnp.exp(top - joined) for top in moved], joined, total


def weighted_sum(weights, states):
    matrix, vector = 0.0, 0.0
    for weight, state in zip(weights, states):
        matrix = matrix + weight * state[0]
        vector = vector + weight * state[1]
    return matrix, vector


def quad_kernel(*refs):
    *refs, out_ref, scalar_ref = refs
    places = partners(len(refs))
    weights, top, decay = weights_of(*read_scalars(refs, scalar_ref, places))
    for place, weight in enumerate(weights):
        scalar_ref[0, place : place + 1, :] = weight
    weights = [scalar_ref[0, pl.ds(place, 1), :] for place in places]
    store(out_ref, (*weighted_sum(weights, [load(ref) for ref in refs]), top, decay))


def later_side(axis, bit):
    return (lax.axis_index(axis) & bit) != 0


def butterfly_kernel(axis, bit, *refs):
    total_ref, other_ref, *before_refs, out_total, out_before = refs
    is_later = later_side(axis, bit)
    total, other = load(total_ref), load(other_ref)
    before = load(before_refs[0]) if before_refs else nothing(total)
    store(out_total, join(choose(is_later, other, total), choose(is_later, total, other)))
    store(out_before, choose(is_later, join(other, before), before))


def gather_kernel(axis, bit, own_ref, other_ref, out_ref):
    is_later = later_side(axis, bit)
    count = out_ref.shape[0] // 2
    for place in range(count):
        own = own_ref[place] if own_ref.ndim == 3 else own_ref[...]
        other = other_ref[place] if other_ref.ndim == 3 else other_ref[...]
        out_ref[place] = jnp.where(is_later, other, own)
        out_ref[count + place] = jnp.where(is_later, own, other)


def prefix_kernel(quad, own_ref, other_ref, within_ref, *refs):
    *refs, scalar_ref, weight_ref = refs
    pieces, out_refs = refs[:quad], refs[quad:]
    places = partners(quad)
    me = lax.axis_index(AXES[0])
    even = (me & 1) == 0
    within = load(within_ref)
    sums = [(load(own_ref.at[pair]), load(other_ref.at[pair])) for pair in range(own_ref.shape[0])]
    tops, decays, earlier = [], [], []
    for own, other in sums:
        for one, two in ((own, other), (other, own)):
            before = len(tops) < me
            tops.append(jnp.where(before, jnp.where(even, one[2], two[2]), floor_value))
            decays.append(jnp.where(before, jnp.where(even, one[3], two[3]), 0.0))
            earlier.append(before)
    weights, top, _ = weights_of(tops + [within[2]], decays + [within[3]])
    weights[:-1] = [jnp.where(before, w, 0.0) for before, w in zip(earlier, weights)]
    terms = [(weights[-1], within)]
    for pair, (own, other) in enumerate(sums):
        one, two = weights[2 * pair], weights[2 * pair + 1]
        terms.append((jnp.where(even, one, two), own))
        terms.append((jnp.where(even, two, one), other))
    start = (*weighted_sum(*zip(*terms)), top)
    tops, decays = read_scalars(pieces, scalar_ref, places)
    zero = jnp.zeros_like(tops[0])
    for place in range(quad):
        weights, joined, _ = weights_of([start[2]] + tops[:place], [zero] + decays[:place])
        weights += [zero] * (quad - place)
        for index, weight in enumerate(weights):
            weight_ref[place, index : index + 1, :] = weight
        scalar_ref[0, place : place + 1, :] = joined
    states = [start] + [load(piece) for piece in pieces]
    for place, out_ref in zip(places, out_refs):
        weights = [weight_ref[place, 0:1, :]]
        weights += [weight_ref[place, pl.ds(1 + index, 1), :] for index in places]
        top = scalar_ref[0, pl.ds(place, 1), :]
        store(out_ref, (*weighted_sum(weights, states), top, zero))


CUMUL, ROW_LEVEL, INNER_DEN = range(3)


def inner_kernel(q_ref, k_ref, v_ref, in_ref, fo_ref, num_ref, stat_ref):
    heads, length = in_ref.shape
    key_dim = q_ref.shape[1] // heads
    value_dim = v_ref.shape[1] // heads
    logf = log_forget(fo_ref[...])
    level = in_ref[...] - cumulative_rows(logf)
    cumul = cumulative_columns(logf)
    causal = triangle(length, True)
    for head in range(heads):
        queries = q_ref[:, head * key_dim : (head + 1) * key_dim]
        keys = k_ref[:, head * key_dim : (head + 1) * key_dim]
        values = v_ref[:, head * value_dim : (head + 1) * value_dim]
        scores = dot_last(queries, keys) * (key_dim**-0.5)
        masked = jnp.where(causal, level[head : head + 1, :], -jnp.inf)
        row_level = jnp.max(masked, axis=1, keepdims=True)
        weighted = jnp.exp(masked - row_level) * scores
        stat_ref[head, :, CUMUL : CUMUL + 1] = cumul[:, head : head + 1]
        stat_ref[head, :, ROW_LEVEL : ROW_LEVEL + 1] = row_level
        stat_ref[head, :, INNER_DEN : INNER_DEN + 1] = jnp.sum(weighted, axis=1, keepdims=True)
        num_ref[head] = dot(weighted.astype(jnp.bfloat16), values)


def add_carried(head, q_ref, num_ref, stat_ref, message_ref):
    length, value_dim = num_ref.shape[1:]
    key_dim = q_ref.shape[1] // num_ref.shape[0]
    parts = value_dim // LANES
    scaling = key_dim**-0.5
    query = q_ref[:, pl.ds(pl.multiple_of(head * key_dim, LANES), key_dim)]
    matrix = jnp.concatenate(
        [message_ref[part * key_dim : (part + 1) * key_dim, :] for part in range(parts)], 1
    )
    high, low = split_two(matrix)
    carried = dot(jnp.concatenate([query, query], axis=1), jnp.concatenate([high, low], axis=0))
    stats = stat_ref[head]
    cumul, row_level, inner_den = (stats[:, place : place + 1] for place in range(3))
    top = tail_row(message_ref, TOP)[:, 0:1]
    carried_den = jnp.sum(
        query.astype(jnp.float32) * tail_row(message_ref, VECTOR), axis=1, keepdims=True
    )
    joined = jnp.maximum(row_level, top)
    inner_factor = jnp.exp(row_level - joined)
    outer_factor = jnp.exp(top - joined) * scaling
    denom = inner_factor * inner_den + outer_factor * carried_den
    inverse = 1.0 / jnp.maximum(jnp.abs(denom), jnp.exp(-(cumul + joined)))
    return (inner_factor * inverse) * num_ref[head] + (outer_factor * inverse) * carried


def part_kernel(steps, q_ref, num_ref, stat_ref, *refs):
    places = partners(num_ref.shape[0])
    count = len(steps)
    for step, message_ref, out_ref in zip(steps, refs[:count], refs[count:]):
        head = places[step]
        out_ref[...] = add_carried(head, q_ref, num_ref, stat_ref, message_ref).astype(
            out_ref.dtype
        )


def last_kernel(q_ref, num_ref, stat_ref, message_ref, *refs):
    *done_refs, out_hbm, own_ref, done = refs
    heads, _, value_dim = num_ref.shape
    places = partners(heads)

    def place(step, source):
        columns = pl.ds(pl.multiple_of(places[step] * value_dim, LANES), value_dim)
        copy = pltpu.make_async_copy(source, out_hbm.at[:, columns], done.at[step])
        copy.start()
        return copy

    copies = [place(step, ref) for step, ref in enumerate(done_refs)]
    own_ref[...] = add_carried(places[-1], q_ref, num_ref, stat_ref, message_ref).astype(
        own_ref.dtype
    )
    copies.append(place(heads - 1, own_ref))
    for copy in copies:
        copy.wait()


def swap(array, axis, step):
    count = lax.axis_size(axis)
    return lax.ppermute(array, axis, [(place, place ^ step) for place in range(count)])


def exchange(pieces):
    steps = zip(pieces[1:], distances(len(pieces))[1:])
    return [pieces[0]] + [swap(piece, AXES[1], distance) for piece, distance in steps]


def on_device(groups, group_length, queries, key_vectors, value_vectors, input_gate, forget_gate):
    heads, length = input_gate.shape
    key_dim = queries.shape[1] // heads
    value_dim = value_vectors.shape[1] // heads
    message = jax.ShapeDtypeStruct(
        (value_dim // LANES * key_dim + TAIL, LANES), jnp.float32
    )
    messages = (message,) * heads
    params = pltpu.CompilerParams(vmem_limit_bytes=48 * 1024 * 1024)
    hbm = pl.BlockSpec(memory_space=pltpu.HBM)
    scalars = pltpu.VMEM((3, heads, LANES), jnp.float32)
    output = jax.ShapeDtypeStruct((length, heads * value_dim), jnp.bfloat16)
    operands = (key_vectors, value_vectors, input_gate, forget_gate)
    own = pl.pallas_call(
        state_kernel,
        out_shape=messages,
        in_specs=[hbm] * len(operands),
        scratch_shapes=[pltpu.VMEM(array.shape, array.dtype) for array in operands]
        + [scalars, pltpu.SemaphoreType.DMA((len(operands),))],
        compiler_params=params,
    )(*(pltpu.with_memory_space_constraint(array, pltpu.HBM) for array in operands))
    pieces = exchange(own)
    inner_num, stats = pl.pallas_call(
        inner_kernel,
        out_shape=(
            jax.ShapeDtypeStruct((heads, length, value_dim), jnp.float32),
            jax.ShapeDtypeStruct((heads, length, 3), jnp.float32),
        ),
        compiler_params=params,
    )(queries, *operands)
    total = pl.pallas_call(
        quad_kernel, out_shape=message, scratch_shapes=[scalars], compiler_params=params
    )(*pieces)
    within = []
    bit = heads
    while bit < group_length:
        total, *within = pl.pallas_call(
            functools.partial(butterfly_kernel, AXES[1], bit),
            out_shape=(message, message),
            compiler_params=params,
        )(total, swap(total, AXES[1], bit), *within)
        bit *= 2
    sums = total
    bit, count = 2, 1
    while bit < groups:
        count *= 2
        sums = pl.pallas_call(
            functools.partial(gather_kernel, AXES[0], bit),
            out_shape=jax.ShapeDtypeStruct((count,) + message.shape, message.dtype),
            compiler_params=params,
        )(sums, swap(sums, AXES[0], bit))
        bit *= 2
    states = pl.pallas_call(
        functools.partial(prefix_kernel, heads),
        out_shape=messages,
        scratch_shapes=[scalars, pltpu.VMEM((heads, 1 + heads, LANES), jnp.float32)],
        compiler_params=params,
    )(sums, swap(sums, AXES[0], 1), *within, *pieces)
    carried = exchange(states)
    column = jax.ShapeDtypeStruct((length, value_dim), output.dtype)
    columns = {}
    for steps in [(0, *range(2, heads - 1)), (1,)]:
        outs = pl.pallas_call(
            functools.partial(part_kernel, steps),
            out_shape=(column,) * len(steps),
            compiler_params=params,
        )(queries, inner_num, stats, *(carried[step] for step in steps))
        columns.update(zip(steps, outs))
    return pl.pallas_call(
        last_kernel,
        out_shape=output,
        out_specs=hbm,
        scratch_shapes=[
            pltpu.VMEM(column.shape, column.dtype),
            pltpu.SemaphoreType.DMA((heads,)),
        ],
        compiler_params=params,
    )(queries, inner_num, stats, carried[-1], *(columns[step] for step in range(heads - 1)))


def solution(mesh):
    return jax.shard_map(
        functools.partial(on_device, mesh.shape["grp"], mesh.shape["seq"]),
        mesh=mesh,
        in_specs=(
            P(AXES, None),
            P(AXES, None),
            P(AXES, None),
            P(None, AXES),
            P(None, AXES),
        ),
        out_specs=P(AXES, None),
        check_vma=False,
    )
```

```python
import functools

import jax
import jax.numpy as jnp
from jax import lax
from jax.experimental import pallas as pl
from jax.experimental.pallas import tpu as pltpu
from jax.sharding import PartitionSpec as P

floor_value = -1e30
LANES = 128
AXES = ("grp", "seq")


def split_two(x):
    high = x.astype(jnp.bfloat16)
    low = (x - high.astype(jnp.float32)).astype(jnp.bfloat16)
    return high, low


def split_three(x):
    high = x.astype(jnp.bfloat16)
    rest = x - high.astype(jnp.float32)
    mid = rest.astype(jnp.bfloat16)
    low = (rest - mid.astype(jnp.float32)).astype(jnp.bfloat16)
    return high, mid, low


def dot(a, b):
    return jnp.dot(a, b, preferred_element_type=jnp.float32)


def dot_last(a, b):
    return lax.dot_general(a, b, (((1,), (1,)), ((), ())), preferred_element_type=jnp.float32)


def log_forget(forget):
    return jnp.minimum(forget, 0.0) - jnp.log1p(jnp.exp(-jnp.abs(forget)))


def triangle(length, lower):
    rows = lax.broadcasted_iota(jnp.int32, (length, length), 0)
    cols = lax.broadcasted_iota(jnp.int32, (length, length), 1)
    return rows >= cols if lower else rows <= cols


def cumulative_rows(logf):
    ones = triangle(logf.shape[1], False).astype(jnp.bfloat16)
    high, mid, low = split_three(logf)
    return (dot(low, ones) + dot(mid, ones)) + dot(high, ones)


def cumulative_columns(logf):
    ones = triangle(logf.shape[1], True).astype(jnp.bfloat16)
    high, mid, low = split_three(logf)
    return (dot_last(ones, low) + dot_last(ones, mid)) + dot_last(ones, high)


TAIL = 8
VECTOR, TOP, DECAY = range(3)


def member(quad):
    return lax.rem(lax.axis_index(AXES[1]), quad)


def distances(quad):
    return [0, *range(quad - 1, 0, -1)]


def partners(quad):
    return [member(quad) ^ distance for distance in distances(quad)]


def tail_rows(vector, top, decay):
    rest = jnp.zeros((TAIL - 3, vector.shape[1]), jnp.float32)
    return jnp.concatenate([vector, top, decay, rest], axis=0)


def tail_row(ref, row):
    first = ref.shape[0] - TAIL + row
    return ref[first : first + 1, :]


def load(ref):
    return (ref[0 : ref.shape[0] - TAIL, :], *(tail_row(ref, row) for row in range(3)))


def store(ref, state):
    matrix, *tail = state
    ref[0 : matrix.shape[0], :] = matrix
    ref[matrix.shape[0] :, :] = tail_rows(*tail)


def join(earlier, later):
    early_matrix, early_vector, early_top, early_decay = earlier
    late_matrix, late_vector, late_top, late_decay = later
    moved = early_top + late_decay
    joined = jnp.maximum(moved, late_top)
    early_weight, late_weight = jnp.exp(moved - joined), jnp.exp(late_top - joined)
    return (
        early_weight * early_matrix + late_weight * late_matrix,
        early_weight * early_vector + late_weight * late_vector,
        joined,
        early_decay + late_decay,
    )


def choose(condition, one, other):
    return jax.tree.map(lambda a, b: jnp.where(condition, a, b), one, other)


def nothing(like):
    matrix, vector, top, decay = like
    zero = jnp.zeros_like(decay)
    return jnp.zeros_like(matrix), jnp.zeros_like(vector), zero + floor_value, zero


def state_kernel(k_hbm, v_hbm, in_hbm, fo_hbm, *refs):
    *out_refs, k_ref, v_ref, in_ref, fo_ref, scalar_ref, arrived = refs
    copies = [
        pltpu.make_async_copy(source, target, arrived.at[place])
        for place, (source, target) in enumerate(
            ((fo_hbm, fo_ref), (in_hbm, in_ref), (k_hbm, k_ref), (v_hbm, v_ref))
        )
    ]
    for copy in copies:
        copy.start()
    heads, length = in_ref.shape
    key_dim = k_ref.shape[1] // heads
    value_dim = v_ref.shape[1] // heads
    parts = value_dim // LANES
    copies[0].wait()
    cumul = cumulative_rows(log_forget(fo_ref[...]))
    copies[1].wait()
    level = in_ref[...] - cumul
    level_top = jnp.max(level, axis=1, keepdims=True)
    decay = cumul[:, length - 1 : length]
    scalar_ref[0] = jnp.exp(level - level_top)
    scalar_ref[1] = jnp.broadcast_to(decay + level_top, (heads, length))
    scalar_ref[2] = jnp.broadcast_to(decay, (heads, length))
    copies[2].wait()
    copies[3].wait()
    for head, out_ref in zip(partners(heads), out_refs):
        keys = k_ref[:, pl.ds(pl.multiple_of(head * key_dim, LANES), key_dim)]
        values = v_ref[:, pl.ds(pl.multiple_of(head * value_dim, LANES), value_dim)]
        row, top, decay = (scalar_ref[place, pl.ds(head, 1), :] for place in range(3))
        high, low = split_two(keys.astype(jnp.float32).T * row)
        matrix = dot(
            jnp.concatenate([high, low], axis=1), jnp.concatenate([values, values], axis=0)
        )
        for part in range(parts):
            out_ref[part * key_dim : (part + 1) * key_dim, :] = matrix[
                :, part * LANES : (part + 1) * LANES
            ]
        high, mid, low = split_three(row)
        vector = (dot(low, keys) + dot(mid, keys)) + dot(high, keys)
        out_ref[parts * key_dim :, :] = tail_rows(vector, top, decay)


def read_scalars(refs, scalar_ref, places):
    for place, ref in zip(places, refs):
        scalar_ref[0, pl.ds(place, 1), :] = tail_row(ref, TOP)
        scalar_ref[1, pl.ds(place, 1), :] = tail_row(ref, DECAY)
    count = len(refs)
    tops = [scalar_ref[0, place : place + 1, :] for place in range(count)]
    decays = [scalar_ref[1, place : place + 1, :] for place in range(count)]
    return tops, decays


def weights_of(tops, decays):
    moved, total = [], jnp.zeros_like(decays[0])
    for top, decay in zip(reversed(tops), reversed(decays)):
        moved.append(top + total)
        total = total + decay
    moved.reverse()
    joined = functools.reduce(jnp.maximum, moved)
    return [jnp.exp(top - joined) for top in moved], joined, total


def weighted_sum(weights, states):
    matrix, vector = 0.0, 0.0
    for weight, state in zip(weights, states):
        matrix = matrix + weight * state[0]
        vector = vector + weight * state[1]
    return matrix, vector


def quad_kernel(*refs):
    *refs, out_ref, scalar_ref = refs
    places = partners(len(refs))
    weights, top, decay = weights_of(*read_scalars(refs, scalar_ref, places))
    for place, weight in enumerate(weights):
        scalar_ref[0, place : place + 1, :] = weight
    weights = [scalar_ref[0, pl.ds(place, 1), :] for place in places]
    store(out_ref, (*weighted_sum(weights, [load(ref) for ref in refs]), top, decay))


def later_side(axis, bit):
    return (lax.axis_index(axis) & bit) != 0


def butterfly_kernel(axis, bit, *refs):
    total_ref, other_ref, *before_refs, out_total, out_before = refs
    is_later = later_side(axis, bit)
    total, other = load(total_ref), load(other_ref)
    before = load(before_refs[0]) if before_refs else nothing(total)
    store(out_total, join(choose(is_later, other, total), choose(is_later, total, other)))
    store(out_before, choose(is_later, join(other, before), before))


def gather_kernel(axis, bit, own_ref, other_ref, out_ref):
    is_later = later_side(axis, bit)
    count = out_ref.shape[0] // 2
    for place in range(count):
        own = own_ref[place] if own_ref.ndim == 3 else own_ref[...]
        other = other_ref[place] if other_ref.ndim == 3 else other_ref[...]
        out_ref[place] = jnp.where(is_later, other, own)
        out_ref[count + place] = jnp.where(is_later, own, other)


def prefix_kernel(quad, own_ref, other_ref, within_ref, *refs):
    *refs, scalar_ref, weight_ref = refs
    pieces, out_refs = refs[:quad], refs[quad:]
    places = partners(quad)
    me = lax.axis_index(AXES[0])
    even = (me & 1) == 0
    within = load(within_ref)
    sums = [(load(own_ref.at[pair]), load(other_ref.at[pair])) for pair in range(own_ref.shape[0])]
    tops, decays, earlier = [], [], []
    for own, other in sums:
        for one, two in ((own, other), (other, own)):
            before = len(tops) < me
            tops.append(jnp.where(before, jnp.where(even, one[2], two[2]), floor_value))
            decays.append(jnp.where(before, jnp.where(even, one[3], two[3]), 0.0))
            earlier.append(before)
    weights, top, _ = weights_of(tops + [within[2]], decays + [within[3]])
    weights[:-1] = [jnp.where(before, w, 0.0) for before, w in zip(earlier, weights)]
    terms = [(weights[-1], within)]
    for pair, (own, other) in enumerate(sums):
        one, two = weights[2 * pair], weights[2 * pair + 1]
        terms.append((jnp.where(even, one, two), own))
        terms.append((jnp.where(even, two, one), other))
    start = (*weighted_sum(*zip(*terms)), top)
    tops, decays = read_scalars(pieces, scalar_ref, places)
    zero = jnp.zeros_like(tops[0])
    for place in range(quad):
        weights, joined, _ = weights_of([start[2]] + tops[:place], [zero] + decays[:place])
        weights += [zero] * (quad - place)
        for index, weight in enumerate(weights):
            weight_ref[place, index : index + 1, :] = weight
        scalar_ref[0, place : place + 1, :] = joined
    states = [start] + [load(piece) for piece in pieces]
    for place, out_ref in zip(places, out_refs):
        weights = [weight_ref[place, 0:1, :]]
        weights += [weight_ref[place, pl.ds(1 + index, 1), :] for index in places]
        top = scalar_ref[0, pl.ds(place, 1), :]
        store(out_ref, (*weighted_sum(weights, states), top, zero))


CUMUL, ROW_LEVEL, INNER_DEN = range(3)


def inner_kernel(q_ref, k_ref, v_ref, in_ref, fo_ref, num_ref, stat_ref):
    heads, length = in_ref.shape
    key_dim = q_ref.shape[1] // heads
    value_dim = v_ref.shape[1] // heads
    logf = log_forget(fo_ref[...])
    level = in_ref[...] - cumulative_rows(logf)
    cumul = cumulative_columns(logf)
    causal = triangle(length, True)
    for head in range(heads):
        queries = q_ref[:, head * key_dim : (head + 1) * key_dim]
        keys = k_ref[:, head * key_dim : (head + 1) * key_dim]
        values = v_ref[:, head * value_dim : (head + 1) * value_dim]
        scores = dot_last(queries, keys) * (key_dim**-0.5)
        masked = jnp.where(causal, level[head : head + 1, :], -jnp.inf)
        row_level = jnp.max(masked, axis=1, keepdims=True)
        weighted = jnp.exp(masked - row_level) * scores
        stat_ref[head, :, CUMUL : CUMUL + 1] = cumul[:, head : head + 1]
        stat_ref[head, :, ROW_LEVEL : ROW_LEVEL + 1] = row_level
        stat_ref[head, :, INNER_DEN : INNER_DEN + 1] = jnp.sum(weighted, axis=1, keepdims=True)
        num_ref[head] = dot(weighted.astype(jnp.bfloat16), values)


def add_carried(head, q_ref, num_ref, stat_ref, message_ref):
    length, value_dim = num_ref.shape[1:]
    key_dim = q_ref.shape[1] // num_ref.shape[0]
    parts = value_dim // LANES
    scaling = key_dim**-0.5
    query = q_ref[:, pl.ds(pl.multiple_of(head * key_dim, LANES), key_dim)]
    matrix = jnp.concatenate(
        [message_ref[part * key_dim : (part + 1) * key_dim, :] for part in range(parts)], 1
    )
    high, low = split_two(matrix)
    carried = dot(jnp.concatenate([query, query], axis=1), jnp.concatenate([high, low], axis=0))
    stats = stat_ref[head]
    cumul, row_level, inner_den = (stats[:, place : place + 1] for place in range(3))
    top = tail_row(message_ref, TOP)[:, 0:1]
    carried_den = jnp.sum(
        query.astype(jnp.float32) * tail_row(message_ref, VECTOR), axis=1, keepdims=True
    )
    joined = jnp.maximum(row_level, top)
    inner_factor = jnp.exp(row_level - joined)
    outer_factor = jnp.exp(top - joined) * scaling
    denom = inner_factor * inner_den + outer_factor * carried_den
    inverse = 1.0 / jnp.maximum(jnp.abs(denom), jnp.exp(-(cumul + joined)))
    return (inner_factor * inverse) * num_ref[head] + (outer_factor * inverse) * carried


def part_kernel(steps, q_ref, num_ref, stat_ref, *refs):
    places = partners(num_ref.shape[0])
    count = len(steps)
    for step, message_ref, out_ref in zip(steps, refs[:count], refs[count:]):
        head = places[step]
        out_ref[...] = add_carried(head, q_ref, num_ref, stat_ref, message_ref).astype(
            out_ref.dtype
        )


def last_kernel(q_ref, num_ref, stat_ref, message_ref, *refs):
    *done_refs, out_hbm, own_ref, done = refs
    heads, _, value_dim = num_ref.shape
    places = partners(heads)

    def place(step, source):
        columns = pl.ds(pl.multiple_of(places[step] * value_dim, LANES), value_dim)
        copy = pltpu.make_async_copy(source, out_hbm.at[:, columns], done.at[step])
        copy.start()
        return copy

    copies = [place(step, ref) for step, ref in enumerate(done_refs)]
    own_ref[...] = add_carried(places[-1], q_ref, num_ref, stat_ref, message_ref).astype(
        own_ref.dtype
    )
    copies.append(place(heads - 1, own_ref))
    for copy in copies:
        copy.wait()


def swap(array, axis, step):
    count = lax.axis_size(axis)
    return lax.ppermute(array, axis, [(place, place ^ step) for place in range(count)])


def exchange(pieces):
    steps = zip(pieces[1:], distances(len(pieces))[1:])
    return [pieces[0]] + [swap(piece, AXES[1], distance) for piece, distance in steps]


def on_device(groups, group_length, queries, key_vectors, value_vectors, input_gate, forget_gate):
    heads, length = input_gate.shape
    key_dim = queries.shape[1] // heads
    value_dim = value_vectors.shape[1] // heads
    message = jax.ShapeDtypeStruct(
        (value_dim // LANES * key_dim + TAIL, LANES), jnp.float32
    )
    messages = (message,) * heads
    params = pltpu.CompilerParams(vmem_limit_bytes=48 * 1024 * 1024)
    hbm = pl.BlockSpec(memory_space=pltpu.HBM)
    scalars = pltpu.VMEM((3, heads, LANES), jnp.float32)
    output = jax.ShapeDtypeStruct((length, heads * value_dim), jnp.bfloat16)
    operands = (key_vectors, value_vectors, input_gate, forget_gate)
    own = pl.pallas_call(
        state_kernel,
        out_shape=messages,
        in_specs=[hbm] * len(operands),
        scratch_shapes=[pltpu.VMEM(array.shape, array.dtype) for array in operands]
        + [scalars, pltpu.SemaphoreType.DMA((len(operands),))],
        compiler_params=params,
    )(*(pltpu.with_memory_space_constraint(array, pltpu.HBM) for array in operands))
    pieces = exchange(own)
    inner_num, stats = pl.pallas_call(
        inner_kernel,
        out_shape=(
            jax.ShapeDtypeStruct((heads, length, value_dim), jnp.float32),
            jax.ShapeDtypeStruct((heads, length, 3), jnp.float32),
        ),
        compiler_params=params,
    )(queries, *operands)
    total = pl.pallas_call(
        quad_kernel, out_shape=message, scratch_shapes=[scalars], compiler_params=params
    )(*pieces)
    within = []
    bit = heads
    while bit < group_length:
        total, *within = pl.pallas_call(
            functools.partial(butterfly_kernel, AXES[1], bit),
            out_shape=(message, message),
            compiler_params=params,
        )(total, swap(total, AXES[1], bit), *within)
        bit *= 2
    sums = total
    bit, count = 2, 1
    while bit < groups:
        count *= 2
        sums = pl.pallas_call(
            functools.partial(gather_kernel, AXES[0], bit),
            out_shape=jax.ShapeDtypeStruct((count,) + message.shape, message.dtype),
            compiler_params=params,
        )(sums, swap(sums, AXES[0], bit))
        bit *= 2
    states = pl.pallas_call(
        functools.partial(prefix_kernel, heads),
        out_shape=messages,
        scratch_shapes=[scalars, pltpu.VMEM((heads, 1 + heads, LANES), jnp.float32)],
        compiler_params=params,
    )(sums, swap(sums, AXES[0], 1), *within, *pieces)
    carried = exchange(states)
    column = jax.ShapeDtypeStruct((length, value_dim), output.dtype)
    columns = {}
    for steps in [(0, *range(2, heads - 1)), (1,)]:
        outs = pl.pallas_call(
            functools.partial(part_kernel, steps),
            out_shape=(column,) * len(steps),
            compiler_params=params,
        )(queries, inner_num, stats, *(carried[step] for step in steps))
        columns.update(zip(steps, outs))
    return pl.pallas_call(
        last_kernel,
        out_shape=output,
        out_specs=hbm,
        scratch_shapes=[
            pltpu.VMEM(column.shape, column.dtype),
            pltpu.SemaphoreType.DMA((heads,)),
        ],
        compiler_params=params,
    )(queries, inner_num, stats, carried[-1], *(columns[step] for step in range(heads - 1)))


def solution(mesh):
    return jax.shard_map(
        functools.partial(on_device, mesh.shape["grp"], mesh.shape["seq"]),
        mesh=mesh,
        in_specs=(
            P(AXES, None),
            P(AXES, None),
            P(AXES, None),
            P(None, AXES),
            P(None, AXES),
        ),
        out_specs=P(AXES, None),
        check_vma=False,
    )
```

```python
import functools

import jax
import jax.numpy as jnp
from jax import lax
from jax.experimental import pallas as pl
from jax.experimental.pallas import tpu as pltpu
from jax.sharding import PartitionSpec as P

floor_value = -1e30
LANES = 128
AXES = ("grp", "seq")


def split_two(x):
    high = x.astype(jnp.bfloat16)
    low = (x - high.astype(jnp.float32)).astype(jnp.bfloat16)
    return high, low


def split_three(x):
    high = x.astype(jnp.bfloat16)
    rest = x - high.astype(jnp.float32)
    mid = rest.astype(jnp.bfloat16)
    low = (rest - mid.astype(jnp.float32)).astype(jnp.bfloat16)
    return high, mid, low


def dot(a, b):
    return jnp.dot(a, b, preferred_element_type=jnp.float32)


def dot_last(a, b):
    return lax.dot_general(a, b, (((1,), (1,)), ((), ())), preferred_element_type=jnp.float32)


def log_forget(forget):
    return jnp.minimum(forget, 0.0) - jnp.log1p(jnp.exp(-jnp.abs(forget)))


def triangle(length, lower):
    rows = lax.broadcasted_iota(jnp.int32, (length, length), 0)
    cols = lax.broadcasted_iota(jnp.int32, (length, length), 1)
    return rows >= cols if lower else rows <= cols


def dot_exact(x, b):
    count = x.shape[0]
    terms = [term.astype(jnp.float32) for term in split_three(x)]
    stacked = dot(jnp.concatenate(terms, axis=0).astype(jnp.bfloat16), b)
    high, mid, low = (stacked[term * count : (term + 1) * count, :] for term in range(3))
    return (low + mid) + high


def cumulative_rows(logf):
    return dot_exact(logf, triangle(logf.shape[1], False).astype(jnp.bfloat16))


def cumulative_columns(logf):
    ones = triangle(logf.shape[1], True).astype(jnp.bfloat16)
    high, mid, low = split_three(logf)
    return (dot_last(ones, low) + dot_last(ones, mid)) + dot_last(ones, high)


TAIL = 8
VECTOR, TOP, DECAY = range(3)


def member(quad):
    return lax.rem(lax.axis_index(AXES[1]), quad)


def partners(quad):
    return [member(quad) ^ step for step in range(quad)]


def tail_rows(vector, top, decay):
    rest = jnp.zeros((TAIL - 3, vector.shape[1]), jnp.float32)
    return jnp.concatenate([vector, top, decay, rest], axis=0)


def tail_row(ref, row):
    first = ref.shape[0] - TAIL + row
    return ref[first : first + 1, :]


def load(ref):
    return (ref[0 : ref.shape[0] - TAIL, :], *(tail_row(ref, row) for row in range(3)))


def store(ref, state):
    matrix, *tail = state
    ref[0 : matrix.shape[0], :] = matrix
    ref[matrix.shape[0] :, :] = tail_rows(*tail)


def join(earlier, later):
    early_matrix, early_vector, early_top, early_decay = earlier
    late_matrix, late_vector, late_top, late_decay = later
    moved = early_top + late_decay
    joined = jnp.maximum(moved, late_top)
    early_weight, late_weight = jnp.exp(moved - joined), jnp.exp(late_top - joined)
    return (
        early_weight * early_matrix + late_weight * late_matrix,
        early_weight * early_vector + late_weight * late_vector,
        joined,
        early_decay + late_decay,
    )


def choose(condition, one, other):
    return jax.tree.map(lambda a, b: jnp.where(condition, a, b), one, other)


def nothing(like):
    matrix, vector, top, decay = like
    zero = jnp.zeros_like(decay)
    return jnp.zeros_like(matrix), jnp.zeros_like(vector), zero + floor_value, zero


def state_kernel(k_hbm, v_hbm, in_hbm, fo_hbm, *refs):
    *out_refs, k_ref, v_ref, in_ref, fo_ref, scalar_ref, arrived = refs
    copies = [
        pltpu.make_async_copy(source, target, arrived.at[place])
        for place, (source, target) in enumerate(
            ((fo_hbm, fo_ref), (in_hbm, in_ref), (k_hbm, k_ref), (v_hbm, v_ref))
        )
    ]
    for copy in copies:
        copy.start()
    heads, length = in_ref.shape
    key_dim = k_ref.shape[1] // heads
    value_dim = v_ref.shape[1] // heads
    parts = value_dim // LANES
    copies[0].wait()
    cumul = cumulative_rows(log_forget(fo_ref[...]))
    copies[1].wait()
    level = in_ref[...] - cumul
    level_top = jnp.max(level, axis=1, keepdims=True)
    decay = cumul[:, length - 1 : length]
    scalar_ref[0] = jnp.exp(level - level_top)
    scalar_ref[1] = jnp.broadcast_to(decay + level_top, (heads, length))
    scalar_ref[2] = jnp.broadcast_to(decay, (heads, length))
    copies[2].wait()
    copies[3].wait()
    for head, out_ref in zip(partners(heads), out_refs):
        keys = k_ref[:, pl.ds(pl.multiple_of(head * key_dim, LANES), key_dim)]
        values = v_ref[:, pl.ds(pl.multiple_of(head * value_dim, LANES), value_dim)]
        row, top, decay = (scalar_ref[place, pl.ds(head, 1), :] for place in range(3))
        high, low = split_two(keys.astype(jnp.float32).T * row)
        matrix = dot(
            jnp.concatenate([high, low], axis=1), jnp.concatenate([values, values], axis=0)
        )
        for part in range(parts):
            out_ref[part * key_dim : (part + 1) * key_dim, :] = matrix[
                :, part * LANES : (part + 1) * LANES
            ]
        vector = dot_exact(row, keys)
        out_ref[parts * key_dim :, :] = tail_rows(vector, top, decay)


def read_scalars(refs, scalar_ref, places):
    for place, ref in zip(places, refs):
        scalar_ref[0, pl.ds(place, 1), :] = tail_row(ref, TOP)
        scalar_ref[1, pl.ds(place, 1), :] = tail_row(ref, DECAY)
    count = len(refs)
    tops = [scalar_ref[0, place : place + 1, :] for place in range(count)]
    decays = [scalar_ref[1, place : place + 1, :] for place in range(count)]
    return tops, decays


def weights_of(tops, decays):
    moved, total = [], jnp.zeros_like(decays[0])
    for top, decay in zip(reversed(tops), reversed(decays)):
        moved.append(top + total)
        total = total + decay
    moved.reverse()
    joined = functools.reduce(jnp.maximum, moved)
    return [jnp.exp(top - joined) for top in moved], joined, total


def weighted_sum(weights, states):
    matrix, vector = 0.0, 0.0
    for weight, state in zip(weights, states):
        matrix = matrix + weight * state[0]
        vector = vector + weight * state[1]
    return matrix, vector


def quad_kernel(*refs):
    *refs, out_ref, scalar_ref = refs
    places = partners(len(refs))
    weights, top, decay = weights_of(*read_scalars(refs, scalar_ref, places))
    for place, weight in enumerate(weights):
        scalar_ref[0, place : place + 1, :] = weight
    weights = [scalar_ref[0, pl.ds(place, 1), :] for place in places]
    store(out_ref, (*weighted_sum(weights, [load(ref) for ref in refs]), top, decay))


def later_side(axis, bit):
    return (lax.axis_index(axis) & bit) != 0


def butterfly_kernel(axis, bit, *refs):
    total_ref, other_ref, *before_refs, out_total, out_before = refs
    is_later = later_side(axis, bit)
    total, other = load(total_ref), load(other_ref)
    before = load(before_refs[0]) if before_refs else nothing(total)
    store(out_total, join(choose(is_later, other, total), choose(is_later, total, other)))
    store(out_before, choose(is_later, join(other, before), before))


def gather_kernel(axis, bit, own_ref, other_ref, out_ref):
    is_later = later_side(axis, bit)
    count = out_ref.shape[0] // 2
    for place in range(count):
        own = own_ref[place] if own_ref.ndim == 3 else own_ref[...]
        other = other_ref[place] if other_ref.ndim == 3 else other_ref[...]
        out_ref[place] = jnp.where(is_later, other, own)
        out_ref[count + place] = jnp.where(is_later, own, other)


def prefix_kernel(quad, own_ref, other_ref, within_ref, *refs):
    *refs, scalar_ref, weight_ref = refs
    pieces, out_refs = refs[:quad], refs[quad:]
    places = partners(quad)
    me = lax.axis_index(AXES[0])
    even = (me & 1) == 0
    within = load(within_ref)
    sums = [(load(own_ref.at[pair]), load(other_ref.at[pair])) for pair in range(own_ref.shape[0])]
    tops, decays, earlier = [], [], []
    for own, other in sums:
        for one, two in ((own, other), (other, own)):
            before = len(tops) < me
            tops.append(jnp.where(before, jnp.where(even, one[2], two[2]), floor_value))
            decays.append(jnp.where(before, jnp.where(even, one[3], two[3]), 0.0))
            earlier.append(before)
    weights, top, _ = weights_of(tops + [within[2]], decays + [within[3]])
    weights[:-1] = [jnp.where(before, w, 0.0) for before, w in zip(earlier, weights)]
    terms = [(weights[-1], within)]
    for pair, (own, other) in enumerate(sums):
        one, two = weights[2 * pair], weights[2 * pair + 1]
        terms.append((jnp.where(even, one, two), own))
        terms.append((jnp.where(even, two, one), other))
    start = (*weighted_sum(*zip(*terms)), top)
    tops, decays = read_scalars(pieces, scalar_ref, places)
    zero = jnp.zeros_like(tops[0])
    for place in range(quad):
        weights, joined, _ = weights_of([start[2]] + tops[:place], [zero] + decays[:place])
        weights += [zero] * (quad - place)
        for index, weight in enumerate(weights):
            weight_ref[place, index : index + 1, :] = weight
        scalar_ref[0, place : place + 1, :] = joined
    states = [start] + [load(piece) for piece in pieces]
    for place, out_ref in zip(places, out_refs):
        weights = [weight_ref[place, 0:1, :]]
        weights += [weight_ref[place, pl.ds(1 + index, 1), :] for index in places]
        top = scalar_ref[0, pl.ds(place, 1), :]
        store(out_ref, (*weighted_sum(weights, states), top, zero))


CUMUL, ROW_LEVEL, INNER_DEN = range(3)


def inner_kernel(q_ref, k_ref, v_ref, in_ref, fo_ref, num_ref, stat_ref):
    heads, length = in_ref.shape
    key_dim = q_ref.shape[1] // heads
    value_dim = v_ref.shape[1] // heads
    logf = log_forget(fo_ref[...])
    level = in_ref[...] - cumulative_rows(logf)
    cumul = cumulative_columns(logf)
    causal = triangle(length, True)
    for head in range(heads):
        queries = q_ref[:, head * key_dim : (head + 1) * key_dim]
        keys = k_ref[:, head * key_dim : (head + 1) * key_dim]
        values = v_ref[:, head * value_dim : (head + 1) * value_dim]
        scores = dot_last(queries, keys) * (key_dim**-0.5)
        masked = jnp.where(causal, level[head : head + 1, :], -jnp.inf)
        row_level = jnp.max(masked, axis=1, keepdims=True)
        weighted = jnp.exp(masked - row_level) * scores
        stat_ref[head, :, CUMUL : CUMUL + 1] = cumul[:, head : head + 1]
        stat_ref[head, :, ROW_LEVEL : ROW_LEVEL + 1] = row_level
        stat_ref[head, :, INNER_DEN : INNER_DEN + 1] = jnp.sum(weighted, axis=1, keepdims=True)
        num_ref[head] = dot(weighted.astype(jnp.bfloat16), values)


def add_carried(head, q_ref, num_ref, stat_ref, message_ref):
    length, value_dim = num_ref.shape[1:]
    key_dim = q_ref.shape[1] // num_ref.shape[0]
    parts = value_dim // LANES
    scaling = key_dim**-0.5
    query = q_ref[:, pl.ds(pl.multiple_of(head * key_dim, LANES), key_dim)]
    matrix = jnp.concatenate(
        [message_ref[part * key_dim : (part + 1) * key_dim, :] for part in range(parts)], 1
    )
    high, low = split_two(matrix)
    carried = dot(jnp.concatenate([query, query], axis=1), jnp.concatenate([high, low], axis=0))
    stats = stat_ref[head]
    cumul, row_level, inner_den = (stats[:, place : place + 1] for place in range(3))
    top = tail_row(message_ref, TOP)[:, 0:1]
    carried_den = jnp.sum(
        query.astype(jnp.float32) * tail_row(message_ref, VECTOR), axis=1, keepdims=True
    )
    joined = jnp.maximum(row_level, top)
    inner_factor = jnp.exp(row_level - joined)
    outer_factor = jnp.exp(top - joined) * scaling
    denom = inner_factor * inner_den + outer_factor * carried_den
    inverse = 1.0 / jnp.maximum(jnp.abs(denom), jnp.exp(-(cumul + joined)))
    return (inner_factor * inverse) * num_ref[head] + (outer_factor * inverse) * carried


def part_kernel(steps, q_ref, num_ref, stat_ref, *refs):
    places = partners(num_ref.shape[0])
    count = len(steps)
    for step, message_ref, out_ref in zip(steps, refs[:count], refs[count:]):
        head = places[step]
        out_ref[...] = add_carried(head, q_ref, num_ref, stat_ref, message_ref).astype(
            out_ref.dtype
        )


def last_kernel(q_ref, num_ref, stat_ref, message_ref, *refs):
    *done_refs, out_hbm, own_ref, done = refs
    heads, _, value_dim = num_ref.shape
    places = partners(heads)

    def place(step, source):
        columns = pl.ds(pl.multiple_of(places[step] * value_dim, LANES), value_dim)
        copy = pltpu.make_async_copy(source, out_hbm.at[:, columns], done.at[step])
        copy.start()
        return copy

    copies = [place(step, ref) for step, ref in enumerate(done_refs)]
    own_ref[...] = add_carried(places[-1], q_ref, num_ref, stat_ref, message_ref).astype(
        own_ref.dtype
    )
    copies.append(place(heads - 1, own_ref))
    for copy in copies:
        copy.wait()


def swap(array, axis, step):
    count = lax.axis_size(axis)
    return lax.ppermute(array, axis, [(place, place ^ step) for place in range(count)])


def exchange(pieces):
    return [pieces[0]] + [swap(pieces[step], AXES[1], step) for step in range(1, len(pieces))]


def on_device(groups, group_length, queries, key_vectors, value_vectors, input_gate, forget_gate):
    heads, length = input_gate.shape
    key_dim = queries.shape[1] // heads
    value_dim = value_vectors.shape[1] // heads
    message = jax.ShapeDtypeStruct(
        (value_dim // LANES * key_dim + TAIL, LANES), jnp.float32
    )
    messages = (message,) * heads
    params = pltpu.CompilerParams(vmem_limit_bytes=48 * 1024 * 1024)
    hbm = pl.BlockSpec(memory_space=pltpu.HBM)
    scalars = pltpu.VMEM((3, heads, LANES), jnp.float32)
    output = jax.ShapeDtypeStruct((length, heads * value_dim), jnp.bfloat16)
    operands = (key_vectors, value_vectors, input_gate, forget_gate)
    own = pl.pallas_call(
        state_kernel,
        out_shape=messages,
        in_specs=[hbm] * len(operands),
        scratch_shapes=[pltpu.VMEM(array.shape, array.dtype) for array in operands]
        + [scalars, pltpu.SemaphoreType.DMA((len(operands),))],
        compiler_params=params,
    )(*(pltpu.with_memory_space_constraint(array, pltpu.HBM) for array in operands))
    pieces = exchange(own)
    inner_num, stats = pl.pallas_call(
        inner_kernel,
        out_shape=(
            jax.ShapeDtypeStruct((heads, length, value_dim), jnp.float32),
            jax.ShapeDtypeStruct((heads, length, 3), jnp.float32),
        ),
        compiler_params=params,
    )(queries, *operands)
    total = pl.pallas_call(
        quad_kernel, out_shape=message, scratch_shapes=[scalars], compiler_params=params
    )(*pieces)
    within = []
    bit = heads
    while bit < group_length:
        total, *within = pl.pallas_call(
            functools.partial(butterfly_kernel, AXES[1], bit),
            out_shape=(message, message),
            compiler_params=params,
        )(total, swap(total, AXES[1], bit), *within)
        bit *= 2
    sums = total
    bit, count = 2, 1
    while bit < groups:
        count *= 2
        sums = pl.pallas_call(
            functools.partial(gather_kernel, AXES[0], bit),
            out_shape=jax.ShapeDtypeStruct((count,) + message.shape, message.dtype),
            compiler_params=params,
        )(sums, swap(sums, AXES[0], bit))
        bit *= 2
    states = pl.pallas_call(
        functools.partial(prefix_kernel, heads),
        out_shape=messages,
        scratch_shapes=[scalars, pltpu.VMEM((heads, 1 + heads, LANES), jnp.float32)],
        compiler_params=params,
    )(sums, swap(sums, AXES[0], 1), *within, *pieces)
    carried = exchange(states)
    column = jax.ShapeDtypeStruct((length, value_dim), output.dtype)
    columns = []
    for steps in [(0, 1)] + [(step,) for step in range(2, heads - 1)]:
        columns += pl.pallas_call(
            functools.partial(part_kernel, steps),
            out_shape=(column,) * len(steps),
            compiler_params=params,
        )(queries, inner_num, stats, *(carried[step] for step in steps))
    return pl.pallas_call(
        last_kernel,
        out_shape=output,
        out_specs=hbm,
        scratch_shapes=[
            pltpu.VMEM(column.shape, column.dtype),
            pltpu.SemaphoreType.DMA((heads,)),
        ],
        compiler_params=params,
    )(queries, inner_num, stats, carried[-1], *columns)


def solution(mesh):
    return jax.shard_map(
        functools.partial(on_device, mesh.shape["grp"], mesh.shape["seq"]),
        mesh=mesh,
        in_specs=(
            P(AXES, None),
            P(AXES, None),
            P(AXES, None),
            P(None, AXES),
            P(None, AXES),
        ),
        out_specs=P(AXES, None),
        check_vma=False,
    )
```

```python
import functools

import jax
import jax.numpy as jnp
from jax import lax
from jax.experimental import pallas as pl
from jax.experimental.pallas import tpu as pltpu
from jax.sharding import PartitionSpec as P

floor_value = -1e30
LANES = 128
AXES = ("grp", "seq")


def split_two(x):
    high = x.astype(jnp.bfloat16)
    low = (x - high.astype(jnp.float32)).astype(jnp.bfloat16)
    return high, low


def split_three(x):
    high = x.astype(jnp.bfloat16)
    rest = x - high.astype(jnp.float32)
    mid = rest.astype(jnp.bfloat16)
    low = (rest - mid.astype(jnp.float32)).astype(jnp.bfloat16)
    return high, mid, low


def dot(a, b):
    return jnp.dot(a, b, preferred_element_type=jnp.float32)


def dot_last(a, b):
    return lax.dot_general(a, b, (((1,), (1,)), ((), ())), preferred_element_type=jnp.float32)


def log_forget(forget):
    return jnp.minimum(forget, 0.0) - jnp.log1p(jnp.exp(-jnp.abs(forget)))


def triangle(length, lower):
    rows = lax.broadcasted_iota(jnp.int32, (length, length), 0)
    cols = lax.broadcasted_iota(jnp.int32, (length, length), 1)
    return rows >= cols if lower else rows <= cols


def cumulative_rows(logf):
    ones = triangle(logf.shape[1], False).astype(jnp.bfloat16)
    high, mid, low = split_three(logf)
    return (dot(low, ones) + dot(mid, ones)) + dot(high, ones)


def cumulative_columns(logf):
    ones = triangle(logf.shape[1], True).astype(jnp.bfloat16)
    high, mid, low = split_three(logf)
    return (dot_last(ones, low) + dot_last(ones, mid)) + dot_last(ones, high)


TAIL = 8
VECTOR, TOP, DECAY = range(3)


def member(quad):
    return lax.rem(lax.axis_index(AXES[1]), quad)


def tail_rows(vector, top, decay):
    rest = jnp.zeros((TAIL - 3, vector.shape[1]), jnp.float32)
    return jnp.concatenate([vector, top, decay, rest], axis=0)


def put_state(ref, state, top, decay):
    matrix_rows = ref.shape[0] - TAIL
    ref[0:matrix_rows, :] = state[0:matrix_rows, :]
    place = lax.broadcasted_iota(jnp.int32, (TAIL, ref.shape[1]), 0)
    tail = jnp.where(place == TOP, top, state[matrix_rows:, :])
    ref[matrix_rows:, :] = jnp.where(place == DECAY, decay, tail)


def tail_row(ref, row):
    first = ref.shape[0] - TAIL + row
    return ref[first : first + 1, :]


def state_kernel(k_hbm, v_hbm, in_hbm, fo_hbm, *refs):
    *out_refs, k_ref, v_ref, in_ref, fo_ref, scalar_ref, arrived = refs
    copies = [
        pltpu.make_async_copy(source, target, arrived.at[place])
        for place, (source, target) in enumerate(
            ((fo_hbm, fo_ref), (in_hbm, in_ref), (k_hbm, k_ref), (v_hbm, v_ref))
        )
    ]
    for copy in copies:
        copy.start()
    heads, length = in_ref.shape
    key_dim = k_ref.shape[1] // heads
    value_dim = v_ref.shape[1] // heads
    parts = value_dim // LANES
    copies[0].wait()
    cumul = cumulative_rows(log_forget(fo_ref[...]))
    copies[1].wait()
    level = in_ref[...] - cumul
    level_top = jnp.max(level, axis=1, keepdims=True)
    decay = cumul[:, length - 1 : length]
    scalar_ref[0] = jnp.exp(level - level_top)
    scalar_ref[1] = jnp.broadcast_to(decay + level_top, (heads, length))
    scalar_ref[2] = jnp.broadcast_to(decay, (heads, length))
    copies[2].wait()
    copies[3].wait()
    me = member(heads)
    for step in range(heads):
        head = me ^ step
        keys = k_ref[:, pl.ds(pl.multiple_of(head * key_dim, LANES), key_dim)]
        values = v_ref[:, pl.ds(pl.multiple_of(head * value_dim, LANES), value_dim)]
        row, top, decay = (scalar_ref[place, pl.ds(head, 1), :] for place in range(3))
        high, low = split_two(keys.astype(jnp.float32).T * row)
        matrix = dot(
            jnp.concatenate([high, low], axis=1), jnp.concatenate([values, values], axis=0)
        )
        high, mid, low = split_three(row)
        vector = (dot(low, keys) + dot(mid, keys)) + dot(high, keys)
        for part in range(parts):
            out_ref = out_refs[part * heads + step]
            out_ref[0:key_dim, :] = matrix[:, part * LANES : (part + 1) * LANES]
            out_ref[key_dim:, :] = tail_rows(vector, top, decay)


def read_scalars(refs, scalar_ref, me):
    for step, ref in enumerate(refs):
        scalar_ref[0, pl.ds(me ^ step, 1), :] = tail_row(ref, TOP)
        scalar_ref[1, pl.ds(me ^ step, 1), :] = tail_row(ref, DECAY)
    count = len(refs)
    tops = [scalar_ref[0, place : place + 1, :] for place in range(count)]
    decays = [scalar_ref[1, place : place + 1, :] for place in range(count)]
    return tops, decays


def weights_of(tops, decays):
    moved, total = [], jnp.zeros_like(decays[0])
    for top, decay in zip(reversed(tops), reversed(decays)):
        moved.append(top + total)
        total = total + decay
    moved.reverse()
    joined = functools.reduce(jnp.maximum, moved)
    return [jnp.exp(top - joined) for top in moved], joined, total


def quad_kernel(*refs):
    *refs, out_ref, scalar_ref = refs
    me = member(len(refs))
    weights, top, decay = weights_of(*read_scalars(refs, scalar_ref, me))
    for place, weight in enumerate(weights):
        scalar_ref[0, place : place + 1, :] = weight
    total = 0.0
    for step, ref in enumerate(refs):
        total = total + scalar_ref[0, pl.ds(me ^ step, 1), :] * ref[...]
    put_state(out_ref, total, top, decay)


def later_side(axis, bit):
    return (lax.axis_index(axis) & bit) != 0


def extend(is_later, other_ref, before_ref):
    other_top = tail_row(other_ref, TOP)
    if before_ref is None:
        decay = jnp.where(is_later, tail_row(other_ref, DECAY), 0.0)
        return (
            jnp.where(is_later, other_ref[...], 0.0),
            jnp.where(is_later, other_top, floor_value),
            decay,
        )
    before_top = tail_row(before_ref, TOP)
    before_decay = tail_row(before_ref, DECAY)
    moved = other_top + before_decay
    top = jnp.where(is_later, jnp.maximum(moved, before_top), before_top)
    other_weight = jnp.where(is_later, jnp.exp(moved - top), 0.0)
    state = other_weight * other_ref[...] + jnp.exp(before_top - top) * before_ref[...]
    decay = jnp.where(is_later, tail_row(other_ref, DECAY), 0.0) + before_decay
    return state, top, decay


def butterfly_kernel(axis, bit, *refs):
    total_ref, other_ref, *before, out_total, out_before = refs
    is_later = later_side(axis, bit)
    own_top, own_decay = tail_row(total_ref, TOP), tail_row(total_ref, DECAY)
    other_top, other_decay = tail_row(other_ref, TOP), tail_row(other_ref, DECAY)
    own_moved = own_top + jnp.where(is_later, 0.0, other_decay)
    other_moved = other_top + jnp.where(is_later, own_decay, 0.0)
    top = jnp.maximum(own_moved, other_moved)
    total = (
        jnp.exp(own_moved - top) * total_ref[...] + jnp.exp(other_moved - top) * other_ref[...]
    )
    put_state(out_total, total, top, own_decay + other_decay)
    put_state(out_before, *extend(is_later, other_ref, before[0] if before else None))


def prefix_kernel(axis, bit, quad, parts, *refs):
    others, befores, refs = refs[:parts], refs[parts : 2 * parts], refs[2 * parts :]
    *refs, scalar_ref, weight_ref = refs
    pieces = [refs[part * quad : (part + 1) * quad] for part in range(parts)]
    out_refs = refs[parts * quad :]
    me = member(quad)
    is_later = later_side(axis, bit)
    starts = [extend(is_later, other, before) for other, before in zip(others, befores)]
    top = starts[0][1]
    tops, decays = read_scalars(pieces[0], scalar_ref, me)
    zero = jnp.zeros_like(top)
    rows = others[0].shape[0]
    for place in range(quad):
        weights, joined, _ = weights_of([top] + tops[:place], [zero] + decays[:place])
        weights += [zero] * (quad - place)
        for index, weight in enumerate(weights):
            weight_ref[place, index : index + 1, :] = weight
        scalar_ref[0, place : place + 1, :] = joined
    for step, out_ref in enumerate(out_refs):
        place = me ^ step
        weights = [weight_ref[place, pl.ds(1 + (me ^ index), 1), :] for index in range(quad)]
        for part, (start, _, _) in enumerate(starts):
            state = weight_ref[place, 0:1, :] * start
            for weight, piece in zip(weights, pieces[part]):
                state = state + weight * piece[...]
            first = part * (rows - TAIL)
            out_ref[first : first + rows - TAIL, :] = state[0 : rows - TAIL, :]
        vector = state[rows - TAIL : rows - TAIL + 1, :]
        tail = tail_rows(vector, scalar_ref[0, pl.ds(place, 1), :], zero)
        out_ref[out_ref.shape[0] - TAIL :, :] = tail


CUMUL, ROW_LEVEL, INNER_DEN = range(3)


def inner_kernel(q_ref, k_ref, v_ref, in_ref, fo_ref, num_ref, stat_ref):
    heads, length = in_ref.shape
    key_dim = q_ref.shape[1] // heads
    value_dim = v_ref.shape[1] // heads
    logf = log_forget(fo_ref[...])
    level = in_ref[...] - cumulative_rows(logf)
    cumul = cumulative_columns(logf)
    causal = triangle(length, True)
    for head in range(heads):
        queries = q_ref[:, head * key_dim : (head + 1) * key_dim]
        keys = k_ref[:, head * key_dim : (head + 1) * key_dim]
        values = v_ref[:, head * value_dim : (head + 1) * value_dim]
        scores = dot_last(queries, keys) * (key_dim**-0.5)
        masked = jnp.where(causal, level[head : head + 1, :], -jnp.inf)
        row_level = jnp.max(masked, axis=1, keepdims=True)
        weighted = jnp.exp(masked - row_level) * scores
        stat_ref[head, :, CUMUL : CUMUL + 1] = cumul[:, head : head + 1]
        stat_ref[head, :, ROW_LEVEL : ROW_LEVEL + 1] = row_level
        stat_ref[head, :, INNER_DEN : INNER_DEN + 1] = jnp.sum(weighted, axis=1, keepdims=True)
        num_ref[head] = dot(weighted.astype(jnp.bfloat16), values)


def add_carried(head, q_ref, num_ref, stat_ref, message_ref):
    length, value_dim = num_ref.shape[1:]
    key_dim = q_ref.shape[1] // num_ref.shape[0]
    parts = value_dim // LANES
    scaling = key_dim**-0.5
    query = q_ref[:, pl.ds(pl.multiple_of(head * key_dim, LANES), key_dim)]
    matrix = jnp.concatenate(
        [message_ref[part * key_dim : (part + 1) * key_dim, :] for part in range(parts)], 1
    )
    high, low = split_two(matrix)
    carried = dot(jnp.concatenate([query, query], axis=1), jnp.concatenate([high, low], axis=0))
    stats = stat_ref[head]
    cumul, row_level, inner_den = (stats[:, place : place + 1] for place in range(3))
    top = tail_row(message_ref, TOP)[:, 0:1]
    carried_den = jnp.sum(
        query.astype(jnp.float32) * tail_row(message_ref, VECTOR), axis=1, keepdims=True
    )
    joined = jnp.maximum(row_level, top)
    inner_factor = jnp.exp(row_level - joined)
    outer_factor = jnp.exp(top - joined) * scaling
    denom = inner_factor * inner_den + outer_factor * carried_den
    inverse = 1.0 / jnp.maximum(jnp.abs(denom), jnp.exp(-(cumul + joined)))
    return (inner_factor * inverse) * num_ref[head] + (outer_factor * inverse) * carried


def part_kernel(steps, q_ref, num_ref, stat_ref, *refs):
    me = member(num_ref.shape[0])
    count = len(steps)
    for step, message_ref, out_ref in zip(steps, refs[:count], refs[count:]):
        head = me ^ step
        out_ref[...] = add_carried(head, q_ref, num_ref, stat_ref, message_ref).astype(
            out_ref.dtype
        )


def last_kernel(q_ref, num_ref, stat_ref, message_ref, *refs):
    *done_refs, out_hbm, own_ref, done = refs
    heads, _, value_dim = num_ref.shape
    me = member(heads)

    def place(step, source):
        columns = pl.ds(pl.multiple_of((me ^ step) * value_dim, LANES), value_dim)
        copy = pltpu.make_async_copy(source, out_hbm.at[:, columns], done.at[step])
        copy.start()
        return copy

    copies = [place(step, ref) for step, ref in enumerate(done_refs)]
    own_ref[...] = add_carried(me ^ (heads - 1), q_ref, num_ref, stat_ref, message_ref).astype(
        own_ref.dtype
    )
    copies.append(place(heads - 1, own_ref))
    for copy in copies:
        copy.wait()


def swap(array, axis, step):
    count = lax.axis_size(axis)
    return lax.ppermute(array, axis, [(place, place ^ step) for place in range(count)])


def exchange(pieces):
    return [pieces[0]] + [
        swap(pieces[step], AXES[1], step) for step in range(1, len(pieces))
    ]


def on_device(groups, group_length, queries, key_vectors, value_vectors, input_gate, forget_gate):
    heads, length = input_gate.shape
    key_dim = queries.shape[1] // heads
    value_dim = value_vectors.shape[1] // heads
    parts = value_dim // LANES
    whole = jax.ShapeDtypeStruct((parts * key_dim + TAIL, LANES), jnp.float32)
    message = jax.ShapeDtypeStruct((key_dim + TAIL, LANES), jnp.float32)
    messages = (message,) * heads
    params = pltpu.CompilerParams(vmem_limit_bytes=48 * 1024 * 1024)
    hbm = pl.BlockSpec(memory_space=pltpu.HBM)
    scalars = pltpu.VMEM((3, heads, LANES), jnp.float32)
    output = jax.ShapeDtypeStruct((length, heads * value_dim), jnp.bfloat16)
    operands = (key_vectors, value_vectors, input_gate, forget_gate)
    levels = []
    for axis, bit, size in ((AXES[1], heads, group_length), (AXES[0], 1, groups)):
        while bit < size:
            levels.append((axis, bit))
            bit *= 2

    own = pl.pallas_call(
        state_kernel,
        out_shape=messages * parts,
        in_specs=[hbm] * len(operands),
        scratch_shapes=[pltpu.VMEM(array.shape, array.dtype) for array in operands]
        + [scalars, pltpu.SemaphoreType.DMA((len(operands),))],
        compiler_params=params,
    )(*(pltpu.with_memory_space_constraint(array, pltpu.HBM) for array in operands))
    inner_num, stats = pl.pallas_call(
        inner_kernel,
        out_shape=(
            jax.ShapeDtypeStruct((heads, length, value_dim), jnp.float32),
            jax.ShapeDtypeStruct((heads, length, 3), jnp.float32),
        ),
        compiler_params=params,
    )(queries, *operands)
    join_quad = pl.pallas_call(
        quad_kernel, out_shape=message, scratch_shapes=[scalars], compiler_params=params
    )
    pieces = [exchange(own[part * heads : (part + 1) * heads]) for part in range(parts)]
    totals = [join_quad(*array) for array in pieces]
    before = [[] for _ in range(parts)]
    for axis, bit in levels[:-1]:
        join_level = pl.pallas_call(
            functools.partial(butterfly_kernel, axis, bit),
            out_shape=(message, message),
            compiler_params=params,
        )
        others = [swap(array, axis, bit) for array in totals]
        for part in range(parts):
            totals[part], *before[part] = join_level(totals[part], others[part], *before[part])
    others = [swap(array, *levels[-1]) for array in totals]
    starts = []
    for part in range(parts):
        starts += before[part]
    states = pl.pallas_call(
        functools.partial(prefix_kernel, *levels[-1], heads, parts),
        out_shape=(whole,) * heads,
        scratch_shapes=[scalars, pltpu.VMEM((heads, 1 + heads, LANES), jnp.float32)],
        compiler_params=params,
    )(*others, *starts, *(piece for chunk in pieces for piece in chunk))
    carried = exchange(states)
    column = jax.ShapeDtypeStruct((length, value_dim), output.dtype)
    columns = []
    for steps in [(0, 1)] + [(step,) for step in range(2, heads - 1)]:
        columns += pl.pallas_call(
            functools.partial(part_kernel, steps),
            out_shape=(column,) * len(steps),
            compiler_params=params,
        )(queries, inner_num, stats, *(carried[step] for step in steps))
    return pl.pallas_call(
        last_kernel,
        out_shape=output,
        out_specs=hbm,
        scratch_shapes=[
            pltpu.VMEM(column.shape, column.dtype),
            pltpu.SemaphoreType.DMA((heads,)),
        ],
        compiler_params=params,
    )(queries, inner_num, stats, carried[-1], *columns)


def solution(mesh):
    return jax.shard_map(
        functools.partial(on_device, mesh.shape["grp"], mesh.shape["seq"]),
        mesh=mesh,
        in_specs=(
            P(AXES, None),
            P(AXES, None),
            P(AXES, None),
            P(None, AXES),
            P(None, AXES),
        ),
        out_specs=P(AXES, None),
        check_vma=False,
    )
```

```python
import functools

import jax
import jax.numpy as jnp
from jax import lax
from jax.experimental import pallas as pl
from jax.experimental.pallas import tpu as pltpu
from jax.sharding import PartitionSpec as P

floor_value = -1e30
LANES = 128
AXES = ("grp", "seq")


def split_two(x):
    high = x.astype(jnp.bfloat16)
    low = (x - high.astype(jnp.float32)).astype(jnp.bfloat16)
    return high, low


def split_three(x):
    high = x.astype(jnp.bfloat16)
    rest = x - high.astype(jnp.float32)
    mid = rest.astype(jnp.bfloat16)
    low = (rest - mid.astype(jnp.float32)).astype(jnp.bfloat16)
    return high, mid, low


def dot(a, b):
    return jnp.dot(a, b, preferred_element_type=jnp.float32)


def dot_last(a, b):
    return lax.dot_general(a, b, (((1,), (1,)), ((), ())), preferred_element_type=jnp.float32)


def log_forget(forget):
    return jnp.minimum(forget, 0.0) - jnp.log1p(jnp.exp(-jnp.abs(forget)))


def triangle(length, lower):
    rows = lax.broadcasted_iota(jnp.int32, (length, length), 0)
    cols = lax.broadcasted_iota(jnp.int32, (length, length), 1)
    return rows >= cols if lower else rows <= cols


def cumulative_rows(logf):
    ones = triangle(logf.shape[1], False).astype(jnp.bfloat16)
    high, mid, low = split_three(logf)
    return (dot(low, ones) + dot(mid, ones)) + dot(high, ones)


def cumulative_columns(logf):
    ones = triangle(logf.shape[1], True).astype(jnp.bfloat16)
    high, mid, low = split_three(logf)
    return (dot_last(ones, low) + dot_last(ones, mid)) + dot_last(ones, high)


TAIL = 8
VECTOR, TOP, DECAY = range(3)


def member(quad):
    return lax.rem(lax.axis_index(AXES[1]), quad)


def tail_rows(vector, top, decay):
    rest = jnp.zeros((TAIL - 3, vector.shape[1]), jnp.float32)
    return jnp.concatenate([vector, top, decay, rest], axis=0)


def put_state(ref, state, top, decay):
    matrix_rows = ref.shape[0] - TAIL
    ref[0:matrix_rows, :] = state[0:matrix_rows, :]
    place = lax.broadcasted_iota(jnp.int32, (TAIL, ref.shape[1]), 0)
    tail = jnp.where(place == TOP, top, state[matrix_rows:, :])
    ref[matrix_rows:, :] = jnp.where(place == DECAY, decay, tail)


def tail_row(ref, row):
    first = ref.shape[0] - TAIL + row
    return ref[first : first + 1, :]


def state_kernel(k_hbm, v_hbm, in_hbm, fo_hbm, *refs):
    *out_refs, k_ref, v_ref, in_ref, fo_ref, scalar_ref, arrived = refs
    copies = [
        pltpu.make_async_copy(source, target, arrived.at[place])
        for place, (source, target) in enumerate(
            ((fo_hbm, fo_ref), (in_hbm, in_ref), (k_hbm, k_ref), (v_hbm, v_ref))
        )
    ]
    for copy in copies:
        copy.start()
    heads, length = in_ref.shape
    key_dim = k_ref.shape[1] // heads
    value_dim = v_ref.shape[1] // heads
    parts = value_dim // LANES
    copies[0].wait()
    cumul = cumulative_rows(log_forget(fo_ref[...]))
    copies[1].wait()
    level = in_ref[...] - cumul
    level_top = jnp.max(level, axis=1, keepdims=True)
    decay = cumul[:, length - 1 : length]
    scalar_ref[0] = jnp.exp(level - level_top)
    scalar_ref[1] = jnp.broadcast_to(decay + level_top, (heads, length))
    scalar_ref[2] = jnp.broadcast_to(decay, (heads, length))
    copies[2].wait()
    copies[3].wait()
    me = member(heads)
    for step in range(heads):
        head = me ^ step
        keys = k_ref[:, pl.ds(pl.multiple_of(head * key_dim, LANES), key_dim)]
        values = v_ref[:, pl.ds(pl.multiple_of(head * value_dim, LANES), value_dim)]
        row, top, decay = (scalar_ref[place, pl.ds(head, 1), :] for place in range(3))
        high, low = split_two(keys.astype(jnp.float32).T * row)
        matrix = dot(
            jnp.concatenate([high, low], axis=1), jnp.concatenate([values, values], axis=0)
        )
        high, mid, low = split_three(row)
        vector = (dot(low, keys) + dot(mid, keys)) + dot(high, keys)
        for part in range(parts):
            out_ref = out_refs[part * heads + step]
            out_ref[0:key_dim, :] = matrix[:, part * LANES : (part + 1) * LANES]
            out_ref[key_dim:, :] = tail_rows(vector, top, decay)


def read_scalars(refs, scalar_ref, me):
    for step, ref in enumerate(refs):
        scalar_ref[0, pl.ds(me ^ step, 1), :] = tail_row(ref, TOP)
        scalar_ref[1, pl.ds(me ^ step, 1), :] = tail_row(ref, DECAY)
    count = len(refs)
    tops = [scalar_ref[0, place : place + 1, :] for place in range(count)]
    decays = [scalar_ref[1, place : place + 1, :] for place in range(count)]
    return tops, decays


def weights_of(tops, decays):
    moved, total = [], jnp.zeros_like(decays[0])
    for top, decay in zip(reversed(tops), reversed(decays)):
        moved.append(top + total)
        total = total + decay
    moved.reverse()
    joined = functools.reduce(jnp.maximum, moved)
    return [jnp.exp(top - joined) for top in moved], joined, total


def quad_kernel(order, *refs):
    *refs, out_ref, scalar_ref = refs
    refs = [refs[order.index(step)] for step in range(len(order))]
    me = member(len(refs))
    weights, top, decay = weights_of(*read_scalars(refs, scalar_ref, me))
    for place, weight in enumerate(weights):
        scalar_ref[0, place : place + 1, :] = weight
    total = 0.0
    for step, ref in enumerate(refs):
        total = total + scalar_ref[0, pl.ds(me ^ step, 1), :] * ref[...]
    put_state(out_ref, total, top, decay)


def later_side(axis, bit):
    return (lax.axis_index(axis) & bit) != 0


def extend(is_later, other_ref, before_ref):
    other_top = tail_row(other_ref, TOP)
    if before_ref is None:
        decay = jnp.where(is_later, tail_row(other_ref, DECAY), 0.0)
        return (
            jnp.where(is_later, other_ref[...], 0.0),
            jnp.where(is_later, other_top, floor_value),
            decay,
        )
    before_top = tail_row(before_ref, TOP)
    before_decay = tail_row(before_ref, DECAY)
    moved = other_top + before_decay
    top = jnp.where(is_later, jnp.maximum(moved, before_top), before_top)
    other_weight = jnp.where(is_later, jnp.exp(moved - top), 0.0)
    state = other_weight * other_ref[...] + jnp.exp(before_top - top) * before_ref[...]
    decay = jnp.where(is_later, tail_row(other_ref, DECAY), 0.0) + before_decay
    return state, top, decay


def butterfly_kernel(axis, bit, *refs):
    total_ref, other_ref, *before, out_total, out_before = refs
    is_later = later_side(axis, bit)
    own_top, own_decay = tail_row(total_ref, TOP), tail_row(total_ref, DECAY)
    other_top, other_decay = tail_row(other_ref, TOP), tail_row(other_ref, DECAY)
    own_moved = own_top + jnp.where(is_later, 0.0, other_decay)
    other_moved = other_top + jnp.where(is_later, own_decay, 0.0)
    top = jnp.maximum(own_moved, other_moved)
    total = (
        jnp.exp(own_moved - top) * total_ref[...] + jnp.exp(other_moved - top) * other_ref[...]
    )
    put_state(out_total, total, top, own_decay + other_decay)
    put_state(out_before, *extend(is_later, other_ref, before[0] if before else None))


def prefix_kernel(axis, bit, quad, parts, *refs):
    others, befores, refs = refs[:parts], refs[parts : 2 * parts], refs[2 * parts :]
    *refs, scalar_ref, weight_ref = refs
    pieces = [refs[part * quad : (part + 1) * quad] for part in range(parts)]
    out_refs = refs[parts * quad :]
    me = member(quad)
    is_later = later_side(axis, bit)
    starts = [extend(is_later, other, before) for other, before in zip(others, befores)]
    top = starts[0][1]
    tops, decays = read_scalars(pieces[0], scalar_ref, me)
    zero = jnp.zeros_like(top)
    rows = others[0].shape[0]
    for place in range(quad):
        weights, joined, _ = weights_of([top] + tops[:place], [zero] + decays[:place])
        weights += [zero] * (quad - place)
        for index, weight in enumerate(weights):
            weight_ref[place, index : index + 1, :] = weight
        scalar_ref[0, place : place + 1, :] = joined
    for step, out_ref in enumerate(out_refs):
        place = me ^ step
        weights = [weight_ref[place, pl.ds(1 + (me ^ index), 1), :] for index in range(quad)]
        for part, (start, _, _) in enumerate(starts):
            state = weight_ref[place, 0:1, :] * start
            for weight, piece in zip(weights, pieces[part]):
                state = state + weight * piece[...]
            first = part * (rows - TAIL)
            out_ref[first : first + rows - TAIL, :] = state[0 : rows - TAIL, :]
        vector = state[rows - TAIL : rows - TAIL + 1, :]
        tail = tail_rows(vector, scalar_ref[0, pl.ds(place, 1), :], zero)
        out_ref[out_ref.shape[0] - TAIL :, :] = tail


CUMUL, ROW_LEVEL, INNER_DEN = range(3)


def inner_kernel(q_ref, k_ref, v_ref, in_ref, fo_ref, num_ref, stat_ref):
    heads, length = in_ref.shape
    key_dim = q_ref.shape[1] // heads
    value_dim = v_ref.shape[1] // heads
    logf = log_forget(fo_ref[...])
    level = in_ref[...] - cumulative_rows(logf)
    cumul = cumulative_columns(logf)
    causal = triangle(length, True)
    for head in range(heads):
        queries = q_ref[:, head * key_dim : (head + 1) * key_dim]
        keys = k_ref[:, head * key_dim : (head + 1) * key_dim]
        values = v_ref[:, head * value_dim : (head + 1) * value_dim]
        scores = dot_last(queries, keys) * (key_dim**-0.5)
        masked = jnp.where(causal, level[head : head + 1, :], -jnp.inf)
        row_level = jnp.max(masked, axis=1, keepdims=True)
        weighted = jnp.exp(masked - row_level) * scores
        stat_ref[head, :, CUMUL : CUMUL + 1] = cumul[:, head : head + 1]
        stat_ref[head, :, ROW_LEVEL : ROW_LEVEL + 1] = row_level
        stat_ref[head, :, INNER_DEN : INNER_DEN + 1] = jnp.sum(weighted, axis=1, keepdims=True)
        num_ref[head] = dot(weighted.astype(jnp.bfloat16), values)


def add_carried(head, q_ref, num_ref, stat_ref, message_ref):
    length, value_dim = num_ref.shape[1:]
    key_dim = q_ref.shape[1] // num_ref.shape[0]
    parts = value_dim // LANES
    scaling = key_dim**-0.5
    query = q_ref[:, pl.ds(pl.multiple_of(head * key_dim, LANES), key_dim)]
    matrix = jnp.concatenate(
        [message_ref[part * key_dim : (part + 1) * key_dim, :] for part in range(parts)], 1
    )
    high, low = split_two(matrix)
    carried = dot(jnp.concatenate([query, query], axis=1), jnp.concatenate([high, low], axis=0))
    stats = stat_ref[head]
    cumul, row_level, inner_den = (stats[:, place : place + 1] for place in range(3))
    top = tail_row(message_ref, TOP)[:, 0:1]
    carried_den = jnp.sum(
        query.astype(jnp.float32) * tail_row(message_ref, VECTOR), axis=1, keepdims=True
    )
    joined = jnp.maximum(row_level, top)
    inner_factor = jnp.exp(row_level - joined)
    outer_factor = jnp.exp(top - joined) * scaling
    denom = inner_factor * inner_den + outer_factor * carried_den
    inverse = 1.0 / jnp.maximum(jnp.abs(denom), jnp.exp(-(cumul + joined)))
    return (inner_factor * inverse) * num_ref[head] + (outer_factor * inverse) * carried


def part_kernel(steps, q_ref, num_ref, stat_ref, *refs):
    me = member(num_ref.shape[0])
    count = len(steps)
    for step, message_ref, out_ref in zip(steps, refs[:count], refs[count:]):
        head = me ^ step
        out_ref[...] = add_carried(head, q_ref, num_ref, stat_ref, message_ref).astype(
            out_ref.dtype
        )


def last_kernel(q_ref, num_ref, stat_ref, message_ref, *refs):
    *done_refs, out_hbm, own_ref, done = refs
    heads, _, value_dim = num_ref.shape
    me = member(heads)

    def place(step, source):
        columns = pl.ds(pl.multiple_of((me ^ step) * value_dim, LANES), value_dim)
        copy = pltpu.make_async_copy(source, out_hbm.at[:, columns], done.at[step])
        copy.start()
        return copy

    copies = [place(step, ref) for step, ref in enumerate(done_refs)]
    own_ref[...] = add_carried(me ^ (heads - 1), q_ref, num_ref, stat_ref, message_ref).astype(
        own_ref.dtype
    )
    copies.append(place(heads - 1, own_ref))
    for copy in copies:
        copy.wait()


def swap(array, axis, step):
    count = lax.axis_size(axis)
    return lax.ppermute(array, axis, [(place, place ^ step) for place in range(count)])


def exchange(pieces):
    return [pieces[0]] + [
        swap(pieces[step], AXES[1], step) for step in range(1, len(pieces))
    ]


def on_device(groups, group_length, queries, key_vectors, value_vectors, input_gate, forget_gate):
    heads, length = input_gate.shape
    key_dim = queries.shape[1] // heads
    value_dim = value_vectors.shape[1] // heads
    parts = value_dim // LANES
    whole = jax.ShapeDtypeStruct((parts * key_dim + TAIL, LANES), jnp.float32)
    message = jax.ShapeDtypeStruct((key_dim + TAIL, LANES), jnp.float32)
    messages = (message,) * heads
    params = pltpu.CompilerParams(vmem_limit_bytes=48 * 1024 * 1024)
    hbm = pl.BlockSpec(memory_space=pltpu.HBM)
    scalars = pltpu.VMEM((3, heads, LANES), jnp.float32)
    output = jax.ShapeDtypeStruct((length, heads * value_dim), jnp.bfloat16)
    operands = (key_vectors, value_vectors, input_gate, forget_gate)
    levels = []
    for axis, bit, size in ((AXES[1], heads, group_length), (AXES[0], 1, groups)):
        while bit < size:
            levels.append((axis, bit))
            bit *= 2

    own = pl.pallas_call(
        state_kernel,
        out_shape=messages * parts,
        in_specs=[hbm] * len(operands),
        scratch_shapes=[pltpu.VMEM(array.shape, array.dtype) for array in operands]
        + [scalars, pltpu.SemaphoreType.DMA((len(operands),))],
        compiler_params=params,
    )(*(pltpu.with_memory_space_constraint(array, pltpu.HBM) for array in operands))
    inner_num, stats = pl.pallas_call(
        inner_kernel,
        out_shape=(
            jax.ShapeDtypeStruct((heads, length, value_dim), jnp.float32),
            jax.ShapeDtypeStruct((heads, length, 3), jnp.float32),
        ),
        compiler_params=params,
    )(queries, *operands)
    pieces = [exchange(own[part * heads : (part + 1) * heads]) for part in range(parts)]
    totals = []
    for part, chunk in enumerate(pieces):
        order = list(range(heads)) if part else [0, heads - 1, *range(1, heads - 1)]
        totals.append(
            pl.pallas_call(
                functools.partial(quad_kernel, order),
                out_shape=message,
                scratch_shapes=[scalars],
                compiler_params=params,
            )(*(chunk[step] for step in order))
        )
    before = [[] for _ in range(parts)]
    for axis, bit in levels[:-1]:
        join_level = pl.pallas_call(
            functools.partial(butterfly_kernel, axis, bit),
            out_shape=(message, message),
            compiler_params=params,
        )
        others = [swap(array, axis, bit) for array in totals]
        for part in range(parts):
            totals[part], *before[part] = join_level(totals[part], others[part], *before[part])
    others = [swap(array, *levels[-1]) for array in totals]
    starts = []
    for part in range(parts):
        starts += before[part]
    states = pl.pallas_call(
        functools.partial(prefix_kernel, *levels[-1], heads, parts),
        out_shape=(whole,) * heads,
        scratch_shapes=[scalars, pltpu.VMEM((heads, 1 + heads, LANES), jnp.float32)],
        compiler_params=params,
    )(*others, *starts, *(piece for chunk in pieces for piece in chunk))
    carried = exchange(states)
    column = jax.ShapeDtypeStruct((length, value_dim), output.dtype)
    columns = []
    for steps in [(0, 1)] + [(step,) for step in range(2, heads - 1)]:
        columns += pl.pallas_call(
            functools.partial(part_kernel, steps),
            out_shape=(column,) * len(steps),
            compiler_params=params,
        )(queries, inner_num, stats, *(carried[step] for step in steps))
    return pl.pallas_call(
        last_kernel,
        out_shape=output,
        out_specs=hbm,
        scratch_shapes=[
            pltpu.VMEM(column.shape, column.dtype),
            pltpu.SemaphoreType.DMA((heads,)),
        ],
        compiler_params=params,
    )(queries, inner_num, stats, carried[-1], *columns)


def solution(mesh):
    return jax.shard_map(
        functools.partial(on_device, mesh.shape["grp"], mesh.shape["seq"]),
        mesh=mesh,
        in_specs=(
            P(AXES, None),
            P(AXES, None),
            P(AXES, None),
            P(None, AXES),
            P(None, AXES),
        ),
        out_specs=P(AXES, None),
        check_vma=False,
    )
```

```python
import functools

import jax
import jax.numpy as jnp
from jax import lax
from jax.experimental import pallas as pl
from jax.experimental.pallas import tpu as pltpu
from jax.sharding import PartitionSpec as P

floor_value = -1e30
LANES = 128
AXES = ("grp", "seq")


def split_two(x):
    high = x.astype(jnp.bfloat16)
    low = (x - high.astype(jnp.float32)).astype(jnp.bfloat16)
    return high, low


def split_three(x):
    high = x.astype(jnp.bfloat16)
    rest = x - high.astype(jnp.float32)
    mid = rest.astype(jnp.bfloat16)
    low = (rest - mid.astype(jnp.float32)).astype(jnp.bfloat16)
    return high, mid, low


def dot(a, b):
    return jnp.dot(a, b, preferred_element_type=jnp.float32)


def dot_last(a, b):
    return lax.dot_general(a, b, (((1,), (1,)), ((), ())), preferred_element_type=jnp.float32)


def log_forget(forget):
    return jnp.minimum(forget, 0.0) - jnp.log1p(jnp.exp(-jnp.abs(forget)))


def triangle(length, lower):
    rows = lax.broadcasted_iota(jnp.int32, (length, length), 0)
    cols = lax.broadcasted_iota(jnp.int32, (length, length), 1)
    return rows >= cols if lower else rows <= cols


def cumulative_rows(logf):
    ones = triangle(logf.shape[1], False).astype(jnp.bfloat16)
    high, mid, low = split_three(logf)
    return (dot(low, ones) + dot(mid, ones)) + dot(high, ones)


def cumulative_columns(logf):
    ones = triangle(logf.shape[1], True).astype(jnp.bfloat16)
    high, mid, low = split_three(logf)
    return (dot_last(ones, low) + dot_last(ones, mid)) + dot_last(ones, high)


TAIL = 8
VECTOR, TOP, DECAY = range(3)


def member(quad):
    return lax.rem(lax.axis_index(AXES[1]), quad)


def tail_rows(vector, top, decay):
    rest = jnp.zeros((TAIL - 3, vector.shape[1]), jnp.float32)
    return jnp.concatenate([vector, top, decay, rest], axis=0)


def put_state(ref, state, top, decay):
    matrix_rows = ref.shape[0] - TAIL
    ref[0:matrix_rows, :] = state[0:matrix_rows, :]
    place = lax.broadcasted_iota(jnp.int32, (TAIL, ref.shape[1]), 0)
    tail = jnp.where(place == TOP, top, state[matrix_rows:, :])
    ref[matrix_rows:, :] = jnp.where(place == DECAY, decay, tail)


def tail_row(ref, row):
    first = ref.shape[0] - TAIL + row
    return ref[first : first + 1, :]


def state_kernel(k_hbm, v_hbm, in_hbm, fo_hbm, *refs):
    *out_refs, k_ref, v_ref, in_ref, fo_ref, scalar_ref, arrived = refs
    copies = [
        pltpu.make_async_copy(source, target, arrived.at[place])
        for place, (source, target) in enumerate(
            ((fo_hbm, fo_ref), (in_hbm, in_ref), (k_hbm, k_ref), (v_hbm, v_ref))
        )
    ]
    for copy in copies:
        copy.start()
    heads, length = in_ref.shape
    key_dim = k_ref.shape[1] // heads
    value_dim = v_ref.shape[1] // heads
    parts = value_dim // LANES
    copies[0].wait()
    cumul = cumulative_rows(log_forget(fo_ref[...]))
    copies[1].wait()
    level = in_ref[...] - cumul
    level_top = jnp.max(level, axis=1, keepdims=True)
    decay = cumul[:, length - 1 : length]
    scalar_ref[0] = jnp.exp(level - level_top)
    scalar_ref[1] = jnp.broadcast_to(decay + level_top, (heads, length))
    scalar_ref[2] = jnp.broadcast_to(decay, (heads, length))
    copies[2].wait()
    copies[3].wait()
    me = member(heads)
    for step in range(heads):
        head = me ^ step
        keys = k_ref[:, pl.ds(pl.multiple_of(head * key_dim, LANES), key_dim)]
        values = v_ref[:, pl.ds(pl.multiple_of(head * value_dim, LANES), value_dim)]
        row, top, decay = (scalar_ref[place, pl.ds(head, 1), :] for place in range(3))
        high, low = split_two(keys.astype(jnp.float32).T * row)
        matrix = dot(
            jnp.concatenate([high, low], axis=1), jnp.concatenate([values, values], axis=0)
        )
        high, mid, low = split_three(row)
        vector = (dot(low, keys) + dot(mid, keys)) + dot(high, keys)
        for part in range(parts):
            out_ref = out_refs[part * heads + step]
            out_ref[0:key_dim, :] = matrix[:, part * LANES : (part + 1) * LANES]
            out_ref[key_dim:, :] = tail_rows(vector, top, decay)


def read_scalars(refs, scalar_ref, me):
    for step, ref in enumerate(refs):
        scalar_ref[0, pl.ds(me ^ step, 1), :] = tail_row(ref, TOP)
        scalar_ref[1, pl.ds(me ^ step, 1), :] = tail_row(ref, DECAY)
    count = len(refs)
    tops = [scalar_ref[0, place : place + 1, :] for place in range(count)]
    decays = [scalar_ref[1, place : place + 1, :] for place in range(count)]
    return tops, decays


def weights_of(tops, decays):
    moved, total = [], jnp.zeros_like(decays[0])
    for top, decay in zip(reversed(tops), reversed(decays)):
        moved.append(top + total)
        total = total + decay
    moved.reverse()
    joined = functools.reduce(jnp.maximum, moved)
    return [jnp.exp(top - joined) for top in moved], joined, total


def quad_kernel(order, *refs):
    *refs, out_ref, scalar_ref = refs
    refs = [refs[order.index(step)] for step in range(len(order))]
    me = member(len(refs))
    weights, top, decay = weights_of(*read_scalars(refs, scalar_ref, me))
    for place, weight in enumerate(weights):
        scalar_ref[0, place : place + 1, :] = weight
    total = 0.0
    for step, ref in enumerate(refs):
        total = total + scalar_ref[0, pl.ds(me ^ step, 1), :] * ref[...]
    put_state(out_ref, total, top, decay)


def later_side(axis, bit):
    return (lax.axis_index(axis) & bit) != 0


def extend(is_later, other_ref, before_ref):
    other_top = tail_row(other_ref, TOP)
    if before_ref is None:
        decay = jnp.where(is_later, tail_row(other_ref, DECAY), 0.0)
        return (
            jnp.where(is_later, other_ref[...], 0.0),
            jnp.where(is_later, other_top, floor_value),
            decay,
        )
    before_top = tail_row(before_ref, TOP)
    before_decay = tail_row(before_ref, DECAY)
    moved = other_top + before_decay
    top = jnp.where(is_later, jnp.maximum(moved, before_top), before_top)
    other_weight = jnp.where(is_later, jnp.exp(moved - top), 0.0)
    state = other_weight * other_ref[...] + jnp.exp(before_top - top) * before_ref[...]
    decay = jnp.where(is_later, tail_row(other_ref, DECAY), 0.0) + before_decay
    return state, top, decay


def butterfly_kernel(axis, bit, *refs):
    total_ref, other_ref, *before, out_total, out_before = refs
    is_later = later_side(axis, bit)
    own_top, own_decay = tail_row(total_ref, TOP), tail_row(total_ref, DECAY)
    other_top, other_decay = tail_row(other_ref, TOP), tail_row(other_ref, DECAY)
    own_moved = own_top + jnp.where(is_later, 0.0, other_decay)
    other_moved = other_top + jnp.where(is_later, own_decay, 0.0)
    top = jnp.maximum(own_moved, other_moved)
    total = (
        jnp.exp(own_moved - top) * total_ref[...] + jnp.exp(other_moved - top) * other_ref[...]
    )
    put_state(out_total, total, top, own_decay + other_decay)
    put_state(out_before, *extend(is_later, other_ref, before[0] if before else None))


def prefix_kernel(axis, bit, quad, parts, *refs):
    others, befores, refs = refs[:parts], refs[parts : 2 * parts], refs[2 * parts :]
    *refs, scalar_ref, weight_ref = refs
    pieces = [refs[part * quad : (part + 1) * quad] for part in range(parts)]
    out_refs = refs[parts * quad :]
    me = member(quad)
    is_later = later_side(axis, bit)
    starts = [extend(is_later, other, before) for other, before in zip(others, befores)]
    top = starts[0][1]
    tops, decays = read_scalars(pieces[0], scalar_ref, me)
    zero = jnp.zeros_like(top)
    rows = others[0].shape[0]
    for place in range(quad):
        weights, joined, _ = weights_of([top] + tops[:place], [zero] + decays[:place])
        weights += [zero] * (quad - place)
        for index, weight in enumerate(weights):
            weight_ref[place, index : index + 1, :] = weight
        scalar_ref[0, place : place + 1, :] = joined
    for step, out_ref in enumerate(out_refs):
        place = me ^ step
        weights = [weight_ref[place, pl.ds(1 + (me ^ index), 1), :] for index in range(quad)]
        for part, (start, _, _) in enumerate(starts):
            state = weight_ref[place, 0:1, :] * start
            for weight, piece in zip(weights, pieces[part]):
                state = state + weight * piece[...]
            first = part * (rows - TAIL)
            out_ref[first : first + rows - TAIL, :] = state[0 : rows - TAIL, :]
        vector = state[rows - TAIL : rows - TAIL + 1, :]
        tail = tail_rows(vector, scalar_ref[0, pl.ds(place, 1), :], zero)
        out_ref[out_ref.shape[0] - TAIL :, :] = tail


CUMUL, ROW_LEVEL, INNER_DEN = range(3)


def inner_kernel(q_ref, k_ref, v_ref, in_ref, fo_ref, num_ref, stat_ref):
    heads, length = in_ref.shape
    key_dim = q_ref.shape[1] // heads
    value_dim = v_ref.shape[1] // heads
    logf = log_forget(fo_ref[...])
    level = in_ref[...] - cumulative_rows(logf)
    cumul = cumulative_columns(logf)
    causal = triangle(length, True)
    for head in range(heads):
        queries = q_ref[:, head * key_dim : (head + 1) * key_dim]
        keys = k_ref[:, head * key_dim : (head + 1) * key_dim]
        values = v_ref[:, head * value_dim : (head + 1) * value_dim]
        scores = dot_last(queries, keys) * (key_dim**-0.5)
        masked = jnp.where(causal, level[head : head + 1, :], -jnp.inf)
        row_level = jnp.max(masked, axis=1, keepdims=True)
        weighted = jnp.exp(masked - row_level) * scores
        stat_ref[head, :, CUMUL : CUMUL + 1] = cumul[:, head : head + 1]
        stat_ref[head, :, ROW_LEVEL : ROW_LEVEL + 1] = row_level
        stat_ref[head, :, INNER_DEN : INNER_DEN + 1] = jnp.sum(weighted, axis=1, keepdims=True)
        num_ref[head] = dot(weighted.astype(jnp.bfloat16), values)


def add_carried(head, q_ref, num_ref, stat_ref, message_ref):
    length, value_dim = num_ref.shape[1:]
    key_dim = q_ref.shape[1] // num_ref.shape[0]
    parts = value_dim // LANES
    scaling = key_dim**-0.5
    query = q_ref[:, pl.ds(pl.multiple_of(head * key_dim, LANES), key_dim)]
    matrix = jnp.concatenate(
        [message_ref[part * key_dim : (part + 1) * key_dim, :] for part in range(parts)], 1
    )
    high, low = split_two(matrix)
    carried = dot(jnp.concatenate([query, query], axis=1), jnp.concatenate([high, low], axis=0))
    stats = stat_ref[head]
    cumul, row_level, inner_den = (stats[:, place : place + 1] for place in range(3))
    top = tail_row(message_ref, TOP)[:, 0:1]
    carried_den = jnp.sum(
        query.astype(jnp.float32) * tail_row(message_ref, VECTOR), axis=1, keepdims=True
    )
    joined = jnp.maximum(row_level, top)
    inner_factor = jnp.exp(row_level - joined)
    outer_factor = jnp.exp(top - joined) * scaling
    denom = inner_factor * inner_den + outer_factor * carried_den
    inverse = 1.0 / jnp.maximum(jnp.abs(denom), jnp.exp(-(cumul + joined)))
    return (inner_factor * inverse) * num_ref[head] + (outer_factor * inverse) * carried


def part_kernel(steps, q_ref, num_ref, stat_ref, *refs):
    me = member(num_ref.shape[0])
    count = len(steps)
    for step, message_ref, out_ref in zip(steps, refs[:count], refs[count:]):
        head = me ^ step
        out_ref[...] = add_carried(head, q_ref, num_ref, stat_ref, message_ref).astype(
            out_ref.dtype
        )


def last_kernel(q_ref, num_ref, stat_ref, message_ref, *refs):
    *done_refs, out_hbm, own_ref, done = refs
    heads, _, value_dim = num_ref.shape
    me = member(heads)

    def place(step, source):
        columns = pl.ds(pl.multiple_of((me ^ step) * value_dim, LANES), value_dim)
        copy = pltpu.make_async_copy(source, out_hbm.at[:, columns], done.at[step])
        copy.start()
        return copy

    copies = [place(step, ref) for step, ref in enumerate(done_refs)]
    own_ref[...] = add_carried(me ^ (heads - 1), q_ref, num_ref, stat_ref, message_ref).astype(
        own_ref.dtype
    )
    copies.append(place(heads - 1, own_ref))
    for copy in copies:
        copy.wait()


def swap(array, axis, step):
    count = lax.axis_size(axis)
    return lax.ppermute(array, axis, [(place, place ^ step) for place in range(count)])


def exchange(pieces):
    return [pieces[0]] + [
        swap(pieces[step], AXES[1], step) for step in range(1, len(pieces))
    ]


def on_device(groups, group_length, queries, key_vectors, value_vectors, input_gate, forget_gate):
    heads, length = input_gate.shape
    key_dim = queries.shape[1] // heads
    value_dim = value_vectors.shape[1] // heads
    parts = value_dim // LANES
    whole = jax.ShapeDtypeStruct((parts * key_dim + TAIL, LANES), jnp.float32)
    message = jax.ShapeDtypeStruct((key_dim + TAIL, LANES), jnp.float32)
    messages = (message,) * heads
    params = pltpu.CompilerParams(vmem_limit_bytes=48 * 1024 * 1024)
    hbm = pl.BlockSpec(memory_space=pltpu.HBM)
    scalars = pltpu.VMEM((3, heads, LANES), jnp.float32)
    output = jax.ShapeDtypeStruct((length, heads * value_dim), jnp.bfloat16)
    operands = (key_vectors, value_vectors, input_gate, forget_gate)
    levels = []
    for axis, bit, size in ((AXES[1], heads, group_length), (AXES[0], 1, groups)):
        while bit < size:
            levels.append((axis, bit))
            bit *= 2

    own = pl.pallas_call(
        state_kernel,
        out_shape=messages * parts,
        in_specs=[hbm] * len(operands),
        scratch_shapes=[pltpu.VMEM(array.shape, array.dtype) for array in operands]
        + [scalars, pltpu.SemaphoreType.DMA((len(operands),))],
        compiler_params=params,
    )(*(pltpu.with_memory_space_constraint(array, pltpu.HBM) for array in operands))
    inner_num, stats = pl.pallas_call(
        inner_kernel,
        out_shape=(
            jax.ShapeDtypeStruct((heads, length, value_dim), jnp.float32),
            jax.ShapeDtypeStruct((heads, length, 3), jnp.float32),
        ),
        compiler_params=params,
    )(queries, *operands)
    pieces = [exchange(own[part * heads : (part + 1) * heads]) for part in range(parts)]
    totals = []
    for part, chunk in enumerate(pieces):
        order = list(range(heads)) if part else [0, *range(heads - 1, 0, -1)]
        totals.append(
            pl.pallas_call(
                functools.partial(quad_kernel, order),
                out_shape=message,
                scratch_shapes=[scalars],
                compiler_params=params,
            )(*(chunk[step] for step in order))
        )
    before = [[] for _ in range(parts)]
    for axis, bit in levels[:-1]:
        join_level = pl.pallas_call(
            functools.partial(butterfly_kernel, axis, bit),
            out_shape=(message, message),
            compiler_params=params,
        )
        others = [swap(array, axis, bit) for array in totals]
        for part in range(parts):
            totals[part], *before[part] = join_level(totals[part], others[part], *before[part])
    others = [swap(array, *levels[-1]) for array in totals]
    starts = []
    for part in range(parts):
        starts += before[part]
    states = pl.pallas_call(
        functools.partial(prefix_kernel, *levels[-1], heads, parts),
        out_shape=(whole,) * heads,
        scratch_shapes=[scalars, pltpu.VMEM((heads, 1 + heads, LANES), jnp.float32)],
        compiler_params=params,
    )(*others, *starts, *(piece for chunk in pieces for piece in chunk))
    carried = exchange(states)
    column = jax.ShapeDtypeStruct((length, value_dim), output.dtype)
    columns = []
    for steps in [(0, 1)] + [(step,) for step in range(2, heads - 1)]:
        columns += pl.pallas_call(
            functools.partial(part_kernel, steps),
            out_shape=(column,) * len(steps),
            compiler_params=params,
        )(queries, inner_num, stats, *(carried[step] for step in steps))
    return pl.pallas_call(
        last_kernel,
        out_shape=output,
        out_specs=hbm,
        scratch_shapes=[
            pltpu.VMEM(column.shape, column.dtype),
            pltpu.SemaphoreType.DMA((heads,)),
        ],
        compiler_params=params,
    )(queries, inner_num, stats, carried[-1], *columns)


def solution(mesh):
    return jax.shard_map(
        functools.partial(on_device, mesh.shape["grp"], mesh.shape["seq"]),
        mesh=mesh,
        in_specs=(
            P(AXES, None),
            P(AXES, None),
            P(AXES, None),
            P(None, AXES),
            P(None, AXES),
        ),
        out_specs=P(AXES, None),
        check_vma=False,
    )
```

```python
import functools

import jax
import jax.numpy as jnp
from jax import lax
from jax.experimental import pallas as pl
from jax.experimental.pallas import tpu as pltpu
from jax.sharding import PartitionSpec as P

floor_value = -1e30
LANES = 128
AXES = ("grp", "seq")


def split_two(x):
    high = x.astype(jnp.bfloat16)
    low = (x - high.astype(jnp.float32)).astype(jnp.bfloat16)
    return high, low


def split_three(x):
    high = x.astype(jnp.bfloat16)
    rest = x - high.astype(jnp.float32)
    mid = rest.astype(jnp.bfloat16)
    low = (rest - mid.astype(jnp.float32)).astype(jnp.bfloat16)
    return high, mid, low


def dot(a, b):
    return jnp.dot(a, b, preferred_element_type=jnp.float32)


def dot_last(a, b):
    return lax.dot_general(a, b, (((1,), (1,)), ((), ())), preferred_element_type=jnp.float32)


def log_forget(forget):
    return jnp.minimum(forget, 0.0) - jnp.log1p(jnp.exp(-jnp.abs(forget)))


def triangle(length, lower):
    rows = lax.broadcasted_iota(jnp.int32, (length, length), 0)
    cols = lax.broadcasted_iota(jnp.int32, (length, length), 1)
    return rows >= cols if lower else rows <= cols


def dot_exact(x, b):
    count = x.shape[0]
    terms = [term.astype(jnp.float32) for term in split_three(x)]
    stacked = dot(jnp.concatenate(terms, axis=0).astype(jnp.bfloat16), b)
    high, mid, low = (stacked[term * count : (term + 1) * count, :] for term in range(3))
    return (low + mid) + high


def cumulative_rows(logf):
    return dot_exact(logf, triangle(logf.shape[1], False).astype(jnp.bfloat16))


def cumulative_columns(logf):
    ones = triangle(logf.shape[1], True).astype(jnp.bfloat16)
    high, mid, low = split_three(logf)
    return (dot_last(ones, low) + dot_last(ones, mid)) + dot_last(ones, high)


TAIL = 8
VECTOR, TOP, DECAY = range(3)


def member(quad):
    return lax.rem(lax.axis_index(AXES[1]), quad)


def tail_rows(vector, top, decay):
    rest = jnp.zeros((TAIL - 3, vector.shape[1]), jnp.float32)
    return jnp.concatenate([vector, top, decay, rest], axis=0)


def put_state(ref, state, top, decay):
    matrix_rows = ref.shape[0] - TAIL
    ref[0:matrix_rows, :] = state[0:matrix_rows, :]
    place = lax.broadcasted_iota(jnp.int32, (TAIL, ref.shape[1]), 0)
    tail = jnp.where(place == TOP, top, state[matrix_rows:, :])
    ref[matrix_rows:, :] = jnp.where(place == DECAY, decay, tail)


def tail_row(ref, row):
    first = ref.shape[0] - TAIL + row
    return ref[first : first + 1, :]


def state_kernel(k_hbm, v_hbm, in_hbm, fo_hbm, *refs):
    *out_refs, k_ref, v_ref, in_ref, fo_ref, scalar_ref, arrived = refs
    copies = [
        pltpu.make_async_copy(source, target, arrived.at[place])
        for place, (source, target) in enumerate(
            ((fo_hbm, fo_ref), (in_hbm, in_ref), (k_hbm, k_ref), (v_hbm, v_ref))
        )
    ]
    for copy in copies:
        copy.start()
    heads, length = in_ref.shape
    key_dim = k_ref.shape[1] // heads
    value_dim = v_ref.shape[1] // heads
    parts = value_dim // LANES
    copies[0].wait()
    cumul = cumulative_rows(log_forget(fo_ref[...]))
    copies[1].wait()
    level = in_ref[...] - cumul
    level_top = jnp.max(level, axis=1, keepdims=True)
    decay = cumul[:, length - 1 : length]
    scalar_ref[0] = jnp.exp(level - level_top)
    scalar_ref[1] = jnp.broadcast_to(decay + level_top, (heads, length))
    scalar_ref[2] = jnp.broadcast_to(decay, (heads, length))
    copies[2].wait()
    copies[3].wait()
    me = member(heads)
    for step in range(heads):
        head = me ^ step
        keys = k_ref[:, pl.ds(pl.multiple_of(head * key_dim, LANES), key_dim)]
        values = v_ref[:, pl.ds(pl.multiple_of(head * value_dim, LANES), value_dim)]
        row, top, decay = (scalar_ref[place, pl.ds(head, 1), :] for place in range(3))
        high, low = split_two(keys.astype(jnp.float32).T * row)
        matrix = dot(
            jnp.concatenate([high, low], axis=1), jnp.concatenate([values, values], axis=0)
        )
        vector = dot_exact(row, keys)
        for part in range(parts):
            out_ref = out_refs[part * heads + step]
            out_ref[0:key_dim, :] = matrix[:, part * LANES : (part + 1) * LANES]
            out_ref[key_dim:, :] = tail_rows(vector, top, decay)


def read_scalars(refs, scalar_ref, me):
    for step, ref in enumerate(refs):
        scalar_ref[0, pl.ds(me ^ step, 1), :] = tail_row(ref, TOP)
        scalar_ref[1, pl.ds(me ^ step, 1), :] = tail_row(ref, DECAY)
    count = len(refs)
    tops = [scalar_ref[0, place : place + 1, :] for place in range(count)]
    decays = [scalar_ref[1, place : place + 1, :] for place in range(count)]
    return tops, decays


def weights_of(tops, decays):
    moved, total = [], jnp.zeros_like(decays[0])
    for top, decay in zip(reversed(tops), reversed(decays)):
        moved.append(top + total)
        total = total + decay
    moved.reverse()
    joined = functools.reduce(jnp.maximum, moved)
    return [jnp.exp(top - joined) for top in moved], joined, total


def quad_kernel(order, *refs):
    *refs, out_ref, scalar_ref = refs
    refs = [refs[order.index(step)] for step in range(len(order))]
    me = member(len(refs))
    weights, top, decay = weights_of(*read_scalars(refs, scalar_ref, me))
    for place, weight in enumerate(weights):
        scalar_ref[0, place : place + 1, :] = weight
    total = 0.0
    for step, ref in enumerate(refs):
        total = total + scalar_ref[0, pl.ds(me ^ step, 1), :] * ref[...]
    put_state(out_ref, total, top, decay)


def later_side(axis, bit):
    return (lax.axis_index(axis) & bit) != 0


def extend(is_later, other_ref, before_ref):
    other_top = tail_row(other_ref, TOP)
    if before_ref is None:
        decay = jnp.where(is_later, tail_row(other_ref, DECAY), 0.0)
        return (
            jnp.where(is_later, other_ref[...], 0.0),
            jnp.where(is_later, other_top, floor_value),
            decay,
        )
    before_top = tail_row(before_ref, TOP)
    before_decay = tail_row(before_ref, DECAY)
    moved = other_top + before_decay
    top = jnp.where(is_later, jnp.maximum(moved, before_top), before_top)
    other_weight = jnp.where(is_later, jnp.exp(moved - top), 0.0)
    state = other_weight * other_ref[...] + jnp.exp(before_top - top) * before_ref[...]
    decay = jnp.where(is_later, tail_row(other_ref, DECAY), 0.0) + before_decay
    return state, top, decay


def butterfly_kernel(axis, bit, *refs):
    total_ref, other_ref, *before, out_total, out_before = refs
    is_later = later_side(axis, bit)
    own_top, own_decay = tail_row(total_ref, TOP), tail_row(total_ref, DECAY)
    other_top, other_decay = tail_row(other_ref, TOP), tail_row(other_ref, DECAY)
    own_moved = own_top + jnp.where(is_later, 0.0, other_decay)
    other_moved = other_top + jnp.where(is_later, own_decay, 0.0)
    top = jnp.maximum(own_moved, other_moved)
    total = (
        jnp.exp(own_moved - top) * total_ref[...] + jnp.exp(other_moved - top) * other_ref[...]
    )
    put_state(out_total, total, top, own_decay + other_decay)
    put_state(out_before, *extend(is_later, other_ref, before[0] if before else None))


def prefix_kernel(axis, bit, quad, parts, *refs):
    others, befores, refs = refs[:parts], refs[parts : 2 * parts], refs[2 * parts :]
    *refs, scalar_ref, weight_ref = refs
    pieces = [refs[part * quad : (part + 1) * quad] for part in range(parts)]
    out_refs = refs[parts * quad :]
    me = member(quad)
    is_later = later_side(axis, bit)
    starts = [extend(is_later, other, before) for other, before in zip(others, befores)]
    top = starts[0][1]
    tops, decays = read_scalars(pieces[0], scalar_ref, me)
    zero = jnp.zeros_like(top)
    rows = others[0].shape[0]
    for place in range(quad):
        weights, joined, _ = weights_of([top] + tops[:place], [zero] + decays[:place])
        weights += [zero] * (quad - place)
        for index, weight in enumerate(weights):
            weight_ref[place, index : index + 1, :] = weight
        scalar_ref[0, place : place + 1, :] = joined
    for step, out_ref in enumerate(out_refs):
        place = me ^ step
        weights = [weight_ref[place, pl.ds(1 + (me ^ index), 1), :] for index in range(quad)]
        for part, (start, _, _) in enumerate(starts):
            state = weight_ref[place, 0:1, :] * start
            for weight, piece in zip(weights, pieces[part]):
                state = state + weight * piece[...]
            first = part * (rows - TAIL)
            out_ref[first : first + rows - TAIL, :] = state[0 : rows - TAIL, :]
        vector = state[rows - TAIL : rows - TAIL + 1, :]
        tail = tail_rows(vector, scalar_ref[0, pl.ds(place, 1), :], zero)
        out_ref[out_ref.shape[0] - TAIL :, :] = tail


CUMUL, ROW_LEVEL, INNER_DEN = range(3)


def inner_kernel(q_ref, k_ref, v_ref, in_ref, fo_ref, num_ref, stat_ref):
    heads, length = in_ref.shape
    key_dim = q_ref.shape[1] // heads
    value_dim = v_ref.shape[1] // heads
    logf = log_forget(fo_ref[...])
    level = in_ref[...] - cumulative_rows(logf)
    cumul = cumulative_columns(logf)
    causal = triangle(length, True)
    for head in range(heads):
        queries = q_ref[:, head * key_dim : (head + 1) * key_dim]
        keys = k_ref[:, head * key_dim : (head + 1) * key_dim]
        values = v_ref[:, head * value_dim : (head + 1) * value_dim]
        scores = dot_last(queries, keys) * (key_dim**-0.5)
        masked = jnp.where(causal, level[head : head + 1, :], -jnp.inf)
        row_level = jnp.max(masked, axis=1, keepdims=True)
        weighted = jnp.exp(masked - row_level) * scores
        stat_ref[head, :, CUMUL : CUMUL + 1] = cumul[:, head : head + 1]
        stat_ref[head, :, ROW_LEVEL : ROW_LEVEL + 1] = row_level
        stat_ref[head, :, INNER_DEN : INNER_DEN + 1] = jnp.sum(weighted, axis=1, keepdims=True)
        num_ref[head] = dot(weighted.astype(jnp.bfloat16), values)


def add_carried(head, q_ref, num_ref, stat_ref, message_ref):
    length, value_dim = num_ref.shape[1:]
    key_dim = q_ref.shape[1] // num_ref.shape[0]
    parts = value_dim // LANES
    scaling = key_dim**-0.5
    query = q_ref[:, pl.ds(pl.multiple_of(head * key_dim, LANES), key_dim)]
    matrix = jnp.concatenate(
        [message_ref[part * key_dim : (part + 1) * key_dim, :] for part in range(parts)], 1
    )
    high, low = split_two(matrix)
    carried = dot(jnp.concatenate([query, query], axis=1), jnp.concatenate([high, low], axis=0))
    stats = stat_ref[head]
    cumul, row_level, inner_den = (stats[:, place : place + 1] for place in range(3))
    top = tail_row(message_ref, TOP)[:, 0:1]
    carried_den = jnp.sum(
        query.astype(jnp.float32) * tail_row(message_ref, VECTOR), axis=1, keepdims=True
    )
    joined = jnp.maximum(row_level, top)
    inner_factor = jnp.exp(row_level - joined)
    outer_factor = jnp.exp(top - joined) * scaling
    denom = inner_factor * inner_den + outer_factor * carried_den
    inverse = 1.0 / jnp.maximum(jnp.abs(denom), jnp.exp(-(cumul + joined)))
    return (inner_factor * inverse) * num_ref[head] + (outer_factor * inverse) * carried


def part_kernel(steps, q_ref, num_ref, stat_ref, *refs):
    me = member(num_ref.shape[0])
    count = len(steps)
    for step, message_ref, out_ref in zip(steps, refs[:count], refs[count:]):
        head = me ^ step
        out_ref[...] = add_carried(head, q_ref, num_ref, stat_ref, message_ref).astype(
            out_ref.dtype
        )


def last_kernel(q_ref, num_ref, stat_ref, message_ref, *refs):
    *done_refs, out_hbm, own_ref, done = refs
    heads, _, value_dim = num_ref.shape
    me = member(heads)

    def place(step, source):
        columns = pl.ds(pl.multiple_of((me ^ step) * value_dim, LANES), value_dim)
        copy = pltpu.make_async_copy(source, out_hbm.at[:, columns], done.at[step])
        copy.start()
        return copy

    copies = [place(step, ref) for step, ref in enumerate(done_refs)]
    own_ref[...] = add_carried(me ^ (heads - 1), q_ref, num_ref, stat_ref, message_ref).astype(
        own_ref.dtype
    )
    copies.append(place(heads - 1, own_ref))
    for copy in copies:
        copy.wait()


def swap(array, axis, step):
    count = lax.axis_size(axis)
    return lax.ppermute(array, axis, [(place, place ^ step) for place in range(count)])


def exchange(pieces):
    return [pieces[0]] + [
        swap(pieces[step], AXES[1], step) for step in range(1, len(pieces))
    ]


def on_device(groups, group_length, queries, key_vectors, value_vectors, input_gate, forget_gate):
    heads, length = input_gate.shape
    key_dim = queries.shape[1] // heads
    value_dim = value_vectors.shape[1] // heads
    parts = value_dim // LANES
    whole = jax.ShapeDtypeStruct((parts * key_dim + TAIL, LANES), jnp.float32)
    message = jax.ShapeDtypeStruct((key_dim + TAIL, LANES), jnp.float32)
    messages = (message,) * heads
    params = pltpu.CompilerParams(vmem_limit_bytes=48 * 1024 * 1024)
    hbm = pl.BlockSpec(memory_space=pltpu.HBM)
    scalars = pltpu.VMEM((3, heads, LANES), jnp.float32)
    output = jax.ShapeDtypeStruct((length, heads * value_dim), jnp.bfloat16)
    operands = (key_vectors, value_vectors, input_gate, forget_gate)
    levels = []
    for axis, bit, size in ((AXES[1], heads, group_length), (AXES[0], 1, groups)):
        while bit < size:
            levels.append((axis, bit))
            bit *= 2

    own = pl.pallas_call(
        state_kernel,
        out_shape=messages * parts,
        in_specs=[hbm] * len(operands),
        scratch_shapes=[pltpu.VMEM(array.shape, array.dtype) for array in operands]
        + [scalars, pltpu.SemaphoreType.DMA((len(operands),))],
        compiler_params=params,
    )(*(pltpu.with_memory_space_constraint(array, pltpu.HBM) for array in operands))
    inner_num, stats = pl.pallas_call(
        inner_kernel,
        out_shape=(
            jax.ShapeDtypeStruct((heads, length, value_dim), jnp.float32),
            jax.ShapeDtypeStruct((heads, length, 3), jnp.float32),
        ),
        compiler_params=params,
    )(queries, *operands)
    pieces = [exchange(own[part * heads : (part + 1) * heads]) for part in range(parts)]
    totals = []
    for part, chunk in enumerate(pieces):
        order = list(range(heads)) if part else [0, heads - 1, *range(1, heads - 1)]
        totals.append(
            pl.pallas_call(
                functools.partial(quad_kernel, order),
                out_shape=message,
                scratch_shapes=[scalars],
                compiler_params=params,
            )(*(chunk[step] for step in order))
        )
    before = [[] for _ in range(parts)]
    for axis, bit in levels[:-1]:
        join_level = pl.pallas_call(
            functools.partial(butterfly_kernel, axis, bit),
            out_shape=(message, message),
            compiler_params=params,
        )
        others = [swap(array, axis, bit) for array in totals]
        for part in range(parts):
            totals[part], *before[part] = join_level(totals[part], others[part], *before[part])
    others = [swap(array, *levels[-1]) for array in totals]
    starts = []
    for part in range(parts):
        starts += before[part]
    states = pl.pallas_call(
        functools.partial(prefix_kernel, *levels[-1], heads, parts),
        out_shape=(whole,) * heads,
        scratch_shapes=[scalars, pltpu.VMEM((heads, 1 + heads, LANES), jnp.float32)],
        compiler_params=params,
    )(*others, *starts, *(piece for chunk in pieces for piece in chunk))
    carried = exchange(states)
    column = jax.ShapeDtypeStruct((length, value_dim), output.dtype)
    columns = []
    for steps in [(0, 1)] + [(step,) for step in range(2, heads - 1)]:
        columns += pl.pallas_call(
            functools.partial(part_kernel, steps),
            out_shape=(column,) * len(steps),
            compiler_params=params,
        )(queries, inner_num, stats, *(carried[step] for step in steps))
    return pl.pallas_call(
        last_kernel,
        out_shape=output,
        out_specs=hbm,
        scratch_shapes=[
            pltpu.VMEM(column.shape, column.dtype),
            pltpu.SemaphoreType.DMA((heads,)),
        ],
        compiler_params=params,
    )(queries, inner_num, stats, carried[-1], *columns)


def solution(mesh):
    return jax.shard_map(
        functools.partial(on_device, mesh.shape["grp"], mesh.shape["seq"]),
        mesh=mesh,
        in_specs=(
            P(AXES, None),
            P(AXES, None),
            P(AXES, None),
            P(None, AXES),
            P(None, AXES),
        ),
        out_specs=P(AXES, None),
        check_vma=False,
    )
```
